32 devices in a mesh: head: 4 (over y, x), wide: 8 (over z, core).
Axes of the slice: x: 2, y: 2, z: 4, core: 2. Of those that a mesh axis runs over, the one named last changes fastest.
Arguments:
- inputs: bfloat16 [4096, 2048], P(('head', 'wide')), may hold values from -6 to 6
- attn_gain: float32 [2048], replicated, may hold values from 0.1 to 1.9
- query_weight: bfloat16 [2048, 2048], P(None, 'head'), may hold values from -0.125 to 0.125
- key_projection: bfloat16 [2048, 1024], P(None, 'head'), may hold values from -0.125 to 0.125
- value_projection: bfloat16 [2048, 1024], P(None, 'head'), may hold values from -0.125 to 0.125
- attn_gate_weight: bfloat16 [2048, 2048], P(None, 'head'), may hold values from -0.125 to 0.125
- output_weight: bfloat16 [2048, 2048], P('head'), may hold values from -1.5 to 1.5
- query_gain: float32 [128], replicated, may hold values from 0.1 to 1.9
- key_gain: float32 [128], replicated, may hold values from 0.1 to 1.9
- ffn_gain: float32 [2048], replicated, may hold values from 0.1 to 1.9
- ffn_gate_weight: bfloat16 [2048, 6144], P(None, 'wide'), may hold values from -0.125 to 0.125
- ffn_up_weight: bfloat16 [2048, 6144], P(None, 'wide'), may hold values from -0.125 to 0.125
- ffn_down_weight: bfloat16 [6144, 2048], P('wide'), may hold values from -0.109375 to 0.109375
- doc_lengths: int32 [1, 8], replicated, may hold values from 1 to 2560, 4096 in all within a row
- cotangent: bfloat16 [4096, 2048], P(('head', 'wide')), may hold values from -11 to 11
Outputs:
- outputs: bfloat16 [4096, 2048], P(('head', 'wide'))
- input_grad: float32 [4096, 2048], P(('head', 'wide'))
- attn_gain_grad: float32 [2048], replicated
- query_grad: float32 [2048, 2048], P('wide', 'head')
- key_grad: float32 [2048, 1024], P('wide', 'head')
- value_grad: float32 [2048, 1024], P('wide', 'head')
- attn_gate_grad: float32 [2048, 2048], P('wide', 'head')
- output_grad: float32 [2048, 2048], P('head', 'wide')
- query_gain_grad: float32 [128], replicated
- key_gain_grad: float32 [128], replicated
- ffn_gain_grad: float32 [2048], replicated
- ffn_gate_grad: float32 [2048, 6144], P('head', 'wide')
- ffn_up_grad: float32 [2048, 6144], P('head', 'wide')
- ffn_down_grad: float32 [6144, 2048], P('wide', 'head')
The draws below stay inside these ranges and needn't reach their ends.
Inputs may be any that keep to these rules, and one draw needn't show every extreme that they name: `doc_lengths`: each row's 8 lengths sum to 4096, and the longest of each row is 2560.
All inputs are finite; a program needn't handle non-finite values.
Results may differ from the reference program's by a relative error of at most 0.024.
Values may be sent and summed in bfloat16 or wider, within the bound.
A program may use at most 256 MiB of HBM per device.

```python
import math
import jax
import jax.numpy as jnp
import numpy as np
from jax import lax

EMBED_WIDTH = 2048
QUERY_HEADS = 16
KEY_VALUE_HEADS = 8
HEAD_SIZE = 128
FF = 6144
DOCS = 8
PACKED_LENGTH = 4096
MOST_DOC = 2560
TOKENS = 4096
PACKED_ROWS = 1


def draw_cotangent(key, part):
    key = jax.random.fold_in(key, 7)
    row_frac = jnp.arange(TOKENS, dtype=jnp.float32) / TOKENS
    raw_draw = jnp.clip(jax.random.normal(key, (TOKENS, EMBED_WIDTH), jnp.float32), -6.0, 6.0)
    row_scale = 0.6 + 1.2 * row_frac
    return (raw_draw * row_scale[:, None]).astype(jnp.bfloat16)


def levels(rng, dims, shards, least, high):
    loudness = 1.0
    for dim, shards_of in shards:
        steps = jax.random.uniform(jax.random.fold_in(jax.random.fold_in(rng, 6), dim), (shards_of,), jnp.float32, least / len(shards), high / len(shards))
        loudness = loudness * jnp.repeat(jnp.exp(steps), dims[dim] // shards_of).reshape((-1,) + (1,) * (len(dims) - 1 - dim))
    return loudness


def split_up(amount, total, limit, slope):
    weights = [(1 << 20) // math.isqrt(grade ** slope) + 1 for grade in range(2, amount + 1)]
    surplus, holding = total - limit - (amount - 1), [1] * (amount - 1)
    while surplus > 0:
        movable = [i for i in range(amount - 1) if holding[i] < limit]
        mass, left = sum([weights[i] for i in movable]), surplus
        for i in movable:
            more = min(limit - holding[i], max(1, left * weights[i] // mass), surplus)
            holding[i] = holding[i] + more
            surplus = surplus - more
    return np.array([limit] + holding)


def uneven_parts(own_key, amount, total, bound, skew):
    if amount == 2:
        one = jax.random.randint(own_key, (), max(1, total - bound), min(bound, total - 1) + 1)
        return jnp.stack([one, total - one])
    sizes = jnp.asarray(split_up(amount, total, bound, skew), jnp.int32)
    couples = (amount - 1) // 2
    donor, receiver = sizes[1:1 + 2 * couples:2], sizes[2:2 + 2 * couples:2]
    margin = jnp.minimum(donor - 1, bound - receiver)
    passed = jax.random.randint(jax.random.fold_in(own_key, 1), (couples,), 0, 1 << 20) % (margin + 1)
    sizes = sizes.at[1:1 + 2 * couples:2].set(donor - passed).at[2:2 + 2 * couples:2].set(receiver + passed)
    return sizes[jax.random.permutation(jax.random.fold_in(own_key, 2), amount)]


def scatter_about(rng, dims, width, limit, split=(), kind=jnp.bfloat16):
    gain = levels(rng, dims, split, -0.22, 0.18) if split else 1.0
    entries = jax.random.normal(rng, dims, jnp.float32) * width * gain
    return jnp.minimum(jnp.maximum(entries, -limit), limit).astype(kind)


def setup_inputs(seed: int = 0) -> dict:
    seeds = jax.random.split(jax.random.key(seed), 16)
    return {
        "inputs": scatter_about(seeds[0], (TOKENS, EMBED_WIDTH), 1.0, 6.0, ((0, 32),)),
        "attn_gain": jnp.clip(1.0 + 0.18 * jax.random.normal(seeds[1], (EMBED_WIDTH,), jnp.float32), 0.1, 1.9),
        "query_weight": scatter_about(seeds[2], (EMBED_WIDTH, QUERY_HEADS * HEAD_SIZE), EMBED_WIDTH ** -0.5, 0.125, ((1, 4),)),
        "key_projection": scatter_about(seeds[3], (EMBED_WIDTH, KEY_VALUE_HEADS * HEAD_SIZE), EMBED_WIDTH ** -0.5, 0.125, ((1, 4),)),
        "value_projection": scatter_about(seeds[4], (EMBED_WIDTH, KEY_VALUE_HEADS * HEAD_SIZE), EMBED_WIDTH ** -0.5, 0.125, ((1, 4),)),
        "attn_gate_weight": scatter_about(seeds[5], (EMBED_WIDTH, QUERY_HEADS * HEAD_SIZE), EMBED_WIDTH ** -0.5, 0.125, ((1, 4),)),
        "output_weight": scatter_about(seeds[6], (QUERY_HEADS * HEAD_SIZE, EMBED_WIDTH), (max(EMBED_WIDTH // 128, 4)) ** -0.5, 1.5, ((0, 4),)),
        "query_gain": jnp.clip(1.0 + 0.18 * jax.random.normal(seeds[7], (HEAD_SIZE,), jnp.float32), 0.1, 1.9),
        "key_gain": jnp.clip(1.0 + 0.18 * jax.random.normal(seeds[8], (HEAD_SIZE,), jnp.float32), 0.1, 1.9),
        "ffn_gain": jnp.clip(1.0 + 0.18 * jax.random.normal(seeds[9], (EMBED_WIDTH,), jnp.float32), 0.1, 1.9),
        "ffn_gate_weight": scatter_about(seeds[10], (EMBED_WIDTH, FF), EMBED_WIDTH ** -0.5, 0.125, ((1, 8),)),
        "ffn_up_weight": scatter_about(seeds[11], (EMBED_WIDTH, FF), EMBED_WIDTH ** -0.5, 0.125, ((1, 8),)),
        "ffn_down_weight": scatter_about(seeds[12], (FF, EMBED_WIDTH), (FF // 2) ** -0.5, 0.109375, ((0, 8),)),
        "doc_lengths": jax.vmap(lambda own: uneven_parts(own, DOCS, PACKED_LENGTH, MOST_DOC, 2))(jax.random.split(seeds[13], PACKED_ROWS)).reshape((PACKED_ROWS, DOCS)).astype(jnp.int32),
        "cotangent": draw_cotangent(jax.random.fold_in(seeds[15], 71), 0),
    }


EPS = 1e-06
THETA = 1000000.0
NEG = -1e+30
HIGH = lax.Precision.HIGHEST

@jax.custom_vjp
def low(v):
    return lax.optimization_barrier(v.astype(jnp.bfloat16)).astype(jnp.float32)

@jax.custom_vjp
def low_back(v):
    return v

def low_keep(v):
    return (low(v), None)

def low_pass(kept, grad):
    return (grad,)

def back_keep(v):
    return (v, None)

def back_low(kept, grad):
    return (low(grad),)
low.defvjp(low_keep, low_pass)
low_back.defvjp(back_keep, back_low)

def matmul(left_mat, right_mat):
    return jnp.dot(left_mat, right_mat, precision=HIGH, preferred_element_type=jnp.float32)

def rms_apply(values, gain_vec):
    return values * lax.rsqrt(lax.optimization_barrier(jnp.mean(values * values, axis=-1, keepdims=True)) + EPS) * gain_vec

def token_tables(doc_lengths, token_ids):
    lengths = doc_lengths.reshape(-1).astype(jnp.int32)
    doc_ends = jnp.cumsum(lengths).astype(jnp.int32)
    before = doc_ends[None, :] <= token_ids[:, None]
    document_segment = lax.optimization_barrier(jnp.sum(before.astype(jnp.int32), axis=1)).astype(jnp.int32)
    doc_first = lax.optimization_barrier(jnp.sum(jnp.where(before, lengths[None, :], 0), axis=1)).astype(jnp.int32)
    return (document_segment, token_ids - doc_first)

def rotary(position, head_width):
    half_width = head_width // 2
    inverse = THETA ** (-(jnp.arange(half_width, dtype=jnp.float32) * 2.0 / head_width))
    angles = position.astype(jnp.float32)[:, None] * inverse[None, :]
    cosine = jnp.cos(angles)
    sine_tab = jnp.sin(angles)
    return (jnp.concatenate([cosine, cosine], axis=1), jnp.concatenate([sine_tab, sine_tab], axis=1))

def head_prep(pre_proj, gain_vec, cosine, sine_tab):
    row_count = pre_proj.shape[0]
    head_width = gain_vec.shape[0]
    half_width = head_width // 2
    per_head = rms_apply(pre_proj.reshape(row_count, -1, head_width), gain_vec)
    turned = jnp.concatenate([-per_head[..., half_width:], per_head[..., :half_width]], axis=-1)
    rotated = per_head * cosine[:, None, :] + turned * sine_tab[:, None, :]
    return rotated.reshape(row_count, -1)

def attend_group(query_grp, key_grp, value_grp, allowed):
    raw_scores = jnp.einsum('qhd,kd->hqk', query_grp, key_grp, precision=HIGH)
    raw_scores = low_back(raw_scores)
    scores = jnp.where(allowed[None], raw_scores * query_grp.shape[-1] ** (-0.5), NEG)
    prob_low = low(jax.nn.softmax(scores, axis=-1))
    return jnp.einsum('hqk,kd->qhd', prob_low, value_grp, precision=HIGH)

def attend_row(query_single_row, key_single_row, value_single_row, segment_row):
    length_per_row = query_single_row.shape[0]
    positions = jnp.arange(length_per_row, dtype=jnp.int32)
    allowed = (segment_row[:, None] == segment_row[None, :]) & (positions[None, :] <= positions[:, None])
    query_per_head = query_single_row.reshape(length_per_row, KEY_VALUE_HEADS, QUERY_HEADS // KEY_VALUE_HEADS, HEAD_SIZE).transpose(1, 0, 2, 3)
    key_per_head = key_single_row.reshape(length_per_row, KEY_VALUE_HEADS, HEAD_SIZE).transpose(1, 0, 2)
    value_per_head = value_single_row.reshape(length_per_row, KEY_VALUE_HEADS, HEAD_SIZE).transpose(1, 0, 2)
    checked = jax.checkpoint(attend_group)

    def group_call(operands):
        return checked(operands[0], operands[1], operands[2], allowed)
    result = lax.map(group_call, (query_per_head, key_per_head, value_per_head))
    return result.transpose(1, 0, 2, 3).reshape(length_per_row, QUERY_HEADS * HEAD_SIZE)

def attend_all(query_entire, key_entire, value_entire, document_segment):

    def row_invocation(operands):
        return attend_row(operands[0], operands[1], operands[2], operands[3])
    stacked_rows = lax.map(row_invocation, (query_entire.reshape(PACKED_ROWS, PACKED_LENGTH, QUERY_HEADS * HEAD_SIZE), key_entire.reshape(PACKED_ROWS, PACKED_LENGTH, KEY_VALUE_HEADS * HEAD_SIZE), value_entire.reshape(PACKED_ROWS, PACKED_LENGTH, KEY_VALUE_HEADS * HEAD_SIZE), document_segment.reshape(PACKED_ROWS, PACKED_LENGTH)))
    return stacked_rows.reshape(TOKENS, QUERY_HEADS * HEAD_SIZE)

def reference(inputs, attn_gain, query_weight, key_projection, value_projection, attn_gate_weight, output_weight, query_gain, key_gain, ffn_gain, ffn_gate_weight, ffn_up_weight, ffn_down_weight, doc_lengths, cotangent):
    token_ids = jnp.arange(TOKENS, dtype=jnp.int32)
    document_segment, position = token_tables(doc_lengths, token_ids)
    cosine, sine_tab = rotary(position, HEAD_SIZE)

    def block_forward(block_in, input_scale, query_mat, key_mat, value_mat, gate_mat, out_mat, query_scale, key_scale, ffn_scale, ffn_gate_mat, ffn_up_mat, ffn_down_mat):
        normed = low(rms_apply(block_in, input_scale))
        query_pre = low_back(matmul(normed, query_mat))
        key_pre = low_back(matmul(normed, key_mat))
        values = low(low_back(matmul(normed, value_mat)))
        gate_pre = low_back(matmul(normed, gate_mat))
        queries = low(head_prep(query_pre, query_scale, cosine, sine_tab))
        keys_rot = low(head_prep(key_pre, key_scale, cosine, sine_tab))
        attended = low_back(attend_all(queries, keys_rot, values, document_segment))
        gated = low(attended * jax.nn.sigmoid(gate_pre))
        middle = block_in + low_back(matmul(gated, out_mat))
        ffn_normed = low(rms_apply(middle, ffn_scale))
        gate_val = low_back(matmul(ffn_normed, ffn_gate_mat))
        up_val = low_back(matmul(ffn_normed, ffn_up_mat))
        hidden = low(jax.nn.silu(gate_val) * up_val)
        return middle + matmul(hidden, ffn_down_mat)
    result, pull_back = jax.vjp(block_forward, inputs.astype(jnp.float32), attn_gain.astype(jnp.float32), query_weight.astype(jnp.float32), key_projection.astype(jnp.float32), value_projection.astype(jnp.float32), attn_gate_weight.astype(jnp.float32), output_weight.astype(jnp.float32), query_gain.astype(jnp.float32), key_gain.astype(jnp.float32), ffn_gain.astype(jnp.float32), ffn_gate_weight.astype(jnp.float32), ffn_up_weight.astype(jnp.float32), ffn_down_weight.astype(jnp.float32))
    grads = pull_back(cotangent.astype(jnp.float32))
    return (result.astype(jnp.bfloat16), grads[0], grads[1], grads[2], grads[3], grads[4], grads[5], grads[6], grads[7], grads[8], grads[9], grads[10], grads[11], grads[12])
```

```python
import jax
import jax.numpy as jnp
from jax import lax
from jax.experimental import pallas as pl
from jax.experimental.pallas import tpu as pltpu
from jax.sharding import PartitionSpec as P

EPS = 1e-06
THETA = 1000000.0
VMEM_LIMIT = 56 << 20


def rms_apply(values, gain_vec):
    return values * lax.rsqrt(jnp.mean(values * values, axis=-1, keepdims=True) + EPS) * gain_vec


def token_tables(doc_lengths, token_ids):
    lengths = doc_lengths.reshape(-1)
    doc_ends = jnp.cumsum(lengths)
    before = doc_ends[None, :] <= token_ids[:, None]
    document_segment = jnp.sum(before.astype(jnp.int32), axis=1)
    doc_first = jnp.sum(jnp.where(before, lengths[None, :], 0), axis=1)
    return (document_segment, token_ids - doc_first, doc_first)


def rotary(position, head_width):
    half_width = head_width // 2
    inverse = THETA ** (-(jnp.arange(half_width, dtype=jnp.float32) * 2.0 / head_width))
    angles = position.astype(jnp.float32)[:, None] * inverse[None, :]
    cosine = jnp.cos(angles)
    sine_tab = jnp.sin(angles)
    return (
        jnp.concatenate([cosine, cosine], axis=1),
        jnp.concatenate([sine_tab, sine_tab], axis=1),
    )


def head_prep(pre_proj, gain_vec, cosine, sine_tab):
    row_count = pre_proj.shape[0]
    head_width = gain_vec.shape[0]
    half_width = head_width // 2
    per_head = rms_apply(pre_proj.reshape(row_count, -1, head_width), gain_vec)
    turned = jnp.concatenate([-per_head[..., half_width:], per_head[..., :half_width]], axis=-1)
    rotated = per_head * cosine[:, None, :] + turned * sine_tab[:, None, :]
    return rotated.reshape(row_count, -1)


def swiglu(gate_in, up_in):
    return jax.nn.silu(gate_in) * up_in


LANES = 128
KEY_BLOCK = 512
LOG2E = 1.4426950408889634


def attention_forward_kernel(
    start_ref, query_ref, key_ref, value_ref, first_ref, gate_ref, att_ref, inv_ref, gated_ref, acc
):
    blocks = start_ref.shape[0]
    groups = key_ref.shape[1] // LANES
    per = query_ref.shape[1] // key_ref.shape[1]
    rows = query_ref.shape[0] // blocks
    wide_count = key_ref.shape[0] // query_ref.shape[0]
    wide_pos = lax.axis_index("wide")
    step = KEY_BLOCK
    factor = LANES ** (-0.5) * LOG2E

    @pl.loop(0, blocks)
    def _(blk):
        here = pl.ds(pl.multiple_of(blk * rows, rows), rows)
        first_tok = (blk * wide_count + wide_pos) * rows
        key_lane = lax.broadcasted_iota(jnp.int32, (rows, step), 1)
        query_row = lax.broadcasted_iota(jnp.int32, (rows, step), 0) + first_tok
        upper = key_lane - query_row
        lower = key_lane - first_ref[here, :]
        queries = [
            jnp.concatenate(
                [
                    query_ref[here, (g * per + j) * LANES : (g * per + j + 1) * LANES]
                    for j in range(per)
                ],
                axis=0,
            )
            for g in range(groups)
        ]
        acc[...] = jnp.zeros_like(acc)

        @pl.loop(start_ref[blk] // step, (first_tok + rows + step - 1) // step)
        def _(tile):
            base = tile * step
            there = pl.ds(pl.multiple_of(base, step), step)
            allowed = (upper <= -base) & (lower >= -base)
            allowed = jnp.concatenate([allowed] * per, axis=0)
            for g in range(groups):
                cols = slice(g * LANES, (g + 1) * LANES)
                scores = lax.dot_general(
                    queries[g], key_ref[there, cols], (((1,), (1,)), ((), ())),
                    preferred_element_type=jnp.float32,
                )
                probs = jnp.where(allowed, jnp.exp2(scores * factor), 0.0).astype(jnp.bfloat16)
                values = jnp.concatenate(
                    [value_ref[there, cols], jnp.ones((step, LANES), jnp.bfloat16)], axis=1
                )
                acc[g] += jnp.dot(probs, values, preferred_element_type=jnp.float32)

        for g in range(groups):
            for j in range(per):
                part = acc[g, j * rows : (j + 1) * rows, :]
                cols = slice((g * per + j) * LANES, (g * per + j + 1) * LANES)
                inverse = 1.0 / part[:, LANES:]
                out = part[:, :LANES] * inverse
                att_ref[here, cols] = out
                inv_ref[here, cols] = inverse
                gated_ref[here, cols] = (out * jax.nn.sigmoid(gate_ref[here, cols])).astype(
                    jnp.bfloat16
                )


def attention_forward(query_low, key_all, value_all, starts, firsts, gate_pre):
    rows, width = query_low.shape
    groups = key_all.shape[1] // LANES
    per = width // key_all.shape[1]
    blocks = starts.shape[0]
    vmem = pl.BlockSpec(memory_space=pltpu.VMEM)
    return pl.pallas_call(
        attention_forward_kernel,
        out_shape=(
            jax.ShapeDtypeStruct((rows, width), jnp.float32),
            jax.ShapeDtypeStruct((rows, width), jnp.float32),
            jax.ShapeDtypeStruct((rows, width), jnp.bfloat16),
        ),
        in_specs=[pl.BlockSpec(memory_space=pltpu.SMEM)] + [vmem] * 5,
        out_specs=(vmem, vmem, vmem),
        scratch_shapes=[pltpu.VMEM((groups, per * (rows // blocks), 2 * LANES), jnp.float32)],
        compiler_params=pltpu.CompilerParams(vmem_limit_bytes=VMEM_LIMIT),
        cost_estimate=pl.CostEstimate(
            flops=4 * rows * width * 2048, bytes_accessed=12 << 20, transcendentals=0
        ),
        name="attention_forward",
    )(starts, query_low, key_all, value_all, firsts, gate_pre)


def attention_backward_kernel(
    start_ref, query_ref, grad_ref, att_ref, inv_ref, key_ref, keyt_ref, value_ref, first_ref,
    dq_ref, dk_ref, dv_ref, dk_acc, dv_acc, dqt,
):
    blocks = start_ref.shape[0]
    groups = key_ref.shape[1] // LANES
    per = query_ref.shape[1] // key_ref.shape[1]
    rows = query_ref.shape[0] // blocks
    wide_count = key_ref.shape[0] // query_ref.shape[0]
    wide_pos = lax.axis_index("wide")
    step = KEY_BLOCK
    scale = LANES ** (-0.5)
    dk_acc[...] = jnp.zeros_like(dk_acc)
    dv_acc[...] = jnp.zeros_like(dv_acc)

    @pl.loop(0, blocks)
    def _(blk):
        here = pl.ds(pl.multiple_of(blk * rows, rows), rows)
        first_tok = (blk * wide_count + wide_pos) * rows
        key_row = lax.broadcasted_iota(jnp.int32, (step, rows), 0)
        query_lane = lax.broadcasted_iota(jnp.int32, (step, rows), 1) + first_tok
        upper = key_row - query_lane
        lower = key_row - jnp.transpose(
            jnp.broadcast_to(first_ref[here, :], (rows, LANES))
        )[0:1, :]
        queries, grads, deltas = [], [], []
        for g in range(groups):
            qs, gs, ds = [], [], []
            for j in range(per):
                cols = slice((g * per + j) * LANES, (g * per + j + 1) * LANES)
                grad = grad_ref[here, cols].astype(jnp.float32)
                inverse = inv_ref[here, cols]
                both = grad * inverse
                delta = jnp.sum(both * att_ref[here, cols], axis=1, keepdims=True)
                ds.append(jnp.transpose(jnp.broadcast_to(delta, (rows, LANES)))[0:1, :])
                qs.append(query_ref[here, cols])
                gs.append(both.astype(jnp.bfloat16))
            queries.append(jnp.concatenate(qs, axis=0))
            grads.append(jnp.concatenate(gs, axis=0))
            deltas.append(jnp.concatenate(ds, axis=1))
        dqt[...] = jnp.zeros_like(dqt)

        @pl.loop(start_ref[blk] // step, (first_tok + rows + step - 1) // step)
        def _(tile):
            base = tile * step
            there = pl.ds(pl.multiple_of(base, step), step)
            allowed = (upper <= -base) & (lower >= -base)
            allowed = jnp.concatenate([allowed] * per, axis=1)
            for g in range(groups):
                cols = slice(g * LANES, (g + 1) * LANES)
                scores = lax.dot_general(
                    key_ref[there, cols], queries[g], (((1,), (1,)), ((), ())),
                    preferred_element_type=jnp.float32,
                )
                probs = jnp.where(allowed, jnp.exp2(scores * (scale * LOG2E)), 0.0)
                dprobs = lax.dot_general(
                    value_ref[there, cols], grads[g], (((1,), (1,)), ((), ())),
                    preferred_element_type=jnp.float32,
                )
                dscores = (probs * (dprobs - deltas[g]) * scale).astype(jnp.bfloat16)
                dv_acc[there, cols] += jnp.dot(
                    probs.astype(jnp.bfloat16), grads[g], preferred_element_type=jnp.float32
                )
                dk_acc[there, cols] += jnp.dot(
                    dscores, queries[g], preferred_element_type=jnp.float32
                )
                dqt[g] += jnp.dot(
                    keyt_ref[cols, there], dscores, preferred_element_type=jnp.float32
                )

        for g in range(groups):
            for j in range(per):
                cols = slice((g * per + j) * LANES, (g * per + j + 1) * LANES)
                dq_ref[here, cols] = jnp.transpose(dqt[g, :, j * rows : (j + 1) * rows])

    dk_ref[...] = dk_acc[...].astype(dk_ref.dtype)
    dv_ref[...] = dv_acc[...].astype(dv_ref.dtype)


def attention_backward(
    query_low, grad_low, attended, inverse, key_all, value_all, starts, firsts
):
    rows, width = query_low.shape
    keys, kv_width = key_all.shape
    groups = kv_width // LANES
    per = width // kv_width
    blocks = starts.shape[0]
    vmem = pl.BlockSpec(memory_space=pltpu.VMEM)
    return pl.pallas_call(
        attention_backward_kernel,
        out_shape=(
            jax.ShapeDtypeStruct((rows, width), jnp.float32),
            jax.ShapeDtypeStruct((keys, kv_width), jnp.bfloat16),
            jax.ShapeDtypeStruct((keys, kv_width), jnp.bfloat16),
        ),
        in_specs=[pl.BlockSpec(memory_space=pltpu.SMEM)] + [vmem] * 8,
        out_specs=(vmem, vmem, vmem),
        scratch_shapes=[
            pltpu.VMEM((keys, kv_width), jnp.float32),
            pltpu.VMEM((keys, kv_width), jnp.float32),
            pltpu.VMEM((groups, LANES, per * (rows // blocks)), jnp.float32),
        ],
        compiler_params=pltpu.CompilerParams(vmem_limit_bytes=VMEM_LIMIT),
        cost_estimate=pl.CostEstimate(
            flops=10 * rows * width * 2048, bytes_accessed=20 << 20, transcendentals=0
        ),
        name="attention_backward",
    )(starts, query_low, grad_low, attended, inverse, key_all, key_all.T, value_all, firsts)


def contract_rows(left_mat, right_mat):
    return lax.dot_general(
        left_mat, right_mat, (((0,), (0,)), ((), ())), preferred_element_type=jnp.float32
    )


def contract_cols(left_mat, right_mat):
    return lax.dot_general(
        left_mat, right_mat, (((1,), (1,)), ((), ())), preferred_element_type=jnp.float32
    )


def shards(
    inputs,
    attn_gain,
    query_weight,
    key_projection,
    value_projection,
    attn_gate_weight,
    output_weight,
    query_gain,
    key_gain,
    ffn_gain,
    ffn_gate_weight,
    ffn_up_weight,
    ffn_down_weight,
    doc_lengths,
    cotangent,
):
    tok_dev = inputs.shape[0]
    head_width = query_gain.shape[0]
    head_count = lax.axis_size("head")
    wide_count = lax.axis_size("wide")
    query_rows = tok_dev * head_count
    wide_pos = lax.axis_index("wide")
    local_ids = jnp.arange(query_rows, dtype=jnp.int32)
    query_tok = (local_ids // tok_dev * wide_count + wide_pos) * tok_dev + local_ids % tok_dev
    query_seg, query_pos, query_first = token_tables(doc_lengths, query_tok)
    starts = query_first[::tok_dev]
    firsts = query_first[:, None]
    cosine, sine_tab = rotary(query_pos, head_width)
    block_in = inputs.astype(jnp.float32)
    normed, input_norm_back = jax.vjp(rms_apply, block_in, attn_gain)
    normed_low = normed.astype(jnp.bfloat16)
    gathered = lax.all_gather(normed_low, "head", axis=0, tiled=True)
    query_pre = jnp.dot(gathered, query_weight, preferred_element_type=jnp.float32)
    key_pre = jnp.dot(gathered, key_projection, preferred_element_type=jnp.float32)
    value_pre = jnp.dot(gathered, value_projection, preferred_element_type=jnp.float32)
    gate_pre = jnp.dot(gathered, attn_gate_weight, preferred_element_type=jnp.float32)

    def prep_heads(pre_proj, gain_vec):
        return head_prep(pre_proj, gain_vec, cosine, sine_tab)

    query_rot, query_back = jax.vjp(prep_heads, query_pre, query_gain)
    key_rot, key_back = jax.vjp(prep_heads, key_pre, key_gain)
    query_low = query_rot.astype(jnp.bfloat16)
    key_low = key_rot.astype(jnp.bfloat16)
    value_low = value_pre.astype(jnp.bfloat16)
    key_wide, value_wide = (
        lax.all_gather(key_low, "wide", axis=0, tiled=True),
        lax.all_gather(value_low, "wide", axis=0, tiled=True),
    )
    kv_width = key_wide.shape[1]

    def natural_order(matrix):
        return (
            matrix.reshape(wide_count, head_count, tok_dev, kv_width)
            .transpose(1, 0, 2, 3)
            .reshape(-1, kv_width)
        )

    def gathered_order(matrix):
        return (
            matrix.reshape(head_count, wide_count, tok_dev, kv_width)
            .transpose(1, 0, 2, 3)
            .reshape(-1, kv_width)
        )

    key_entire = natural_order(key_wide)
    value_entire = natural_order(value_wide)
    attended, inverse, gated_low = attention_forward(
        query_low, key_entire, value_entire, starts, firsts, gate_pre
    )
    gate_sig = jax.nn.sigmoid(gate_pre)
    attn_terms = jnp.dot(gated_low, output_weight, preferred_element_type=jnp.float32)
    attn_out = lax.psum_scatter(
        attn_terms.astype(jnp.bfloat16), "head", scatter_dimension=0, tiled=True
    ).astype(jnp.float32)
    middle = block_in + attn_out
    ffn_normed, ffn_norm_back = jax.vjp(rms_apply, middle, ffn_gain)
    ffn_low = ffn_normed.astype(jnp.bfloat16)
    ffn_rows, cot_rows = (
        lax.all_gather(ffn_low, "wide", axis=0, tiled=True),
        lax.all_gather(cotangent, "wide", axis=0, tiled=True),
    )
    gate_val = jnp.dot(ffn_rows, ffn_gate_weight, preferred_element_type=jnp.float32)
    up_val = jnp.dot(ffn_rows, ffn_up_weight, preferred_element_type=jnp.float32)
    hidden_val, swiglu_back = jax.vjp(swiglu, gate_val, up_val)
    hidden_low = hidden_val.astype(jnp.bfloat16)
    down_terms = jnp.dot(hidden_low, ffn_down_weight, preferred_element_type=jnp.float32)
    ffn_out = lax.psum_scatter(
        down_terms.astype(jnp.bfloat16), "wide", scatter_dimension=0, tiled=True
    ).astype(jnp.float32)
    outputs = (middle + ffn_out).astype(jnp.bfloat16)
    hidden_grad = contract_cols(cot_rows, ffn_down_weight)
    gate_grad, up_grad = swiglu_back(hidden_grad)
    gate_grad_low = gate_grad.astype(jnp.bfloat16)
    up_grad_low = up_grad.astype(jnp.bfloat16)
    down_wgrad = contract_rows(hidden_low, cot_rows)
    gate_wgrad = contract_rows(ffn_rows, gate_grad_low)
    up_wgrad = contract_rows(ffn_rows, up_grad_low)
    ffn_terms = contract_cols(gate_grad_low, ffn_gate_weight) + contract_cols(
        up_grad_low, ffn_up_weight
    )
    ffn_normed_grad = lax.psum_scatter(
        ffn_terms.astype(jnp.bfloat16), "wide", scatter_dimension=0, tiled=True
    ).astype(jnp.float32)
    middle_norm_grad, ffn_gain_part = ffn_norm_back(ffn_normed_grad)
    middle_grad = cotangent.astype(jnp.float32) + middle_norm_grad
    middle_low = middle_grad.astype(jnp.bfloat16)
    back_rows = lax.all_gather(middle_low, "head", axis=0, tiled=True)
    gated_grad = contract_cols(back_rows, output_weight)
    out_wgrad = contract_rows(gated_low, back_rows)
    attended_grad_low = (gated_grad * gate_sig).astype(jnp.bfloat16)
    gate_pre_grad_low = (gated_grad * attended * gate_sig * (1.0 - gate_sig)).astype(jnp.bfloat16)
    query_rot_grad, key_natural, value_natural = attention_backward(
        query_low, attended_grad_low, attended, inverse, key_entire, value_entire, starts, firsts
    )
    key_terms = gathered_order(key_natural)
    value_terms = gathered_order(value_natural)
    key_rot_grad, value_sum = (
        lax.psum_scatter(
            key_terms.astype(jnp.bfloat16), "wide", scatter_dimension=0, tiled=True
        ).astype(jnp.float32),
        lax.psum_scatter(
            value_terms.astype(jnp.bfloat16), "wide", scatter_dimension=0, tiled=True
        ).astype(jnp.float32),
    )
    query_pre_grad, query_gain_part = query_back(query_rot_grad)
    key_pre_grad, key_gain_part = key_back(key_rot_grad)
    query_pre_low = query_pre_grad.astype(jnp.bfloat16)
    key_pre_low = key_pre_grad.astype(jnp.bfloat16)
    value_grad_low = value_sum.astype(jnp.bfloat16)
    query_wgrad = contract_rows(gathered, query_pre_low)
    key_wgrad = contract_rows(gathered, key_pre_low)
    value_wgrad = contract_rows(gathered, value_grad_low)
    attn_gate_wgrad = contract_rows(gathered, gate_pre_grad_low)
    normed_terms = (
        contract_cols(query_pre_low, query_weight)
        + contract_cols(key_pre_low, key_projection)
        + contract_cols(value_grad_low, value_projection)
        + contract_cols(gate_pre_grad_low, attn_gate_weight)
    )
    normed_grad = lax.psum_scatter(
        normed_terms.astype(jnp.bfloat16), "head", scatter_dimension=0, tiled=True
    ).astype(jnp.float32)
    input_norm_grad, attn_gain_part = input_norm_back(normed_grad)
    input_grad = middle_grad + input_norm_grad
    query_grad, key_grad, value_grad, attn_gate_grad, output_grad = (
        lax.psum_scatter(
            query_wgrad.astype(jnp.bfloat16), "wide", scatter_dimension=0, tiled=True
        ).astype(jnp.float32),
        lax.psum_scatter(
            key_wgrad.astype(jnp.bfloat16), "wide", scatter_dimension=0, tiled=True
        ).astype(jnp.float32),
        lax.psum_scatter(
            value_wgrad.astype(jnp.bfloat16), "wide", scatter_dimension=0, tiled=True
        ).astype(jnp.float32),
        lax.psum_scatter(
            attn_gate_wgrad.astype(jnp.bfloat16), "wide", scatter_dimension=0, tiled=True
        ).astype(jnp.float32),
        lax.psum_scatter(
            out_wgrad.astype(jnp.bfloat16), "wide", scatter_dimension=1, tiled=True
        ).astype(jnp.float32),
    )
    ffn_gate_grad, ffn_up_grad, ffn_down_grad = (
        lax.psum_scatter(
            gate_wgrad.astype(jnp.bfloat16), "head", scatter_dimension=0, tiled=True
        ).astype(jnp.float32),
        lax.psum_scatter(
            up_wgrad.astype(jnp.bfloat16), "head", scatter_dimension=0, tiled=True
        ).astype(jnp.float32),
        lax.psum_scatter(
            down_wgrad.astype(jnp.bfloat16), "head", scatter_dimension=1, tiled=True
        ).astype(jnp.float32),
    )
    attn_gain_grad, ffn_gain_grad, query_gain_grad, key_gain_grad = lax.psum(
        (attn_gain_part, ffn_gain_part, query_gain_part, key_gain_part), ("head", "wide")
    )
    return (
        outputs,
        input_grad,
        attn_gain_grad,
        query_grad,
        key_grad,
        value_grad,
        attn_gate_grad,
        output_grad,
        query_gain_grad,
        key_gain_grad,
        ffn_gain_grad,
        ffn_gate_grad,
        ffn_up_grad,
        ffn_down_grad,
    )


def solution(mesh):
    placed = (
        P(("head", "wide"), None),
        P(),
        P(None, "head"),
        P(None, "head"),
        P(None, "head"),
        P(None, "head"),
        P("head", None),
        P(),
        P(),
        P(),
        P(None, "wide"),
        P(None, "wide"),
        P("wide", None),
        P(),
        P(("head", "wide"), None),
    )
    return jax.shard_map(
        shards,
        mesh=mesh,
        in_specs=placed,
        out_specs=(
            P(("head", "wide"), None),
            P(("head", "wide"), None),
            P(),
            P("wide", "head"),
            P("wide", "head"),
            P("wide", "head"),
            P("wide", "head"),
            P("head", "wide"),
            P(),
            P(),
            P(),
            P("head", "wide"),
            P("head", "wide"),
            P("wide", "head"),
        ),
        check_vma=False,
    )
```

```python
import jax
import jax.numpy as jnp
from jax import lax
from jax.experimental import pallas as pl
from jax.experimental.pallas import tpu as pltpu
from jax.sharding import PartitionSpec as P

EPS = 1e-06
THETA = 1000000.0
VMEM_LIMIT = 62 << 20


def rms_apply(values, gain_vec):
    return values * lax.rsqrt(jnp.mean(values * values, axis=-1, keepdims=True) + EPS) * gain_vec


def token_tables(doc_lengths, token_ids):
    lengths = doc_lengths.reshape(-1)
    doc_ends = jnp.cumsum(lengths)
    before = doc_ends[None, :] <= token_ids[:, None]
    document_segment = jnp.sum(before.astype(jnp.int32), axis=1)
    doc_first = jnp.sum(jnp.where(before, lengths[None, :], 0), axis=1)
    return (document_segment, token_ids - doc_first, doc_first)


def rotary(position, head_width):
    half_width = head_width // 2
    inverse = THETA ** (-(jnp.arange(half_width, dtype=jnp.float32) * 2.0 / head_width))
    angles = position.astype(jnp.float32)[:, None] * inverse[None, :]
    cosine = jnp.cos(angles)
    sine_tab = jnp.sin(angles)
    return (
        jnp.concatenate([cosine, cosine], axis=1),
        jnp.concatenate([sine_tab, sine_tab], axis=1),
    )


def head_prep(pre_proj, gain_vec, cosine, sine_tab):
    row_count = pre_proj.shape[0]
    head_width = gain_vec.shape[0]
    half_width = head_width // 2
    per_head = rms_apply(pre_proj.reshape(row_count, -1, head_width), gain_vec)
    turned = jnp.concatenate([-per_head[..., half_width:], per_head[..., :half_width]], axis=-1)
    rotated = per_head * cosine[:, None, :] + turned * sine_tab[:, None, :]
    return rotated.reshape(row_count, -1)


MESH = pl.DeviceIdType.MESH
ANY = pl.BlockSpec(memory_space=pl.ANY)
VMEM = pl.BlockSpec(memory_space=pltpu.VMEM)
DMA = pltpu.SemaphoreType.DMA
SIDES = (0, 1)


class Ring:
    def __init__(self, size, pos, index, device):
        self.size, self.pos, self.half = size, pos, size // 2
        self._index, self._device = index, device

    def at(self, offset):
        return lax.rem(self.pos + (offset + 2 * self.size), self.size)

    def index(self, offset):
        return self._index(self.at(offset))

    def device(self, offset):
        return self._device(self.at(offset))


def head_ring():
    size = lax.axis_size("head")
    spread = size // 2
    own, wide = lax.axis_index("head"), lax.axis_index("wide")
    major, minor = lax.div(own, 2), lax.rem(own, 2)
    pos = major + minor * (size - 1 - 2 * major)

    def index(place):
        upper = lax.div(place, spread)
        return 2 * (place + upper * (size - 1 - 2 * place)) + upper

    return Ring(size, pos, index, lambda place: (index(place), wide))


def wide_ring():
    size = lax.axis_size("wide") // 2
    head, wide = lax.axis_index("head"), lax.axis_index("wide")
    core = lax.rem(wide, 2)
    ring = Ring(
        size, lax.div(wide, 2), lambda place: place, lambda place: (head, 2 * place + core)
    )
    ring.core = core
    ring.sibling = (head, wide + 1 - 2 * core)
    return ring


def meet(devices):
    barrier = pltpu.get_barrier_semaphore()
    for device in devices:
        pl.semaphore_signal(barrier, inc=1, device_id=device, device_id_type=MESH)
    pl.semaphore_wait(barrier, len(devices))


def neighbours(*rings):
    found = []
    for ring in rings:
        found += [ring.device(1), ring.device(-1)]
        if hasattr(ring, "sibling"):
            found.append(ring.sibling)
    return found


def remote(src, dst, send, recv, device):
    return pltpu.make_async_remote_copy(
        src_ref=src, dst_ref=dst, send_sem=send, recv_sem=recv, device_id=device,
        device_id_type=MESH,
    )


class Gather:
    def __init__(self, ring, slot, rows, send, recv):
        self.ring, self.slot, self.rows = ring, slot, rows
        self.send, self.recv = send, recv

    def span(self, hop, side):
        if 2 * hop == self.ring.size:
            return side * (self.rows // 2), self.rows // 2
        return 0, self.rows

    def copy(self, hop, side):
        way = 1 - 2 * side
        ref = self.slot(self.ring.index(-way * (hop - 1)), *self.span(hop, side))
        return remote(
            ref, ref, self.send.at[side, hop - 1], self.recv.at[side, hop - 1],
            self.ring.device(way),
        )

    def start(self, hop):
        for side in SIDES:
            self.copy(hop, side).start()

    def arrive(self, hop):
        for side in SIDES:
            self.copy(hop, side).wait_recv()

    def finish(self):
        for hop in range(1, self.ring.half + 1):
            for side in SIDES:
                self.copy(hop, side).wait_send()


class PairGather(Gather):
    def __init__(self, ring, slot, rows, send, recv, pass_send, pass_recv):
        core = ring.core
        super().__init__(
            ring, lambda index, start, size: slot(2 * index + core, start, size), rows, send, recv
        )
        self.pass_send, self.pass_recv = pass_send, pass_recv

    def handed(self, hop, side):
        way = 1 - 2 * side
        span = self.span(hop, side) if hop else (0, self.rows)
        ref = self.slot(self.ring.index(-way * hop), *span)
        return remote(
            ref, ref, self.pass_send.at[side, hop], self.pass_recv.at[side, hop],
            self.ring.sibling,
        )

    def hand(self, hop):
        for side in SIDES if hop else (0,):
            self.handed(hop, side).start()

    def take(self, hop):
        for side in SIDES if hop else (0,):
            self.handed(hop, side).wait_recv()

    def begin(self):
        self.start(1)
        self.hand(0)

    def finish(self):
        super().finish()
        for hop in range(self.ring.half + 1):
            for side in SIDES if hop else (0,):
                self.handed(hop, side).wait_send()


def row_loop(rows, chunk, body):
    @pl.loop(0, rows // chunk)
    def _(step):
        body(pl.multiple_of(step * chunk, chunk))


class Scatter:
    def __init__(self, ring, part, rows, into, send, recv):
        self.ring, self.part, self.rows, self.into = ring, part, rows, into
        self.send, self.recv = send, recv

    def span(self, hop, side):
        if 2 * hop == self.ring.size:
            return side * (self.rows // 2), self.rows // 2
        return 0, self.rows

    def copy(self, hop, side):
        way = 1 - 2 * side
        first, count = self.span(hop, side)
        ref, base = self.part(self.ring.index(way * hop))
        return remote(
            ref.at[pl.ds(base + first, count)],
            self.into.at[side, hop - 1, pl.ds(first, count)],
            self.send.at[side, hop - 1], self.recv.at[side, hop - 1], self.ring.device(way),
        )

    def start(self, hop, sides=SIDES):
        for side in sides:
            self.copy(hop, side).start()

    def fold(self, hop, side):
        way = 1 - 2 * side
        self.copy(hop + 1, side).wait_recv()
        first, count = self.span(hop + 1, side)
        ref, base = self.part(self.ring.index(way * hop))
        chunk = min(count, 32)

        def add(row):
            there = pl.ds(pl.multiple_of(base + first + row, chunk), chunk)
            here = pl.ds(pl.multiple_of(first + row, chunk), chunk)
            ref[there, :] = (
                ref[there, :].astype(jnp.float32)
                + self.into[side, hop, here, :].astype(jnp.float32)
            ).astype(ref.dtype)

        row_loop(count, chunk, add)

    def advance(self, hop):
        for side in SIDES:
            self.fold(hop, side)
            self.copy(hop, side).start()

    def arrive(self):
        for side in SIDES:
            self.copy(1, side).wait_recv()

    def total(self, row, count):
        ref, base = self.part(self.ring.index(0))
        there = pl.ds(pl.multiple_of(base + row, count), count)
        here = pl.ds(row, count)
        return (
            ref[there, :].astype(jnp.float32)
            + self.into[0, 0, here, :].astype(jnp.float32)
            + self.into[1, 0, here, :].astype(jnp.float32)
        )

    def finish(self):
        for hop in range(1, self.ring.half + 1):
            for side in SIDES:
                self.copy(hop, side).wait_send()


class PairScatter(Scatter):
    def __init__(self, ring, terms, rows, passed, into, send, recv, pass_send, pass_recv):
        core = ring.core
        super().__init__(
            ring, lambda index: (terms, (2 * index + core) * rows), rows, into, send, recv
        )
        self.terms, self.passed = terms, passed
        self.pass_send, self.pass_recv = pass_send, pass_recv

    def handed(self, offset):
        ring = self.ring
        index = ring.index(offset)
        other = pl.multiple_of((2 * index + 1 - ring.core) * self.rows, self.rows)
        slot = offset % ring.size
        return remote(
            self.terms.at[pl.ds(other, self.rows)],
            self.passed.at[slot],
            self.pass_send.at[slot], self.pass_recv.at[slot], ring.sibling,
        )

    def hand(self, offset):
        self.handed(offset).start()

    def merge(self, offset):
        self.handed(offset).wait_recv()
        slot = offset % self.ring.size
        ref, base = self.part(self.ring.index(offset))
        chunk = 32

        def add(row):
            there = pl.ds(pl.multiple_of(base + row, chunk), chunk)
            ref[there, :] = (
                ref[there, :].astype(jnp.float32)
                + self.passed[slot, pl.ds(row, chunk), :].astype(jnp.float32)
            ).astype(ref.dtype)

        row_loop(self.rows, chunk, add)

    def finish(self):
        super().finish()
        for offset in range(self.ring.size):
            self.handed(offset).wait_send()


def offsets(ring):
    order = [ring.half]
    for hop in range(ring.half - 1, 0, -1):
        order += [hop, -hop]
    return order + [0]


def ring_sems(size):
    return [DMA((2, size // 2)), DMA((2, size // 2))]


def pass_sems(size):
    return [DMA((2, size // 2 + 1)), DMA((2, size // 2 + 1))]


def dot_nn(left, right):
    return jnp.dot(left, right, preferred_element_type=jnp.float32)


def dot_nt(left, right):
    return lax.dot_general(
        left, right, (((1,), (1,)), ((), ())), preferred_element_type=jnp.float32
    )


def dot_tn(left, right):
    return lax.dot_general(
        left, right, (((0,), (0,)), ((), ())), preferred_element_type=jnp.float32
    )


LANES = 128
KEY_BLOCK = 512
LOG2E = 1.4426950408889634


def attention_forward_kernel(
    start_ref, query_ref, key_ref, value_ref, first_ref, gate_ref, att_ref, inv_ref, gated_ref, acc
):
    blocks = start_ref.shape[0]
    groups = key_ref.shape[1] // LANES
    per = query_ref.shape[1] // key_ref.shape[1]
    rows = query_ref.shape[0] // blocks
    wide_count = key_ref.shape[0] // query_ref.shape[0]
    wide_pos = lax.axis_index("wide")
    step = KEY_BLOCK
    factor = LANES ** (-0.5) * LOG2E

    @pl.loop(0, blocks)
    def _(blk):
        here = pl.ds(pl.multiple_of(blk * rows, rows), rows)
        first_tok = (blk * wide_count + wide_pos) * rows
        key_lane = lax.broadcasted_iota(jnp.int32, (rows, step), 1)
        query_row = lax.broadcasted_iota(jnp.int32, (rows, step), 0) + first_tok
        upper = key_lane - query_row
        lower = key_lane - first_ref[here, :]
        queries = [
            jnp.concatenate(
                [
                    query_ref[here, (g * per + j) * LANES : (g * per + j + 1) * LANES]
                    for j in range(per)
                ],
                axis=0,
            )
            for g in range(groups)
        ]
        acc[...] = jnp.zeros_like(acc)

        @pl.loop(start_ref[blk] // step, (first_tok + rows + step - 1) // step)
        def _(tile):
            base = tile * step
            there = pl.ds(pl.multiple_of(base, step), step)
            allowed = (upper <= -base) & (lower >= -base)
            allowed = jnp.concatenate([allowed] * per, axis=0)
            for g in range(groups):
                cols = slice(g * LANES, (g + 1) * LANES)
                scores = lax.dot_general(
                    queries[g], key_ref[there, cols], (((1,), (1,)), ((), ())),
                    preferred_element_type=jnp.float32,
                )
                probs = jnp.where(allowed, jnp.exp2(scores * factor), 0.0).astype(jnp.bfloat16)
                values = jnp.concatenate(
                    [value_ref[there, cols], jnp.ones((step, LANES), jnp.bfloat16)], axis=1
                )
                acc[g] += jnp.dot(probs, values, preferred_element_type=jnp.float32)

        for g in range(groups):
            for j in range(per):
                part = acc[g, j * rows : (j + 1) * rows, :]
                cols = slice((g * per + j) * LANES, (g * per + j + 1) * LANES)
                inverse = 1.0 / part[:, LANES:]
                out = part[:, :LANES] * inverse
                att_ref[here, cols] = out
                inv_ref[here, cols] = inverse
                gated_ref[here, cols] = (out * jax.nn.sigmoid(gate_ref[here, cols])).astype(
                    jnp.bfloat16
                )


def attention_forward(query_low, key_all, value_all, starts, firsts, gate_pre):
    rows, width = query_low.shape
    groups = key_all.shape[1] // LANES
    per = width // key_all.shape[1]
    blocks = starts.shape[0]
    vmem = pl.BlockSpec(memory_space=pltpu.VMEM)
    return pl.pallas_call(
        attention_forward_kernel,
        out_shape=(
            jax.ShapeDtypeStruct((rows, width), jnp.float32),
            jax.ShapeDtypeStruct((rows, width), jnp.float32),
            jax.ShapeDtypeStruct((rows, width), jnp.bfloat16),
        ),
        in_specs=[pl.BlockSpec(memory_space=pltpu.SMEM)] + [vmem] * 5,
        out_specs=(vmem, vmem, vmem),
        scratch_shapes=[pltpu.VMEM((groups, per * (rows // blocks), 2 * LANES), jnp.float32)],
        compiler_params=pltpu.CompilerParams(vmem_limit_bytes=VMEM_LIMIT),
        cost_estimate=pl.CostEstimate(
            flops=4 * rows * width * 2048, bytes_accessed=12 << 20, transcendentals=0
        ),
        name="attention_forward",
    )(starts, query_low, key_all, value_all, firsts, gate_pre)


def attention_backward_kernel(
    start_ref, query_ref, grad_ref, att_ref, inv_ref, key_ref, keyt_ref, value_ref, first_ref,
    dq_ref, dk_ref, dv_ref, dk_acc, dv_acc, dqt,
):
    blocks = start_ref.shape[0]
    groups = key_ref.shape[1] // LANES
    per = query_ref.shape[1] // key_ref.shape[1]
    rows = query_ref.shape[0] // blocks
    wide_count = key_ref.shape[0] // query_ref.shape[0]
    wide_pos = lax.axis_index("wide")
    step = KEY_BLOCK
    scale = LANES ** (-0.5)
    dk_acc[...] = jnp.zeros_like(dk_acc)
    dv_acc[...] = jnp.zeros_like(dv_acc)

    @pl.loop(0, blocks)
    def _(blk):
        here = pl.ds(pl.multiple_of(blk * rows, rows), rows)
        first_tok = (blk * wide_count + wide_pos) * rows
        key_row = lax.broadcasted_iota(jnp.int32, (step, rows), 0)
        query_lane = lax.broadcasted_iota(jnp.int32, (step, rows), 1) + first_tok
        upper = key_row - query_lane
        lower = key_row - jnp.transpose(
            jnp.broadcast_to(first_ref[here, :], (rows, LANES))
        )[0:1, :]
        queries, grads, deltas = [], [], []
        for g in range(groups):
            qs, gs, ds = [], [], []
            for j in range(per):
                cols = slice((g * per + j) * LANES, (g * per + j + 1) * LANES)
                grad = grad_ref[here, cols].astype(jnp.float32)
                inverse = inv_ref[here, cols]
                both = grad * inverse
                delta = jnp.sum(both * att_ref[here, cols], axis=1, keepdims=True)
                ds.append(jnp.transpose(jnp.broadcast_to(delta, (rows, LANES)))[0:1, :])
                qs.append(query_ref[here, cols])
                gs.append(both.astype(jnp.bfloat16))
            queries.append(jnp.concatenate(qs, axis=0))
            grads.append(jnp.concatenate(gs, axis=0))
            deltas.append(jnp.concatenate(ds, axis=1))
        dqt[...] = jnp.zeros_like(dqt)

        @pl.loop(start_ref[blk] // step, (first_tok + rows + step - 1) // step)
        def _(tile):
            base = tile * step
            there = pl.ds(pl.multiple_of(base, step), step)
            allowed = (upper <= -base) & (lower >= -base)
            allowed = jnp.concatenate([allowed] * per, axis=1)
            for g in range(groups):
                cols = slice(g * LANES, (g + 1) * LANES)
                scores = lax.dot_general(
                    key_ref[there, cols], queries[g], (((1,), (1,)), ((), ())),
                    preferred_element_type=jnp.float32,
                )
                probs = jnp.where(allowed, jnp.exp2(scores * (scale * LOG2E)), 0.0)
                dprobs = lax.dot_general(
                    value_ref[there, cols], grads[g], (((1,), (1,)), ((), ())),
                    preferred_element_type=jnp.float32,
                )
                dscores = (probs * (dprobs - deltas[g]) * scale).astype(jnp.bfloat16)
                dv_acc[there, cols] += jnp.dot(
                    probs.astype(jnp.bfloat16), grads[g], preferred_element_type=jnp.float32
                )
                dk_acc[there, cols] += jnp.dot(
                    dscores, queries[g], preferred_element_type=jnp.float32
                )
                dqt[g] += jnp.dot(
                    keyt_ref[cols, there], dscores, preferred_element_type=jnp.float32
                )

        for g in range(groups):
            for j in range(per):
                cols = slice((g * per + j) * LANES, (g * per + j + 1) * LANES)
                dq_ref[here, cols] = jnp.transpose(dqt[g, :, j * rows : (j + 1) * rows])

    dk_ref[...] = dk_acc[...].astype(dk_ref.dtype)
    dv_ref[...] = dv_acc[...].astype(dv_ref.dtype)


def attention_backward(
    query_low, grad_low, attended, inverse, key_all, value_all, starts, firsts
):
    rows, width = query_low.shape
    keys, kv_width = key_all.shape
    groups = kv_width // LANES
    per = width // kv_width
    blocks = starts.shape[0]
    vmem = pl.BlockSpec(memory_space=pltpu.VMEM)
    return pl.pallas_call(
        attention_backward_kernel,
        out_shape=(
            jax.ShapeDtypeStruct((rows, width), jnp.float32),
            jax.ShapeDtypeStruct((keys, kv_width), jnp.bfloat16),
            jax.ShapeDtypeStruct((keys, kv_width), jnp.bfloat16),
        ),
        in_specs=[pl.BlockSpec(memory_space=pltpu.SMEM)] + [vmem] * 8,
        out_specs=(vmem, vmem, vmem),
        scratch_shapes=[
            pltpu.VMEM((keys, kv_width), jnp.float32),
            pltpu.VMEM((keys, kv_width), jnp.float32),
            pltpu.VMEM((groups, LANES, per * (rows // blocks)), jnp.float32),
        ],
        compiler_params=pltpu.CompilerParams(vmem_limit_bytes=VMEM_LIMIT),
        cost_estimate=pl.CostEstimate(
            flops=10 * rows * width * 2048, bytes_accessed=20 << 20, transcendentals=0
        ),
        name="attention_backward",
    )(starts, query_low, grad_low, attended, inverse, key_all, key_all.T, value_all, firsts)


def ffn_kernel(
    gated_ref, x_ref, cot_ref, gain_ref, wo_any, wg_any, wu_any, wd_any,
    out_ref, mgrad_ref, gain_out, back_any, rows_any, cots_any, hid_any, gg_any, ug_any,
    wo, wg, wu, wd, cots, rows, hidden_grad, hid, gg, ug, passed, into, passed2,
    into2, hterms, hinto, middle, back, local_sem,
    hs, hr, cs, cr, cps, cpr, fs, fr, fps, fpr, s1, r1, ps1, pr1, s2, r2, ps2, pr2, bs, br,
):
    tok, width = x_ref.shape
    hidden_width = wg_any.shape[1]
    head, wide = head_ring(), wide_ring()
    pair = 2 * tok
    loads = [
        pltpu.make_async_copy(src, dst, local_sem.at[i])
        for i, (src, dst) in enumerate(((wo_any, wo), (wd_any, wd), (wg_any, wg), (wu_any, wu)))
    ]
    for load in loads:
        load.start()
    own_wide = pl.multiple_of(lax.axis_index("wide") * tok, tok)
    own_head = pl.multiple_of(lax.axis_index("head") * tok, tok)
    cots[pl.ds(own_wide, tok), :] = cot_ref[...]
    meet(neighbours(head, wide))

    def slot_of(ref):
        return lambda index, start, size: ref.at[pl.ds(index * tok + start, size)]

    cot_gather = PairGather(wide, slot_of(cots), tok, cs, cr, cps, cpr)
    row_gather = PairGather(wide, slot_of(rows), tok, fs, fr, fps, fpr)
    back_gather = Gather(head, slot_of(back), tok, bs, br)
    head_scatter = Scatter(head, lambda index: (hterms, index * tok), tok, hinto, hs, hr)
    grad_scatter = PairScatter(wide, cots, tok, passed, into, s1, r1, ps1, pr1)
    out_scatter = PairScatter(wide, rows, tok, passed2, into2, s2, r2, ps2, pr2)

    def group_of(offset):
        return pl.ds(pl.multiple_of(wide.index(offset) * pair, pair), pair)

    def col_loop(total, step, body):
        @pl.loop(0, total // step)
        def _(i):
            body(pl.ds(pl.multiple_of(i * step, step), step))

    tile = 256
    cot_gather.begin()

    def out_part(offset, own):
        index = head.index(offset)
        here = pl.ds(pl.multiple_of(index * tok, tok), tok)

        def body(cols):
            value = dot_nn(gated_ref[here, :], wo[:, cols])
            if own:
                middle[:, cols] = x_ref[:, cols].astype(jnp.float32) + value
            else:
                hterms[here, cols] = value.astype(jnp.bfloat16)

        col_loop(width, tile, body)

    def hidden_part(offset):
        here = group_of(offset)

        def body(cols):
            hidden_grad[here, cols] = dot_nt(cots[here, :], wd[cols, :])

        col_loop(hidden_width, tile if hidden_width % tile == 0 else LANES, body)

    loads[0].wait()
    out_part(head.half, False)
    head_scatter.start(head.half)
    for hop in range(head.half - 1, 0, -1):
        out_part(hop, False)
        out_part(-hop, False)
    out_part(0, True)
    loads[1].wait()
    cot_gather.take(0)
    hidden_part(0)
    for hop in range(head.half - 1, 0, -1):
        head_scatter.advance(hop)
    for hop in range(1, wide.half):
        cot_gather.arrive(hop)
        cot_gather.start(hop + 1)
        cot_gather.hand(hop)
        cot_gather.take(hop)
        hidden_part(hop)
        hidden_part(-hop)
    head_scatter.arrive()

    gain = gain_ref[...]

    def forward_norm(row):
        here = pl.ds(row, 32)
        value = (
            middle[here, :]
            + hinto[0, 0, here, :].astype(jnp.float32)
            + hinto[1, 0, here, :].astype(jnp.float32)
        )
        middle[here, :] = value
        scale = lax.rsqrt(jnp.mean(value * value, axis=-1, keepdims=True) + EPS)
        rows[pl.ds(pl.multiple_of(own_wide + row, 32), 32), :] = (value * scale * gain).astype(
            jnp.bfloat16
        )

    row_loop(tok, 32, forward_norm)
    row_gather.begin()
    cot_gather.arrive(wide.half)
    cot_gather.hand(wide.half)
    cot_gather.take(wide.half)
    hidden_part(wide.half)
    cot_gather.finish()
    stores = [
        pltpu.make_async_copy(src, dst, local_sem.at[4 + i])
        for i, (src, dst) in enumerate(
            ((rows, rows_any), (cots, cots_any), (hid, hid_any), (gg, gg_any), (ug, ug_any))
        )
    ]
    stores[1].start()
    loads[2].wait()
    loads[3].wait()

    def unit(offset):
        here = group_of(offset)

        def body(cols):
            gate = dot_nn(rows[here, :], wg[:, cols])
            up = dot_nn(rows[here, :], wu[:, cols])
            grad = hidden_grad[here, cols]
            sig = jax.nn.sigmoid(gate)
            act = gate * sig
            hid[here, cols] = (act * up).astype(jnp.bfloat16)
            gg[here, cols] = (grad * up * (sig + act * (1.0 - sig))).astype(jnp.bfloat16)
            ug[here, cols] = (grad * act).astype(jnp.bfloat16)

        col_loop(hidden_width, tile if hidden_width % tile == 0 else LANES, body)

    row_gather.take(0)
    unit(0)
    for hop in range(1, wide.half):
        row_gather.arrive(hop)
        row_gather.start(hop + 1)
        row_gather.hand(hop)
        row_gather.take(hop)
        unit(hop)
        unit(-hop)
    row_gather.arrive(wide.half)
    row_gather.hand(wide.half)
    row_gather.take(wide.half)
    unit(wide.half)

    def grad_terms(offset):
        here = group_of(offset)

        def body(cols):
            value = dot_nt(gg[here, :], wg[cols, :]) + dot_nt(ug[here, :], wu[cols, :])
            cots[here, cols] = value.astype(jnp.bfloat16)

        col_loop(width, tile, body)
        grad_scatter.hand(offset)

    def down_terms(offset):
        here = group_of(offset)

        def body(cols):
            rows[here, cols] = dot_nn(hid[here, :], wd[:, cols]).astype(jnp.bfloat16)

        col_loop(width, tile, body)
        out_scatter.hand(offset)

    order = offsets(wide)
    stores[1].wait()
    grad_terms(order[0])
    grad_terms(order[1])
    grad_scatter.merge(order[0])
    grad_scatter.start(wide.half)
    for offset in order[2:]:
        grad_terms(offset)
    for hop in range(wide.half - 1, 0, -1):
        grad_scatter.merge(hop)
        grad_scatter.merge(-hop)
        grad_scatter.advance(hop)
    grad_scatter.merge(0)

    for store in stores[2:]:
        store.start()
    row_gather.finish()
    stores[0].start()
    stores[0].wait()
    for offset in order:
        down_terms(offset)
    out_scatter.merge(order[0])
    grad_scatter.arrive()

    def backward_norm(row, gain_sum):
        here = pl.ds(row, 32)
        value = middle[here, :]
        grad = grad_scatter.total(row, 32)
        scale = lax.rsqrt(jnp.mean(value * value, axis=-1, keepdims=True) + EPS)
        scaled = value * scale
        weighted = grad * gain
        mean = jnp.mean(scaled * weighted, axis=-1, keepdims=True)
        total = cot_ref[here, :].astype(jnp.float32) + scale * (weighted - scaled * mean)
        mgrad_ref[here, :] = total
        back[pl.ds(pl.multiple_of(own_head + row, 32), 32), :] = total.astype(jnp.bfloat16)
        return gain_sum + jnp.sum(grad * scaled, axis=0, keepdims=True)

    gain_out[...] = lax.fori_loop(
        0, tok // 32,
        lambda i, carried: backward_norm(pl.multiple_of(i * 32, 32), carried),
        jnp.zeros((1, width), jnp.float32),
    )
    back_gather.start(1)
    out_scatter.start(wide.half)
    for offset in order[1:]:
        out_scatter.merge(offset)
    for hop in range(wide.half - 1, 0, -1):
        out_scatter.advance(hop)
    for hop in range(1, head.half):
        back_gather.arrive(hop)
        back_gather.start(hop + 1)
    back_gather.arrive(head.half)
    back_gather.finish()
    keep = pltpu.make_async_copy(back, back_any, local_sem.at[9])
    keep.start()
    out_scatter.arrive()

    def finish_out(row):
        here = pl.ds(row, 32)
        out_ref[here, :] = (middle[here, :] + out_scatter.total(row, 32)).astype(jnp.bfloat16)

    row_loop(tok, 32, finish_out)
    head_scatter.finish()
    grad_scatter.finish()
    out_scatter.finish()
    for store in stores[2:]:
        store.wait()
    keep.wait()


def ffn_block(gated_low, inputs, cotangent, ffn_gain, out_w, gate_w, up_w, down_w):
    tok, width = inputs.shape
    head_count, wide_count = lax.axis_size("head"), lax.axis_size("wide")
    chips = wide_count // 2
    hidden_width = gate_w.shape[1]
    low, full = jnp.bfloat16, jnp.float32
    all_rows = wide_count * tok
    back_rows = head_count * tok
    shape = jax.ShapeDtypeStruct
    vm = pltpu.VMEM
    return pl.pallas_call(
        ffn_kernel,
        out_shape=(
            shape((tok, width), low),
            shape((tok, width), full),
            shape((1, width), full),
            shape((back_rows, width), low),
            shape((all_rows, width), low),
            shape((all_rows, width), low),
            shape((all_rows, hidden_width), low),
            shape((all_rows, hidden_width), low),
            shape((all_rows, hidden_width), low),
        ),
        in_specs=[VMEM] * 4 + [ANY] * 4,
        out_specs=tuple([VMEM] * 3 + [ANY] * 6),
        scratch_shapes=[
            vm(out_w.shape, low), vm(gate_w.shape, low), vm(up_w.shape, low),
            vm(down_w.shape, low),
            vm((all_rows, width), low), vm((all_rows, width), low),
            vm((all_rows, hidden_width), full),
            vm((all_rows, hidden_width), low), vm((all_rows, hidden_width), low),
            vm((all_rows, hidden_width), low),
            vm((chips, tok, width), low),
            vm((2, chips // 2, tok, width), low),
            vm((chips, tok, width), low),
            vm((2, chips // 2, tok, width), low),
            vm((back_rows, width), low), vm((2, head_count // 2, tok, width), low),
            vm((tok, width), full), vm((back_rows, width), low),
            DMA((10,)),
            *ring_sems(head_count),
            *ring_sems(chips), *pass_sems(chips),
            *ring_sems(chips), *pass_sems(chips),
            *ring_sems(chips), DMA((chips,)), DMA((chips,)),
            *ring_sems(chips), DMA((chips,)), DMA((chips,)),
            *ring_sems(head_count),
        ],
        compiler_params=pltpu.CompilerParams(
            collective_id=1, has_side_effects=True, vmem_limit_bytes=VMEM_LIMIT
        ),
        cost_estimate=pl.CostEstimate(
            flops=10 * all_rows * width * hidden_width, bytes_accessed=200 << 20, transcendentals=0
        ),
        name="ffn_block",
    )(gated_low, inputs, cotangent, ffn_gain[None], out_w, gate_w, up_w, down_w)


def contract_rows(left_mat, right_mat):
    return lax.dot_general(
        left_mat, right_mat, (((0,), (0,)), ((), ())), preferred_element_type=jnp.float32
    )


def contract_cols(left_mat, right_mat):
    return lax.dot_general(
        left_mat, right_mat, (((1,), (1,)), ((), ())), preferred_element_type=jnp.float32
    )


def shards(
    inputs,
    attn_gain,
    query_weight,
    key_projection,
    value_projection,
    attn_gate_weight,
    output_weight,
    query_gain,
    key_gain,
    ffn_gain,
    ffn_gate_weight,
    ffn_up_weight,
    ffn_down_weight,
    doc_lengths,
    cotangent,
):
    tok_dev = inputs.shape[0]
    head_width = query_gain.shape[0]
    head_count = lax.axis_size("head")
    wide_count = lax.axis_size("wide")
    query_rows = tok_dev * head_count
    wide_pos = lax.axis_index("wide")
    local_ids = jnp.arange(query_rows, dtype=jnp.int32)
    query_tok = (local_ids // tok_dev * wide_count + wide_pos) * tok_dev + local_ids % tok_dev
    query_seg, query_pos, query_first = token_tables(doc_lengths, query_tok)
    starts = query_first[::tok_dev]
    firsts = query_first[:, None]
    cosine, sine_tab = rotary(query_pos, head_width)
    block_in = inputs.astype(jnp.float32)
    normed, input_norm_back = jax.vjp(rms_apply, block_in, attn_gain)
    normed_low = normed.astype(jnp.bfloat16)
    gathered = lax.all_gather(normed_low, "head", axis=0, tiled=True)
    query_pre = jnp.dot(gathered, query_weight, preferred_element_type=jnp.float32)
    key_pre = jnp.dot(gathered, key_projection, preferred_element_type=jnp.float32)
    value_pre = jnp.dot(gathered, value_projection, preferred_element_type=jnp.float32)
    gate_pre = jnp.dot(gathered, attn_gate_weight, preferred_element_type=jnp.float32)

    def prep_heads(pre_proj, gain_vec):
        return head_prep(pre_proj, gain_vec, cosine, sine_tab)

    query_rot, query_back = jax.vjp(prep_heads, query_pre, query_gain)
    key_rot, key_back = jax.vjp(prep_heads, key_pre, key_gain)
    query_low = query_rot.astype(jnp.bfloat16)
    key_low = key_rot.astype(jnp.bfloat16)
    value_low = value_pre.astype(jnp.bfloat16)
    key_wide, value_wide = (
        lax.all_gather(key_low, "wide", axis=0, tiled=True),
        lax.all_gather(value_low, "wide", axis=0, tiled=True),
    )
    kv_width = key_wide.shape[1]

    def natural_order(matrix):
        return (
            matrix.reshape(wide_count, head_count, tok_dev, kv_width)
            .transpose(1, 0, 2, 3)
            .reshape(-1, kv_width)
        )

    def gathered_order(matrix):
        return (
            matrix.reshape(head_count, wide_count, tok_dev, kv_width)
            .transpose(1, 0, 2, 3)
            .reshape(-1, kv_width)
        )

    key_entire = natural_order(key_wide)
    value_entire = natural_order(value_wide)
    attended, inverse, gated_low = attention_forward(
        query_low, key_entire, value_entire, starts, firsts, gate_pre
    )
    gate_sig = jax.nn.sigmoid(gate_pre)
    (
        outputs,
        middle_grad,
        ffn_gain_part,
        back_rows,
        ffn_rows,
        cot_rows,
        hidden_low,
        gate_grad_low,
        up_grad_low,
    ) = ffn_block(
        gated_low,
        inputs,
        cotangent,
        ffn_gain,
        output_weight,
        ffn_gate_weight,
        ffn_up_weight,
        ffn_down_weight,
    )
    ffn_gain_part = ffn_gain_part[0]
    down_wgrad = contract_rows(hidden_low, cot_rows)
    gate_wgrad = contract_rows(ffn_rows, gate_grad_low)
    up_wgrad = contract_rows(ffn_rows, up_grad_low)
    gated_grad = contract_cols(back_rows, output_weight)
    out_wgrad = contract_rows(gated_low, back_rows)
    attended_grad_low = (gated_grad * gate_sig).astype(jnp.bfloat16)
    gate_pre_grad_low = (gated_grad * attended * gate_sig * (1.0 - gate_sig)).astype(jnp.bfloat16)
    query_rot_grad, key_natural, value_natural = attention_backward(
        query_low, attended_grad_low, attended, inverse, key_entire, value_entire, starts, firsts
    )
    key_terms = gathered_order(key_natural)
    value_terms = gathered_order(value_natural)
    key_rot_grad, value_sum = (
        lax.psum_scatter(
            key_terms.astype(jnp.bfloat16), "wide", scatter_dimension=0, tiled=True
        ).astype(jnp.float32),
        lax.psum_scatter(
            value_terms.astype(jnp.bfloat16), "wide", scatter_dimension=0, tiled=True
        ).astype(jnp.float32),
    )
    query_pre_grad, query_gain_part = query_back(query_rot_grad)
    key_pre_grad, key_gain_part = key_back(key_rot_grad)
    query_pre_low = query_pre_grad.astype(jnp.bfloat16)
    key_pre_low = key_pre_grad.astype(jnp.bfloat16)
    value_grad_low = value_sum.astype(jnp.bfloat16)
    query_wgrad = contract_rows(gathered, query_pre_low)
    key_wgrad = contract_rows(gathered, key_pre_low)
    value_wgrad = contract_rows(gathered, value_grad_low)
    attn_gate_wgrad = contract_rows(gathered, gate_pre_grad_low)
    normed_terms = (
        contract_cols(query_pre_low, query_weight)
        + contract_cols(key_pre_low, key_projection)
        + contract_cols(value_grad_low, value_projection)
        + contract_cols(gate_pre_grad_low, attn_gate_weight)
    )
    normed_grad = lax.psum_scatter(
        normed_terms.astype(jnp.bfloat16), "head", scatter_dimension=0, tiled=True
    ).astype(jnp.float32)
    input_norm_grad, attn_gain_part = input_norm_back(normed_grad)
    input_grad = middle_grad + input_norm_grad
    query_grad, key_grad, value_grad, attn_gate_grad, output_grad = (
        lax.psum_scatter(
            query_wgrad.astype(jnp.bfloat16), "wide", scatter_dimension=0, tiled=True
        ).astype(jnp.float32),
        lax.psum_scatter(
            key_wgrad.astype(jnp.bfloat16), "wide", scatter_dimension=0, tiled=True
        ).astype(jnp.float32),
        lax.psum_scatter(
            value_wgrad.astype(jnp.bfloat16), "wide", scatter_dimension=0, tiled=True
        ).astype(jnp.float32),
        lax.psum_scatter(
            attn_gate_wgrad.astype(jnp.bfloat16), "wide", scatter_dimension=0, tiled=True
        ).astype(jnp.float32),
        lax.psum_scatter(
            out_wgrad.astype(jnp.bfloat16), "wide", scatter_dimension=1, tiled=True
        ).astype(jnp.float32),
    )
    ffn_gate_grad, ffn_up_grad, ffn_down_grad = (
        lax.psum_scatter(
            gate_wgrad.astype(jnp.bfloat16), "head", scatter_dimension=0, tiled=True
        ).astype(jnp.float32),
        lax.psum_scatter(
            up_wgrad.astype(jnp.bfloat16), "head", scatter_dimension=0, tiled=True
        ).astype(jnp.float32),
        lax.psum_scatter(
            down_wgrad.astype(jnp.bfloat16), "head", scatter_dimension=1, tiled=True
        ).astype(jnp.float32),
    )
    attn_gain_grad, ffn_gain_grad, query_gain_grad, key_gain_grad = lax.psum(
        (attn_gain_part, ffn_gain_part, query_gain_part, key_gain_part), ("head", "wide")
    )
    return (
        outputs,
        input_grad,
        attn_gain_grad,
        query_grad,
        key_grad,
        value_grad,
        attn_gate_grad,
        output_grad,
        query_gain_grad,
        key_gain_grad,
        ffn_gain_grad,
        ffn_gate_grad,
        ffn_up_grad,
        ffn_down_grad,
    )


def solution(mesh):
    placed = (
        P(("head", "wide"), None),
        P(),
        P(None, "head"),
        P(None, "head"),
        P(None, "head"),
        P(None, "head"),
        P("head", None),
        P(),
        P(),
        P(),
        P(None, "wide"),
        P(None, "wide"),
        P("wide", None),
        P(),
        P(("head", "wide"), None),
    )
    return jax.shard_map(
        shards,
        mesh=mesh,
        in_specs=placed,
        out_specs=(
            P(("head", "wide"), None),
            P(("head", "wide"), None),
            P(),
            P("wide", "head"),
            P("wide", "head"),
            P("wide", "head"),
            P("wide", "head"),
            P("head", "wide"),
            P(),
            P(),
            P(),
            P("head", "wide"),
            P("head", "wide"),
            P("wide", "head"),
        ),
        check_vma=False,
    )
```

```python
import jax
import jax.numpy as jnp
from jax import lax
from jax.experimental import pallas as pl
from jax.experimental.pallas import tpu as pltpu
from jax.sharding import PartitionSpec as P

EPS = 1e-06
THETA = 1000000.0
VMEM_LIMIT = 63 << 20


def rms_apply(values, gain_vec):
    return values * lax.rsqrt(jnp.mean(values * values, axis=-1, keepdims=True) + EPS) * gain_vec


def token_tables(doc_lengths, token_ids):
    lengths = doc_lengths.reshape(-1)
    doc_ends = jnp.cumsum(lengths)
    before = doc_ends[None, :] <= token_ids[:, None]
    document_segment = jnp.sum(before.astype(jnp.int32), axis=1)
    doc_first = jnp.sum(jnp.where(before, lengths[None, :], 0), axis=1)
    return (document_segment, token_ids - doc_first, doc_first)


def rotary(position, head_width):
    half_width = head_width // 2
    inverse = THETA ** (-(jnp.arange(half_width, dtype=jnp.float32) * 2.0 / head_width))
    angles = position.astype(jnp.float32)[:, None] * inverse[None, :]
    cosine = jnp.cos(angles)
    sine_tab = jnp.sin(angles)
    return (
        jnp.concatenate([cosine, cosine], axis=1),
        jnp.concatenate([sine_tab, sine_tab], axis=1),
    )


def head_prep(pre_proj, gain_vec, cosine, sine_tab):
    row_count = pre_proj.shape[0]
    head_width = gain_vec.shape[0]
    half_width = head_width // 2
    per_head = rms_apply(pre_proj.reshape(row_count, -1, head_width), gain_vec)
    turned = jnp.concatenate([-per_head[..., half_width:], per_head[..., :half_width]], axis=-1)
    rotated = per_head * cosine[:, None, :] + turned * sine_tab[:, None, :]
    return rotated.reshape(row_count, -1)


MESH = pl.DeviceIdType.MESH
ANY = pl.BlockSpec(memory_space=pl.ANY)
VMEM = pl.BlockSpec(memory_space=pltpu.VMEM)
DMA = pltpu.SemaphoreType.DMA
SIDES = (0, 1)


class Ring:
    def __init__(self, size, pos, index, device):
        self.size, self.pos, self.half = size, pos, size // 2
        self._index, self._device = index, device

    def at(self, offset):
        return lax.rem(self.pos + (offset + 2 * self.size), self.size)

    def index(self, offset):
        return self._index(self.at(offset))

    def device(self, offset):
        return self._device(self.at(offset))


def head_ring():
    size = lax.axis_size("head")
    spread = size // 2
    own, wide = lax.axis_index("head"), lax.axis_index("wide")
    major, minor = lax.div(own, 2), lax.rem(own, 2)
    pos = major + minor * (size - 1 - 2 * major)

    def index(place):
        upper = lax.div(place, spread)
        return 2 * (place + upper * (size - 1 - 2 * place)) + upper

    return Ring(size, pos, index, lambda place: (index(place), wide))


def wide_ring():
    size = lax.axis_size("wide") // 2
    head, wide = lax.axis_index("head"), lax.axis_index("wide")
    core = lax.rem(wide, 2)
    ring = Ring(
        size, lax.div(wide, 2), lambda place: place, lambda place: (head, 2 * place + core)
    )
    ring.core = core
    ring.sibling = (head, wide + 1 - 2 * core)
    return ring


def meet(devices):
    barrier = pltpu.get_barrier_semaphore()
    for device in devices:
        pl.semaphore_signal(barrier, inc=1, device_id=device, device_id_type=MESH)
    pl.semaphore_wait(barrier, len(devices))


def neighbours(*rings):
    found = []
    for ring in rings:
        found += [ring.device(1), ring.device(-1)]
        if hasattr(ring, "sibling"):
            found.append(ring.sibling)
    return found


def remote(src, dst, send, recv, device):
    return pltpu.make_async_remote_copy(
        src_ref=src, dst_ref=dst, send_sem=send, recv_sem=recv, device_id=device,
        device_id_type=MESH,
    )


class Gather:
    def __init__(self, ring, slot, rows, send, recv):
        self.ring, self.slot, self.rows = ring, slot, rows
        self.send, self.recv = send, recv

    def span(self, hop, side):
        if 2 * hop == self.ring.size:
            return side * (self.rows // 2), self.rows // 2
        return 0, self.rows

    def copy(self, hop, side):
        way = 1 - 2 * side
        ref = self.slot(self.ring.index(-way * (hop - 1)), *self.span(hop, side))
        return remote(
            ref, ref, self.send.at[side, hop - 1], self.recv.at[side, hop - 1],
            self.ring.device(way),
        )

    def start(self, hop):
        for side in SIDES:
            self.copy(hop, side).start()

    def arrive(self, hop):
        for side in SIDES:
            self.copy(hop, side).wait_recv()

    def finish(self):
        for hop in range(1, self.ring.half + 1):
            for side in SIDES:
                self.copy(hop, side).wait_send()


class PairGather(Gather):
    def __init__(self, ring, slot, rows, send, recv, pass_send, pass_recv):
        core = ring.core
        super().__init__(
            ring, lambda index, start, size: slot(2 * index + core, start, size), rows, send, recv
        )
        self.pass_send, self.pass_recv = pass_send, pass_recv

    def handed(self, hop, side):
        way = 1 - 2 * side
        span = self.span(hop, side) if hop else (0, self.rows)
        ref = self.slot(self.ring.index(-way * hop), *span)
        return remote(
            ref, ref, self.pass_send.at[side, hop], self.pass_recv.at[side, hop],
            self.ring.sibling,
        )

    def hand(self, hop):
        for side in SIDES if hop else (0,):
            self.handed(hop, side).start()

    def take(self, hop):
        for side in SIDES if hop else (0,):
            self.handed(hop, side).wait_recv()

    def begin(self):
        self.start(1)
        self.hand(0)

    def finish(self):
        super().finish()
        for hop in range(self.ring.half + 1):
            for side in SIDES if hop else (0,):
                self.handed(hop, side).wait_send()


def row_loop(rows, chunk, body):
    @pl.loop(0, rows // chunk)
    def _(step):
        body(pl.multiple_of(step * chunk, chunk))


class Scatter:
    def __init__(self, ring, part, rows, into, send, recv):
        self.ring, self.part, self.rows, self.into = ring, part, rows, into
        self.send, self.recv = send, recv

    def span(self, hop, side):
        if 2 * hop == self.ring.size:
            return side * (self.rows // 2), self.rows // 2
        return 0, self.rows

    def copy(self, hop, side):
        way = 1 - 2 * side
        first, count = self.span(hop, side)
        ref, base = self.part(self.ring.index(way * hop))
        return remote(
            ref.at[pl.ds(base + first, count)],
            self.into.at[side, pl.ds((hop - 1) * self.rows + self.inside(hop, first), count)],
            self.send.at[side, hop - 1], self.recv.at[side, hop - 1], self.ring.device(way),
        )

    def inside(self, hop, row):
        return row % (self.rows // 2) if 2 * hop == self.ring.size else row

    def start(self, hop):
        for side in SIDES:
            self.copy(hop, side).start()

    def fold(self, hop, side):
        way = 1 - 2 * side
        self.copy(hop + 1, side).wait_recv()
        first, count = self.span(hop + 1, side)
        ref, base = self.part(self.ring.index(way * hop))
        chunk = min(count, 32)

        def add(row):
            there = pl.ds(pl.multiple_of(base + first + row, chunk), chunk)
            start = hop * self.rows + self.inside(hop + 1, first)
            here = pl.ds(pl.multiple_of(start + row, chunk), chunk)
            ref[there, :] = (
                ref[there, :].astype(jnp.float32) + self.into[side, here, :].astype(jnp.float32)
            ).astype(ref.dtype)

        row_loop(count, chunk, add)

    def advance(self, hop):
        for side in SIDES:
            self.fold(hop, side)
            self.copy(hop, side).start()

    def arrive(self):
        for side in SIDES:
            self.copy(1, side).wait_recv()

    def total(self, row, count):
        ref, base = self.part(self.ring.index(0))
        there = pl.ds(pl.multiple_of(base + row, count), count)
        here = pl.ds(row, count)
        return (
            ref[there, :].astype(jnp.float32)
            + self.into[0, here, :].astype(jnp.float32)
            + self.into[1, here, :].astype(jnp.float32)
        )

    def finish(self):
        for hop in range(1, self.ring.half + 1):
            for side in SIDES:
                self.copy(hop, side).wait_send()


class PairScatter(Scatter):
    def __init__(self, ring, terms, rows, passed, into, send, recv, pass_send, pass_recv):
        core = ring.core
        super().__init__(
            ring, lambda index: (terms, (2 * index + core) * rows), rows, into, send, recv
        )
        self.terms, self.passed = terms, passed
        self.pass_send, self.pass_recv = pass_send, pass_recv

    def handed(self, offset):
        ring = self.ring
        index = ring.index(offset)
        other = pl.multiple_of((2 * index + 1 - ring.core) * self.rows, self.rows)
        slot = offset % ring.size
        return remote(
            self.terms.at[pl.ds(other, self.rows)],
            self.passed.at[slot],
            self.pass_send.at[slot], self.pass_recv.at[slot], ring.sibling,
        )

    def hand(self, offset):
        self.handed(offset).start()

    def merge(self, offset):
        self.handed(offset).wait_recv()
        slot = offset % self.ring.size
        ref, base = self.part(self.ring.index(offset))
        chunk = 32

        def add(row):
            there = pl.ds(pl.multiple_of(base + row, chunk), chunk)
            ref[there, :] = (
                ref[there, :].astype(jnp.float32)
                + self.passed[slot, pl.ds(row, chunk), :].astype(jnp.float32)
            ).astype(ref.dtype)

        row_loop(self.rows, chunk, add)

    def finish(self):
        super().finish()
        for offset in range(self.ring.size):
            self.handed(offset).wait_send()


def offsets(ring):
    order = [ring.half]
    for hop in range(ring.half - 1, 0, -1):
        order += [hop, -hop]
    return order + [0]


def into_shape(size, rows, columns):
    return pltpu.VMEM((2, (size - 1) * rows // 2, columns), jnp.bfloat16)


def everyone(*rings):
    found = []
    for ring in rings:
        found += [ring.device(offset) for offset in range(1, ring.size)]
        if hasattr(ring, "sibling"):
            found.append(ring.sibling)
    return found


def ring_sems(size):
    return [DMA((2, size // 2)), DMA((2, size // 2))]


def pass_sems(size):
    return [DMA((2, size // 2 + 1)), DMA((2, size // 2 + 1))]


def dot_nn(left, right):
    return jnp.dot(left, right, preferred_element_type=jnp.float32)


def dot_nt(left, right):
    return lax.dot_general(
        left, right, (((1,), (1,)), ((), ())), preferred_element_type=jnp.float32
    )


def dot_tn(left, right):
    return lax.dot_general(
        left, right, (((0,), (0,)), ((), ())), preferred_element_type=jnp.float32
    )


LANES = 128
KEY_BLOCK = 512
LOG2E = 1.4426950408889634


def attention_forward_kernel(
    start_ref, query_ref, key_ref, value_ref, first_ref, gate_ref, att_ref, inv_ref, gated_ref, acc
):
    blocks = start_ref.shape[0]
    groups = key_ref.shape[1] // LANES
    per = query_ref.shape[1] // key_ref.shape[1]
    rows = query_ref.shape[0] // blocks
    wide_count = key_ref.shape[0] // query_ref.shape[0]
    wide_pos = lax.axis_index("wide")
    step = KEY_BLOCK
    factor = LANES ** (-0.5) * LOG2E

    @pl.loop(0, blocks)
    def _(blk):
        here = pl.ds(pl.multiple_of(blk * rows, rows), rows)
        first_tok = (blk * wide_count + wide_pos) * rows
        key_lane = lax.broadcasted_iota(jnp.int32, (rows, step), 1)
        query_row = lax.broadcasted_iota(jnp.int32, (rows, step), 0) + first_tok
        upper = key_lane - query_row
        lower = key_lane - first_ref[here, :]
        queries = [
            jnp.concatenate(
                [
                    query_ref[here, (g * per + j) * LANES : (g * per + j + 1) * LANES]
                    for j in range(per)
                ],
                axis=0,
            )
            for g in range(groups)
        ]
        acc[...] = jnp.zeros_like(acc)

        @pl.loop(start_ref[blk] // step, (first_tok + rows + step - 1) // step)
        def _(tile):
            base = tile * step
            there = pl.ds(pl.multiple_of(base, step), step)
            allowed = (upper <= -base) & (lower >= -base)
            allowed = jnp.concatenate([allowed] * per, axis=0)
            for g in range(groups):
                cols = slice(g * LANES, (g + 1) * LANES)
                scores = lax.dot_general(
                    queries[g], key_ref[there, cols], (((1,), (1,)), ((), ())),
                    preferred_element_type=jnp.float32,
                )
                probs = jnp.where(allowed, jnp.exp2(scores * factor), 0.0).astype(jnp.bfloat16)
                values = jnp.concatenate(
                    [value_ref[there, cols], jnp.ones((step, LANES), jnp.bfloat16)], axis=1
                )
                acc[g] += jnp.dot(probs, values, preferred_element_type=jnp.float32)

        for g in range(groups):
            for j in range(per):
                part = acc[g, j * rows : (j + 1) * rows, :]
                cols = slice((g * per + j) * LANES, (g * per + j + 1) * LANES)
                inverse = 1.0 / part[:, LANES:]
                out = part[:, :LANES] * inverse
                att_ref[here, cols] = out
                inv_ref[here, cols] = inverse
                gated_ref[here, cols] = (out * jax.nn.sigmoid(gate_ref[here, cols])).astype(
                    jnp.bfloat16
                )


def attention_forward(query_low, key_all, value_all, starts, firsts, gate_pre):
    rows, width = query_low.shape
    groups = key_all.shape[1] // LANES
    per = width // key_all.shape[1]
    blocks = starts.shape[0]
    vmem = pl.BlockSpec(memory_space=pltpu.VMEM)
    return pl.pallas_call(
        attention_forward_kernel,
        out_shape=(
            jax.ShapeDtypeStruct((rows, width), jnp.float32),
            jax.ShapeDtypeStruct((rows, width), jnp.float32),
            jax.ShapeDtypeStruct((rows, width), jnp.bfloat16),
        ),
        in_specs=[pl.BlockSpec(memory_space=pltpu.SMEM)] + [vmem] * 5,
        out_specs=(vmem, vmem, vmem),
        scratch_shapes=[pltpu.VMEM((groups, per * (rows // blocks), 2 * LANES), jnp.float32)],
        compiler_params=pltpu.CompilerParams(vmem_limit_bytes=VMEM_LIMIT),
        cost_estimate=pl.CostEstimate(
            flops=4 * rows * width * 2048, bytes_accessed=12 << 20, transcendentals=0
        ),
        name="attention_forward",
    )(starts, query_low, key_all, value_all, firsts, gate_pre)


def attention_backward_kernel(
    start_ref, query_ref, grad_ref, att_ref, inv_ref, key_ref, keyt_ref, value_ref, first_ref,
    dq_ref, kv_ref, dk_acc, dv_acc, dqt,
):
    blocks = start_ref.shape[0]
    groups = key_ref.shape[1] // LANES
    per = query_ref.shape[1] // key_ref.shape[1]
    rows = query_ref.shape[0] // blocks
    wide_count = key_ref.shape[0] // query_ref.shape[0]
    wide_pos = lax.axis_index("wide")
    step = KEY_BLOCK
    scale = LANES ** (-0.5)
    dk_acc[...] = jnp.zeros_like(dk_acc)
    dv_acc[...] = jnp.zeros_like(dv_acc)

    @pl.loop(0, blocks)
    def _(blk):
        here = pl.ds(pl.multiple_of(blk * rows, rows), rows)
        first_tok = (blk * wide_count + wide_pos) * rows
        key_row = lax.broadcasted_iota(jnp.int32, (step, rows), 0)
        query_lane = lax.broadcasted_iota(jnp.int32, (step, rows), 1) + first_tok
        upper = key_row - query_lane
        lower = key_row - jnp.transpose(
            jnp.broadcast_to(first_ref[here, :], (rows, LANES))
        )[0:1, :]
        queries, grads, deltas = [], [], []
        for g in range(groups):
            qs, gs, ds = [], [], []
            for j in range(per):
                cols = slice((g * per + j) * LANES, (g * per + j + 1) * LANES)
                grad = grad_ref[here, cols].astype(jnp.float32)
                inverse = inv_ref[here, cols]
                both = grad * inverse
                delta = jnp.sum(both * att_ref[here, cols], axis=1, keepdims=True)
                ds.append(jnp.transpose(jnp.broadcast_to(delta, (rows, LANES)))[0:1, :])
                qs.append(query_ref[here, cols])
                gs.append(both.astype(jnp.bfloat16))
            queries.append(jnp.concatenate(qs, axis=0))
            grads.append(jnp.concatenate(gs, axis=0))
            deltas.append(jnp.concatenate(ds, axis=1))
        dqt[...] = jnp.zeros_like(dqt)

        @pl.loop(start_ref[blk] // step, (first_tok + rows + step - 1) // step)
        def _(tile):
            base = tile * step
            there = pl.ds(pl.multiple_of(base, step), step)
            allowed = (upper <= -base) & (lower >= -base)
            allowed = jnp.concatenate([allowed] * per, axis=1)
            for g in range(groups):
                cols = slice(g * LANES, (g + 1) * LANES)
                scores = lax.dot_general(
                    key_ref[there, cols], queries[g], (((1,), (1,)), ((), ())),
                    preferred_element_type=jnp.float32,
                )
                probs = jnp.where(allowed, jnp.exp2(scores * (scale * LOG2E)), 0.0)
                dprobs = lax.dot_general(
                    value_ref[there, cols], grads[g], (((1,), (1,)), ((), ())),
                    preferred_element_type=jnp.float32,
                )
                dscores = (probs * (dprobs - deltas[g]) * scale).astype(jnp.bfloat16)
                dv_acc[there, cols] += jnp.dot(
                    probs.astype(jnp.bfloat16), grads[g], preferred_element_type=jnp.float32
                )
                dk_acc[there, cols] += jnp.dot(
                    dscores, queries[g], preferred_element_type=jnp.float32
                )
                dqt[g] += jnp.dot(
                    keyt_ref[cols, there], dscores, preferred_element_type=jnp.float32
                )

        for g in range(groups):
            for j in range(per):
                cols = slice((g * per + j) * LANES, (g * per + j + 1) * LANES)
                dq_ref[here, cols] = jnp.transpose(dqt[g, :, j * rows : (j + 1) * rows])

    width = dk_acc.shape[1]

    @pl.loop(0, wide_count)
    def _(target):
        for blk in range(blocks):
            source = pl.ds(pl.multiple_of((blk * wide_count + target) * rows, rows), rows)
            there = pl.ds(pl.multiple_of((target * blocks + blk) * rows, rows), rows)
            kv_ref[there, :width] = dk_acc[source, :].astype(jnp.bfloat16)
            kv_ref[there, width:] = dv_acc[source, :].astype(jnp.bfloat16)


def attention_backward(
    query_low, grad_low, attended, inverse, key_all, value_all, starts, firsts
):
    rows, width = query_low.shape
    keys, kv_width = key_all.shape
    groups = kv_width // LANES
    per = width // kv_width
    blocks = starts.shape[0]
    vmem = pl.BlockSpec(memory_space=pltpu.VMEM)
    return pl.pallas_call(
        attention_backward_kernel,
        out_shape=(
            jax.ShapeDtypeStruct((rows, width), jnp.float32),
            jax.ShapeDtypeStruct((keys, 2 * kv_width), jnp.bfloat16),
        ),
        in_specs=[pl.BlockSpec(memory_space=pltpu.SMEM)] + [vmem] * 8,
        out_specs=(vmem, vmem),
        scratch_shapes=[
            pltpu.VMEM((keys, kv_width), jnp.float32),
            pltpu.VMEM((keys, kv_width), jnp.float32),
            pltpu.VMEM((groups, LANES, per * (rows // blocks)), jnp.float32),
        ],
        compiler_params=pltpu.CompilerParams(vmem_limit_bytes=VMEM_LIMIT),
        cost_estimate=pl.CostEstimate(
            flops=10 * rows * width * 2048, bytes_accessed=20 << 20, transcendentals=0
        ),
        name="attention_backward",
    )(starts, query_low, grad_low, attended, inverse, key_all, key_all.T, value_all, firsts)


def ffn_kernel(
    gated_ref, x_ref, cot_ref, gain_ref, wo_any, wg_any, wu_any, wd_any,
    out_any, mgrad_ref, gain_out, back_any, down_ref, fgate_any, fup_any,
    wo, wg, wu, wd, cots, rows, hidden_grad, hid, gg, ug, terms_own, passed, into,
    passed2, into2, dterms, dinto, stage, hterms, hinto, middle, back, local_sem,
    ds, dr, hs, hr, cs, cr, cps, cpr, fs, fr, fps, fpr, s1, r1, ps1, pr1, s2, r2, ps2, pr2, bs, br,
):
    tok, width = x_ref.shape
    hidden_width = wg_any.shape[1]
    head, wide = head_ring(), wide_ring()
    pair = 2 * tok
    separate = terms_own.shape[0] > 16
    terms = terms_own if separate else cots
    part = wo_any.shape[1] // lax.axis_size("head")
    loads = [
        pltpu.make_async_copy(src, dst, local_sem.at[i])
        for i, (src, dst) in enumerate(((wo_any, wo), (wd_any, wd), (wg_any, wg), (wu_any, wu)))
    ]
    for load in loads:
        load.start()
    own_wide = pl.multiple_of(lax.axis_index("wide") * tok, tok)
    own_head = pl.multiple_of(lax.axis_index("head") * tok, tok)
    cots[pl.ds(own_wide, tok), :] = cot_ref[...]
    meet(neighbours(head, wide))

    def slot_of(ref):
        return lambda index, start, size: ref.at[pl.ds(index * tok + start, size)]

    cot_gather = PairGather(wide, slot_of(cots), tok, cs, cr, cps, cpr)
    row_gather = PairGather(wide, slot_of(rows), tok, fs, fr, fps, fpr)
    back_gather = Gather(head, slot_of(back), tok, bs, br)
    head_scatter = Scatter(head, lambda index: (hterms, index * tok), tok, hinto, hs, hr)
    grad_scatter = PairScatter(wide, terms, tok, passed, into, s1, r1, ps1, pr1)
    down_scatter = Scatter(
        head, lambda index: (dterms, index * hidden_width), hidden_width, dinto, ds, dr
    )
    out_scatter = PairScatter(wide, rows, tok, passed2, into2, s2, r2, ps2, pr2)

    def group_of(offset):
        return pl.ds(pl.multiple_of(wide.index(offset) * pair, pair), pair)

    def col_loop(total, step, body):
        @pl.loop(0, total // step)
        def _(i):
            body(pl.ds(pl.multiple_of(i * step, step), step))

    tile = 256
    cot_gather.begin()

    def out_part(offset, own):
        index = head.index(offset)
        here = pl.ds(pl.multiple_of(index * tok, tok), tok)

        def body(cols):
            value = dot_nn(gated_ref[here, :], wo[:, cols])
            if own:
                middle[:, cols] = x_ref[:, cols].astype(jnp.float32) + value
            else:
                hterms[here, cols] = value.astype(jnp.bfloat16)

        col_loop(width, tile, body)

    def hidden_part(offset):
        here = group_of(offset)

        def body(cols):
            hidden_grad[here, cols] = dot_nt(cots[here, :], wd[cols, :]).astype(
                hidden_grad.dtype
            )

        col_loop(hidden_width, tile if hidden_width % tile == 0 else LANES, body)

    loads[0].wait()
    out_part(head.half, False)
    head_scatter.start(head.half)
    for hop in range(head.half - 1, 0, -1):
        out_part(hop, False)
        out_part(-hop, False)
    out_part(0, True)
    loads[1].wait()
    cot_gather.take(0)
    hidden_part(0)
    for hop in range(head.half - 1, 0, -1):
        head_scatter.advance(hop)
    for hop in range(1, wide.half):
        cot_gather.arrive(hop)
        cot_gather.start(hop + 1)
        cot_gather.hand(hop)
        cot_gather.take(hop)
        hidden_part(hop)
        hidden_part(-hop)
    head_scatter.arrive()

    gain = gain_ref[...]

    def forward_norm(row):
        here = pl.ds(row, 32)
        value = (
            middle[here, :]
            + hinto[0, here, :].astype(jnp.float32)
            + hinto[1, here, :].astype(jnp.float32)
        )
        middle[here, :] = value
        scale = lax.rsqrt(jnp.mean(value * value, axis=-1, keepdims=True) + EPS)
        rows[pl.ds(pl.multiple_of(own_wide + row, 32), 32), :] = (value * scale * gain).astype(
            jnp.bfloat16
        )

    row_loop(tok, 32, forward_norm)
    row_gather.begin()
    cot_gather.arrive(wide.half)
    cot_gather.hand(wide.half)
    cot_gather.take(wide.half)
    hidden_part(wide.half)
    cot_gather.finish()
    loads[2].wait()
    loads[3].wait()

    def unit(offset):
        here = group_of(offset)

        def body(cols):
            gate = dot_nn(rows[here, :], wg[:, cols])
            up = dot_nn(rows[here, :], wu[:, cols])
            grad = hidden_grad[here, cols].astype(jnp.float32)
            sig = jax.nn.sigmoid(gate)
            act = gate * sig
            hid[here, cols] = (act * up).astype(jnp.bfloat16)
            gg[here, cols] = (grad * up * (sig + act * (1.0 - sig))).astype(jnp.bfloat16)
            ug[here, cols] = (grad * act).astype(jnp.bfloat16)

        col_loop(hidden_width, tile if hidden_width % tile == 0 else LANES, body)

    row_gather.take(0)
    unit(0)
    for hop in range(1, wide.half):
        row_gather.arrive(hop)
        row_gather.start(hop + 1)
        row_gather.hand(hop)
        row_gather.take(hop)
        unit(hop)
        unit(-hop)
    row_gather.arrive(wide.half)
    row_gather.hand(wide.half)
    row_gather.take(wide.half)
    unit(wide.half)

    def grad_terms(offset):
        here = group_of(offset)

        def body(cols):
            value = dot_nt(gg[here, :], wg[cols, :]) + dot_nt(ug[here, :], wu[cols, :])
            terms[here, cols] = value.astype(jnp.bfloat16)

        col_loop(width, tile, body)
        grad_scatter.hand(offset)

    def down_terms(offset):
        here = group_of(offset)

        def body(cols):
            rows[here, cols] = dot_nn(hid[here, :], wd[:, cols]).astype(jnp.bfloat16)

        col_loop(width, tile, body)
        out_scatter.hand(offset)

    def down_grads():
        @pl.loop(0, lax.axis_size("head"))
        def _(index):
            cols = pl.ds(pl.multiple_of(index * part, part), part)

            @pl.loop(0, hidden_width // LANES)
            def _(i):
                lanes = pl.ds(pl.multiple_of(i * LANES, LANES), LANES)
                there = pl.ds(
                    pl.multiple_of(index * hidden_width + i * LANES, LANES), LANES
                )
                dterms[there, :] = dot_tn(hid[:, lanes], cots[:, cols]).astype(jnp.bfloat16)

        down_scatter.start(head.half)

    emit = stage.shape[2]

    def stage_copy(step, out, any_ref, slot):
        there = pl.ds(pl.multiple_of(step * emit, emit), emit)
        return pltpu.make_async_copy(
            stage.at[slot, out], any_ref.at[there], local_sem.at[5 + 2 * slot + out]
        )

    def input_grads():
        @pl.loop(0, width // emit // 2)
        def _(i):
            for slot in SIDES:
                step = 2 * i + slot
                cols = pl.ds(pl.multiple_of(step * emit, emit), emit)

                @pl.when(i > 0)
                def _():
                    for out, any_ref in enumerate((fgate_any, fup_any)):
                        stage_copy(step - 2, out, any_ref, slot).wait()

                left = rows[:, cols]
                stage[slot, 0] = dot_tn(left, gg[...]).astype(jnp.bfloat16)
                stage[slot, 1] = dot_tn(left, ug[...]).astype(jnp.bfloat16)
                for out, any_ref in enumerate((fgate_any, fup_any)):
                    stage_copy(step, out, any_ref, slot).start()

    order = offsets(wide)
    if not separate:
        down_grads()
    grad_terms(order[0])
    grad_terms(order[1])
    grad_scatter.merge(order[0])
    grad_scatter.start(wide.half)
    for offset in order[2:]:
        grad_terms(offset)
    if separate:
        down_grads()
    for hop in range(wide.half - 1, 0, -1):
        grad_scatter.merge(hop)
        grad_scatter.merge(-hop)
        grad_scatter.advance(hop)
    grad_scatter.merge(0)
    input_grads()
    row_gather.finish()
    for offset in order:
        down_terms(offset)
    out_scatter.merge(order[0])
    for hop in range(head.half - 1, 0, -1):
        down_scatter.advance(hop)
    grad_scatter.arrive()

    def backward_norm(row, gain_sum):
        here = pl.ds(row, 32)
        value = middle[here, :]
        grad = grad_scatter.total(row, 32)
        scale = lax.rsqrt(jnp.mean(value * value, axis=-1, keepdims=True) + EPS)
        scaled = value * scale
        weighted = grad * gain
        mean = jnp.mean(scaled * weighted, axis=-1, keepdims=True)
        total = cot_ref[here, :].astype(jnp.float32) + scale * (weighted - scaled * mean)
        mgrad_ref[here, :] = total
        back[pl.ds(pl.multiple_of(own_head + row, 32), 32), :] = total.astype(jnp.bfloat16)
        return gain_sum + jnp.sum(grad * scaled, axis=0, keepdims=True)

    gain_out[...] = lax.fori_loop(
        0, tok // 32,
        lambda i, carried: backward_norm(pl.multiple_of(i * 32, 32), carried),
        jnp.zeros((1, width), jnp.float32),
    )
    back_gather.start(1)
    out_scatter.start(wide.half)
    for offset in order[1:]:
        out_scatter.merge(offset)
    for hop in range(wide.half - 1, 0, -1):
        out_scatter.advance(hop)
    for hop in range(1, head.half):
        back_gather.arrive(hop)
        back_gather.start(hop + 1)
    back_gather.arrive(head.half)
    back_gather.finish()
    keep = pltpu.make_async_copy(back, back_any, local_sem.at[4])
    keep.start()
    out_scatter.arrive()

    def finish_out(row):
        here = pl.ds(row, 32)
        back[here, :] = (middle[here, :] + out_scatter.total(row, 32)).astype(jnp.bfloat16)

    keep.wait()
    row_loop(tok, 32, finish_out)
    result = pltpu.make_async_copy(back.at[pl.ds(0, tok)], out_any, local_sem.at[9])
    result.start()
    down_scatter.arrive()

    def finish_down(row):
        down_ref[pl.ds(row, 32), :] = down_scatter.total(row, 32)

    row_loop(hidden_width, 32, finish_down)
    for scatter in (head_scatter, grad_scatter, out_scatter, down_scatter):
        scatter.finish()
    last = width // emit
    for slot in SIDES:
        for out, any_ref in enumerate((fgate_any, fup_any)):
            stage_copy(last - 2 + slot, out, any_ref, slot).wait()
    result.wait()


def ffn_block(gated_low, inputs, cotangent, ffn_gain, out_w, gate_w, up_w, down_w):
    tok, width = inputs.shape
    head_count, wide_count = lax.axis_size("head"), lax.axis_size("wide")
    chips = wide_count // 2
    hidden_width = gate_w.shape[1]
    low, full = jnp.bfloat16, jnp.float32
    all_rows = wide_count * tok
    back_rows = head_count * tok
    roomy = all_rows * width <= 2 << 20
    shape = jax.ShapeDtypeStruct
    vm = pltpu.VMEM
    return pl.pallas_call(
        ffn_kernel,
        out_shape=(
            shape((tok, width), low),
            shape((tok, width), full),
            shape((1, width), full),
            shape((back_rows, width), low),
            shape((hidden_width, width // head_count), full),
            shape((width, hidden_width), low),
            shape((width, hidden_width), low),
        ),
        in_specs=[VMEM] * 4 + [ANY] * 4,
        out_specs=(ANY, VMEM, VMEM, ANY, VMEM, ANY, ANY),
        scratch_shapes=[
            vm(out_w.shape, low), vm(gate_w.shape, low), vm(up_w.shape, low),
            vm(down_w.shape, low),
            vm((all_rows, width), low), vm((all_rows, width), low),
            vm((all_rows, hidden_width), full if roomy else low),
            vm((all_rows, hidden_width), low), vm((all_rows, hidden_width), low),
            vm((all_rows, hidden_width), low),
            vm((all_rows if roomy else 16, width), low),
            vm((chips, tok, width), low),
            into_shape(chips, tok, width),
            vm((chips, tok, width), low),
            into_shape(chips, tok, width),
            vm((head_count * hidden_width, width // head_count), low),
            into_shape(head_count, hidden_width, width // head_count),
            vm((2, 2, 256 if roomy else 128, hidden_width), low),
            vm((back_rows, width), low), into_shape(head_count, tok, width),
            vm((tok, width), full), vm((back_rows, width), low),
            DMA((10,)),
            *ring_sems(head_count),
            *ring_sems(head_count),
            *ring_sems(chips), *pass_sems(chips),
            *ring_sems(chips), *pass_sems(chips),
            *ring_sems(chips), DMA((chips,)), DMA((chips,)),
            *ring_sems(chips), DMA((chips,)), DMA((chips,)),
            *ring_sems(head_count),
        ],
        compiler_params=pltpu.CompilerParams(
            collective_id=1, has_side_effects=True, vmem_limit_bytes=VMEM_LIMIT
        ),
        cost_estimate=pl.CostEstimate(
            flops=10 * all_rows * width * hidden_width, bytes_accessed=200 << 20, transcendentals=0
        ),
        name="ffn_block",
    )(gated_low, inputs, cotangent, ffn_gain[None], out_w, gate_w, up_w, down_w)


def turn_back(grad, cosine, sine_tab):
    half = LANES // 2
    lane = lax.broadcasted_iota(jnp.int32, grad.shape, 1)
    turned = pltpu.roll(grad * sine_tab, half, 1)
    return grad * cosine + jnp.where(lane < half, turned, -turned)


def unprep(grad, pre_proj, gain, cosine, sine_tab):
    turned = turn_back(grad, cosine, sine_tab)
    scale = lax.rsqrt(jnp.mean(pre_proj * pre_proj, axis=-1, keepdims=True) + EPS)
    scaled = pre_proj * scale
    weighted = turned * gain
    mean = jnp.mean(scaled * weighted, axis=-1, keepdims=True)
    return scale * (weighted - scaled * mean), turned * scaled


def tail_kernel(
    dq_ref, qpre_ref, kpre_ref, ggrad_ref, cos_ref, sin_ref, qgain_ref, kgain_ref, x_ref,
    mgrad_ref, gain_ref, ffn_gain_ref, gated_ref,
    kvp_any, normed_any, back_any, wq_any, wk_any, wv_any, wg_any, fgate_any, fup_any,
    igrad_ref, gains_ref, query_out, key_out, value_out, gate_out, output_out, fgate_out, fup_out,
    kvp, normed, back, wq, wk, wv, wg, fgate, fup, qlow, klow, vlow, early, late, hterms,
    kv_passed, kv_into, early_passed, early_into, late_passed, late_into, hinto, fgate_into,
    fup_into, gain_slots, stage, local_sem,
    kvs, kvr, kvps, kvpr, es, er, eps, epr, ls, lr, lps, lpr, hs, hr, gs, gr, us, ur, gain_send,
    gain_recv,
):
    tok, width = x_ref.shape
    rows = dq_ref.shape[0]
    wide_count = lax.axis_size("wide")
    head_count = lax.axis_size("head")
    head, wide = head_ring(), wide_ring()
    loads = [
        pltpu.make_async_copy(src, dst, local_sem.at[i])
        for i, (src, dst) in enumerate(
            (
                (kvp_any, kvp), (fgate_any, fgate), (fup_any, fup), (normed_any, normed),
                (back_any, back), (wq_any, wq), (wk_any, wk), (wv_any, wv), (wg_any, wg),
            )
        )
    ]
    for load in loads:
        load.start()
    meet(everyone(head, wide))
    kv_width = wk.shape[1]
    q_width = wq.shape[1]
    block = normed.shape[1] // wide_count
    ffn_rows = fgate.shape[0] // head_count
    kv_scatter = PairScatter(wide, kvp, rows, kv_passed, kv_into, kvs, kvr, kvps, kvpr)
    early_scatter = PairScatter(wide, early, block, early_passed, early_into, es, er, eps, epr)
    late_scatter = PairScatter(wide, late, block, late_passed, late_into, ls, lr, lps, lpr)
    head_scatter = Scatter(head, lambda index: (hterms, index * tok), tok, hinto, hs, hr)
    gate_scatter = Scatter(
        head, lambda index: (fgate, index * ffn_rows), ffn_rows, fgate_into, gs, gr
    )
    up_scatter = Scatter(head, lambda index: (fup, index * ffn_rows), ffn_rows, fup_into, us, ur)
    order = offsets(wide)

    loads[0].wait()
    for offset in order:
        kv_scatter.hand(offset)
    loads[1].wait()
    gate_scatter.start(head.half)
    loads[2].wait()
    up_scatter.start(head.half)

    chunk = 128

    def query_back(row, total):
        here = pl.ds(row, chunk)
        for j in range(q_width // LANES):
            cols = slice(j * LANES, (j + 1) * LANES)
            value, terms = unprep(
                dq_ref[here, cols], qpre_ref[here, cols], qgain_ref[...], cos_ref[here, :],
                sin_ref[here, :],
            )
            qlow[here, cols] = value.astype(jnp.bfloat16)
            total = total + jnp.sum(terms, axis=0, keepdims=True)
        return total

    def over_rows(count, body, start):
        return lax.fori_loop(
            0, count // chunk, lambda i, carried: body(pl.multiple_of(i * chunk, chunk), carried),
            start,
        )

    qgain_sum = over_rows(rows, query_back, jnp.zeros((1, LANES), jnp.float32))

    kv_scatter.merge(order[0])
    kv_scatter.start(wide.half)
    loads[3].wait()
    loads[4].wait()

    def early_part(offset):
        index = wide.index(offset)

        @pl.loop(0, 2)
        def _(core):
            target = 2 * index + core
            cols = pl.ds(pl.multiple_of(target * block, block), block)
            there = pl.ds(pl.multiple_of(target * block, block), block)
            left = normed[:, cols]
            early[there, :q_width] = dot_tn(left, qlow[...]).astype(jnp.bfloat16)
            early[there, q_width : 2 * q_width] = dot_tn(left, ggrad_ref[...]).astype(jnp.bfloat16)
            out = dot_tn(gated_ref[...], back[:, cols]).astype(jnp.bfloat16)
            for piece in range(q_width // block):
                early[there, 2 * q_width + piece * block : 2 * q_width + (piece + 1) * block] = out[
                    piece * block : (piece + 1) * block, :
                ]

        early_scatter.hand(offset)

    for offset in order:
        early_part(offset)
    for offset in order[1:]:
        kv_scatter.merge(offset)
    early_scatter.merge(order[0])
    for hop in range(wide.half - 1, 0, -1):
        kv_scatter.advance(hop)
    early_scatter.start(wide.half)
    for hop in range(head.half - 1, 0, -1):
        gate_scatter.advance(hop)
        up_scatter.advance(hop)
    for offset in order[1:]:
        early_scatter.merge(offset)
    for load in loads[5:]:
        load.wait()
    kv_scatter.arrive()

    def key_back(row, total):
        here = pl.ds(row, chunk)
        both = kv_scatter.total(row, chunk)
        for j in range(kv_width // LANES):
            cols = slice(j * LANES, (j + 1) * LANES)
            value, terms = unprep(
                both[:, cols], kpre_ref[here, cols], kgain_ref[...], cos_ref[here, :],
                sin_ref[here, :],
            )
            klow[here, cols] = value.astype(jnp.bfloat16)
            total = total + jnp.sum(terms, axis=0, keepdims=True)
        vlow[here, :] = both[:, kv_width:].astype(jnp.bfloat16)
        return total

    kgain_sum = over_rows(rows, key_back, jnp.zeros((1, LANES), jnp.float32))

    def head_part(offset):
        here = pl.ds(pl.multiple_of(head.index(offset) * tok, tok), tok)

        @pl.loop(0, width // 256)
        def _(i):
            cols = pl.ds(pl.multiple_of(i * 256, 256), 256)
            value = dot_nt(qlow[here, :], wq[cols, :]) + dot_nt(ggrad_ref[here, :], wg[cols, :])
            value += dot_nt(klow[here, :], wk[cols, :]) + dot_nt(vlow[here, :], wv[cols, :])
            hterms[here, cols] = value.astype(jnp.bfloat16)

    head_part(head.half)
    head_scatter.start(head.half)

    def late_part(offset):
        index = wide.index(offset)

        @pl.loop(0, 2)
        def _(core):
            target = 2 * index + core
            cols = pl.ds(pl.multiple_of(target * block, block), block)
            left = normed[:, cols]
            late[cols, :kv_width] = dot_tn(left, klow[...]).astype(jnp.bfloat16)
            late[cols, kv_width:] = dot_tn(left, vlow[...]).astype(jnp.bfloat16)

        late_scatter.hand(offset)

    late_part(order[0])
    for hop in range(wide.half - 1, 0, -1):
        early_scatter.advance(hop)
    for offset in order[1:]:
        late_part(offset)
    late_scatter.merge(order[0])
    late_scatter.start(wide.half)
    for hop in range(head.half - 1, 0, -1):
        head_part(hop)
        head_part(-hop)
        head_scatter.advance(hop)
    head_part(0)
    for offset in order[1:]:
        late_scatter.merge(offset)
    for hop in range(wide.half - 1, 0, -1):
        late_scatter.advance(hop)

    gate_scatter.arrive()
    up_scatter.arrive()
    emit = 64
    pending = [None, None]
    for step in range(ffn_rows // emit):
        for which, (scatter, out) in enumerate(((gate_scatter, fgate_out), (up_scatter, fup_out))):
            if pending[which] is not None:
                pending[which].wait()
            stage[which] = scatter.total(step * emit, emit)
            pending[which] = pltpu.make_async_copy(
                stage.at[which], out.at[pl.ds(step * emit, emit)], local_sem.at[9 + which]
            )
            pending[which].start()

    head_scatter.arrive()
    gain = gain_ref[...]

    def input_back(row, total):
        here = pl.ds(row, 32)
        value = x_ref[here, :].astype(jnp.float32)
        grad = head_scatter.total(row, 32)
        scale = lax.rsqrt(jnp.mean(value * value, axis=-1, keepdims=True) + EPS)
        scaled = value * scale
        weighted = grad * gain
        mean = jnp.mean(scaled * weighted, axis=-1, keepdims=True)
        igrad_ref[here, :] = mgrad_ref[here, :] + scale * (weighted - scaled * mean)
        return total + jnp.sum(grad * scaled, axis=0, keepdims=True)

    gain_sum = lax.fori_loop(
        0, tok // 32, lambda i, carried: input_back(pl.multiple_of(i * 32, 32), carried),
        jnp.zeros((1, width), jnp.float32),
    )
    chips = wide.size
    pair_slot, chip_slot = 0, 2
    head_slot = 2 + chips
    mine = gain_slots.at[pair_slot]
    mine[...] = jnp.zeros(mine.shape, jnp.float32)
    mine[0:1, :] = gain_sum
    mine[1:2, :] = ffn_gain_ref[...]
    mine[2:3, 0:LANES] = qgain_sum
    mine[3:4, 0:LANES] = kgain_sum
    swap = remote(
        mine, gain_slots.at[1], gain_send.at[0], gain_recv.at[0], wide.sibling
    )
    swap.start()
    swap.wait_recv()

    def spread(ring, own, base, sem):
        here = gain_slots.at[base + own]
        copies = [
            remote(here, here, gain_send.at[sem + d], gain_recv.at[sem + d], ring.device(d))
            for d in range(1, ring.size)
        ]
        for copy in copies:
            copy.start()
        for copy in copies:
            copy.wait_recv()
        return copies

    own_chip = wide.index(0)
    gain_slots[chip_slot + own_chip] = gain_slots[0] + gain_slots[1]
    sent = [swap] + spread(wide, own_chip, chip_slot, 0)
    total = gain_slots[chip_slot]
    for i in range(1, chips):
        total = total + gain_slots[chip_slot + i]
    own_head = lax.axis_index("head")
    gain_slots[head_slot + own_head] = total
    sent += spread(head, own_head, head_slot, chips - 1)
    total = gain_slots[head_slot]
    for i in range(1, head_count):
        total = total + gain_slots[head_slot + i]
    gains_ref[...] = total

    early_scatter.arrive()

    def early_out(row):
        here = pl.ds(row, 32)
        both = early_scatter.total(row, 32)
        query_out[here, :] = both[:, :q_width]
        gate_out[here, :] = both[:, q_width : 2 * q_width]
        for piece in range(q_width // block):
            output_out[pl.ds(pl.multiple_of(piece * block + row, 32), 32), :] = both[
                :, 2 * q_width + piece * block : 2 * q_width + (piece + 1) * block
            ]

    row_loop(block, 32, early_out)
    late_scatter.arrive()

    def late_out(row):
        here = pl.ds(row, 32)
        both = late_scatter.total(row, 32)
        key_out[here, :] = both[:, :kv_width]
        value_out[here, :] = both[:, kv_width:]

    row_loop(block, 32, late_out)
    for scatter in (
        kv_scatter, early_scatter, late_scatter, head_scatter, gate_scatter, up_scatter
    ):
        scatter.finish()
    for copy in sent:
        copy.wait_send()
    for copy in pending:
        copy.wait()


def tail_block(
    dq, kv_parts, query_pre, key_pre, gate_grad, cosine, sine_tab, query_gain, key_gain, inputs,
    middle_grad, attn_gain, ffn_gain_part, gated_low, normed, back_rows, weights, fgate, fup,
):
    tok, width = inputs.shape
    head_count, wide_count = lax.axis_size("head"), lax.axis_size("wide")
    chips = wide_count // 2
    rows, q_width = dq.shape
    kv_width = key_pre.shape[1]
    block = width // wide_count
    hidden_width = fgate.shape[1]
    ffn_rows = width // head_count
    low, full = jnp.bfloat16, jnp.float32
    shape, vm = jax.ShapeDtypeStruct, pltpu.VMEM
    early_width = 3 * q_width
    pair = [*ring_sems(chips), DMA((chips,)), DMA((chips,))]
    peers = chips + head_count
    return pl.pallas_call(
        tail_kernel,
        out_shape=(
            shape((tok, width), full),
            shape((8, width), full),
            shape((block, q_width), full),
            shape((block, kv_width), full),
            shape((block, kv_width), full),
            shape((block, q_width), full),
            shape((q_width, block), full),
            shape((ffn_rows, hidden_width), full),
            shape((ffn_rows, hidden_width), full),
        ),
        in_specs=[VMEM] * 13 + [ANY] * 9,
        out_specs=tuple([VMEM] * 7 + [ANY] * 2),
        scratch_shapes=[
            vm(kv_parts.shape, low), vm(normed.shape, low), vm(back_rows.shape, low),
            *[vm(weight.shape, low) for weight in weights],
            vm(fgate.shape, low), vm(fup.shape, low),
            vm((rows, q_width), low), vm((rows, kv_width), low), vm((rows, kv_width), low),
            vm((width, early_width), low), vm((width, 2 * kv_width), low),
            vm((head_count * tok, width), low),
            vm((chips, rows, 2 * kv_width), low), into_shape(chips, rows, 2 * kv_width),
            vm((chips, block, early_width), low), into_shape(chips, block, early_width),
            vm((chips, block, 2 * kv_width), low), into_shape(chips, block, 2 * kv_width),
            into_shape(head_count, tok, width),
            into_shape(head_count, ffn_rows, hidden_width),
            into_shape(head_count, ffn_rows, hidden_width),
            vm((2 + chips + head_count, 8, width), full),
            vm((2, 64, hidden_width), full),
            DMA((11,)),
            *pair, *pair, *pair,
            *ring_sems(head_count), *ring_sems(head_count), *ring_sems(head_count),
            DMA((peers,)), DMA((peers,)),
        ],
        compiler_params=pltpu.CompilerParams(
            collective_id=2, has_side_effects=True, vmem_limit_bytes=VMEM_LIMIT
        ),
        cost_estimate=pl.CostEstimate(
            flops=20 * rows * width * q_width, bytes_accessed=300 << 20, transcendentals=0
        ),
        name="tail_block",
    )(
        dq, query_pre, key_pre, gate_grad, cosine, sine_tab, query_gain[None], key_gain[None],
        inputs, middle_grad, attn_gain[None], ffn_gain_part, gated_low,
        kv_parts, normed, back_rows, *weights, fgate, fup,
    )


def contract_cols(left_mat, right_mat):
    return lax.dot_general(
        left_mat, right_mat, (((1,), (1,)), ((), ())), preferred_element_type=jnp.float32
    )


def shards(
    inputs,
    attn_gain,
    query_weight,
    key_projection,
    value_projection,
    attn_gate_weight,
    output_weight,
    query_gain,
    key_gain,
    ffn_gain,
    ffn_gate_weight,
    ffn_up_weight,
    ffn_down_weight,
    doc_lengths,
    cotangent,
):
    tok_dev = inputs.shape[0]
    head_width = query_gain.shape[0]
    head_count = lax.axis_size("head")
    wide_count = lax.axis_size("wide")
    query_rows = tok_dev * head_count
    wide_pos = lax.axis_index("wide")
    local_ids = jnp.arange(query_rows, dtype=jnp.int32)
    query_tok = (local_ids // tok_dev * wide_count + wide_pos) * tok_dev + local_ids % tok_dev
    query_seg, query_pos, query_first = token_tables(doc_lengths, query_tok)
    starts = query_first[::tok_dev]
    firsts = query_first[:, None]
    cosine, sine_tab = rotary(query_pos, head_width)
    block_in = inputs.astype(jnp.float32)
    normed_low = rms_apply(block_in, attn_gain).astype(jnp.bfloat16)
    gathered = lax.all_gather(normed_low, "head", axis=0, tiled=True)
    query_pre = jnp.dot(gathered, query_weight, preferred_element_type=jnp.float32)
    key_pre = jnp.dot(gathered, key_projection, preferred_element_type=jnp.float32)
    value_pre = jnp.dot(gathered, value_projection, preferred_element_type=jnp.float32)
    gate_pre = jnp.dot(gathered, attn_gate_weight, preferred_element_type=jnp.float32)

    def prep_heads(pre_proj, gain_vec):
        return head_prep(pre_proj, gain_vec, cosine, sine_tab)

    query_rot = prep_heads(query_pre, query_gain)
    key_rot = prep_heads(key_pre, key_gain)
    query_low = query_rot.astype(jnp.bfloat16)
    key_low = key_rot.astype(jnp.bfloat16)
    value_low = value_pre.astype(jnp.bfloat16)
    key_wide, value_wide = (
        lax.all_gather(key_low, "wide", axis=0, tiled=True),
        lax.all_gather(value_low, "wide", axis=0, tiled=True),
    )
    kv_width = key_wide.shape[1]

    def natural_order(matrix):
        return (
            matrix.reshape(wide_count, head_count, tok_dev, kv_width)
            .transpose(1, 0, 2, 3)
            .reshape(-1, kv_width)
        )

    key_entire = natural_order(key_wide)
    value_entire = natural_order(value_wide)
    attended, inverse, gated_low = attention_forward(
        query_low, key_entire, value_entire, starts, firsts, gate_pre
    )
    gate_sig = jax.nn.sigmoid(gate_pre)
    (
        outputs,
        middle_grad,
        ffn_gain_part,
        back_rows,
        ffn_down_grad,
        gate_wgrad,
        up_wgrad,
    ) = ffn_block(
        gated_low,
        inputs,
        cotangent,
        ffn_gain,
        output_weight,
        ffn_gate_weight,
        ffn_up_weight,
        ffn_down_weight,
    )
    gated_grad = contract_cols(back_rows, output_weight)
    attended_grad_low = (gated_grad * gate_sig).astype(jnp.bfloat16)
    gate_pre_grad_low = (gated_grad * attended * gate_sig * (1.0 - gate_sig)).astype(jnp.bfloat16)
    query_rot_grad, kv_parts = attention_backward(
        query_low, attended_grad_low, attended, inverse, key_entire, value_entire, starts, firsts
    )
    (
        input_grad,
        gains,
        query_grad,
        key_grad,
        value_grad,
        attn_gate_grad,
        output_grad,
        ffn_gate_grad,
        ffn_up_grad,
    ) = tail_block(
        query_rot_grad,
        kv_parts,
        query_pre,
        key_pre,
        gate_pre_grad_low,
        cosine,
        sine_tab,
        query_gain,
        key_gain,
        inputs,
        middle_grad,
        attn_gain,
        ffn_gain_part,
        gated_low,
        gathered,
        back_rows,
        (query_weight, key_projection, value_projection, attn_gate_weight),
        gate_wgrad,
        up_wgrad,
    )
    attn_gain_grad, ffn_gain_grad = gains[0], gains[1]
    query_gain_grad, key_gain_grad = gains[2, :head_width], gains[3, :head_width]
    return (
        outputs,
        input_grad,
        attn_gain_grad,
        query_grad,
        key_grad,
        value_grad,
        attn_gate_grad,
        output_grad,
        query_gain_grad,
        key_gain_grad,
        ffn_gain_grad,
        ffn_gate_grad,
        ffn_up_grad,
        ffn_down_grad,
    )


def solution(mesh):
    placed = (
        P(("head", "wide"), None),
        P(),
        P(None, "head"),
        P(None, "head"),
        P(None, "head"),
        P(None, "head"),
        P("head", None),
        P(),
        P(),
        P(),
        P(None, "wide"),
        P(None, "wide"),
        P("wide", None),
        P(),
        P(("head", "wide"), None),
    )
    return jax.shard_map(
        shards,
        mesh=mesh,
        in_specs=placed,
        out_specs=(
            P(("head", "wide"), None),
            P(("head", "wide"), None),
            P(),
            P("wide", "head"),
            P("wide", "head"),
            P("wide", "head"),
            P("wide", "head"),
            P("head", "wide"),
            P(),
            P(),
            P(),
            P("head", "wide"),
            P("head", "wide"),
            P("wide", "head"),
        ),
        check_vma=False,
    )
```

```python
import jax
import jax.numpy as jnp
from jax import lax
from jax.experimental import pallas as pl
from jax.experimental.pallas import tpu as pltpu
from jax.sharding import PartitionSpec as P

EPS = 1e-06
THETA = 1000000.0
VMEM_LIMIT = 63 << 20


def token_tables(doc_lengths, token_ids):
    lengths = doc_lengths.reshape(-1)
    doc_ends = jnp.cumsum(lengths)
    before = doc_ends[None, :] <= token_ids[:, None]
    document_segment = jnp.sum(before.astype(jnp.int32), axis=1)
    doc_first = jnp.sum(jnp.where(before, lengths[None, :], 0), axis=1)
    return (document_segment, token_ids - doc_first, doc_first)


def rotary(position, head_width):
    half_width = head_width // 2
    inverse = THETA ** (-(jnp.arange(half_width, dtype=jnp.float32) * 2.0 / head_width))
    angles = position.astype(jnp.float32)[:, None] * inverse[None, :]
    cosine = jnp.cos(angles)
    sine_tab = jnp.sin(angles)
    return (
        jnp.concatenate([cosine, cosine], axis=1),
        jnp.concatenate([sine_tab, sine_tab], axis=1),
    )


MESH = pl.DeviceIdType.MESH
ANY = pl.BlockSpec(memory_space=pl.ANY)
VMEM = pl.BlockSpec(memory_space=pltpu.VMEM)
DMA = pltpu.SemaphoreType.DMA
SIDES = (0, 1)


class Ring:
    def __init__(self, size, pos, index, device):
        self.size, self.pos, self.half = size, pos, size // 2
        self._index, self._device = index, device

    def at(self, offset):
        return lax.rem(self.pos + (offset + 2 * self.size), self.size)

    def index(self, offset):
        return self._index(self.at(offset))

    def device(self, offset):
        return self._device(self.at(offset))


def head_ring():
    size = lax.axis_size("head")
    spread = size // 2
    own, wide = lax.axis_index("head"), lax.axis_index("wide")
    major, minor = lax.div(own, 2), lax.rem(own, 2)
    pos = major + minor * (size - 1 - 2 * major)

    def index(place):
        upper = lax.div(place, spread)
        return 2 * (place + upper * (size - 1 - 2 * place)) + upper

    return Ring(size, pos, index, lambda place: (index(place), wide))


def wide_ring():
    size = lax.axis_size("wide") // 2
    head, wide = lax.axis_index("head"), lax.axis_index("wide")
    core = lax.rem(wide, 2)
    ring = Ring(
        size, lax.div(wide, 2), lambda place: place, lambda place: (head, 2 * place + core)
    )
    ring.core = core
    ring.sibling = (head, wide + 1 - 2 * core)
    return ring


def meet(devices):
    barrier = pltpu.get_barrier_semaphore()
    for device in devices:
        pl.semaphore_signal(barrier, inc=1, device_id=device, device_id_type=MESH)
    pl.semaphore_wait(barrier, len(devices))


def neighbours(*rings):
    found = []
    for ring in rings:
        found += [ring.device(1), ring.device(-1)]
        if hasattr(ring, "sibling"):
            found.append(ring.sibling)
    return found


def remote(src, dst, send, recv, device):
    return pltpu.make_async_remote_copy(
        src_ref=src, dst_ref=dst, send_sem=send, recv_sem=recv, device_id=device,
        device_id_type=MESH,
    )


class Gather:
    def __init__(self, ring, slot, rows, send, recv):
        self.ring, self.slot, self.rows = ring, slot, rows
        self.send, self.recv = send, recv

    def span(self, hop, side):
        if 2 * hop == self.ring.size:
            return side * (self.rows // 2), self.rows // 2
        return 0, self.rows

    def copy(self, hop, side):
        way = 1 - 2 * side
        ref = self.slot(self.ring.index(-way * (hop - 1)), *self.span(hop, side))
        return remote(
            ref, ref, self.send.at[side, hop - 1], self.recv.at[side, hop - 1],
            self.ring.device(way),
        )

    def start(self, hop):
        for side in SIDES:
            self.copy(hop, side).start()

    def arrive(self, hop):
        for side in SIDES:
            self.copy(hop, side).wait_recv()

    def finish(self):
        for hop in range(1, self.ring.half + 1):
            for side in SIDES:
                self.copy(hop, side).wait_send()


class PairGather(Gather):
    def __init__(self, ring, slot, rows, send, recv, pass_send, pass_recv):
        core = ring.core
        super().__init__(
            ring, lambda index, start, size: slot(2 * index + core, start, size), rows, send, recv
        )
        self.pass_send, self.pass_recv = pass_send, pass_recv

    def handed(self, hop, side):
        way = 1 - 2 * side
        span = self.span(hop, side) if hop else (0, self.rows)
        ref = self.slot(self.ring.index(-way * hop), *span)
        return remote(
            ref, ref, self.pass_send.at[side, hop], self.pass_recv.at[side, hop],
            self.ring.sibling,
        )

    def hand(self, hop):
        for side in SIDES if hop else (0,):
            self.handed(hop, side).start()

    def take(self, hop):
        for side in SIDES if hop else (0,):
            self.handed(hop, side).wait_recv()

    def begin(self):
        self.start(1)
        self.hand(0)

    def finish(self):
        super().finish()
        for hop in range(self.ring.half + 1):
            for side in SIDES if hop else (0,):
                self.handed(hop, side).wait_send()


def row_loop(rows, chunk, body):
    @pl.loop(0, rows // chunk)
    def _(step):
        body(pl.multiple_of(step * chunk, chunk))


class Scatter:
    def __init__(self, ring, part, rows, into, send, recv):
        self.ring, self.part, self.rows, self.into = ring, part, rows, into
        self.send, self.recv = send, recv

    def span(self, hop, side):
        if 2 * hop == self.ring.size:
            return side * (self.rows // 2), self.rows // 2
        return 0, self.rows

    def copy(self, hop, side):
        way = 1 - 2 * side
        first, count = self.span(hop, side)
        ref, base = self.part(self.ring.index(way * hop))
        return remote(
            ref.at[pl.ds(base + first, count)],
            self.into.at[side, pl.ds((hop - 1) * self.rows + self.inside(hop, first), count)],
            self.send.at[side, hop - 1], self.recv.at[side, hop - 1], self.ring.device(way),
        )

    def inside(self, hop, row):
        return row % (self.rows // 2) if 2 * hop == self.ring.size else row

    def start(self, hop):
        for side in SIDES:
            self.copy(hop, side).start()

    def fold(self, hop, side):
        way = 1 - 2 * side
        self.copy(hop + 1, side).wait_recv()
        first, count = self.span(hop + 1, side)
        ref, base = self.part(self.ring.index(way * hop))
        chunk = min(count, 32)

        def add(row):
            there = pl.ds(pl.multiple_of(base + first + row, chunk), chunk)
            start = hop * self.rows + self.inside(hop + 1, first)
            here = pl.ds(pl.multiple_of(start + row, chunk), chunk)
            ref[there, :] = (
                ref[there, :].astype(jnp.float32) + self.into[side, here, :].astype(jnp.float32)
            ).astype(ref.dtype)

        row_loop(count, chunk, add)

    def advance(self, hop):
        for side in SIDES:
            self.fold(hop, side)
            self.copy(hop, side).start()

    def arrive(self):
        for side in SIDES:
            self.copy(1, side).wait_recv()

    def total(self, row, count):
        ref, base = self.part(self.ring.index(0))
        there = pl.ds(pl.multiple_of(base + row, count), count)
        here = pl.ds(row, count)
        return (
            ref[there, :].astype(jnp.float32)
            + self.into[0, here, :].astype(jnp.float32)
            + self.into[1, here, :].astype(jnp.float32)
        )

    def finish(self):
        for hop in range(1, self.ring.half + 1):
            for side in SIDES:
                self.copy(hop, side).wait_send()


class PairScatter(Scatter):
    def __init__(self, ring, terms, rows, passed, into, send, recv, pass_send, pass_recv):
        core = ring.core
        super().__init__(
            ring, lambda index: (terms, (2 * index + core) * rows), rows, into, send, recv
        )
        self.terms, self.passed = terms, passed
        self.pass_send, self.pass_recv = pass_send, pass_recv

    def handed(self, offset):
        ring = self.ring
        index = ring.index(offset)
        other = pl.multiple_of((2 * index + 1 - ring.core) * self.rows, self.rows)
        slot = offset % ring.size
        return remote(
            self.terms.at[pl.ds(other, self.rows)],
            self.passed.at[slot],
            self.pass_send.at[slot], self.pass_recv.at[slot], ring.sibling,
        )

    def hand(self, offset):
        self.handed(offset).start()

    def merge(self, offset):
        self.handed(offset).wait_recv()
        slot = offset % self.ring.size
        ref, base = self.part(self.ring.index(offset))
        chunk = 32

        def add(row):
            there = pl.ds(pl.multiple_of(base + row, chunk), chunk)
            ref[there, :] = (
                ref[there, :].astype(jnp.float32)
                + self.passed[slot, pl.ds(row, chunk), :].astype(jnp.float32)
            ).astype(ref.dtype)

        row_loop(self.rows, chunk, add)

    def finish(self):
        super().finish()
        for offset in range(self.ring.size):
            self.handed(offset).wait_send()


def offsets(ring):
    order = [ring.half]
    for hop in range(ring.half - 1, 0, -1):
        order += [hop, -hop]
    return order + [0]


def into_shape(size, rows, columns):
    return pltpu.VMEM((2, (size - 1) * rows // 2, columns), jnp.bfloat16)


def everyone(*rings):
    found = []
    for ring in rings:
        found += [ring.device(offset) for offset in range(1, ring.size)]
        if hasattr(ring, "sibling"):
            found.append(ring.sibling)
    return found


def ring_sems(size):
    return [DMA((2, size // 2)), DMA((2, size // 2))]


def pass_sems(size):
    return [DMA((2, size // 2 + 1)), DMA((2, size // 2 + 1))]


def dot_nn(left, right):
    return jnp.dot(left, right, preferred_element_type=jnp.float32)


def dot_nt(left, right):
    return lax.dot_general(
        left, right, (((1,), (1,)), ((), ())), preferred_element_type=jnp.float32
    )


def dot_tn(left, right):
    return lax.dot_general(
        left, right, (((0,), (0,)), ((), ())), preferred_element_type=jnp.float32
    )


LANES = 128
KEY_BLOCK = 512
LOG2E = 1.4426950408889634


def attention_forward_kernel(
    start_ref, query_ref, kv_ref, first_ref, gate_ref, att_ref, inv_ref, gated_ref, acc
):
    blocks = start_ref.shape[0]
    kv_width = kv_ref.shape[1] // 2
    groups = kv_width // LANES
    per = query_ref.shape[1] // kv_width
    rows = query_ref.shape[0] // blocks
    wide_count = kv_ref.shape[0] // query_ref.shape[0]
    wide_pos = lax.axis_index("wide")
    step = KEY_BLOCK
    factor = LANES ** (-0.5) * LOG2E

    @pl.loop(0, blocks)
    def _(blk):
        here = pl.ds(pl.multiple_of(blk * rows, rows), rows)
        first_tok = (blk * wide_count + wide_pos) * rows
        key_lane = lax.broadcasted_iota(jnp.int32, (rows, step), 1)
        query_row = lax.broadcasted_iota(jnp.int32, (rows, step), 0) + first_tok
        upper = key_lane - query_row
        lower = key_lane - first_ref[here, :]
        queries = [
            jnp.concatenate(
                [
                    query_ref[here, (g * per + j) * LANES : (g * per + j + 1) * LANES]
                    for j in range(per)
                ],
                axis=0,
            )
            for g in range(groups)
        ]
        acc[...] = jnp.zeros_like(acc)

        @pl.loop(start_ref[blk] // step, (first_tok + rows + step - 1) // step)
        def _(tile):
            base = tile * step
            there = pl.ds(pl.multiple_of(base, step), step)
            allowed = (upper <= -base) & (lower >= -base)
            allowed = jnp.concatenate([allowed] * per, axis=0)
            for g in range(groups):
                cols = slice(g * LANES, (g + 1) * LANES)
                value_cols = slice(kv_width + g * LANES, kv_width + (g + 1) * LANES)
                scores = lax.dot_general(
                    queries[g], kv_ref[there, cols], (((1,), (1,)), ((), ())),
                    preferred_element_type=jnp.float32,
                )
                probs = jnp.where(allowed, jnp.exp2(scores * factor), 0.0).astype(jnp.bfloat16)
                values = jnp.concatenate(
                    [kv_ref[there, value_cols], jnp.ones((step, LANES), jnp.bfloat16)], axis=1
                )
                acc[g] += jnp.dot(probs, values, preferred_element_type=jnp.float32)

        for g in range(groups):
            for j in range(per):
                part = acc[g, j * rows : (j + 1) * rows, :]
                cols = slice((g * per + j) * LANES, (g * per + j + 1) * LANES)
                inverse = 1.0 / part[:, LANES:]
                out = part[:, :LANES] * inverse
                att_ref[here, cols] = out
                inv_ref[here, cols] = inverse
                gated_ref[here, cols] = (out * jax.nn.sigmoid(gate_ref[here, cols])).astype(
                    jnp.bfloat16
                )


def attention_forward(query_low, kv_all, starts, firsts, gate_pre):
    rows, width = query_low.shape
    groups = (kv_all.shape[1] // 2) // LANES
    per = width // (kv_all.shape[1] // 2)
    blocks = starts.shape[0]
    vmem = pl.BlockSpec(memory_space=pltpu.VMEM)
    return pl.pallas_call(
        attention_forward_kernel,
        out_shape=(
            jax.ShapeDtypeStruct((rows, width), jnp.float32),
            jax.ShapeDtypeStruct((rows, width), jnp.float32),
            jax.ShapeDtypeStruct((rows, width), jnp.bfloat16),
        ),
        in_specs=[pl.BlockSpec(memory_space=pltpu.SMEM)] + [vmem] * 4,
        out_specs=(vmem, vmem, vmem),
        scratch_shapes=[pltpu.VMEM((groups, per * (rows // blocks), 2 * LANES), jnp.float32)],
        compiler_params=pltpu.CompilerParams(vmem_limit_bytes=VMEM_LIMIT),
        cost_estimate=pl.CostEstimate(
            flops=4 * rows * width * 2048, bytes_accessed=12 << 20, transcendentals=0
        ),
        name="attention_forward",
    )(starts, query_low, kv_all, firsts, gate_pre)


def attention_backward_kernel(
    start_ref, query_ref, grad_ref, att_ref, inv_ref, kvs_ref, first_ref,
    dq_ref, kv_ref, dk_acc, dv_acc, dqt, keyt,
):
    blocks = start_ref.shape[0]
    kv_width = kvs_ref.shape[1] // 2
    groups = kv_width // LANES
    per = query_ref.shape[1] // kv_width
    rows = query_ref.shape[0] // blocks
    wide_count = kvs_ref.shape[0] // query_ref.shape[0]
    wide_pos = lax.axis_index("wide")
    step = KEY_BLOCK
    scale = LANES ** (-0.5)
    dk_acc[...] = jnp.zeros_like(dk_acc)
    dv_acc[...] = jnp.zeros_like(dv_acc)

    @pl.loop(0, kvs_ref.shape[0] // step)
    def _(tile):
        there = pl.ds(pl.multiple_of(tile * step, step), step)
        for g in range(groups):
            cols = slice(g * LANES, (g + 1) * LANES)
            keyt[cols, there] = jnp.transpose(kvs_ref[there, cols])

    @pl.loop(0, blocks)
    def _(blk):
        here = pl.ds(pl.multiple_of(blk * rows, rows), rows)
        first_tok = (blk * wide_count + wide_pos) * rows
        key_row = lax.broadcasted_iota(jnp.int32, (step, rows), 0)
        query_lane = lax.broadcasted_iota(jnp.int32, (step, rows), 1) + first_tok
        upper = key_row - query_lane
        lower = key_row - jnp.transpose(
            jnp.broadcast_to(first_ref[here, :], (rows, LANES))
        )[0:1, :]
        queries, grads, deltas = [], [], []
        for g in range(groups):
            qs, gs, ds = [], [], []
            for j in range(per):
                cols = slice((g * per + j) * LANES, (g * per + j + 1) * LANES)
                grad = grad_ref[here, cols].astype(jnp.float32)
                inverse = inv_ref[here, cols]
                both = grad * inverse
                delta = jnp.sum(both * att_ref[here, cols], axis=1, keepdims=True)
                ds.append(jnp.transpose(jnp.broadcast_to(delta, (rows, LANES)))[0:1, :])
                qs.append(query_ref[here, cols])
                gs.append(both.astype(jnp.bfloat16))
            queries.append(jnp.concatenate(qs, axis=0))
            grads.append(jnp.concatenate(gs, axis=0))
            deltas.append(jnp.concatenate(ds, axis=1))
        dqt[...] = jnp.zeros_like(dqt)

        @pl.loop(start_ref[blk] // step, (first_tok + rows + step - 1) // step)
        def _(tile):
            base = tile * step
            there = pl.ds(pl.multiple_of(base, step), step)
            allowed = (upper <= -base) & (lower >= -base)
            allowed = jnp.concatenate([allowed] * per, axis=1)
            for g in range(groups):
                cols = slice(g * LANES, (g + 1) * LANES)
                value_cols = slice(kv_width + g * LANES, kv_width + (g + 1) * LANES)
                scores = lax.dot_general(
                    kvs_ref[there, cols], queries[g], (((1,), (1,)), ((), ())),
                    preferred_element_type=jnp.float32,
                )
                probs = jnp.where(allowed, jnp.exp2(scores * (scale * LOG2E)), 0.0)
                dprobs = lax.dot_general(
                    kvs_ref[there, value_cols], grads[g], (((1,), (1,)), ((), ())),
                    preferred_element_type=jnp.float32,
                )
                dscores = (probs * (dprobs - deltas[g]) * scale).astype(jnp.bfloat16)
                dv_acc[there, cols] += jnp.dot(
                    probs.astype(jnp.bfloat16), grads[g], preferred_element_type=jnp.float32
                )
                dk_acc[there, cols] += jnp.dot(
                    dscores, queries[g], preferred_element_type=jnp.float32
                )
                dqt[g] += jnp.dot(
                    keyt[cols, there], dscores, preferred_element_type=jnp.float32
                )

        for g in range(groups):
            for j in range(per):
                cols = slice((g * per + j) * LANES, (g * per + j + 1) * LANES)
                dq_ref[here, cols] = jnp.transpose(dqt[g, :, j * rows : (j + 1) * rows])

    width = dk_acc.shape[1]

    @pl.loop(0, wide_count)
    def _(target):
        for blk in range(blocks):
            source = pl.ds(pl.multiple_of((blk * wide_count + target) * rows, rows), rows)
            there = pl.ds(pl.multiple_of((target * blocks + blk) * rows, rows), rows)
            kv_ref[there, :width] = dk_acc[source, :].astype(jnp.bfloat16)
            kv_ref[there, width:] = dv_acc[source, :].astype(jnp.bfloat16)


def attention_backward(
    query_low, grad_low, attended, inverse, kv_all, starts, firsts
):
    rows, width = query_low.shape
    keys, kv_width = kv_all.shape[0], kv_all.shape[1] // 2
    groups = kv_width // LANES
    per = width // kv_width
    blocks = starts.shape[0]
    vmem = pl.BlockSpec(memory_space=pltpu.VMEM)
    return pl.pallas_call(
        attention_backward_kernel,
        out_shape=(
            jax.ShapeDtypeStruct((rows, width), jnp.float32),
            jax.ShapeDtypeStruct((keys, 2 * kv_width), jnp.bfloat16),
        ),
        in_specs=[pl.BlockSpec(memory_space=pltpu.SMEM)] + [vmem] * 6,
        out_specs=(vmem, vmem),
        scratch_shapes=[
            pltpu.VMEM((keys, kv_width), jnp.float32),
            pltpu.VMEM((keys, kv_width), jnp.float32),
            pltpu.VMEM((groups, LANES, per * (rows // blocks)), jnp.float32),
            pltpu.VMEM((kv_width, keys), jnp.bfloat16),
        ],
        compiler_params=pltpu.CompilerParams(vmem_limit_bytes=VMEM_LIMIT),
        cost_estimate=pl.CostEstimate(
            flops=10 * rows * width * 2048, bytes_accessed=20 << 20, transcendentals=0
        ),
        name="attention_backward",
    )(starts, query_low, grad_low, attended, inverse, kv_all, firsts)


def ffn_kernel(
    gated_ref, x_ref, cot_ref, gain_ref, wo_any, wg_any, wu_any, wd_any,
    out_any, mgrad_ref, gain_out, back_any, down_ref, fgate_any, fup_any,
    wo, wg, wu, wd, cots, rows, hidden_grad, hid, gg, ug, terms_own, passed, into,
    passed2, into2, dterms, dinto, stage, hterms, hinto, middle, back, local_sem,
    ds, dr, hs, hr, cs, cr, cps, cpr, fs, fr, fps, fpr, s1, r1, ps1, pr1, s2, r2, ps2, pr2, bs, br,
):
    tok, width = x_ref.shape
    hidden_width = wg_any.shape[1]
    head, wide = head_ring(), wide_ring()
    pair = 2 * tok
    separate = terms_own.shape[0] > 16
    terms = terms_own if separate else cots
    part = wo_any.shape[1] // lax.axis_size("head")
    loads = [
        pltpu.make_async_copy(src, dst, local_sem.at[i])
        for i, (src, dst) in enumerate(((wo_any, wo), (wd_any, wd), (wg_any, wg), (wu_any, wu)))
    ]
    for load in loads:
        load.start()
    own_wide = pl.multiple_of(lax.axis_index("wide") * tok, tok)
    own_head = pl.multiple_of(lax.axis_index("head") * tok, tok)
    cots[pl.ds(own_wide, tok), :] = cot_ref[...]
    meet(neighbours(head, wide))

    def slot_of(ref):
        return lambda index, start, size: ref.at[pl.ds(index * tok + start, size)]

    cot_gather = PairGather(wide, slot_of(cots), tok, cs, cr, cps, cpr)
    row_gather = PairGather(wide, slot_of(rows), tok, fs, fr, fps, fpr)
    back_gather = Gather(head, slot_of(back), tok, bs, br)
    head_scatter = Scatter(head, lambda index: (hterms, index * tok), tok, hinto, hs, hr)
    grad_scatter = PairScatter(wide, terms, tok, passed, into, s1, r1, ps1, pr1)
    down_scatter = Scatter(
        head, lambda index: (dterms, index * hidden_width), hidden_width, dinto, ds, dr
    )
    out_scatter = PairScatter(wide, rows, tok, passed2, into2, s2, r2, ps2, pr2)

    def group_of(offset):
        return pl.ds(pl.multiple_of(wide.index(offset) * pair, pair), pair)

    def col_loop(total, step, body):
        @pl.loop(0, total // step)
        def _(i):
            body(pl.ds(pl.multiple_of(i * step, step), step))

    tile = 256
    cot_gather.begin()

    def out_part(offset, own):
        index = head.index(offset)
        here = pl.ds(pl.multiple_of(index * tok, tok), tok)

        def body(cols):
            value = dot_nn(gated_ref[here, :], wo[:, cols])
            if own:
                middle[:, cols] = x_ref[:, cols].astype(jnp.float32) + value
            else:
                hterms[here, cols] = value.astype(jnp.bfloat16)

        col_loop(width, tile, body)

    def hidden_part(offset):
        here = group_of(offset)

        def body(cols):
            hidden_grad[here, cols] = dot_nt(cots[here, :], wd[cols, :]).astype(
                hidden_grad.dtype
            )

        col_loop(hidden_width, tile if hidden_width % tile == 0 else LANES, body)

    loads[0].wait()
    out_part(head.half, False)
    head_scatter.start(head.half)
    for hop in range(head.half - 1, 0, -1):
        out_part(hop, False)
        out_part(-hop, False)
    out_part(0, True)
    loads[1].wait()
    cot_gather.take(0)
    hidden_part(0)
    for hop in range(head.half - 1, 0, -1):
        head_scatter.advance(hop)
    for hop in range(1, wide.half):
        cot_gather.arrive(hop)
        cot_gather.start(hop + 1)
        cot_gather.hand(hop)
        cot_gather.take(hop)
        hidden_part(hop)
        hidden_part(-hop)
    head_scatter.arrive()

    gain = gain_ref[...]

    def forward_norm(row):
        here = pl.ds(row, 32)
        value = (
            middle[here, :]
            + hinto[0, here, :].astype(jnp.float32)
            + hinto[1, here, :].astype(jnp.float32)
        )
        middle[here, :] = value
        scale = lax.rsqrt(jnp.mean(value * value, axis=-1, keepdims=True) + EPS)
        rows[pl.ds(pl.multiple_of(own_wide + row, 32), 32), :] = (value * scale * gain).astype(
            jnp.bfloat16
        )

    row_loop(tok, 32, forward_norm)
    row_gather.begin()
    cot_gather.arrive(wide.half)
    cot_gather.hand(wide.half)
    cot_gather.take(wide.half)
    hidden_part(wide.half)
    cot_gather.finish()
    loads[2].wait()
    loads[3].wait()

    def unit(offset):
        here = group_of(offset)

        def body(cols):
            gate = dot_nn(rows[here, :], wg[:, cols])
            up = dot_nn(rows[here, :], wu[:, cols])
            grad = hidden_grad[here, cols].astype(jnp.float32)
            sig = jax.nn.sigmoid(gate)
            act = gate * sig
            hid[here, cols] = (act * up).astype(jnp.bfloat16)
            gg[here, cols] = (grad * up * (sig + act * (1.0 - sig))).astype(jnp.bfloat16)
            ug[here, cols] = (grad * act).astype(jnp.bfloat16)

        col_loop(hidden_width, tile if hidden_width % tile == 0 else LANES, body)

    row_gather.take(0)
    unit(0)
    for hop in range(1, wide.half):
        row_gather.arrive(hop)
        row_gather.start(hop + 1)
        row_gather.hand(hop)
        row_gather.take(hop)
        unit(hop)
        unit(-hop)
    row_gather.arrive(wide.half)
    row_gather.hand(wide.half)
    row_gather.take(wide.half)
    unit(wide.half)

    def grad_terms(offset):
        here = group_of(offset)

        def body(cols):
            value = dot_nt(gg[here, :], wg[cols, :]) + dot_nt(ug[here, :], wu[cols, :])
            terms[here, cols] = value.astype(jnp.bfloat16)

        col_loop(width, tile, body)
        grad_scatter.hand(offset)

    def down_terms(offset):
        here = group_of(offset)

        def body(cols):
            rows[here, cols] = dot_nn(hid[here, :], wd[:, cols]).astype(jnp.bfloat16)

        col_loop(width, tile, body)
        out_scatter.hand(offset)

    def down_grads():
        @pl.loop(0, lax.axis_size("head"))
        def _(index):
            cols = pl.ds(pl.multiple_of(index * part, part), part)

            @pl.loop(0, hidden_width // LANES)
            def _(i):
                lanes = pl.ds(pl.multiple_of(i * LANES, LANES), LANES)
                there = pl.ds(
                    pl.multiple_of(index * hidden_width + i * LANES, LANES), LANES
                )
                dterms[there, :] = dot_tn(hid[:, lanes], cots[:, cols]).astype(jnp.bfloat16)

        down_scatter.start(head.half)

    emit = stage.shape[2]

    def stage_copy(step, out, any_ref, slot):
        there = pl.ds(pl.multiple_of(step * emit, emit), emit)
        return pltpu.make_async_copy(
            stage.at[slot, out], any_ref.at[there], local_sem.at[5 + 2 * slot + out]
        )

    def input_grads():
        @pl.loop(0, width // emit // 2)
        def _(i):
            for slot in SIDES:
                step = 2 * i + slot
                cols = pl.ds(pl.multiple_of(step * emit, emit), emit)

                @pl.when(i > 0)
                def _():
                    for out, any_ref in enumerate((fgate_any, fup_any)):
                        stage_copy(step - 2, out, any_ref, slot).wait()

                left = rows[:, cols]
                stage[slot, 0] = dot_tn(left, gg[...]).astype(jnp.bfloat16)
                stage[slot, 1] = dot_tn(left, ug[...]).astype(jnp.bfloat16)
                for out, any_ref in enumerate((fgate_any, fup_any)):
                    stage_copy(step, out, any_ref, slot).start()

    order = offsets(wide)
    if not separate:
        down_grads()
    grad_terms(order[0])
    grad_terms(order[1])
    grad_scatter.merge(order[0])
    grad_scatter.start(wide.half)
    for offset in order[2:]:
        grad_terms(offset)
    if separate:
        down_grads()
    for hop in range(wide.half - 1, 0, -1):
        grad_scatter.merge(hop)
        grad_scatter.merge(-hop)
        grad_scatter.advance(hop)
    grad_scatter.merge(0)
    input_grads()
    row_gather.finish()
    for offset in order:
        down_terms(offset)
    out_scatter.merge(order[0])
    for hop in range(head.half - 1, 0, -1):
        down_scatter.advance(hop)
    grad_scatter.arrive()

    def backward_norm(row, gain_sum):
        here = pl.ds(row, 32)
        value = middle[here, :]
        grad = grad_scatter.total(row, 32)
        scale = lax.rsqrt(jnp.mean(value * value, axis=-1, keepdims=True) + EPS)
        scaled = value * scale
        weighted = grad * gain
        mean = jnp.mean(scaled * weighted, axis=-1, keepdims=True)
        total = cot_ref[here, :].astype(jnp.float32) + scale * (weighted - scaled * mean)
        mgrad_ref[here, :] = total
        back[pl.ds(pl.multiple_of(own_head + row, 32), 32), :] = total.astype(jnp.bfloat16)
        return gain_sum + jnp.sum(grad * scaled, axis=0, keepdims=True)

    gain_out[...] = lax.fori_loop(
        0, tok // 32,
        lambda i, carried: backward_norm(pl.multiple_of(i * 32, 32), carried),
        jnp.zeros((1, width), jnp.float32),
    )
    back_gather.start(1)
    out_scatter.start(wide.half)
    for offset in order[1:]:
        out_scatter.merge(offset)
    for hop in range(wide.half - 1, 0, -1):
        out_scatter.advance(hop)
    for hop in range(1, head.half):
        back_gather.arrive(hop)
        back_gather.start(hop + 1)
    back_gather.arrive(head.half)
    back_gather.finish()
    keep = pltpu.make_async_copy(back, back_any, local_sem.at[4])
    keep.start()
    out_scatter.arrive()

    def finish_out(row):
        here = pl.ds(row, 32)
        back[here, :] = (middle[here, :] + out_scatter.total(row, 32)).astype(jnp.bfloat16)

    keep.wait()
    row_loop(tok, 32, finish_out)
    result = pltpu.make_async_copy(back.at[pl.ds(0, tok)], out_any, local_sem.at[9])
    result.start()
    down_scatter.arrive()

    def finish_down(row):
        down_ref[pl.ds(row, 32), :] = down_scatter.total(row, 32)

    row_loop(hidden_width, 32, finish_down)
    for scatter in (head_scatter, grad_scatter, out_scatter, down_scatter):
        scatter.finish()
    last = width // emit
    for slot in SIDES:
        for out, any_ref in enumerate((fgate_any, fup_any)):
            stage_copy(last - 2 + slot, out, any_ref, slot).wait()
    result.wait()


def ffn_block(gated_low, inputs, cotangent, ffn_gain, out_w, gate_w, up_w, down_w):
    tok, width = inputs.shape
    head_count, wide_count = lax.axis_size("head"), lax.axis_size("wide")
    chips = wide_count // 2
    hidden_width = gate_w.shape[1]
    low, full = jnp.bfloat16, jnp.float32
    all_rows = wide_count * tok
    back_rows = head_count * tok
    roomy = all_rows * width <= 2 << 20
    shape = jax.ShapeDtypeStruct
    vm = pltpu.VMEM
    return pl.pallas_call(
        ffn_kernel,
        out_shape=(
            shape((tok, width), low),
            shape((tok, width), full),
            shape((1, width), full),
            shape((back_rows, width), low),
            shape((hidden_width, width // head_count), full),
            shape((width, hidden_width), low),
            shape((width, hidden_width), low),
        ),
        in_specs=[VMEM] * 4 + [ANY] * 4,
        out_specs=(ANY, VMEM, VMEM, ANY, VMEM, ANY, ANY),
        scratch_shapes=[
            vm(out_w.shape, low), vm(gate_w.shape, low), vm(up_w.shape, low),
            vm(down_w.shape, low),
            vm((all_rows, width), low), vm((all_rows, width), low),
            vm((all_rows, hidden_width), full if roomy else low),
            vm((all_rows, hidden_width), low), vm((all_rows, hidden_width), low),
            vm((all_rows, hidden_width), low),
            vm((all_rows if roomy else 16, width), low),
            vm((chips, tok, width), low),
            into_shape(chips, tok, width),
            vm((chips, tok, width), low),
            into_shape(chips, tok, width),
            vm((head_count * hidden_width, width // head_count), low),
            into_shape(head_count, hidden_width, width // head_count),
            vm((2, 2, 256 if roomy else 128, hidden_width), low),
            vm((back_rows, width), low), into_shape(head_count, tok, width),
            vm((tok, width), full), vm((back_rows, width), low),
            DMA((10,)),
            *ring_sems(head_count),
            *ring_sems(head_count),
            *ring_sems(chips), *pass_sems(chips),
            *ring_sems(chips), *pass_sems(chips),
            *ring_sems(chips), DMA((chips,)), DMA((chips,)),
            *ring_sems(chips), DMA((chips,)), DMA((chips,)),
            *ring_sems(head_count),
        ],
        compiler_params=pltpu.CompilerParams(
            collective_id=1, has_side_effects=True, vmem_limit_bytes=VMEM_LIMIT
        ),
        cost_estimate=pl.CostEstimate(
            flops=10 * all_rows * width * hidden_width, bytes_accessed=200 << 20, transcendentals=0
        ),
        name="ffn_block",
    )(gated_low, inputs, cotangent, ffn_gain[None], out_w, gate_w, up_w, down_w)


def turn(values, cosine, sine_tab):
    half = LANES // 2
    lane = lax.broadcasted_iota(jnp.int32, values.shape, 1)
    turned = pltpu.roll(values, half, 1)
    return values * cosine + jnp.where(lane < half, -turned, turned) * sine_tab


def prep(pre_proj, gain, cosine, sine_tab):
    scale = lax.rsqrt(jnp.mean(pre_proj * pre_proj, axis=-1, keepdims=True) + EPS)
    return turn(pre_proj * scale * gain, cosine, sine_tab).astype(jnp.bfloat16)


def front_kernel(
    x_ref, gain_ref, cos_ref, sin_ref, qgain_ref, kgain_ref, wq_any, wk_any, wv_any, wg_any,
    query_ref, qpre_ref, kpre_ref, gpre_ref, normed_any, kv_any,
    wq, wk, wv, wg, normed, kv, local_sem, hs, hr, ks, kr, kps, kpr,
):
    tok, width = x_ref.shape
    kv_width = wk_any.shape[1]
    q_width = wq_any.shape[1]
    wide_count, head_count = lax.axis_size("wide"), lax.axis_size("head")
    head, wide = head_ring(), wide_ring()
    loads = [
        pltpu.make_async_copy(src, dst, local_sem.at[i])
        for i, (src, dst) in enumerate(((wk_any, wk), (wv_any, wv), (wq_any, wq), (wg_any, wg)))
    ]
    for load in loads:
        load.start()
    own = pl.multiple_of(lax.axis_index("head") * tok, tok)
    own_wide = lax.axis_index("wide")

    def norm(row):
        here = pl.ds(row, 32)
        value = x_ref[here, :].astype(jnp.float32)
        scale = lax.rsqrt(jnp.mean(value * value, axis=-1, keepdims=True) + EPS)
        normed[pl.ds(pl.multiple_of(own + row, 32), 32), :] = (
            value * scale * gain_ref[...]
        ).astype(jnp.bfloat16)

    row_loop(tok, 32, norm)
    meet(neighbours(head, wide))
    gather = Gather(
        head, lambda index, start, size: normed.at[pl.ds(index * tok + start, size)], tok, hs, hr
    )
    gather.start(1)

    def kv_gather(offset):
        slot = offset % head_count
        block = head.index(offset)

        def place(index, start, size):
            return kv.at[pl.ds((block * wide_count + index) * tok + start, size)]

        return PairGather(
            wide, place, tok, ks.at[slot], kr.at[slot], kps.at[slot], kpr.at[slot]
        )

    def project(offset):
        block = head.index(offset)
        here = pl.ds(pl.multiple_of(block * tok, tok), tok)
        there = pl.ds(pl.multiple_of((block * wide_count + own_wide) * tok, tok), tok)
        left = normed[here, :]
        cosine, sine_tab = cos_ref[here, :], sin_ref[here, :]
        pre = dot_nn(left, wk[...])
        kpre_ref[here, :] = pre
        for j in range(kv_width // LANES):
            cols = slice(j * LANES, (j + 1) * LANES)
            kv[there, cols] = prep(pre[:, cols], kgain_ref[...], cosine, sine_tab)
        kv[there, kv_width:] = dot_nn(left, wv[...]).astype(jnp.bfloat16)

    def project_rest(offset):
        block = head.index(offset)
        here = pl.ds(pl.multiple_of(block * tok, tok), tok)
        left = normed[here, :]
        cosine, sine_tab = cos_ref[here, :], sin_ref[here, :]
        pre = dot_nn(left, wq[...])
        qpre_ref[here, :] = pre
        for j in range(q_width // LANES):
            cols = slice(j * LANES, (j + 1) * LANES)
            query_ref[here, cols] = prep(pre[:, cols], qgain_ref[...], cosine, sine_tab)
        gpre_ref[here, :] = dot_nn(left, wg[...])

    gathers = {}

    def launch(offset):
        project(offset)
        gathers[offset] = kv_gather(offset)
        gathers[offset].begin()

    def step(offset, hop):
        gathers[offset].arrive(hop)
        if hop < wide.half:
            gathers[offset].start(hop + 1)
        gathers[offset].hand(hop)

    loads[0].wait()
    loads[1].wait()
    launch(0)
    loads[2].wait()
    loads[3].wait()
    project_rest(0)
    done = [0]
    for hop in range(1, head.half + 1):
        gather.arrive(hop)
        if hop < head.half:
            gather.start(hop + 1)
            launch(hop)
            launch(-hop)
            for offset in done:
                step(offset, 1)
            project_rest(hop)
            project_rest(-hop)
            done = [hop, -hop]
        else:
            launch(hop)
            for offset in done:
                step(offset, 1)
            project_rest(hop)
            done = [hop]
    gather.finish()
    keep = pltpu.make_async_copy(normed, normed_any, local_sem.at[4])
    keep.start()
    for offset in done:
        step(offset, 1)
    for hop in range(2, wide.half + 1):
        for offset in gathers:
            step(offset, hop)
    for each in gathers.values():
        for hop in range(wide.half + 1):
            each.take(hop)
    store = pltpu.make_async_copy(kv, kv_any, local_sem.at[5])
    store.start()
    for each in gathers.values():
        each.finish()
    store.wait()
    keep.wait()


def front_block(inputs, attn_gain, cosine, sine_tab, query_gain, key_gain, weights):
    tok, width = inputs.shape
    head_count, wide_count = lax.axis_size("head"), lax.axis_size("wide")
    chips = wide_count // 2
    q_width, kv_width = weights[0].shape[1], weights[1].shape[1]
    rows = head_count * tok
    low, full = jnp.bfloat16, jnp.float32
    shape, vm = jax.ShapeDtypeStruct, pltpu.VMEM
    half = chips // 2
    return pl.pallas_call(
        front_kernel,
        out_shape=(
            shape((rows, q_width), low),
            shape((rows, q_width), full),
            shape((rows, kv_width), full),
            shape((rows, q_width), full),
            shape((rows, width), low),
            shape((rows * wide_count, 2 * kv_width), low),
        ),
        in_specs=[VMEM] * 6 + [ANY] * 4,
        out_specs=tuple([VMEM] * 4 + [ANY] * 2),
        scratch_shapes=[
            *[vm(weight.shape, low) for weight in weights],
            vm((rows, width), low),
            vm((rows * wide_count, 2 * kv_width), low),
            DMA((6,)),
            *ring_sems(head_count),
            DMA((head_count, 2, half)), DMA((head_count, 2, half)),
            DMA((head_count, 2, half + 1)), DMA((head_count, 2, half + 1)),
        ],
        compiler_params=pltpu.CompilerParams(
            collective_id=3, has_side_effects=True, vmem_limit_bytes=VMEM_LIMIT
        ),
        cost_estimate=pl.CostEstimate(
            flops=2 * rows * width * (2 * q_width + 2 * kv_width), bytes_accessed=100 << 20,
            transcendentals=0,
        ),
        name="front_block",
    )(
        inputs, attn_gain[None], cosine, sine_tab, query_gain[None], key_gain[None], *weights
    )


def turn_back(grad, cosine, sine_tab):
    half = LANES // 2
    lane = lax.broadcasted_iota(jnp.int32, grad.shape, 1)
    turned = pltpu.roll(grad * sine_tab, half, 1)
    return grad * cosine + jnp.where(lane < half, turned, -turned)


def unprep(grad, pre_proj, gain, cosine, sine_tab):
    turned = turn_back(grad, cosine, sine_tab)
    scale = lax.rsqrt(jnp.mean(pre_proj * pre_proj, axis=-1, keepdims=True) + EPS)
    scaled = pre_proj * scale
    weighted = turned * gain
    mean = jnp.mean(scaled * weighted, axis=-1, keepdims=True)
    return scale * (weighted - scaled * mean), turned * scaled


def tail_kernel(
    dq_ref, qpre_ref, kpre_ref, ggrad_ref, cos_ref, sin_ref, qgain_ref, kgain_ref, x_ref,
    mgrad_ref, gain_ref, ffn_gain_ref, gated_ref,
    kvp_any, normed_any, back_any, wq_any, wk_any, wv_any, wg_any, fgate_any, fup_any,
    igrad_ref, gains_ref, query_out, key_out, value_out, gate_out, output_out, fgate_out, fup_out,
    kvp, normed, back, wq, wk, wv, wg, fgate, fup, qlow, klow, vlow, early, late, hterms,
    kv_passed, kv_into, early_passed, early_into, late_passed, late_into, hinto, fgate_into,
    fup_into, gain_slots, stage, local_sem,
    kvs, kvr, kvps, kvpr, es, er, eps, epr, ls, lr, lps, lpr, hs, hr, gs, gr, us, ur, gain_send,
    gain_recv,
):
    tok, width = x_ref.shape
    rows = dq_ref.shape[0]
    wide_count = lax.axis_size("wide")
    head_count = lax.axis_size("head")
    head, wide = head_ring(), wide_ring()
    loads = [
        pltpu.make_async_copy(src, dst, local_sem.at[i])
        for i, (src, dst) in enumerate(
            (
                (kvp_any, kvp), (fgate_any, fgate), (fup_any, fup), (normed_any, normed),
                (back_any, back), (wq_any, wq), (wk_any, wk), (wv_any, wv), (wg_any, wg),
            )
        )
    ]
    for load in loads:
        load.start()
    meet(everyone(head, wide))
    kv_width = wk.shape[1]
    q_width = wq.shape[1]
    block = normed.shape[1] // wide_count
    ffn_rows = fgate.shape[0] // head_count
    kv_scatter = PairScatter(wide, kvp, rows, kv_passed, kv_into, kvs, kvr, kvps, kvpr)
    early_scatter = PairScatter(wide, early, block, early_passed, early_into, es, er, eps, epr)
    late_scatter = PairScatter(wide, late, block, late_passed, late_into, ls, lr, lps, lpr)
    head_scatter = Scatter(head, lambda index: (hterms, index * tok), tok, hinto, hs, hr)
    gate_scatter = Scatter(
        head, lambda index: (fgate, index * ffn_rows), ffn_rows, fgate_into, gs, gr
    )
    up_scatter = Scatter(head, lambda index: (fup, index * ffn_rows), ffn_rows, fup_into, us, ur)
    order = offsets(wide)

    loads[0].wait()
    for offset in order:
        kv_scatter.hand(offset)
    loads[1].wait()
    gate_scatter.start(head.half)
    loads[2].wait()
    up_scatter.start(head.half)

    chunk = 128

    def query_back(row, total):
        here = pl.ds(row, chunk)
        for j in range(q_width // LANES):
            cols = slice(j * LANES, (j + 1) * LANES)
            value, terms = unprep(
                dq_ref[here, cols], qpre_ref[here, cols], qgain_ref[...], cos_ref[here, :],
                sin_ref[here, :],
            )
            qlow[here, cols] = value.astype(jnp.bfloat16)
            total = total + jnp.sum(terms, axis=0, keepdims=True)
        return total

    def over_rows(count, body, start):
        return lax.fori_loop(
            0, count // chunk, lambda i, carried: body(pl.multiple_of(i * chunk, chunk), carried),
            start,
        )

    qgain_sum = over_rows(rows, query_back, jnp.zeros((1, LANES), jnp.float32))

    kv_scatter.merge(order[0])
    kv_scatter.start(wide.half)
    loads[3].wait()
    loads[4].wait()

    def early_part(offset):
        index = wide.index(offset)

        @pl.loop(0, 2)
        def _(core):
            target = 2 * index + core
            cols = pl.ds(pl.multiple_of(target * block, block), block)
            there = pl.ds(pl.multiple_of(target * block, block), block)
            left = normed[:, cols]
            early[there, :q_width] = dot_tn(left, qlow[...]).astype(jnp.bfloat16)
            early[there, q_width : 2 * q_width] = dot_tn(left, ggrad_ref[...]).astype(jnp.bfloat16)
            out = dot_tn(gated_ref[...], back[:, cols]).astype(jnp.bfloat16)
            for piece in range(q_width // block):
                early[there, 2 * q_width + piece * block : 2 * q_width + (piece + 1) * block] = out[
                    piece * block : (piece + 1) * block, :
                ]

        early_scatter.hand(offset)

    for offset in order:
        early_part(offset)
    for offset in order[1:]:
        kv_scatter.merge(offset)
    early_scatter.merge(order[0])
    for hop in range(wide.half - 1, 0, -1):
        kv_scatter.advance(hop)
    early_scatter.start(wide.half)
    for hop in range(head.half - 1, 0, -1):
        gate_scatter.advance(hop)
        up_scatter.advance(hop)
    for offset in order[1:]:
        early_scatter.merge(offset)
    for load in loads[5:]:
        load.wait()
    kv_scatter.arrive()

    def key_back(row, total):
        here = pl.ds(row, chunk)
        both = kv_scatter.total(row, chunk)
        for j in range(kv_width // LANES):
            cols = slice(j * LANES, (j + 1) * LANES)
            value, terms = unprep(
                both[:, cols], kpre_ref[here, cols], kgain_ref[...], cos_ref[here, :],
                sin_ref[here, :],
            )
            klow[here, cols] = value.astype(jnp.bfloat16)
            total = total + jnp.sum(terms, axis=0, keepdims=True)
        vlow[here, :] = both[:, kv_width:].astype(jnp.bfloat16)
        return total

    kgain_sum = over_rows(rows, key_back, jnp.zeros((1, LANES), jnp.float32))

    def head_part(offset):
        here = pl.ds(pl.multiple_of(head.index(offset) * tok, tok), tok)

        @pl.loop(0, width // 256)
        def _(i):
            cols = pl.ds(pl.multiple_of(i * 256, 256), 256)
            value = dot_nt(qlow[here, :], wq[cols, :]) + dot_nt(ggrad_ref[here, :], wg[cols, :])
            value += dot_nt(klow[here, :], wk[cols, :]) + dot_nt(vlow[here, :], wv[cols, :])
            hterms[here, cols] = value.astype(jnp.bfloat16)

    head_part(head.half)
    head_scatter.start(head.half)

    def late_part(offset):
        index = wide.index(offset)

        @pl.loop(0, 2)
        def _(core):
            target = 2 * index + core
            cols = pl.ds(pl.multiple_of(target * block, block), block)
            left = normed[:, cols]
            late[cols, :kv_width] = dot_tn(left, klow[...]).astype(jnp.bfloat16)
            late[cols, kv_width:] = dot_tn(left, vlow[...]).astype(jnp.bfloat16)

        late_scatter.hand(offset)

    late_part(order[0])
    for hop in range(wide.half - 1, 0, -1):
        early_scatter.advance(hop)
    for offset in order[1:]:
        late_part(offset)
    late_scatter.merge(order[0])
    late_scatter.start(wide.half)
    for hop in range(head.half - 1, 0, -1):
        head_part(hop)
        head_part(-hop)
        head_scatter.advance(hop)
    head_part(0)
    for offset in order[1:]:
        late_scatter.merge(offset)
    for hop in range(wide.half - 1, 0, -1):
        late_scatter.advance(hop)

    gate_scatter.arrive()
    up_scatter.arrive()
    emit = 64
    pending = [None, None]
    for step in range(ffn_rows // emit):
        for which, (scatter, out) in enumerate(((gate_scatter, fgate_out), (up_scatter, fup_out))):
            if pending[which] is not None:
                pending[which].wait()
            stage[which] = scatter.total(step * emit, emit)
            pending[which] = pltpu.make_async_copy(
                stage.at[which], out.at[pl.ds(step * emit, emit)], local_sem.at[9 + which]
            )
            pending[which].start()

    head_scatter.arrive()
    gain = gain_ref[...]

    def input_back(row, total):
        here = pl.ds(row, 32)
        value = x_ref[here, :].astype(jnp.float32)
        grad = head_scatter.total(row, 32)
        scale = lax.rsqrt(jnp.mean(value * value, axis=-1, keepdims=True) + EPS)
        scaled = value * scale
        weighted = grad * gain
        mean = jnp.mean(scaled * weighted, axis=-1, keepdims=True)
        igrad_ref[here, :] = mgrad_ref[here, :] + scale * (weighted - scaled * mean)
        return total + jnp.sum(grad * scaled, axis=0, keepdims=True)

    gain_sum = lax.fori_loop(
        0, tok // 32, lambda i, carried: input_back(pl.multiple_of(i * 32, 32), carried),
        jnp.zeros((1, width), jnp.float32),
    )
    chips = wide.size
    pair_slot, chip_slot = 0, 2
    head_slot = 2 + chips
    mine = gain_slots.at[pair_slot]
    mine[...] = jnp.zeros(mine.shape, jnp.float32)
    mine[0:1, :] = gain_sum
    mine[1:2, :] = ffn_gain_ref[...]
    mine[2:3, 0:LANES] = qgain_sum
    mine[3:4, 0:LANES] = kgain_sum
    swap = remote(
        mine, gain_slots.at[1], gain_send.at[0], gain_recv.at[0], wide.sibling
    )
    swap.start()
    swap.wait_recv()

    def spread(ring, own, base, sem):
        here = gain_slots.at[base + own]
        copies = [
            remote(here, here, gain_send.at[sem + d], gain_recv.at[sem + d], ring.device(d))
            for d in range(1, ring.size)
        ]
        for copy in copies:
            copy.start()
        for copy in copies:
            copy.wait_recv()
        return copies

    own_chip = wide.index(0)
    gain_slots[chip_slot + own_chip] = gain_slots[0] + gain_slots[1]
    sent = [swap] + spread(wide, own_chip, chip_slot, 0)
    total = gain_slots[chip_slot]
    for i in range(1, chips):
        total = total + gain_slots[chip_slot + i]
    own_head = lax.axis_index("head")
    gain_slots[head_slot + own_head] = total
    sent += spread(head, own_head, head_slot, chips - 1)
    total = gain_slots[head_slot]
    for i in range(1, head_count):
        total = total + gain_slots[head_slot + i]
    gains_ref[...] = total

    early_scatter.arrive()

    def early_out(row):
        here = pl.ds(row, 32)
        both = early_scatter.total(row, 32)
        query_out[here, :] = both[:, :q_width]
        gate_out[here, :] = both[:, q_width : 2 * q_width]
        for piece in range(q_width // block):
            output_out[pl.ds(pl.multiple_of(piece * block + row, 32), 32), :] = both[
                :, 2 * q_width + piece * block : 2 * q_width + (piece + 1) * block
            ]

    row_loop(block, 32, early_out)
    late_scatter.arrive()

    def late_out(row):
        here = pl.ds(row, 32)
        both = late_scatter.total(row, 32)
        key_out[here, :] = both[:, :kv_width]
        value_out[here, :] = both[:, kv_width:]

    row_loop(block, 32, late_out)
    for scatter in (
        kv_scatter, early_scatter, late_scatter, head_scatter, gate_scatter, up_scatter
    ):
        scatter.finish()
    for copy in sent:
        copy.wait_send()
    for copy in pending:
        copy.wait()


def tail_block(
    dq, kv_parts, query_pre, key_pre, gate_grad, cosine, sine_tab, query_gain, key_gain, inputs,
    middle_grad, attn_gain, ffn_gain_part, gated_low, normed, back_rows, weights, fgate, fup,
):
    tok, width = inputs.shape
    head_count, wide_count = lax.axis_size("head"), lax.axis_size("wide")
    chips = wide_count // 2
    rows, q_width = dq.shape
    kv_width = key_pre.shape[1]
    block = width // wide_count
    hidden_width = fgate.shape[1]
    ffn_rows = width // head_count
    low, full = jnp.bfloat16, jnp.float32
    shape, vm = jax.ShapeDtypeStruct, pltpu.VMEM
    early_width = 3 * q_width
    pair = [*ring_sems(chips), DMA((chips,)), DMA((chips,))]
    peers = chips + head_count
    return pl.pallas_call(
        tail_kernel,
        out_shape=(
            shape((tok, width), full),
            shape((8, width), full),
            shape((block, q_width), full),
            shape((block, kv_width), full),
            shape((block, kv_width), full),
            shape((block, q_width), full),
            shape((q_width, block), full),
            shape((ffn_rows, hidden_width), full),
            shape((ffn_rows, hidden_width), full),
        ),
        in_specs=[VMEM] * 13 + [ANY] * 9,
        out_specs=tuple([VMEM] * 7 + [ANY] * 2),
        scratch_shapes=[
            vm(kv_parts.shape, low), vm(normed.shape, low), vm(back_rows.shape, low),
            *[vm(weight.shape, low) for weight in weights],
            vm(fgate.shape, low), vm(fup.shape, low),
            vm((rows, q_width), low), vm((rows, kv_width), low), vm((rows, kv_width), low),
            vm((width, early_width), low), vm((width, 2 * kv_width), low),
            vm((head_count * tok, width), low),
            vm((chips, rows, 2 * kv_width), low), into_shape(chips, rows, 2 * kv_width),
            vm((chips, block, early_width), low), into_shape(chips, block, early_width),
            vm((chips, block, 2 * kv_width), low), into_shape(chips, block, 2 * kv_width),
            into_shape(head_count, tok, width),
            into_shape(head_count, ffn_rows, hidden_width),
            into_shape(head_count, ffn_rows, hidden_width),
            vm((2 + chips + head_count, 8, width), full),
            vm((2, 64, hidden_width), full),
            DMA((11,)),
            *pair, *pair, *pair,
            *ring_sems(head_count), *ring_sems(head_count), *ring_sems(head_count),
            DMA((peers,)), DMA((peers,)),
        ],
        compiler_params=pltpu.CompilerParams(
            collective_id=2, has_side_effects=True, vmem_limit_bytes=VMEM_LIMIT
        ),
        cost_estimate=pl.CostEstimate(
            flops=20 * rows * width * q_width, bytes_accessed=300 << 20, transcendentals=0
        ),
        name="tail_block",
    )(
        dq, query_pre, key_pre, gate_grad, cosine, sine_tab, query_gain[None], key_gain[None],
        inputs, middle_grad, attn_gain[None], ffn_gain_part, gated_low,
        kv_parts, normed, back_rows, *weights, fgate, fup,
    )


def contract_cols(left_mat, right_mat):
    return lax.dot_general(
        left_mat, right_mat, (((1,), (1,)), ((), ())), preferred_element_type=jnp.float32
    )


def shards(
    inputs,
    attn_gain,
    query_weight,
    key_projection,
    value_projection,
    attn_gate_weight,
    output_weight,
    query_gain,
    key_gain,
    ffn_gain,
    ffn_gate_weight,
    ffn_up_weight,
    ffn_down_weight,
    doc_lengths,
    cotangent,
):
    tok_dev = inputs.shape[0]
    head_width = query_gain.shape[0]
    head_count = lax.axis_size("head")
    wide_count = lax.axis_size("wide")
    query_rows = tok_dev * head_count
    wide_pos = lax.axis_index("wide")
    local_ids = jnp.arange(query_rows, dtype=jnp.int32)
    query_tok = (local_ids // tok_dev * wide_count + wide_pos) * tok_dev + local_ids % tok_dev
    query_seg, query_pos, query_first = token_tables(doc_lengths, query_tok)
    starts = query_first[::tok_dev]
    firsts = query_first[:, None]
    cosine, sine_tab = rotary(query_pos, head_width)
    weights = (query_weight, key_projection, value_projection, attn_gate_weight)
    query_low, query_pre, key_pre, gate_pre, gathered, kv_all = front_block(
        inputs, attn_gain, cosine, sine_tab, query_gain, key_gain, weights
    )
    attended, inverse, gated_low = attention_forward(
        query_low, kv_all, starts, firsts, gate_pre
    )
    gate_sig = jax.nn.sigmoid(gate_pre)
    (
        outputs,
        middle_grad,
        ffn_gain_part,
        back_rows,
        ffn_down_grad,
        gate_wgrad,
        up_wgrad,
    ) = ffn_block(
        gated_low,
        inputs,
        cotangent,
        ffn_gain,
        output_weight,
        ffn_gate_weight,
        ffn_up_weight,
        ffn_down_weight,
    )
    gated_grad = contract_cols(back_rows, output_weight)
    attended_grad_low = (gated_grad * gate_sig).astype(jnp.bfloat16)
    gate_pre_grad_low = (gated_grad * attended * gate_sig * (1.0 - gate_sig)).astype(jnp.bfloat16)
    query_rot_grad, kv_parts = attention_backward(
        query_low, attended_grad_low, attended, inverse, kv_all, starts, firsts
    )
    (
        input_grad,
        gains,
        query_grad,
        key_grad,
        value_grad,
        attn_gate_grad,
        output_grad,
        ffn_gate_grad,
        ffn_up_grad,
    ) = tail_block(
        query_rot_grad,
        kv_parts,
        query_pre,
        key_pre,
        gate_pre_grad_low,
        cosine,
        sine_tab,
        query_gain,
        key_gain,
        inputs,
        middle_grad,
        attn_gain,
        ffn_gain_part,
        gated_low,
        gathered,
        back_rows,
        weights,
        gate_wgrad,
        up_wgrad,
    )
    attn_gain_grad, ffn_gain_grad = gains[0], gains[1]
    query_gain_grad, key_gain_grad = gains[2, :head_width], gains[3, :head_width]
    return (
        outputs,
        input_grad,
        attn_gain_grad,
        query_grad,
        key_grad,
        value_grad,
        attn_gate_grad,
        output_grad,
        query_gain_grad,
        key_gain_grad,
        ffn_gain_grad,
        ffn_gate_grad,
        ffn_up_grad,
        ffn_down_grad,
    )


def solution(mesh):
    placed = (
        P(("head", "wide"), None),
        P(),
        P(None, "head"),
        P(None, "head"),
        P(None, "head"),
        P(None, "head"),
        P("head", None),
        P(),
        P(),
        P(),
        P(None, "wide"),
        P(None, "wide"),
        P("wide", None),
        P(),
        P(("head", "wide"), None),
    )
    return jax.shard_map(
        shards,
        mesh=mesh,
        in_specs=placed,
        out_specs=(
            P(("head", "wide"), None),
            P(("head", "wide"), None),
            P(),
            P("wide", "head"),
            P("wide", "head"),
            P("wide", "head"),
            P("wide", "head"),
            P("head", "wide"),
            P(),
            P(),
            P(),
            P("head", "wide"),
            P("head", "wide"),
            P("wide", "head"),
        ),
        check_vma=False,
    )
```

```python
import functools

import jax
import jax.numpy as jnp
from jax import lax
from jax.experimental import pallas as pl
from jax.experimental.pallas import tpu as pltpu
from jax.sharding import PartitionSpec as P

EPS = 1e-06
THETA = 1000000.0
VMEM_LIMIT = 63 << 20


def token_position(doc_lengths, token_ids):
    lengths = doc_lengths.reshape(-1)
    before = jnp.cumsum(lengths)[None, :] <= token_ids[:, None]
    return token_ids - jnp.sum(jnp.where(before, lengths[None, :], 0), axis=1)


def rotary(position, head_width):
    half_width = head_width // 2
    inverse = THETA ** (-(jnp.arange(half_width, dtype=jnp.float32) * 2.0 / head_width))
    angles = position.astype(jnp.float32)[:, None] * inverse[None, :]
    cosine = jnp.cos(angles)
    sine_tab = jnp.sin(angles)
    return (
        jnp.concatenate([cosine, cosine], axis=1),
        jnp.concatenate([sine_tab, sine_tab], axis=1),
    )


MESH = pl.DeviceIdType.MESH
ANY = pl.BlockSpec(memory_space=pl.ANY)
VMEM = pl.BlockSpec(memory_space=pltpu.VMEM)
DMA = pltpu.SemaphoreType.DMA
SIDES = (0, 1)


class Ring:
    def __init__(self, size, pos, index, device):
        self.size, self.pos, self.half = size, pos, size // 2
        self._index, self._device = index, device

    def at(self, offset):
        return lax.rem(self.pos + (offset + 2 * self.size), self.size)

    def index(self, offset):
        return self._index(self.at(offset))

    def device(self, offset):
        return self._device(self.at(offset))


def head_ring():
    size = lax.axis_size("head")
    spread = size // 2
    own, wide = lax.axis_index("head"), lax.axis_index("wide")
    major, minor = lax.div(own, 2), lax.rem(own, 2)
    pos = major + minor * (size - 1 - 2 * major)

    def index(place):
        upper = lax.div(place, spread)
        return 2 * (place + upper * (size - 1 - 2 * place)) + upper

    return Ring(size, pos, index, lambda place: (index(place), wide))


def wide_ring():
    size = lax.axis_size("wide") // 2
    head, wide = lax.axis_index("head"), lax.axis_index("wide")
    core = lax.rem(wide, 2)
    ring = Ring(
        size, lax.div(wide, 2), lambda place: place, lambda place: (head, 2 * place + core)
    )
    ring.core = core
    ring.sibling = (head, wide + 1 - 2 * core)
    return ring


def meet(devices):
    barrier = pltpu.get_barrier_semaphore()
    for device in devices:
        pl.semaphore_signal(barrier, inc=1, device_id=device, device_id_type=MESH)
    pl.semaphore_wait(barrier, len(devices))


def neighbours(*rings):
    found = []
    for ring in rings:
        found += [ring.device(1), ring.device(-1)]
        if hasattr(ring, "sibling"):
            found.append(ring.sibling)
    return found


def remote(src, dst, send, recv, device):
    return pltpu.make_async_remote_copy(
        src_ref=src, dst_ref=dst, send_sem=send, recv_sem=recv, device_id=device,
        device_id_type=MESH,
    )


class Gather:
    def __init__(self, ring, slot, rows, send, recv):
        self.ring, self.slot, self.rows = ring, slot, rows
        self.send, self.recv = send, recv

    def span(self, hop, side):
        if 2 * hop == self.ring.size:
            return side * (self.rows // 2), self.rows // 2
        return 0, self.rows

    def copy(self, hop, side):
        way = 1 - 2 * side
        ref = self.slot(self.ring.index(-way * (hop - 1)), *self.span(hop, side))
        return remote(
            ref, ref, self.send.at[side, hop - 1], self.recv.at[side, hop - 1],
            self.ring.device(way),
        )

    def start(self, hop):
        for side in SIDES:
            self.copy(hop, side).start()

    def arrive(self, hop):
        for side in SIDES:
            self.copy(hop, side).wait_recv()

    def finish(self):
        for hop in range(1, self.ring.half + 1):
            for side in SIDES:
                self.copy(hop, side).wait_send()


class PairGather(Gather):
    def __init__(self, ring, slot, rows, send, recv, pass_send, pass_recv):
        core = ring.core
        super().__init__(
            ring, lambda index, start, size: slot(2 * index + core, start, size), rows, send, recv
        )
        self.pass_send, self.pass_recv = pass_send, pass_recv

    def handed(self, hop, side):
        way = 1 - 2 * side
        span = self.span(hop, side) if hop else (0, self.rows)
        ref = self.slot(self.ring.index(-way * hop), *span)
        return remote(
            ref, ref, self.pass_send.at[side, hop], self.pass_recv.at[side, hop],
            self.ring.sibling,
        )

    def hand(self, hop):
        for side in SIDES if hop else (0,):
            self.handed(hop, side).start()

    def take(self, hop):
        for side in SIDES if hop else (0,):
            self.handed(hop, side).wait_recv()

    def begin(self):
        self.start(1)
        self.hand(0)

    def finish(self):
        super().finish()
        for hop in range(self.ring.half + 1):
            for side in SIDES if hop else (0,):
                self.handed(hop, side).wait_send()


def row_loop(rows, chunk, body):
    @pl.loop(0, rows // chunk)
    def _(step):
        body(pl.multiple_of(step * chunk, chunk))


class Scatter:
    def __init__(self, ring, part, rows, into, send, recv):
        self.ring, self.part, self.rows, self.into = ring, part, rows, into
        self.send, self.recv = send, recv

    def span(self, hop, side):
        if 2 * hop == self.ring.size:
            return side * (self.rows // 2), self.rows // 2
        return 0, self.rows

    def copy(self, hop, side):
        way = 1 - 2 * side
        first, count = self.span(hop, side)
        ref, base = self.part(self.ring.index(way * hop))
        return remote(
            ref.at[pl.ds(base + first, count)],
            self.into.at[side, pl.ds((hop - 1) * self.rows + self.inside(hop, first), count)],
            self.send.at[side, hop - 1], self.recv.at[side, hop - 1], self.ring.device(way),
        )

    def inside(self, hop, row):
        return row % (self.rows // 2) if 2 * hop == self.ring.size else row

    def start(self, hop):
        for side in SIDES:
            self.copy(hop, side).start()

    def fold(self, hop, side):
        way = 1 - 2 * side
        self.copy(hop + 1, side).wait_recv()
        first, count = self.span(hop + 1, side)
        ref, base = self.part(self.ring.index(way * hop))
        chunk = min(count, 32)

        def add(row):
            there = pl.ds(pl.multiple_of(base + first + row, chunk), chunk)
            start = hop * self.rows + self.inside(hop + 1, first)
            here = pl.ds(pl.multiple_of(start + row, chunk), chunk)
            ref[there, :] = (
                ref[there, :].astype(jnp.float32) + self.into[side, here, :].astype(jnp.float32)
            ).astype(ref.dtype)

        row_loop(count, chunk, add)

    def advance(self, hop):
        for side in SIDES:
            self.fold(hop, side)
            self.copy(hop, side).start()

    def arrive(self):
        for side in SIDES:
            self.copy(1, side).wait_recv()

    def total(self, row, count):
        ref, base = self.part(self.ring.index(0))
        there = pl.ds(pl.multiple_of(base + row, count), count)
        here = pl.ds(row, count)
        return (
            ref[there, :].astype(jnp.float32)
            + self.into[0, here, :].astype(jnp.float32)
            + self.into[1, here, :].astype(jnp.float32)
        )

    def finish(self):
        for hop in range(1, self.ring.half + 1):
            for side in SIDES:
                self.copy(hop, side).wait_send()


class PairScatter(Scatter):
    def __init__(self, ring, terms, rows, passed, into, send, recv, pass_send, pass_recv):
        core = ring.core
        super().__init__(
            ring, lambda index: (terms, (2 * index + core) * rows), rows, into, send, recv
        )
        self.terms, self.passed = terms, passed
        self.pass_send, self.pass_recv = pass_send, pass_recv

    def handed(self, offset):
        ring = self.ring
        index = ring.index(offset)
        other = pl.multiple_of((2 * index + 1 - ring.core) * self.rows, self.rows)
        slot = offset % ring.size
        return remote(
            self.terms.at[pl.ds(other, self.rows)],
            self.passed.at[slot],
            self.pass_send.at[slot], self.pass_recv.at[slot], ring.sibling,
        )

    def hand(self, offset):
        self.handed(offset).start()

    def merge(self, offset):
        self.handed(offset).wait_recv()
        slot = offset % self.ring.size
        ref, base = self.part(self.ring.index(offset))
        chunk = 32

        def add(row):
            there = pl.ds(pl.multiple_of(base + row, chunk), chunk)
            ref[there, :] = (
                ref[there, :].astype(jnp.float32)
                + self.passed[slot, pl.ds(row, chunk), :].astype(jnp.float32)
            ).astype(ref.dtype)

        row_loop(self.rows, chunk, add)

    def finish(self):
        super().finish()
        for offset in range(self.ring.size):
            self.handed(offset).wait_send()


def offsets(ring):
    order = [ring.half]
    for hop in range(ring.half - 1, 0, -1):
        order += [hop, -hop]
    return order + [0]


def into_shape(size, rows, columns):
    return pltpu.VMEM((2, (size - 1) * rows // 2, columns), jnp.bfloat16)


def everyone(*rings):
    found = []
    for ring in rings:
        found += [ring.device(offset) for offset in range(1, ring.size)]
        if hasattr(ring, "sibling"):
            found.append(ring.sibling)
    return found


def ring_sems(size):
    return [DMA((2, size // 2)), DMA((2, size // 2))]


def pass_sems(size):
    return [DMA((2, size // 2 + 1)), DMA((2, size // 2 + 1))]


NEAR, OTHER, FAR = 0, 1, 2


class LineGather:
    pieces = 2

    def __init__(self, ring, slot, rows, send, recv, pass_send, pass_recv):
        self.ring, self.slot, self.rows = ring, slot, rows // self.pieces
        self.send, self.recv, self.pass_send, self.pass_recv = send, recv, pass_send, pass_recv
        pos = ring.pos
        half, odd = lax.div(pos, 2), lax.rem(pos, 2)
        self.way = 1 - 2 * odd
        self.middle = half + odd == 1

    def offset(self, kind):
        return {NEAR: self.way, OTHER: -self.way, FAR: 2}[kind]

    def ref(self, offset, piece):
        index = 2 * self.ring.index(offset) + self.ring.core
        return self.slot(index, piece * self.rows, self.rows)

    def copy(self, which, offset, kind, piece, way):
        ref = self.ref(offset, piece)
        return remote(
            ref, ref, self.send.at[which, piece], self.recv.at[kind, piece],
            self.ring.device(way),
        )

    def own(self, piece):
        return self.copy(0, 0, NEAR, piece, self.way)

    def own_other(self, piece):
        return self.copy(1, 0, OTHER, piece, -self.way)

    def onward(self, kind, piece):
        arrives = {NEAR: FAR, OTHER: FAR, FAR: OTHER}[kind]
        way = -self.way if kind == NEAR else self.way
        return self.copy(2 + kind, self.offset(kind), arrives, piece, way)

    def incoming(self, kind, piece):
        return self.copy(0, self.offset(kind), kind, piece, self.way)

    def handed(self, kind, piece):
        ref = self.ref(0 if kind is None else self.offset(kind), piece)
        slot = 3 if kind is None else kind
        return remote(
            ref, ref, self.pass_send.at[slot, piece], self.pass_recv.at[slot, piece],
            self.ring.sibling,
        )

    def begin(self):
        for piece in range(self.pieces):
            self.own(piece).start()

            @pl.when(self.middle)
            def _():
                self.own_other(piece).start()

            self.handed(None, piece).start()

    def arrive(self, kind):
        for piece in range(self.pieces):
            self.incoming(kind, piece).wait_recv()

            @pl.when(self.middle)
            def _():
                self.onward(kind, piece).start()

            self.handed(kind, piece).start()

    def take(self, kind):
        for piece in range(self.pieces):
            self.handed(kind, piece).wait_recv()

    def finish(self):
        for piece in range(self.pieces):
            self.own(piece).wait_send()

            @pl.when(self.middle)
            def _():
                self.own_other(piece).wait_send()
                for kind in (NEAR, OTHER, FAR):
                    self.onward(kind, piece).wait_send()

            for kind in (None, NEAR, OTHER, FAR):
                self.handed(kind, piece).wait_send()


class LineScatter(PairScatter):
    pieces = 2

    def __init__(self, *args):
        super().__init__(*args)
        pos = self.ring.pos
        half, odd = lax.div(pos, 2), lax.rem(pos, 2)
        self.way = 1 - 2 * odd
        self.middle = half + odd == 1
        self.waited = set()

    def offset(self, kind):
        return {NEAR: self.way, OTHER: -self.way, FAR: 2, None: 0}[kind]

    def piece_of(self, piece):
        size = self.rows // self.pieces
        return piece * size, size

    def outgoing(self, kind, slot, piece, way):
        first, size = self.piece_of(piece)
        ref, base = self.part(self.ring.index(self.offset(kind)))
        return remote(
            ref.at[pl.ds(pl.multiple_of(base + first, size), size)],
            self.into.at[slot, pl.ds(first, size)],
            self.send.at[kind, piece], self.recv.at[slot, piece], self.ring.device(way),
        )

    def from_end(self, kind, piece):
        return self.outgoing(kind, {OTHER: 0, FAR: 1, NEAR: 2}[kind], piece, self.way)

    def from_middle(self, kind, piece):
        slot = {FAR: 3, OTHER: 4, NEAR: 0}[kind]
        return self.outgoing(kind, slot, piece, self.way if kind == NEAR else -self.way)

    def landed(self, slot, piece):
        first, size = self.piece_of(piece)
        ref = self.into.at[slot, pl.ds(first, size)]
        remote(
            ref, ref, self.send.at[0, piece], self.recv.at[slot, piece], self.ring.device(self.way)
        ).wait_recv()

    def hand_kind(self, kind):
        self.swap(kind).start()

    def swap(self, kind):
        index = self.ring.index(self.offset(kind))
        other = pl.multiple_of((2 * index + 1 - self.ring.core) * self.rows, self.rows)
        slot = 3 if kind is None else kind
        return remote(
            self.terms.at[pl.ds(other, self.rows)], self.passed.at[slot],
            self.pass_send.at[slot], self.pass_recv.at[slot], self.ring.sibling,
        )

    def merge_kind(self, kind):
        self.swap(kind).wait_recv()
        slot = 3 if kind is None else kind
        ref, base = self.part(self.ring.index(self.offset(kind)))

        def add(row):
            there = pl.ds(pl.multiple_of(base + row, 32), 32)
            ref[there, :] = (
                ref[there, :].astype(jnp.float32)
                + self.passed[slot, pl.ds(row, 32), :].astype(jnp.float32)
            ).astype(ref.dtype)

        row_loop(self.rows, 32, add)

    def launch(self, *kinds):
        @pl.when(~self.middle)
        def _():
            for kind in kinds:
                for piece in range(self.pieces):
                    self.from_end(kind, piece).start()

    def sent(self, kind):
        self.waited.add(kind)

        @pl.when(~self.middle)
        def _():
            for piece in range(self.pieces):
                self.from_end(kind, piece).wait_send()

    def relay(self, kind):
        slot = {FAR: 0, OTHER: 1, NEAR: 3}[kind]

        @pl.when(self.middle)
        def _():
            ref, base = self.part(self.ring.index(self.offset(kind)))
            for piece in range(self.pieces):
                first, size = self.piece_of(piece)
                self.landed(slot, piece)

                def add(row):
                    there = pl.ds(pl.multiple_of(base + first + row, 32), 32)
                    here = pl.ds(pl.multiple_of(first + row, 32), 32)
                    ref[there, :] = (
                        ref[there, :].astype(jnp.float32)
                        + self.into[slot, here, :].astype(jnp.float32)
                    ).astype(ref.dtype)

                row_loop(size, 32, add)
                self.from_middle(kind, piece).start()

    def arrive(self):
        @pl.when(self.middle)
        def _():
            for piece in range(self.pieces):
                self.landed(2, piece)
                self.landed(4, piece)

            def add(row):
                here = pl.ds(row, 32)
                self.into[0, here, :] = (
                    self.into[2, here, :].astype(jnp.float32)
                    + self.into[4, here, :].astype(jnp.float32)
                ).astype(self.into.dtype)

            row_loop(self.rows, 32, add)

        @pl.when(~self.middle)
        def _():
            for piece in range(self.pieces):
                self.landed(0, piece)

    def total(self, row, count):
        ref, base = self.part(self.ring.index(0))
        there = pl.ds(pl.multiple_of(base + row, count), count)
        return ref[there, :].astype(jnp.float32) + self.into[0, pl.ds(row, count), :].astype(
            jnp.float32
        )

    def finish(self):
        for piece in range(self.pieces):

            @pl.when(self.middle)
            def _():
                for kind in (NEAR, OTHER, FAR):
                    self.from_middle(kind, piece).wait_send()

            @pl.when(~self.middle)
            def _():
                for kind in (NEAR, OTHER, FAR):
                    if kind not in self.waited:
                        self.from_end(kind, piece).wait_send()

        for kind in (NEAR, OTHER, FAR, None):
            self.swap(kind).wait_send()


def scatter_of(ring):
    return LineScatter if ring.size == 4 else PairScatter


def scatter_into(size, rows, columns):
    if size == 4:
        return pltpu.VMEM((5, rows, columns), jnp.bfloat16)
    return into_shape(size, rows, columns)


def scatter_sems(size):
    passed = [DMA((size,)), DMA((size,))]
    if size == 4:
        pieces = LineScatter.pieces
        return [DMA((3, pieces)), DMA((5, pieces)), *passed]
    return [*ring_sems(size), *passed]


def line_sems():
    pieces = LineGather.pieces
    return [DMA((5, pieces)), DMA((3, pieces)), DMA((4, pieces)), DMA((4, pieces))]


def gather_sems(size):
    return line_sems() if size == 4 else [*ring_sems(size), *pass_sems(size)]


def row_gather_of(ring):
    return LineGather if ring.size == 4 else PairGather


def dot_nn(left, right):
    return jnp.dot(left, right, preferred_element_type=jnp.float32)


def dot_nt(left, right):
    return lax.dot_general(
        left, right, (((1,), (1,)), ((), ())), preferred_element_type=jnp.float32
    )


def dot_tn(left, right):
    return lax.dot_general(
        left, right, (((0,), (0,)), ((), ())), preferred_element_type=jnp.float32
    )


LANES = 128
FORWARD_KEYS = 1024
BACKWARD_KEYS = 512
LOG2E = 1.4426950408889634


def doc_ends(doc_ref):
    ends, total = [], jnp.int32(0)
    for row in range(doc_ref.shape[0]):
        for doc in range(doc_ref.shape[1]):
            total = total + doc_ref[row, doc]
            ends.append(total)
    return ends


def first_of(ends, tokens):
    first = jnp.zeros_like(tokens)
    for end in ends:
        first = jnp.maximum(first, jnp.where(tokens >= end, end, 0))
    return first


def start_all(copies):
    for copy in copies:
        copy.start()


def attention_forward_kernel(
    doc_ref, query_any, kv_any, gate_any, att_any, inv_any, gated_any,
    query, kv, gate, att, inv, gated, acc, kv_sem, in_sem, out_sem,
):
    wide_count = lax.axis_size("wide")
    wide_pos = lax.axis_index("wide")
    kv_width = kv.shape[1] // 2
    groups = kv_width // LANES
    per = query.shape[1] // kv_width
    blocks = kv_sem.shape[0]
    rows = query.shape[0] // blocks
    step = min(FORWARD_KEYS, rows * wide_count)
    factor = LANES ** (-0.5) * LOG2E
    chunk = rows * wide_count

    def kv_copy(blk):
        there = pl.ds(pl.multiple_of(blk * chunk, chunk), chunk)
        return pltpu.make_async_copy(kv_any.at[there], kv.at[there], kv_sem.at[blk])

    early = [
        pltpu.make_async_copy(query_any, query, in_sem.at[0]),
        pltpu.make_async_copy(gate_any, gate, in_sem.at[1]),
    ]
    early[0].start()
    for blk in range(blocks):
        kv_copy(blk).start()
    early[1].start()
    ends = doc_ends(doc_ref)
    early[0].wait()

    def out_copies(blk):
        here = pl.ds(pl.multiple_of(blk * rows, rows), rows)
        return [
            pltpu.make_async_copy(src.at[here], dst.at[here], out_sem.at[i, blk])
            for i, (src, dst) in enumerate(((att, att_any), (inv, inv_any), (gated, gated_any)))
        ]

    @pl.loop(0, blocks)
    def _(blk):
        here = pl.ds(pl.multiple_of(blk * rows, rows), rows)
        first_tok = (blk * wide_count + wide_pos) * rows
        key_lane = lax.broadcasted_iota(jnp.int32, (rows, step), 1)
        tokens = lax.broadcasted_iota(jnp.int32, (rows, 1), 0) + first_tok
        upper = key_lane - tokens
        lower = key_lane - first_of(ends, tokens)
        queries = [
            jnp.concatenate(
                [query[here, (g * per + j) * LANES : (g * per + j + 1) * LANES] for j in range(per)],
                axis=0,
            )
            for g in range(groups)
        ]
        acc[...] = jnp.zeros_like(acc)
        kv_copy(blk).wait()

        @pl.loop(first_of(ends, first_tok) // step, (first_tok + rows + step - 1) // step)
        def _(tile):
            base = tile * step
            there = pl.ds(pl.multiple_of(base, step), step)
            allowed = (upper <= -base) & (lower >= -base)
            allowed = jnp.concatenate([allowed] * per, axis=0)
            for g in range(groups):
                cols = slice(g * LANES, (g + 1) * LANES)
                value_cols = slice(kv_width + g * LANES, kv_width + (g + 1) * LANES)
                scores = dot_nt(queries[g], kv[there, cols])
                probs = jnp.where(allowed, jnp.exp2(scores * factor), 0.0).astype(jnp.bfloat16)
                values = jnp.concatenate(
                    [kv[there, value_cols], jnp.ones((step, LANES), jnp.bfloat16)], axis=1
                )
                acc[g] += dot_nn(probs, values)

        @pl.when(blk == 0)
        def _():
            early[1].wait()

        for g in range(groups):
            for j in range(per):
                part = acc[g, j * rows : (j + 1) * rows, :]
                cols = slice((g * per + j) * LANES, (g * per + j + 1) * LANES)
                inverse = 1.0 / part[:, LANES:]
                out = part[:, :LANES] * inverse
                att[here, cols] = out
                inv[here, cols] = inverse
                gated[here, cols] = (out * jax.nn.sigmoid(gate[here, cols])).astype(jnp.bfloat16)
        start_all(out_copies(blk))

    for blk in range(blocks):
        for copy in out_copies(blk):
            copy.wait()


def attention_forward(doc_lengths, query_low, kv_all, gate_pre):
    rows, width = query_low.shape
    kv_width = kv_all.shape[1] // 2
    groups = kv_width // LANES
    per = width // kv_width
    blocks = lax.axis_size("head")
    low, full = jnp.bfloat16, jnp.float32
    shape, vm = jax.ShapeDtypeStruct, pltpu.VMEM
    return pl.pallas_call(
        attention_forward_kernel,
        out_shape=(
            shape((rows, width), full),
            shape((rows, width), full),
            shape((rows, width), low),
        ),
        in_specs=[pl.BlockSpec(memory_space=pltpu.SMEM)] + [ANY] * 3,
        out_specs=(ANY, ANY, ANY),
        scratch_shapes=[
            vm((rows, width), low), vm(kv_all.shape, low), vm((rows, width), full),
            vm((rows, width), full), vm((rows, width), full), vm((rows, width), low),
            vm((groups, per * (rows // blocks), 2 * LANES), full),
            DMA((blocks,)), DMA((2,)), DMA((3, blocks)),
        ],
        compiler_params=pltpu.CompilerParams(vmem_limit_bytes=VMEM_LIMIT),
        cost_estimate=pl.CostEstimate(
            flops=4 * rows * width * 2048, bytes_accessed=12 << 20, transcendentals=0
        ),
        name="attention_forward",
    )(doc_lengths, query_low, kv_all, gate_pre)


def attention_backward_kernel(
    doc_ref, query_any, att_any, inv_any, gate_any, kv_any, back_any, wo_any,
    dq_any, parts_any, ggrad_any,
    query, att, inv, gate, kv, back, wo, dq, parts, ggrad, dk_acc, dv_acc, dqt, keyt, dout,
    in_sem, out_sem,
):
    wide_count = lax.axis_size("wide")
    wide_pos = lax.axis_index("wide")
    kv_width = kv.shape[1] // 2
    groups = kv_width // LANES
    per = query.shape[1] // kv_width
    blocks = out_sem.shape[1]
    rows = query.shape[0] // blocks
    step = min(BACKWARD_KEYS, rows * wide_count)
    scale = LANES ** (-0.5)
    loads = [
        pltpu.make_async_copy(src, dst, in_sem.at[i])
        for i, (src, dst) in enumerate(
            (
                (back_any, back), (wo_any, wo), (gate_any, gate), (att_any, att),
                (inv_any, inv), (query_any, query), (kv_any, kv),
            )
        )
    ]
    start_all(loads)
    ends = doc_ends(doc_ref)
    dk_acc[...] = jnp.zeros_like(dk_acc)
    dv_acc[...] = jnp.zeros_like(dv_acc)
    for load in loads[:4]:
        load.wait()

    @pl.loop(0, blocks)
    def _(blk):
        here = pl.ds(pl.multiple_of(blk * rows, rows), rows)
        gated_grad = dot_nt(back[here, :], wo[...])
        sig = jax.nn.sigmoid(gate[here, :])
        grad = gated_grad * sig
        dout[here, :] = grad
        ggrad[here, :] = (grad * att[here, :] * (1.0 - sig)).astype(jnp.bfloat16)

    for load in loads[4:]:
        load.wait()

    @pl.loop(0, kv.shape[0] // step)
    def _(tile):
        there = pl.ds(pl.multiple_of(tile * step, step), step)
        for g in range(groups):
            cols = slice(g * LANES, (g + 1) * LANES)
            keyt[cols, there] = jnp.transpose(kv[there, cols])

    def out_copies(blk):
        here = pl.ds(pl.multiple_of(blk * rows, rows), rows)
        return [
            pltpu.make_async_copy(dq.at[here], dq_any.at[here], out_sem.at[0, blk]),
            pltpu.make_async_copy(parts.at[:, here], parts_any.at[:, here], out_sem.at[1, blk]),
            pltpu.make_async_copy(ggrad.at[here], ggrad_any.at[here], out_sem.at[2, blk]),
        ]

    @pl.loop(0, blocks)
    def _(turn_of):
        blk = blocks - 1 - turn_of
        here = pl.ds(pl.multiple_of(blk * rows, rows), rows)
        first_tok = (blk * wide_count + wide_pos) * rows
        key_row = lax.broadcasted_iota(jnp.int32, (step, rows), 0)
        tokens = lax.broadcasted_iota(jnp.int32, (1, rows), 1) + first_tok
        upper = key_row - tokens
        lower = key_row - first_of(ends, tokens)
        queries, grads, deltas = [], [], []
        for g in range(groups):
            qs, gs, ds = [], [], []
            for j in range(per):
                cols = slice((g * per + j) * LANES, (g * per + j + 1) * LANES)
                both = dout[here, cols] * inv[here, cols]
                delta = jnp.sum(both * att[here, cols], axis=1, keepdims=True)
                ds.append(jnp.transpose(jnp.broadcast_to(delta, (rows, LANES)))[0:1, :])
                qs.append(query[here, cols])
                gs.append(both.astype(jnp.bfloat16))
            queries.append(jnp.concatenate(qs, axis=0))
            grads.append(jnp.concatenate(gs, axis=0))
            deltas.append(jnp.concatenate(ds, axis=1))
        dqt[...] = jnp.zeros_like(dqt)

        @pl.loop(first_of(ends, first_tok) // step, (first_tok + rows + step - 1) // step)
        def _(tile):
            base = tile * step
            there = pl.ds(pl.multiple_of(base, step), step)
            allowed = (upper <= -base) & (lower >= -base)
            allowed = jnp.concatenate([allowed] * per, axis=1)
            for g in range(groups):
                cols = slice(g * LANES, (g + 1) * LANES)
                value_cols = slice(kv_width + g * LANES, kv_width + (g + 1) * LANES)
                scores = dot_nt(kv[there, cols], queries[g])
                probs = jnp.where(allowed, jnp.exp2(scores * (scale * LOG2E)), 0.0)
                dprobs = dot_nt(kv[there, value_cols], grads[g])
                dscores = (probs * (dprobs - deltas[g])).astype(jnp.bfloat16)
                dv_acc[there, cols] += dot_nn(probs.astype(jnp.bfloat16), grads[g])
                dk_acc[there, cols] += dot_nn(dscores, queries[g])
                dqt[g] += dot_nn(keyt[cols, there], dscores)

        for g in range(groups):
            for j in range(per):
                cols = slice((g * per + j) * LANES, (g * per + j + 1) * LANES)
                dq[here, cols] = jnp.transpose(dqt[g, :, j * rows : (j + 1) * rows]) * scale

        @pl.loop(0, wide_count)
        def _(target):
            source = pl.ds(pl.multiple_of((blk * wide_count + target) * rows, rows), rows)
            parts[target, here, :kv_width] = (dk_acc[source, :] * scale).astype(jnp.bfloat16)
            parts[target, here, kv_width:] = dv_acc[source, :].astype(jnp.bfloat16)

        start_all(out_copies(blk))

    for blk in range(blocks):
        for copy in out_copies(blk):
            copy.wait()


def attention_backward(
    doc_lengths, query_low, attended, inverse, gate_pre, kv_all, back_rows, out_w
):
    rows, width = query_low.shape
    keys, kv_width = kv_all.shape[0], kv_all.shape[1] // 2
    groups = kv_width // LANES
    per = width // kv_width
    blocks, wide_count = lax.axis_size("head"), lax.axis_size("wide")
    low, full = jnp.bfloat16, jnp.float32
    shape, vm = jax.ShapeDtypeStruct, pltpu.VMEM
    return pl.pallas_call(
        attention_backward_kernel,
        out_shape=(
            shape((rows, width), full),
            shape((wide_count, rows, 2 * kv_width), low),
            shape((rows, width), low),
        ),
        in_specs=[pl.BlockSpec(memory_space=pltpu.SMEM)] + [ANY] * 7,
        out_specs=(ANY, ANY, ANY),
        scratch_shapes=[
            vm((rows, width), low), vm((rows, width), full), vm((rows, width), full),
            vm((rows, width), full), vm(kv_all.shape, low), vm(back_rows.shape, low),
            vm(out_w.shape, low), vm((rows, width), full),
            vm((wide_count, rows, 2 * kv_width), low), vm((rows, width), low),
            vm((keys, kv_width), full), vm((keys, kv_width), full),
            vm((groups, LANES, per * (rows // blocks)), full), vm((kv_width, keys), low),
            vm((rows, width), full),
            DMA((7,)), DMA((3, blocks)),
        ],
        compiler_params=pltpu.CompilerParams(vmem_limit_bytes=VMEM_LIMIT),
        cost_estimate=pl.CostEstimate(
            flops=10 * rows * width * 2048, bytes_accessed=20 << 20, transcendentals=0
        ),
        name="attention_backward",
    )(
        doc_lengths, query_low, attended, inverse, gate_pre, kv_all, back_rows, out_w
    )


def ffn_kernel(
    gated_ref, gain_ref, x_any, cot_any, left_any, wo_any, wg_any, wu_any, wd_any,
    out_any, mgrad_ref, gain_out, back_any, down_any, fgate_any, fup_any, owg_any,
    wo, wg, wu, wd, cots, rows, hid, gg, ug, terms_own, outs_own, passed, into,
    passed2, into2, dterms, dinto, stage, hterms, hinto, middle, back, local_sem,
    ds, dr, hs, hr, cs, cr, cps, cpr, fs, fr, fps, fpr, s1, r1, ps1, pr1, s2, r2, ps2, pr2, bs, br,
):
    tok, width = x_any.shape
    hidden_width = wg_any.shape[1]
    head, wide = head_ring(), wide_ring()
    pair = 2 * tok
    separate = terms_own.shape[0] > 16
    terms = terms_own if separate else cots
    outs = outs_own if separate else rows
    part = wo_any.shape[1] // lax.axis_size("head")
    loads = [
        pltpu.make_async_copy(src, dst, local_sem.at[i])
        for i, (src, dst) in enumerate(((wo_any, wo), (wd_any, wd), (wg_any, wg), (wu_any, wu)))
    ]
    split = left_any.shape[1]
    loads.append(pltpu.make_async_copy(left_any, cots.at[:, pl.ds(0, split)], local_sem.at[10]))
    for load in loads:
        load.start()
    own_wide = pl.multiple_of(lax.axis_index("wide") * tok, tok)
    own_head = pl.multiple_of(lax.axis_index("head") * tok, tok)
    own_loads = [
        pltpu.make_async_copy(
            cot_any.at[:, pl.ds(split, width - split)],
            cots.at[pl.ds(own_wide, tok), pl.ds(split, width - split)],
            local_sem.at[12],
        ),
        pltpu.make_async_copy(x_any, back.at[pl.ds(own_head, tok)], local_sem.at[13]),
    ]
    start_all(own_loads)
    own_loads[0].wait()
    meet(neighbours(head, wide))

    def slot_of(ref):
        return lambda index, start, size: ref.at[pl.ds(index * tok + start, size)]

    def cot_slot(index, start, size):
        return cots.at[pl.ds(index * tok + start, size), pl.ds(split, width - split)]

    cot_gather = PairGather(wide, cot_slot, tok, cs, cr, cps, cpr)
    row_gather = row_gather_of(wide)(wide, slot_of(rows), tok, fs, fr, fps, fpr)
    back_gather = Gather(head, slot_of(back), tok, bs, br)
    head_scatter = Scatter(head, lambda index: (hterms, index * tok), tok, hinto, hs, hr)
    grad_scatter = scatter_of(wide)(wide, terms, tok, passed, into, s1, r1, ps1, pr1)
    down_scatter = Scatter(
        head, lambda index: (dterms, index * hidden_width), hidden_width, dinto, ds, dr
    )
    out_scatter = scatter_of(wide)(wide, outs, tok, passed2, into2, s2, r2, ps2, pr2)

    def group_of(offset):
        return pl.ds(pl.multiple_of(wide.index(offset) * pair, pair), pair)

    def col_loop(total, step, body):
        @pl.loop(0, total // step)
        def _(i):
            body(pl.ds(pl.multiple_of(i * step, step), step))

    tile = 256
    line = wide.size == 4
    cot_gather.begin()

    def out_part(offset, own):
        index = head.index(offset)
        here = pl.ds(pl.multiple_of(index * tok, tok), tok)

        def body(cols):
            value = dot_nn(gated_ref[here, :], wo[:, cols])
            if own:
                middle[:, cols] = back[pl.ds(own_head, tok), cols].astype(jnp.float32) + value
            else:
                hterms[here, cols] = value.astype(jnp.bfloat16)

        col_loop(width, tile, body)

    def hidden_part(offset):
        here = group_of(offset)

        def body(cols):
            hid[here, cols] = dot_nt(cots[here, :], wd[cols, :]).astype(jnp.bfloat16)

        col_loop(hidden_width, hidden_width, body)

    loads[0].wait()
    own_loads[1].wait()
    out_part(head.half, False)
    head_scatter.start(head.half)
    for hop in range(head.half - 1, 0, -1):
        out_part(hop, False)
        out_part(-hop, False)
    out_part(0, True)
    loads[1].wait()
    loads[4].wait()
    mgrad_ref[...] = cots[pl.ds(own_wide, tok), :].astype(jnp.float32)
    cot_gather.take(0)
    hidden_part(0)
    for hop in range(head.half - 1, 0, -1):
        head_scatter.advance(hop)
    for hop in range(1, wide.half):
        cot_gather.arrive(hop)
        cot_gather.start(hop + 1)
        cot_gather.hand(hop)
        cot_gather.take(hop)
        hidden_part(hop)
        hidden_part(-hop)
    head_scatter.arrive()

    gain = gain_ref[...]

    def forward_norm(row):
        here = pl.ds(row, 32)
        value = (
            middle[here, :]
            + hinto[0, here, :].astype(jnp.float32)
            + hinto[1, here, :].astype(jnp.float32)
        )
        middle[here, :] = value
        scale = lax.rsqrt(jnp.mean(value * value, axis=-1, keepdims=True) + EPS)
        rows[pl.ds(pl.multiple_of(own_wide + row, 32), 32), :] = (value * scale * gain).astype(
            jnp.bfloat16
        )

    row_loop(tok, 32, forward_norm)
    row_gather.begin()
    cot_gather.arrive(wide.half)
    cot_gather.hand(wide.half)
    cot_gather.take(wide.half)
    hidden_part(wide.half)
    cot_gather.finish()
    loads[2].wait()
    loads[3].wait()

    def unit(offset):
        here = group_of(offset)

        def body(cols):
            gate = dot_nn(rows[here, :], wg[:, cols])
            up = dot_nn(rows[here, :], wu[:, cols])
            grad = hid[here, cols].astype(jnp.float32)
            sig = jax.nn.sigmoid(gate)
            act = gate * sig
            hid[here, cols] = (act * up).astype(jnp.bfloat16)
            gg[here, cols] = (grad * up * (sig + act * (1.0 - sig))).astype(jnp.bfloat16)
            ug[here, cols] = (grad * act).astype(jnp.bfloat16)

        col_loop(hidden_width, tile if hidden_width % tile == 0 else LANES, body)

    def down_terms(offset):
        here = group_of(offset)

        def body(cols):
            outs[here, cols] = dot_nn(hid[here, :], wd[:, cols]).astype(jnp.bfloat16)

        col_loop(width, width, body)
        if not line:
            out_scatter.hand(offset)

    def down_grads(group, add):
        @pl.loop(0, lax.axis_size("head"))
        def _(index):
            cols = pl.ds(pl.multiple_of(index * part, part), part)
            there = pl.ds(pl.multiple_of(index * hidden_width, LANES), hidden_width)
            value = sum(
                dot_tn(hid[group_of(offset), :], cots[group_of(offset), cols]) for offset in group
            )
            if add:
                value += dterms[there, :].astype(jnp.float32)
            dterms[there, :] = value.astype(jnp.bfloat16)

    def grad_terms(offset):
        here = group_of(offset)

        def body(cols):
            value = dot_nt(gg[here, :], wg[cols, :]) + dot_nt(ug[here, :], wu[cols, :])
            terms[here, cols] = value.astype(jnp.bfloat16)

        col_loop(width, 1024, body)

    emit = stage.shape[2]

    def stage_copy(step, out, any_ref, slot):
        there = pl.ds(pl.multiple_of(step * emit, emit), emit)
        return pltpu.make_async_copy(
            stage.at[slot, out], any_ref.at[there], local_sem.at[5 + 2 * slot + out]
        )

    def input_grads():
        @pl.loop(0, width // emit // 2)
        def _(i):
            for slot in SIDES:
                step = 2 * i + slot
                cols = pl.ds(pl.multiple_of(step * emit, emit), emit)

                @pl.when(i > 0)
                def _():
                    for out, any_ref in enumerate((fgate_any, fup_any)):
                        stage_copy(step - 2, out, any_ref, slot).wait()

                left = rows[:, cols]
                stage[slot, 0] = dot_tn(left, gg[...]).astype(jnp.bfloat16)
                stage[slot, 1] = dot_tn(left, ug[...]).astype(jnp.bfloat16)
                for out, any_ref in enumerate((fgate_any, fup_any)):
                    stage_copy(step, out, any_ref, slot).start()

    order = offsets(wide)

    def near_part(offset):
        unit(offset)
        if separate:
            down_terms(offset)

    def down_pass(kind):
        offset = out_scatter.offset(kind)
        down_terms(offset)
        out_scatter.hand_kind(kind)

    if line:

        def arrived(kind):
            row_gather.arrive(kind)
            row_gather.take(kind)
            unit(row_gather.offset(kind))
            grad_terms(grad_scatter.offset(kind))
            grad_scatter.hand_kind(kind)

        row_gather.take(None)
        unit(0)
        down_pass(None)
        down_grads([0], False)
        arrived(NEAR)
        down_pass(NEAR)
        grad_scatter.merge_kind(NEAR)
        grad_scatter.launch(NEAR)

        @pl.when(row_gather.middle)
        def _():
            arrived(OTHER)
            down_pass(OTHER)
            grad_scatter.merge_kind(OTHER)

        arrived(FAR)
        grad_scatter.merge_kind(FAR)
        grad_scatter.launch(FAR)

        @pl.when(~row_gather.middle)
        def _():
            arrived(OTHER)
            grad_scatter.merge_kind(OTHER)

        grad_scatter.launch(OTHER)
        pl.when(~row_gather.middle)(functools.partial(down_pass, OTHER))
        down_pass(FAR)
        grad_terms(0)
        grad_scatter.hand_kind(None)
        down_grads([1, 2, 3], True)
        down_scatter.start(head.half)
        grad_scatter.relay(OTHER)
        for kind in (OTHER, FAR, NEAR, None):
            out_scatter.merge_kind(kind)
        input_grads()
        out_scatter.launch(OTHER, FAR, NEAR)
        grad_scatter.merge_kind(None)
        grad_scatter.relay(FAR)
        grad_scatter.relay(NEAR)
    else:
        row_gather.take(0)
        near_part(0)
        if separate:
            down_grads([0], False)
        for hop in range(1, wide.half):
            row_gather.arrive(hop)
            row_gather.start(hop + 1)
            row_gather.hand(hop)
            row_gather.take(hop)
            near_part(hop)
            near_part(-hop)
        row_gather.arrive(wide.half)
        row_gather.hand(wide.half)
        row_gather.take(wide.half)
        unit(wide.half)
        if not separate:
            down_grads(order, False)
            down_scatter.start(head.half)
        for offset in order:
            grad_terms(offset)
            grad_scatter.hand(offset)
        grad_scatter.merge(order[0])
        grad_scatter.start(wide.half)
        if separate:
            down_grads(order[:-1], True)
            down_scatter.start(head.half)
            down_terms(order[0])
        for hop in range(wide.half - 1, 0, -1):
            grad_scatter.merge(hop)
            grad_scatter.merge(-hop)
            grad_scatter.advance(hop)
        grad_scatter.merge(0)
        input_grads()
    row_gather.finish()
    if not line:
        if not separate:
            for offset in order:
                down_terms(offset)
        out_scatter.merge(order[0])
    for hop in range(head.half - 1, 0, -1):
        down_scatter.advance(hop)
    grad_scatter.arrive()

    def backward_norm(row, gain_sum):
        here = pl.ds(row, 32)
        value = middle[here, :]
        grad = grad_scatter.total(row, 32)
        scale = lax.rsqrt(jnp.mean(value * value, axis=-1, keepdims=True) + EPS)
        scaled = value * scale
        weighted = grad * gain
        mean = jnp.mean(scaled * weighted, axis=-1, keepdims=True)
        total = mgrad_ref[here, :] + scale * (weighted - scaled * mean)
        mgrad_ref[here, :] = total
        back[pl.ds(pl.multiple_of(own_head + row, 32), 32), :] = total.astype(jnp.bfloat16)
        return gain_sum + jnp.sum(grad * scaled, axis=0, keepdims=True)

    gain_out[...] = lax.fori_loop(
        0, tok // 32,
        lambda i, carried: backward_norm(pl.multiple_of(i * 32, 32), carried),
        jnp.zeros((1, width), jnp.float32),
    )
    back_gather.start(1)
    if line:
        for kind in (FAR, OTHER, NEAR):
            out_scatter.relay(kind)
    else:
        out_scatter.start(wide.half)
        for offset in order[1:]:
            out_scatter.merge(offset)
        for hop in range(wide.half - 1, 0, -1):
            out_scatter.advance(hop)
    for hop in range(1, head.half):
        back_gather.arrive(hop)
        back_gather.start(hop + 1)
    back_gather.arrive(head.half)
    back_gather.finish()
    keep = pltpu.make_async_copy(back, back_any, local_sem.at[4])
    keep.start()
    head_scatter.finish()
    owners = gated_ref.shape[1]

    def out_grads(cols):
        hterms[pl.ds(0, owners), cols] = dot_tn(gated_ref[...], back[:, cols]).astype(jnp.bfloat16)

    col_loop(width, 512, out_grads)
    share = pltpu.make_async_copy(hterms.at[pl.ds(0, owners)], owg_any, local_sem.at[11])
    share.start()
    out_scatter.arrive()

    def finish_out(row):
        here = pl.ds(row, 32)
        back[here, :] = (middle[here, :] + out_scatter.total(row, 32)).astype(jnp.bfloat16)

    keep.wait()
    row_loop(tok, 32, finish_out)
    result = pltpu.make_async_copy(back.at[pl.ds(0, tok)], out_any, local_sem.at[9])
    result.start()
    down_scatter.arrive()

    pending = {}
    places = width // part
    for step in range(hidden_width // LANES):
        place = step % places
        if place in pending:
            pending[place].wait()
        spot = middle.at[:, place * part : (place + 1) * part]
        middle[:, place * part : (place + 1) * part] = down_scatter.total(step * LANES, LANES)
        pending[place] = pltpu.make_async_copy(
            spot, down_any.at[pl.ds(step * LANES, LANES)], local_sem.at[14 + place % 4]
        )
        pending[place].start()
    for scatter in (grad_scatter, out_scatter, down_scatter):
        scatter.finish()
    last = width // emit
    for slot in SIDES:
        for out, any_ref in enumerate((fgate_any, fup_any)):
            stage_copy(last - 2 + slot, out, any_ref, slot).wait()
    result.wait()
    share.wait()
    for copy in pending.values():
        copy.wait()


def ffn_block(gated_low, inputs, cotangent, cot_left, ffn_gain, out_w, gate_w, up_w, down_w):
    tok, width = inputs.shape
    head_count, wide_count = lax.axis_size("head"), lax.axis_size("wide")
    chips = wide_count // 2
    hidden_width = gate_w.shape[1]
    low, full = jnp.bfloat16, jnp.float32
    all_rows = wide_count * tok
    back_rows = head_count * tok
    roomy = all_rows * width <= 2 << 20
    shape = jax.ShapeDtypeStruct
    vm = pltpu.VMEM
    return pl.pallas_call(
        ffn_kernel,
        out_shape=(
            shape((tok, width), low),
            shape((tok, width), full),
            shape((1, width), full),
            shape((back_rows, width), low),
            shape((hidden_width, width // head_count), full),
            shape((width, hidden_width), low),
            shape((width, hidden_width), low),
            shape((gated_low.shape[1], width), low),
        ),
        in_specs=[VMEM] * 2 + [ANY] * 7,
        out_specs=(ANY, VMEM, VMEM, ANY, ANY, ANY, ANY, ANY),
        scratch_shapes=[
            vm(out_w.shape, low), vm(gate_w.shape, low), vm(up_w.shape, low),
            vm(down_w.shape, low),
            vm((all_rows, width), low), vm((all_rows, width), low),
            vm((all_rows, hidden_width), low), vm((all_rows, hidden_width), low),
            vm((all_rows, hidden_width), low),
            vm((all_rows if roomy else 16, width), low),
            vm((all_rows if roomy else 16, width), low),
            vm((chips, tok, width), low),
            scatter_into(chips, tok, width),
            vm((chips, tok, width), low),
            scatter_into(chips, tok, width),
            vm((head_count * hidden_width, width // head_count), low),
            into_shape(head_count, hidden_width, width // head_count),
            vm((2, 2, 128, hidden_width), low),
            vm((back_rows, width), low), into_shape(head_count, tok, width),
            vm((tok, width), full), vm((back_rows, width), low),
            DMA((18,)),
            *ring_sems(head_count),
            *ring_sems(head_count),
            *ring_sems(chips), *pass_sems(chips),
            *gather_sems(chips),
            *scatter_sems(chips),
            *scatter_sems(chips),
            *ring_sems(head_count),
        ],
        compiler_params=pltpu.CompilerParams(
            collective_id=1, has_side_effects=True, vmem_limit_bytes=VMEM_LIMIT
        ),
        cost_estimate=pl.CostEstimate(
            flops=10 * all_rows * width * hidden_width, bytes_accessed=200 << 20, transcendentals=0
        ),
        name="ffn_block",
    )(
        gated_low, ffn_gain[None], inputs, cotangent, cot_left, out_w, gate_w, up_w, down_w
    )


def turn(values, cosine, sine_tab):
    half = LANES // 2
    lane = lax.broadcasted_iota(jnp.int32, values.shape, 1)
    turned = pltpu.roll(values, half, 1)
    return values * cosine + jnp.where(lane < half, -turned, turned) * sine_tab


def prep(pre_proj, gain, cosine, sine_tab):
    scale = lax.rsqrt(jnp.mean(pre_proj * pre_proj, axis=-1, keepdims=True) + EPS)
    return turn(pre_proj * scale * gain, cosine, sine_tab).astype(jnp.bfloat16)


def front_kernel(
    x_ref, gain_ref, cos_ref, sin_ref, qgain_ref, kgain_ref, wq_any, wk_any, wv_any, wg_any,
    query_ref, qpre_ref, kpre_ref, gpre_ref, normed_any, kv_any,
    wq, wk, wv, wg, normed, kv, local_sem, hs, hr, ks, kr, kps, kpr,
):
    tok, width = x_ref.shape
    kv_width = wk_any.shape[1]
    q_width = wq_any.shape[1]
    wide_count, head_count = lax.axis_size("wide"), lax.axis_size("head")
    head, wide = head_ring(), wide_ring()
    loads = [
        pltpu.make_async_copy(src, dst, local_sem.at[i])
        for i, (src, dst) in enumerate(((wk_any, wk), (wv_any, wv), (wq_any, wq), (wg_any, wg)))
    ]
    for load in loads:
        load.start()
    own = pl.multiple_of(lax.axis_index("head") * tok, tok)
    own_wide = lax.axis_index("wide")

    def norm(row):
        here = pl.ds(row, 32)
        value = x_ref[here, :].astype(jnp.float32)
        scale = lax.rsqrt(jnp.mean(value * value, axis=-1, keepdims=True) + EPS)
        normed[pl.ds(pl.multiple_of(own + row, 32), 32), :] = (
            value * scale * gain_ref[...]
        ).astype(jnp.bfloat16)

    row_loop(tok, 32, norm)
    meet(neighbours(head, wide))
    gather = Gather(
        head, lambda index, start, size: normed.at[pl.ds(index * tok + start, size)], tok, hs, hr
    )
    gather.start(1)

    def kv_gather(offset):
        slot = offset % head_count
        block = head.index(offset)

        def place(index, start, size):
            return kv.at[pl.ds((block * wide_count + index) * tok + start, size)]

        return row_gather_of(wide)(
            wide, place, tok, ks.at[slot], kr.at[slot], kps.at[slot], kpr.at[slot]
        )

    def project(offset):
        block = head.index(offset)
        here = pl.ds(pl.multiple_of(block * tok, tok), tok)
        there = pl.ds(pl.multiple_of((block * wide_count + own_wide) * tok, tok), tok)
        left = normed[here, :]
        cosine, sine_tab = cos_ref[here, :], sin_ref[here, :]
        pre = dot_nn(left, wk[...])
        kpre_ref[here, :] = pre
        for j in range(kv_width // LANES):
            cols = slice(j * LANES, (j + 1) * LANES)
            kv[there, cols] = prep(pre[:, cols], kgain_ref[...], cosine, sine_tab)
        kv[there, kv_width:] = dot_nn(left, wv[...]).astype(jnp.bfloat16)

    def project_rest(offset):
        block = head.index(offset)
        here = pl.ds(pl.multiple_of(block * tok, tok), tok)
        left = normed[here, :]
        cosine, sine_tab = cos_ref[here, :], sin_ref[here, :]
        pre = dot_nn(left, wq[...])
        qpre_ref[here, :] = pre
        for j in range(q_width // LANES):
            cols = slice(j * LANES, (j + 1) * LANES)
            query_ref[here, cols] = prep(pre[:, cols], qgain_ref[...], cosine, sine_tab)
        gpre_ref[here, :] = dot_nn(left, wg[...])

    gathers = {}

    def launch(offset):
        project(offset)
        gathers[offset] = kv_gather(offset)
        gathers[offset].begin()

    line = wide.size == 4

    def step(offset, hop):
        each = gathers[offset]
        if line and hop == 1:
            each.arrive(NEAR)

            @pl.when(each.middle)
            def _():
                each.arrive(OTHER)

        elif line:
            each.arrive(FAR)

            @pl.when(~each.middle)
            def _():
                each.arrive(OTHER)

        else:
            each.arrive(hop)
            if hop < wide.half:
                each.start(hop + 1)
            each.hand(hop)

    loads[0].wait()
    loads[1].wait()
    launch(0)
    loads[2].wait()
    loads[3].wait()
    project_rest(0)
    done = [0]
    for hop in range(1, head.half + 1):
        gather.arrive(hop)
        if hop < head.half:
            gather.start(hop + 1)
            launch(hop)
            launch(-hop)
            for offset in done:
                step(offset, 1)
            project_rest(hop)
            project_rest(-hop)
            done = [hop, -hop]
        else:
            launch(hop)
            for offset in done:
                step(offset, 1)
            project_rest(hop)
            done = [hop]
    gather.finish()
    keep = pltpu.make_async_copy(normed, normed_any, local_sem.at[4])
    keep.start()
    for offset in done:
        step(offset, 1)
    for hop in range(2, wide.half + 1):
        for offset in gathers:
            step(offset, hop)
    for each in gathers.values():
        for hop in (None, NEAR, OTHER, FAR) if line else range(wide.half + 1):
            each.take(hop)
    store = pltpu.make_async_copy(kv, kv_any, local_sem.at[5])
    store.start()
    for each in gathers.values():
        each.finish()
    store.wait()
    keep.wait()


def front_block(inputs, attn_gain, cosine, sine_tab, query_gain, key_gain, weights):
    tok, width = inputs.shape
    head_count, wide_count = lax.axis_size("head"), lax.axis_size("wide")
    chips = wide_count // 2
    q_width, kv_width = weights[0].shape[1], weights[1].shape[1]
    rows = head_count * tok
    low, full = jnp.bfloat16, jnp.float32
    shape, vm = jax.ShapeDtypeStruct, pltpu.VMEM
    return pl.pallas_call(
        front_kernel,
        out_shape=(
            shape((rows, q_width), low),
            shape((rows, q_width), full),
            shape((rows, kv_width), full),
            shape((rows, q_width), full),
            shape((rows, width), low),
            shape((rows * wide_count, 2 * kv_width), low),
        ),
        in_specs=[VMEM] * 6 + [ANY] * 4,
        out_specs=tuple([VMEM] * 4 + [ANY] * 2),
        scratch_shapes=[
            *[vm(weight.shape, low) for weight in weights],
            vm((rows, width), low),
            vm((rows * wide_count, 2 * kv_width), low),
            DMA((6,)),
            *ring_sems(head_count),
            *[DMA((head_count, *sem.shape)) for sem in gather_sems(chips)],
        ],
        compiler_params=pltpu.CompilerParams(
            collective_id=3, has_side_effects=True, vmem_limit_bytes=VMEM_LIMIT
        ),
        cost_estimate=pl.CostEstimate(
            flops=2 * rows * width * (2 * q_width + 2 * kv_width), bytes_accessed=100 << 20,
            transcendentals=0,
        ),
        name="front_block",
    )(
        inputs, attn_gain[None], cosine, sine_tab, query_gain[None], key_gain[None], *weights
    )


def turn_back(grad, cosine, sine_tab):
    half = LANES // 2
    lane = lax.broadcasted_iota(jnp.int32, grad.shape, 1)
    turned = pltpu.roll(grad * sine_tab, half, 1)
    return grad * cosine + jnp.where(lane < half, turned, -turned)


def unprep(grad, pre_proj, gain, cosine, sine_tab):
    turned = turn_back(grad, cosine, sine_tab)
    scale = lax.rsqrt(jnp.mean(pre_proj * pre_proj, axis=-1, keepdims=True) + EPS)
    scaled = pre_proj * scale
    weighted = turned * gain
    mean = jnp.mean(scaled * weighted, axis=-1, keepdims=True)
    return scale * (weighted - scaled * mean), turned * scaled


def tail_kernel(
    cos_ref, sin_ref, qgain_ref, kgain_ref, gain_ref, ffn_gain_ref,
    dq_any, qpre_any, kpre_any, ggrad_any, x_any, mgrad_any,
    kvp_any, normed_any, wq_any, wk_any, wv_any, wg_any, fgate_any, fup_any,
    igrad_ref, gains_ref, query_out, key_out, value_out, gate_out, fgate_out, fup_out,
    dq_ref, qpre_ref, kpre_ref, ggrad_ref, x_ref, mgrad_ref, kvp, normed, wq, wk, wv, wg, fgate, fup, qlow, klow, vlow, early, late, hterms,
    kv_passed, kv_into, early_passed, early_into, late_passed, late_into, hinto, fgate_into,
    fup_into, gain_slots, stage, local_sem,
    kvs, kvr, kvps, kvpr, es, er, eps, epr, ls, lr, lps, lpr, hs, hr, gs, gr, us, ur, gain_send,
    gain_recv,
):
    tok, width = x_ref.shape
    rows = dq_ref.shape[0]
    wide_count = lax.axis_size("wide")
    head_count = lax.axis_size("head")
    head, wide = head_ring(), wide_ring()
    loads = [
        pltpu.make_async_copy(src, dst, local_sem.at[i])
        for i, (src, dst) in enumerate(
            (
                (kvp_any, kvp), (fgate_any, fgate), (fup_any, fup), (normed_any, normed),
                (wq_any, wq), (wk_any, wk), (wv_any, wv), (wg_any, wg),
            )
        )
    ]
    more = [
        pltpu.make_async_copy(src, dst, local_sem.at[11 + i])
        for i, (src, dst) in enumerate(
            (
                (dq_any, dq_ref), (qpre_any, qpre_ref), (ggrad_any, ggrad_ref),
                (kpre_any, kpre_ref), (x_any, x_ref), (mgrad_any, mgrad_ref),
            )
        )
    ]
    start_all(loads[:1] + more[:3] + loads[1:] + more[3:])
    meet(everyone(head, wide))
    kv_width = wk.shape[1]
    q_width = wq.shape[1]
    block = normed.shape[1] // wide_count
    ffn_rows = fgate.shape[0] // head_count
    kv_scatter = PairScatter(wide, kvp, rows, kv_passed, kv_into, kvs, kvr, kvps, kvpr)
    early_scatter = PairScatter(wide, early, block, early_passed, early_into, es, er, eps, epr)
    late_scatter = PairScatter(wide, late, block, late_passed, late_into, ls, lr, lps, lpr)
    head_scatter = Scatter(head, lambda index: (hterms, index * tok), tok, hinto, hs, hr)
    gate_scatter = Scatter(
        head, lambda index: (fgate, index * ffn_rows), ffn_rows, fgate_into, gs, gr
    )
    up_scatter = Scatter(head, lambda index: (fup, index * ffn_rows), ffn_rows, fup_into, us, ur)
    order = offsets(wide)

    loads[0].wait()
    for offset in order:
        kv_scatter.hand(offset)
    loads[1].wait()
    gate_scatter.start(head.half)
    loads[2].wait()
    up_scatter.start(head.half)

    for load in more[:3]:
        load.wait()
    chunk = 128

    def query_back(row, total):
        here = pl.ds(row, chunk)
        for j in range(q_width // LANES):
            cols = slice(j * LANES, (j + 1) * LANES)
            value, terms = unprep(
                dq_ref[here, cols], qpre_ref[here, cols], qgain_ref[...], cos_ref[here, :],
                sin_ref[here, :],
            )
            qlow[here, cols] = value.astype(jnp.bfloat16)
            total = total + jnp.sum(terms, axis=0, keepdims=True)
        return total

    def over_rows(count, body, start):
        return lax.fori_loop(
            0, count // chunk, lambda i, carried: body(pl.multiple_of(i * chunk, chunk), carried),
            start,
        )

    qgain_sum = over_rows(rows, query_back, jnp.zeros((1, LANES), jnp.float32))

    kv_scatter.merge(order[0])
    kv_scatter.start(wide.half)
    loads[3].wait()

    def early_part(offset):
        index = wide.index(offset)

        @pl.loop(0, 2)
        def _(core):
            target = 2 * index + core
            cols = pl.ds(pl.multiple_of(target * block, block), block)
            there = pl.ds(pl.multiple_of(target * block, block), block)
            left = normed[:, cols]
            early[there, :q_width] = dot_tn(left, qlow[...]).astype(jnp.bfloat16)
            early[there, q_width:] = dot_tn(left, ggrad_ref[...]).astype(jnp.bfloat16)

    for offset in order:
        early_part(offset)
        early_scatter.hand(offset)
    for offset in order[1:]:
        kv_scatter.merge(offset)
    early_scatter.merge(order[0])
    for hop in range(wide.half - 1, 0, -1):
        kv_scatter.advance(hop)
    early_scatter.start(wide.half)
    for offset in order[1:]:
        early_scatter.merge(offset)
    for hop in range(head.half - 1, 0, -1):
        gate_scatter.advance(hop)
        up_scatter.advance(hop)
    for load in loads[4:] + more[3:]:
        load.wait()
    kv_scatter.arrive()

    def key_back(row, total):
        here = pl.ds(row, chunk)
        both = kv_scatter.total(row, chunk)
        for j in range(kv_width // LANES):
            cols = slice(j * LANES, (j + 1) * LANES)
            value, terms = unprep(
                both[:, cols], kpre_ref[here, cols], kgain_ref[...], cos_ref[here, :],
                sin_ref[here, :],
            )
            klow[here, cols] = value.astype(jnp.bfloat16)
            total = total + jnp.sum(terms, axis=0, keepdims=True)
        vlow[here, :] = both[:, kv_width:].astype(jnp.bfloat16)
        return total

    kgain_sum = over_rows(rows, key_back, jnp.zeros((1, LANES), jnp.float32))

    def head_part(offset):
        here = pl.ds(pl.multiple_of(head.index(offset) * tok, tok), tok)

        @pl.loop(0, width // 256)
        def _(i):
            cols = pl.ds(pl.multiple_of(i * 256, 256), 256)
            value = dot_nt(qlow[here, :], wq[cols, :]) + dot_nt(ggrad_ref[here, :], wg[cols, :])
            value += dot_nt(klow[here, :], wk[cols, :]) + dot_nt(vlow[here, :], wv[cols, :])
            hterms[here, cols] = value.astype(jnp.bfloat16)

    head_part(head.half)
    head_scatter.start(head.half)

    def late_part(offset):
        index = wide.index(offset)

        @pl.loop(0, 2)
        def _(core):
            target = 2 * index + core
            cols = pl.ds(pl.multiple_of(target * block, block), block)
            left = normed[:, cols]
            late[cols, :kv_width] = dot_tn(left, klow[...]).astype(jnp.bfloat16)
            late[cols, kv_width:] = dot_tn(left, vlow[...]).astype(jnp.bfloat16)

    for offset in order:
        late_part(offset)
        late_scatter.hand(offset)
    for hop in range(wide.half - 1, 0, -1):
        early_scatter.advance(hop)
    late_scatter.merge(order[0])
    late_scatter.start(wide.half)
    for hop in range(head.half - 1, 0, -1):
        head_part(hop)
        head_part(-hop)
        head_scatter.advance(hop)
    head_part(0)
    for offset in order[1:]:
        late_scatter.merge(offset)
    for hop in range(wide.half - 1, 0, -1):
        late_scatter.advance(hop)

    gate_scatter.arrive()
    up_scatter.arrive()
    emit = 64
    pending = [None, None]
    for step in range(ffn_rows // emit):
        for which, (scatter, out) in enumerate(((gate_scatter, fgate_out), (up_scatter, fup_out))):
            if pending[which] is not None:
                pending[which].wait()
            stage[which] = scatter.total(step * emit, emit)
            pending[which] = pltpu.make_async_copy(
                stage.at[which], out.at[pl.ds(step * emit, emit)], local_sem.at[9 + which]
            )
            pending[which].start()

    head_scatter.arrive()
    gain = gain_ref[...]

    def input_back(row, total):
        here = pl.ds(row, 32)
        value = x_ref[here, :].astype(jnp.float32)
        grad = head_scatter.total(row, 32)
        scale = lax.rsqrt(jnp.mean(value * value, axis=-1, keepdims=True) + EPS)
        scaled = value * scale
        weighted = grad * gain
        mean = jnp.mean(scaled * weighted, axis=-1, keepdims=True)
        igrad_ref[here, :] = mgrad_ref[here, :] + scale * (weighted - scaled * mean)
        return total + jnp.sum(grad * scaled, axis=0, keepdims=True)

    gain_sum = lax.fori_loop(
        0, tok // 32, lambda i, carried: input_back(pl.multiple_of(i * 32, 32), carried),
        jnp.zeros((1, width), jnp.float32),
    )
    chips = wide.size
    pair_slot, chip_slot = 0, 2
    head_slot = 2 + chips
    mine = gain_slots.at[pair_slot]
    mine[...] = jnp.zeros(mine.shape, jnp.float32)
    mine[0:1, :] = gain_sum
    mine[1:2, :] = ffn_gain_ref[...]
    mine[2:3, 0:LANES] = qgain_sum
    mine[3:4, 0:LANES] = kgain_sum
    swap = remote(
        mine, gain_slots.at[1], gain_send.at[0], gain_recv.at[0], wide.sibling
    )
    swap.start()
    swap.wait_recv()

    def spread(ring, own, base, sem):
        here = gain_slots.at[base + own]
        copies = [
            remote(here, here, gain_send.at[sem + d], gain_recv.at[sem + d], ring.device(d))
            for d in range(1, ring.size)
        ]
        for copy in copies:
            copy.start()
        for copy in copies:
            copy.wait_recv()
        return copies

    own_chip = wide.index(0)
    gain_slots[chip_slot + own_chip] = gain_slots[0] + gain_slots[1]
    sent = [swap] + spread(wide, own_chip, chip_slot, 0)
    total = gain_slots[chip_slot]
    for i in range(1, chips):
        total = total + gain_slots[chip_slot + i]
    own_head = lax.axis_index("head")
    gain_slots[head_slot + own_head] = total
    sent += spread(head, own_head, head_slot, chips - 1)
    total = gain_slots[head_slot]
    for i in range(1, head_count):
        total = total + gain_slots[head_slot + i]
    gains_ref[...] = total

    early_scatter.arrive()

    def early_out(row):
        here = pl.ds(row, 32)
        both = early_scatter.total(row, 32)
        query_out[here, :] = both[:, :q_width]
        gate_out[here, :] = both[:, q_width:]

    row_loop(block, 32, early_out)
    late_scatter.arrive()

    def late_out(row):
        here = pl.ds(row, 32)
        both = late_scatter.total(row, 32)
        key_out[here, :] = both[:, :kv_width]
        value_out[here, :] = both[:, kv_width:]

    row_loop(block, 32, late_out)
    for scatter in (
        kv_scatter, early_scatter, late_scatter, head_scatter, gate_scatter, up_scatter
    ):
        scatter.finish()
    for copy in sent:
        copy.wait_send()
    for copy in pending:
        copy.wait()


def tail_block(
    dq, kv_parts, query_pre, key_pre, gate_grad, cosine, sine_tab, query_gain, key_gain, inputs,
    middle_grad, attn_gain, ffn_gain_part, normed, weights, fgate, fup,
):
    tok, width = inputs.shape
    head_count, wide_count = lax.axis_size("head"), lax.axis_size("wide")
    chips = wide_count // 2
    rows, q_width = dq.shape
    kv_width = key_pre.shape[1]
    block = width // wide_count
    hidden_width = fgate.shape[1]
    ffn_rows = width // head_count
    low, full = jnp.bfloat16, jnp.float32
    shape, vm = jax.ShapeDtypeStruct, pltpu.VMEM
    early_width = 2 * q_width
    pair = [*ring_sems(chips), DMA((chips,)), DMA((chips,))]
    peers = chips + head_count
    return pl.pallas_call(
        tail_kernel,
        out_shape=(
            shape((tok, width), full),
            shape((8, width), full),
            shape((block, q_width), full),
            shape((block, kv_width), full),
            shape((block, kv_width), full),
            shape((block, q_width), full),
            shape((ffn_rows, hidden_width), full),
            shape((ffn_rows, hidden_width), full),
        ),
        in_specs=[VMEM] * 6 + [ANY] * 14,
        out_specs=tuple([VMEM] * 6 + [ANY] * 2),
        scratch_shapes=[
            vm(dq.shape, full), vm(query_pre.shape, full), vm(key_pre.shape, full),
            vm(gate_grad.shape, low), vm(inputs.shape, low), vm(middle_grad.shape, full),
            vm(kv_parts.shape, low), vm(normed.shape, low),
            *[vm(weight.shape, low) for weight in weights],
            vm(fgate.shape, low), vm(fup.shape, low),
            vm((rows, q_width), low), vm((rows, kv_width), low), vm((rows, kv_width), low),
            vm((width, early_width), low), vm((width, 2 * kv_width), low),
            vm((head_count * tok, width), low),
            vm((chips, rows, 2 * kv_width), low), into_shape(chips, rows, 2 * kv_width),
            vm((chips, block, early_width), low), into_shape(chips, block, early_width),
            vm((chips, block, 2 * kv_width), low), into_shape(chips, block, 2 * kv_width),
            into_shape(head_count, tok, width),
            into_shape(head_count, ffn_rows, hidden_width),
            into_shape(head_count, ffn_rows, hidden_width),
            vm((2 + chips + head_count, 8, width), full),
            vm((2, 64, hidden_width), full),
            DMA((17,)),
            *pair, *pair, *pair,
            *ring_sems(head_count), *ring_sems(head_count), *ring_sems(head_count),
            DMA((peers,)), DMA((peers,)),
        ],
        compiler_params=pltpu.CompilerParams(
            collective_id=2, has_side_effects=True, vmem_limit_bytes=VMEM_LIMIT
        ),
        cost_estimate=pl.CostEstimate(
            flops=20 * rows * width * q_width, bytes_accessed=300 << 20, transcendentals=0
        ),
        name="tail_block",
    )(
        cosine, sine_tab, query_gain[None], key_gain[None], attn_gain[None], ffn_gain_part,
        dq, query_pre, key_pre, gate_grad, inputs, middle_grad,
        kv_parts, normed, *weights, fgate, fup,
    )


def shards(
    inputs,
    attn_gain,
    query_weight,
    key_projection,
    value_projection,
    attn_gate_weight,
    output_weight,
    query_gain,
    key_gain,
    ffn_gain,
    ffn_gate_weight,
    ffn_up_weight,
    ffn_down_weight,
    doc_lengths,
    cotangent,
):
    tok_dev = inputs.shape[0]
    head_width = query_gain.shape[0]
    head_count = lax.axis_size("head")
    wide_count = lax.axis_size("wide")
    query_rows = tok_dev * head_count
    wide_pos = lax.axis_index("wide")
    local_ids = jnp.arange(query_rows, dtype=jnp.int32)
    query_tok = (local_ids // tok_dev * wide_count + wide_pos) * tok_dev + local_ids % tok_dev
    query_pos = token_position(doc_lengths, query_tok)
    cosine, sine_tab = rotary(query_pos, head_width)
    cot_left = lax.all_gather(
        cotangent[:, : cotangent.shape[1] // 4], "wide", axis=0, tiled=True
    )
    weights = (query_weight, key_projection, value_projection, attn_gate_weight)
    query_low, query_pre, key_pre, gate_pre, gathered, kv_all = front_block(
        inputs, attn_gain, cosine, sine_tab, query_gain, key_gain, weights
    )
    attended, inverse, gated_low = attention_forward(doc_lengths, query_low, kv_all, gate_pre)
    (
        outputs,
        middle_grad,
        ffn_gain_part,
        back_rows,
        ffn_down_grad,
        gate_wgrad,
        up_wgrad,
        out_wgrad,
    ) = ffn_block(
        gated_low,
        inputs,
        cotangent,
        cot_left,
        ffn_gain,
        output_weight,
        ffn_gate_weight,
        ffn_up_weight,
        ffn_down_weight,
    )
    output_grad = lax.psum_scatter(
        out_wgrad, "wide", scatter_dimension=1, tiled=True
    ).astype(jnp.float32)
    query_rot_grad, kv_parts, gate_pre_grad = attention_backward(
        doc_lengths, query_low, attended, inverse, gate_pre, kv_all, back_rows, output_weight
    )
    kv_parts = kv_parts.reshape(-1, kv_parts.shape[2])
    (
        input_grad,
        gains,
        query_grad,
        key_grad,
        value_grad,
        attn_gate_grad,
        ffn_gate_grad,
        ffn_up_grad,
    ) = tail_block(
        query_rot_grad,
        kv_parts,
        query_pre,
        key_pre,
        gate_pre_grad,
        cosine,
        sine_tab,
        query_gain,
        key_gain,
        inputs,
        middle_grad,
        attn_gain,
        ffn_gain_part,
        gathered,
        weights,
        gate_wgrad,
        up_wgrad,
    )
    attn_gain_grad, ffn_gain_grad = gains[0], gains[1]
    query_gain_grad, key_gain_grad = gains[2, :head_width], gains[3, :head_width]
    return (
        outputs,
        input_grad,
        attn_gain_grad,
        query_grad,
        key_grad,
        value_grad,
        attn_gate_grad,
        output_grad,
        query_gain_grad,
        key_gain_grad,
        ffn_gain_grad,
        ffn_gate_grad,
        ffn_up_grad,
        ffn_down_grad,
    )


def solution(mesh):
    placed = (
        P(("head", "wide"), None),
        P(),
        P(None, "head"),
        P(None, "head"),
        P(None, "head"),
        P(None, "head"),
        P("head", None),
        P(),
        P(),
        P(),
        P(None, "wide"),
        P(None, "wide"),
        P("wide", None),
        P(),
        P(("head", "wide"), None),
    )
    return jax.shard_map(
        shards,
        mesh=mesh,
        in_specs=placed,
        out_specs=(
            P(("head", "wide"), None),
            P(("head", "wide"), None),
            P(),
            P("wide", "head"),
            P("wide", "head"),
            P("wide", "head"),
            P("wide", "head"),
            P("head", "wide"),
            P(),
            P(),
            P(),
            P("head", "wide"),
            P("head", "wide"),
            P("wide", "head"),
        ),
        check_vma=False,
    )
```

```python
import functools

import jax
import jax.numpy as jnp
from jax import lax
from jax.experimental import pallas as pl
from jax.experimental.pallas import tpu as pltpu
from jax.sharding import PartitionSpec as P

EPS = 1e-06
THETA = 1000000.0
VMEM_LIMIT = 63 << 20


def rotation_speed(head_width):
    inverse = THETA ** (-(jnp.arange(head_width // 2, dtype=jnp.float32) * 2.0 / head_width))
    return jnp.concatenate([inverse, inverse])


MESH = pl.DeviceIdType.MESH
ANY = pl.BlockSpec(memory_space=pl.ANY)
VMEM = pl.BlockSpec(memory_space=pltpu.VMEM)
DMA = pltpu.SemaphoreType.DMA
SIDES = (0, 1)


class Ring:
    def __init__(self, size, pos, index, device):
        self.size, self.pos, self.half = size, pos, size // 2
        self._index, self._device = index, device

    def at(self, offset):
        return lax.rem(self.pos + (offset + 2 * self.size), self.size)

    def index(self, offset):
        return self._index(self.at(offset))

    def device(self, offset):
        return self._device(self.at(offset))


def head_ring():
    size = lax.axis_size("head")
    spread = size // 2
    own, wide = lax.axis_index("head"), lax.axis_index("wide")
    major, minor = lax.div(own, 2), lax.rem(own, 2)
    pos = major + minor * (size - 1 - 2 * major)

    def index(place):
        upper = lax.div(place, spread)
        return 2 * (place + upper * (size - 1 - 2 * place)) + upper

    return Ring(size, pos, index, lambda place: (index(place), wide))


def wide_ring():
    size = lax.axis_size("wide") // 2
    head, wide = lax.axis_index("head"), lax.axis_index("wide")
    core = lax.rem(wide, 2)
    ring = Ring(
        size, lax.div(wide, 2), lambda place: place, lambda place: (head, 2 * place + core)
    )
    ring.core = core
    ring.sibling = (head, wide + 1 - 2 * core)
    return ring


def meet(devices):
    barrier = pltpu.get_barrier_semaphore()
    for device in devices:
        pl.semaphore_signal(barrier, inc=1, device_id=device, device_id_type=MESH)
    pl.semaphore_wait(barrier, len(devices))


def neighbours(*rings):
    found = []
    for ring in rings:
        found += [ring.device(1), ring.device(-1)]
        if hasattr(ring, "sibling"):
            found.append(ring.sibling)
    return found


def remote(src, dst, send, recv, device):
    return pltpu.make_async_remote_copy(
        src_ref=src, dst_ref=dst, send_sem=send, recv_sem=recv, device_id=device,
        device_id_type=MESH,
    )


class Gather:
    def __init__(self, ring, slot, rows, send, recv):
        self.ring, self.slot, self.rows = ring, slot, rows
        self.send, self.recv = send, recv

    def span(self, hop, side):
        if 2 * hop == self.ring.size:
            return side * (self.rows // 2), self.rows // 2
        return 0, self.rows

    def copy(self, hop, side):
        way = 1 - 2 * side
        ref = self.slot(self.ring.index(-way * (hop - 1)), *self.span(hop, side))
        return remote(
            ref, ref, self.send.at[side, hop - 1], self.recv.at[side, hop - 1],
            self.ring.device(way),
        )

    def start(self, hop):
        for side in SIDES:
            self.copy(hop, side).start()

    def arrive(self, hop):
        for side in SIDES:
            self.copy(hop, side).wait_recv()

    def finish(self):
        for hop in range(1, self.ring.half + 1):
            for side in SIDES:
                self.copy(hop, side).wait_send()


class PairGather(Gather):
    def __init__(self, ring, slot, rows, send, recv, pass_send, pass_recv):
        core = ring.core
        super().__init__(
            ring, lambda index, start, size: slot(2 * index + core, start, size), rows, send, recv
        )
        self.pass_send, self.pass_recv = pass_send, pass_recv

    def handed(self, hop, side):
        way = 1 - 2 * side
        span = self.span(hop, side) if hop else (0, self.rows)
        ref = self.slot(self.ring.index(-way * hop), *span)
        return remote(
            ref, ref, self.pass_send.at[side, hop], self.pass_recv.at[side, hop],
            self.ring.sibling,
        )

    def hand(self, hop):
        for side in SIDES if hop else (0,):
            self.handed(hop, side).start()

    def take(self, hop):
        for side in SIDES if hop else (0,):
            self.handed(hop, side).wait_recv()

    def begin(self):
        self.start(1)
        self.hand(0)

    def finish(self):
        super().finish()
        for hop in range(self.ring.half + 1):
            for side in SIDES if hop else (0,):
                self.handed(hop, side).wait_send()


def row_loop(rows, chunk, body):
    @pl.loop(0, rows // chunk)
    def _(step):
        body(pl.multiple_of(step * chunk, chunk))


class Scatter:
    def __init__(self, ring, part, rows, into, send, recv):
        self.ring, self.part, self.rows, self.into = ring, part, rows, into
        self.send, self.recv = send, recv

    def span(self, hop, side):
        if 2 * hop == self.ring.size:
            return side * (self.rows // 2), self.rows // 2
        return 0, self.rows

    def copy(self, hop, side):
        way = 1 - 2 * side
        first, count = self.span(hop, side)
        ref, base = self.part(self.ring.index(way * hop))
        return remote(
            ref.at[pl.ds(base + first, count)],
            self.into.at[side, pl.ds((hop - 1) * self.rows + self.inside(hop, first), count)],
            self.send.at[side, hop - 1], self.recv.at[side, hop - 1], self.ring.device(way),
        )

    def inside(self, hop, row):
        return row % (self.rows // 2) if 2 * hop == self.ring.size else row

    def start(self, hop):
        for side in SIDES:
            self.copy(hop, side).start()

    def fold(self, hop, side):
        way = 1 - 2 * side
        self.copy(hop + 1, side).wait_recv()
        first, count = self.span(hop + 1, side)
        ref, base = self.part(self.ring.index(way * hop))
        chunk = min(count, 32)

        def add(row):
            there = pl.ds(pl.multiple_of(base + first + row, chunk), chunk)
            start = hop * self.rows + self.inside(hop + 1, first)
            here = pl.ds(pl.multiple_of(start + row, chunk), chunk)
            ref[there, :] = (
                ref[there, :].astype(jnp.float32) + self.into[side, here, :].astype(jnp.float32)
            ).astype(ref.dtype)

        row_loop(count, chunk, add)

    def advance(self, hop):
        for side in SIDES:
            self.fold(hop, side)
            self.copy(hop, side).start()

    def arrive(self):
        for side in SIDES:
            self.copy(1, side).wait_recv()

    def total(self, row, count):
        ref, base = self.part(self.ring.index(0))
        there = pl.ds(pl.multiple_of(base + row, count), count)
        here = pl.ds(row, count)
        return (
            ref[there, :].astype(jnp.float32)
            + self.into[0, here, :].astype(jnp.float32)
            + self.into[1, here, :].astype(jnp.float32)
        )

    def finish(self):
        for hop in range(1, self.ring.half + 1):
            for side in SIDES:
                self.copy(hop, side).wait_send()


class PairScatter(Scatter):
    def __init__(self, ring, terms, rows, passed, into, send, recv, pass_send, pass_recv):
        core = ring.core
        super().__init__(
            ring, lambda index: (terms, (2 * index + core) * rows), rows, into, send, recv
        )
        self.terms, self.passed = terms, passed
        self.pass_send, self.pass_recv = pass_send, pass_recv

    def handed(self, offset):
        ring = self.ring
        index = ring.index(offset)
        other = pl.multiple_of((2 * index + 1 - ring.core) * self.rows, self.rows)
        slot = offset % ring.size
        return remote(
            self.terms.at[pl.ds(other, self.rows)],
            self.passed.at[slot],
            self.pass_send.at[slot], self.pass_recv.at[slot], ring.sibling,
        )

    def hand(self, offset):
        self.handed(offset).start()

    def merge(self, offset):
        self.handed(offset).wait_recv()
        slot = offset % self.ring.size
        ref, base = self.part(self.ring.index(offset))
        chunk = 32

        def add(row):
            there = pl.ds(pl.multiple_of(base + row, chunk), chunk)
            ref[there, :] = (
                ref[there, :].astype(jnp.float32)
                + self.passed[slot, pl.ds(row, chunk), :].astype(jnp.float32)
            ).astype(ref.dtype)

        row_loop(self.rows, chunk, add)

    def finish(self):
        super().finish()
        for offset in range(self.ring.size):
            self.handed(offset).wait_send()


def offsets(ring):
    order = [ring.half]
    for hop in range(ring.half - 1, 0, -1):
        order += [hop, -hop]
    return order + [0]


def into_shape(size, rows, columns):
    return pltpu.VMEM((2, (size - 1) * rows // 2, columns), jnp.bfloat16)


def everyone(*rings):
    found = []
    for ring in rings:
        found += [ring.device(offset) for offset in range(1, ring.size)]
        if hasattr(ring, "sibling"):
            found.append(ring.sibling)
    return found


def ring_sems(size):
    return [DMA((2, size // 2)), DMA((2, size // 2))]


def pass_sems(size):
    return [DMA((2, size // 2 + 1)), DMA((2, size // 2 + 1))]


NEAR, OTHER, FAR = 0, 1, 2


class LineGather:
    pieces = 2

    def __init__(self, ring, slot, rows, send, recv, pass_send, pass_recv):
        self.ring, self.slot, self.rows = ring, slot, rows // self.pieces
        self.send, self.recv, self.pass_send, self.pass_recv = send, recv, pass_send, pass_recv
        pos = ring.pos
        half, odd = lax.div(pos, 2), lax.rem(pos, 2)
        self.way = 1 - 2 * odd
        self.middle = half + odd == 1

    def offset(self, kind):
        return {NEAR: self.way, OTHER: -self.way, FAR: 2}[kind]

    def ref(self, offset, piece):
        index = 2 * self.ring.index(offset) + self.ring.core
        return self.slot(index, piece * self.rows, self.rows)

    def copy(self, which, offset, kind, piece, way):
        ref = self.ref(offset, piece)
        return remote(
            ref, ref, self.send.at[which, piece], self.recv.at[kind, piece],
            self.ring.device(way),
        )

    def own(self, piece):
        return self.copy(0, 0, NEAR, piece, self.way)

    def own_other(self, piece):
        return self.copy(1, 0, OTHER, piece, -self.way)

    def onward(self, kind, piece):
        arrives = {NEAR: FAR, OTHER: FAR, FAR: OTHER}[kind]
        way = -self.way if kind == NEAR else self.way
        return self.copy(2 + kind, self.offset(kind), arrives, piece, way)

    def incoming(self, kind, piece):
        return self.copy(0, self.offset(kind), kind, piece, self.way)

    def handed(self, kind, piece):
        ref = self.ref(0 if kind is None else self.offset(kind), piece)
        slot = 3 if kind is None else kind
        return remote(
            ref, ref, self.pass_send.at[slot, piece], self.pass_recv.at[slot, piece],
            self.ring.sibling,
        )

    def begin(self):
        for piece in range(self.pieces):
            self.own(piece).start()

            @pl.when(self.middle)
            def _():
                self.own_other(piece).start()

            self.handed(None, piece).start()

    def arrive(self, kind):
        for piece in range(self.pieces):
            self.incoming(kind, piece).wait_recv()

            @pl.when(self.middle)
            def _():
                self.onward(kind, piece).start()

            self.handed(kind, piece).start()

    def take(self, kind):
        for piece in range(self.pieces):
            self.handed(kind, piece).wait_recv()

    def finish(self):
        for piece in range(self.pieces):
            self.own(piece).wait_send()

            @pl.when(self.middle)
            def _():
                self.own_other(piece).wait_send()
                for kind in (NEAR, OTHER, FAR):
                    self.onward(kind, piece).wait_send()

            for kind in (None, NEAR, OTHER, FAR):
                self.handed(kind, piece).wait_send()


class LineScatter(PairScatter):
    pieces = 2

    def __init__(self, *args):
        super().__init__(*args)
        pos = self.ring.pos
        half, odd = lax.div(pos, 2), lax.rem(pos, 2)
        self.way = 1 - 2 * odd
        self.middle = half + odd == 1
        self.waited = set()

    def offset(self, kind):
        return {NEAR: self.way, OTHER: -self.way, FAR: 2, None: 0}[kind]

    def piece_of(self, piece):
        size = self.rows // self.pieces
        return piece * size, size

    def outgoing(self, kind, slot, piece, way):
        first, size = self.piece_of(piece)
        ref, base = self.part(self.ring.index(self.offset(kind)))
        return remote(
            ref.at[pl.ds(pl.multiple_of(base + first, size), size)],
            self.into.at[slot, pl.ds(first, size)],
            self.send.at[kind, piece], self.recv.at[slot, piece], self.ring.device(way),
        )

    def from_end(self, kind, piece):
        return self.outgoing(kind, {OTHER: 0, FAR: 1, NEAR: 2}[kind], piece, self.way)

    def from_middle(self, kind, piece):
        slot = {FAR: 3, OTHER: 4, NEAR: 0}[kind]
        return self.outgoing(kind, slot, piece, self.way if kind == NEAR else -self.way)

    def landed(self, slot, piece):
        first, size = self.piece_of(piece)
        ref = self.into.at[slot, pl.ds(first, size)]
        remote(
            ref, ref, self.send.at[0, piece], self.recv.at[slot, piece], self.ring.device(self.way)
        ).wait_recv()

    def hand_kind(self, kind):
        self.swap(kind).start()

    def swap(self, kind):
        index = self.ring.index(self.offset(kind))
        other = pl.multiple_of((2 * index + 1 - self.ring.core) * self.rows, self.rows)
        slot = 3 if kind is None else kind
        return remote(
            self.terms.at[pl.ds(other, self.rows)], self.passed.at[slot],
            self.pass_send.at[slot], self.pass_recv.at[slot], self.ring.sibling,
        )

    def merge_kind(self, kind):
        self.swap(kind).wait_recv()
        slot = 3 if kind is None else kind
        ref, base = self.part(self.ring.index(self.offset(kind)))

        def add(row):
            there = pl.ds(pl.multiple_of(base + row, 32), 32)
            ref[there, :] = (
                ref[there, :].astype(jnp.float32)
                + self.passed[slot, pl.ds(row, 32), :].astype(jnp.float32)
            ).astype(ref.dtype)

        row_loop(self.rows, 32, add)

    def launch(self, *kinds):
        @pl.when(~self.middle)
        def _():
            for kind in kinds:
                for piece in range(self.pieces):
                    self.from_end(kind, piece).start()

    def sent(self, kind):
        self.waited.add(kind)

        @pl.when(~self.middle)
        def _():
            for piece in range(self.pieces):
                self.from_end(kind, piece).wait_send()

    def relay(self, kind):
        slot = {FAR: 0, OTHER: 1, NEAR: 3}[kind]

        @pl.when(self.middle)
        def _():
            ref, base = self.part(self.ring.index(self.offset(kind)))
            for piece in range(self.pieces):
                first, size = self.piece_of(piece)
                self.landed(slot, piece)

                def add(row):
                    there = pl.ds(pl.multiple_of(base + first + row, 32), 32)
                    here = pl.ds(pl.multiple_of(first + row, 32), 32)
                    ref[there, :] = (
                        ref[there, :].astype(jnp.float32)
                        + self.into[slot, here, :].astype(jnp.float32)
                    ).astype(ref.dtype)

                row_loop(size, 32, add)
                self.from_middle(kind, piece).start()

    def arrive(self):
        @pl.when(self.middle)
        def _():
            for piece in range(self.pieces):
                self.landed(2, piece)
                self.landed(4, piece)

            def add(row):
                here = pl.ds(row, 32)
                self.into[0, here, :] = (
                    self.into[2, here, :].astype(jnp.float32)
                    + self.into[4, here, :].astype(jnp.float32)
                ).astype(self.into.dtype)

            row_loop(self.rows, 32, add)

        @pl.when(~self.middle)
        def _():
            for piece in range(self.pieces):
                self.landed(0, piece)

    def total(self, row, count):
        ref, base = self.part(self.ring.index(0))
        there = pl.ds(pl.multiple_of(base + row, count), count)
        return ref[there, :].astype(jnp.float32) + self.into[0, pl.ds(row, count), :].astype(
            jnp.float32
        )

    def finish(self):
        for piece in range(self.pieces):

            @pl.when(self.middle)
            def _():
                for kind in (NEAR, OTHER, FAR):
                    self.from_middle(kind, piece).wait_send()

            @pl.when(~self.middle)
            def _():
                for kind in (NEAR, OTHER, FAR):
                    if kind not in self.waited:
                        self.from_end(kind, piece).wait_send()

        for kind in (NEAR, OTHER, FAR, None):
            self.swap(kind).wait_send()


def scatter_of(ring):
    return LineScatter if ring.size == 4 else PairScatter


def scatter_into(size, rows, columns):
    if size == 4:
        return pltpu.VMEM((5, rows, columns), jnp.bfloat16)
    return into_shape(size, rows, columns)


def scatter_sems(size):
    passed = [DMA((size,)), DMA((size,))]
    if size == 4:
        pieces = LineScatter.pieces
        return [DMA((3, pieces)), DMA((5, pieces)), *passed]
    return [*ring_sems(size), *passed]


def line_sems():
    pieces = LineGather.pieces
    return [DMA((5, pieces)), DMA((3, pieces)), DMA((4, pieces)), DMA((4, pieces))]


def gather_sems(size):
    return line_sems() if size == 4 else [*ring_sems(size), *pass_sems(size)]


def row_gather_of(ring):
    return LineGather if ring.size == 4 else PairGather


def dot_nn(left, right):
    return jnp.dot(left, right, preferred_element_type=jnp.float32)


def dot_nt(left, right):
    return lax.dot_general(
        left, right, (((1,), (1,)), ((), ())), preferred_element_type=jnp.float32
    )


def dot_tn(left, right):
    return lax.dot_general(
        left, right, (((0,), (0,)), ((), ())), preferred_element_type=jnp.float32
    )


LANES = 128
FORWARD_KEYS = 1024
BACKWARD_KEYS = 512
LOG2E = 1.4426950408889634


def doc_ends(doc_ref):
    ends, total = [], jnp.int32(0)
    for row in range(doc_ref.shape[0]):
        for doc in range(doc_ref.shape[1]):
            total = total + doc_ref[row, doc]
            ends.append(total)
    return ends


def first_of(ends, tokens):
    first = jnp.zeros_like(tokens)
    for end in ends:
        first = jnp.maximum(first, jnp.where(tokens >= end, end, 0))
    return first


def start_all(copies):
    for copy in copies:
        copy.start()


def attention_forward_kernel(
    doc_ref, query_any, kv_any, gate_any, att_any, inv_any, gated_any,
    query, kv, gate, att, inv, gated, acc, kv_sem, in_sem, out_sem,
):
    wide_count = lax.axis_size("wide")
    wide_pos = lax.axis_index("wide")
    kv_width = kv.shape[1] // 2
    groups = kv_width // LANES
    per = query.shape[1] // kv_width
    blocks = kv_sem.shape[0]
    rows = query.shape[0] // blocks
    step = min(FORWARD_KEYS, rows * wide_count)
    factor = LANES ** (-0.5) * LOG2E
    chunk = rows * wide_count

    def kv_copy(blk):
        there = pl.ds(pl.multiple_of(blk * chunk, chunk), chunk)
        return pltpu.make_async_copy(kv_any.at[there], kv.at[there], kv_sem.at[blk])

    early = [
        pltpu.make_async_copy(query_any, query, in_sem.at[0]),
        pltpu.make_async_copy(gate_any, gate, in_sem.at[1]),
    ]
    early[0].start()
    for blk in range(blocks):
        kv_copy(blk).start()
    early[1].start()
    ends = doc_ends(doc_ref)
    early[0].wait()

    def out_copies(blk):
        here = pl.ds(pl.multiple_of(blk * rows, rows), rows)
        return [
            pltpu.make_async_copy(src.at[here], dst.at[here], out_sem.at[i, blk])
            for i, (src, dst) in enumerate(((att, att_any), (inv, inv_any), (gated, gated_any)))
        ]

    @pl.loop(0, blocks)
    def _(blk):
        here = pl.ds(pl.multiple_of(blk * rows, rows), rows)
        first_tok = (blk * wide_count + wide_pos) * rows
        key_lane = lax.broadcasted_iota(jnp.int32, (rows, step), 1)
        tokens = lax.broadcasted_iota(jnp.int32, (rows, 1), 0) + first_tok
        upper = key_lane - tokens
        lower = key_lane - first_of(ends, tokens)
        queries = [
            jnp.concatenate(
                [query[here, (g * per + j) * LANES : (g * per + j + 1) * LANES] for j in range(per)],
                axis=0,
            )
            for g in range(groups)
        ]
        acc[...] = jnp.zeros_like(acc)
        kv_copy(blk).wait()

        @pl.loop(first_of(ends, first_tok) // step, (first_tok + rows + step - 1) // step)
        def _(tile):
            base = tile * step
            there = pl.ds(pl.multiple_of(base, step), step)
            allowed = (upper <= -base) & (lower >= -base)
            allowed = jnp.concatenate([allowed] * per, axis=0)
            for g in range(groups):
                cols = slice(g * LANES, (g + 1) * LANES)
                value_cols = slice(kv_width + g * LANES, kv_width + (g + 1) * LANES)
                scores = dot_nt(queries[g], kv[there, cols])
                probs = jnp.where(allowed, jnp.exp2(scores * factor), 0.0).astype(jnp.bfloat16)
                values = jnp.concatenate(
                    [kv[there, value_cols], jnp.ones((step, LANES), jnp.bfloat16)], axis=1
                )
                acc[g] += dot_nn(probs, values)

        @pl.when(blk == 0)
        def _():
            early[1].wait()

        for g in range(groups):
            for j in range(per):
                part = acc[g, j * rows : (j + 1) * rows, :]
                cols = slice((g * per + j) * LANES, (g * per + j + 1) * LANES)
                inverse = 1.0 / part[:, LANES:]
                out = part[:, :LANES] * inverse
                att[here, cols] = out
                inv[here, cols] = inverse
                gated[here, cols] = (out * jax.nn.sigmoid(gate[here, cols])).astype(jnp.bfloat16)
        start_all(out_copies(blk))

    for blk in range(blocks):
        for copy in out_copies(blk):
            copy.wait()


def attention_forward(doc_lengths, query_low, kv_all, gate_pre):
    rows, width = query_low.shape
    kv_width = kv_all.shape[1] // 2
    groups = kv_width // LANES
    per = width // kv_width
    blocks = lax.axis_size("head")
    low, full = jnp.bfloat16, jnp.float32
    shape, vm = jax.ShapeDtypeStruct, pltpu.VMEM
    return pl.pallas_call(
        attention_forward_kernel,
        out_shape=(
            shape((rows, width), full),
            shape((rows, width), full),
            shape((rows, width), low),
        ),
        in_specs=[pl.BlockSpec(memory_space=pltpu.SMEM)] + [ANY] * 3,
        out_specs=(ANY, ANY, ANY),
        scratch_shapes=[
            vm((rows, width), low), vm(kv_all.shape, low), vm((rows, width), full),
            vm((rows, width), full), vm((rows, width), full), vm((rows, width), low),
            vm((groups, per * (rows // blocks), 2 * LANES), full),
            DMA((blocks,)), DMA((2,)), DMA((3, blocks)),
        ],
        compiler_params=pltpu.CompilerParams(vmem_limit_bytes=VMEM_LIMIT),
        cost_estimate=pl.CostEstimate(
            flops=4 * rows * width * 2048, bytes_accessed=12 << 20, transcendentals=0
        ),
        name="attention_forward",
    )(doc_lengths, query_low, kv_all, gate_pre)


def attention_backward_kernel(
    doc_ref, query_any, att_any, inv_any, gate_any, kv_any, back_any, wo_any,
    dq_any, parts_any, ggrad_any,
    query, att, inv, gate, kv, back, wo, dq, parts, ggrad, dk_acc, dv_acc, dqt, keyt, dout,
    in_sem, out_sem,
):
    wide_count = lax.axis_size("wide")
    wide_pos = lax.axis_index("wide")
    kv_width = kv.shape[1] // 2
    groups = kv_width // LANES
    per = query.shape[1] // kv_width
    blocks = out_sem.shape[1]
    rows = query.shape[0] // blocks
    step = min(BACKWARD_KEYS, rows * wide_count)
    scale = LANES ** (-0.5)
    loads = [
        pltpu.make_async_copy(src, dst, in_sem.at[i])
        for i, (src, dst) in enumerate(
            (
                (back_any, back), (wo_any, wo), (gate_any, gate), (att_any, att),
                (inv_any, inv), (query_any, query), (kv_any, kv),
            )
        )
    ]
    start_all(loads)
    ends = doc_ends(doc_ref)
    dk_acc[...] = jnp.zeros_like(dk_acc)
    dv_acc[...] = jnp.zeros_like(dv_acc)
    for load in loads[:4]:
        load.wait()

    @pl.loop(0, blocks)
    def _(blk):
        here = pl.ds(pl.multiple_of(blk * rows, rows), rows)
        gated_grad = dot_nt(back[here, :], wo[...])
        sig = jax.nn.sigmoid(gate[here, :])
        grad = gated_grad * sig
        dout[here, :] = grad
        ggrad[here, :] = (grad * att[here, :] * (1.0 - sig)).astype(jnp.bfloat16)

    for load in loads[4:]:
        load.wait()

    @pl.loop(0, kv.shape[0] // step)
    def _(tile):
        there = pl.ds(pl.multiple_of(tile * step, step), step)
        for g in range(groups):
            cols = slice(g * LANES, (g + 1) * LANES)
            keyt[cols, there] = jnp.transpose(kv[there, cols])

    def out_copies(blk):
        here = pl.ds(pl.multiple_of(blk * rows, rows), rows)
        return [
            pltpu.make_async_copy(dq.at[here], dq_any.at[here], out_sem.at[0, blk]),
            pltpu.make_async_copy(parts.at[:, here], parts_any.at[:, here], out_sem.at[1, blk]),
            pltpu.make_async_copy(ggrad.at[here], ggrad_any.at[here], out_sem.at[2, blk]),
        ]

    @pl.loop(0, blocks)
    def _(turn_of):
        blk = blocks - 1 - turn_of
        here = pl.ds(pl.multiple_of(blk * rows, rows), rows)
        first_tok = (blk * wide_count + wide_pos) * rows
        key_row = lax.broadcasted_iota(jnp.int32, (step, rows), 0)
        tokens = lax.broadcasted_iota(jnp.int32, (1, rows), 1) + first_tok
        upper = key_row - tokens
        lower = key_row - first_of(ends, tokens)
        queries, grads, deltas = [], [], []
        for g in range(groups):
            qs, gs, ds = [], [], []
            for j in range(per):
                cols = slice((g * per + j) * LANES, (g * per + j + 1) * LANES)
                both = dout[here, cols] * inv[here, cols]
                delta = jnp.sum(both * att[here, cols], axis=1, keepdims=True)
                ds.append(jnp.transpose(jnp.broadcast_to(delta, (rows, LANES)))[0:1, :])
                qs.append(query[here, cols])
                gs.append(both.astype(jnp.bfloat16))
            queries.append(jnp.concatenate(qs, axis=0))
            grads.append(jnp.concatenate(gs, axis=0))
            deltas.append(jnp.concatenate(ds, axis=1))
        dqt[...] = jnp.zeros_like(dqt)

        @pl.loop(first_of(ends, first_tok) // step, (first_tok + rows + step - 1) // step)
        def _(tile):
            base = tile * step
            there = pl.ds(pl.multiple_of(base, step), step)
            allowed = (upper <= -base) & (lower >= -base)
            allowed = jnp.concatenate([allowed] * per, axis=1)
            for g in range(groups):
                cols = slice(g * LANES, (g + 1) * LANES)
                value_cols = slice(kv_width + g * LANES, kv_width + (g + 1) * LANES)
                scores = dot_nt(kv[there, cols], queries[g])
                probs = jnp.where(allowed, jnp.exp2(scores * (scale * LOG2E)), 0.0)
                dprobs = dot_nt(kv[there, value_cols], grads[g])
                dscores = (probs * (dprobs - deltas[g])).astype(jnp.bfloat16)
                dv_acc[there, cols] += dot_nn(probs.astype(jnp.bfloat16), grads[g])
                dk_acc[there, cols] += dot_nn(dscores, queries[g])
                dqt[g] += dot_nn(keyt[cols, there], dscores)

        for g in range(groups):
            for j in range(per):
                cols = slice((g * per + j) * LANES, (g * per + j + 1) * LANES)
                dq[here, cols] = jnp.transpose(dqt[g, :, j * rows : (j + 1) * rows]) * scale

        @pl.loop(0, wide_count)
        def _(target):
            source = pl.ds(pl.multiple_of((blk * wide_count + target) * rows, rows), rows)
            parts[target, here, :kv_width] = (dk_acc[source, :] * scale).astype(jnp.bfloat16)
            parts[target, here, kv_width:] = dv_acc[source, :].astype(jnp.bfloat16)

        start_all(out_copies(blk))

    for blk in range(blocks):
        for copy in out_copies(blk):
            copy.wait()


def attention_backward(
    doc_lengths, query_low, attended, inverse, gate_pre, kv_all, back_rows, out_w
):
    rows, width = query_low.shape
    keys, kv_width = kv_all.shape[0], kv_all.shape[1] // 2
    groups = kv_width // LANES
    per = width // kv_width
    blocks, wide_count = lax.axis_size("head"), lax.axis_size("wide")
    low, full = jnp.bfloat16, jnp.float32
    shape, vm = jax.ShapeDtypeStruct, pltpu.VMEM
    return pl.pallas_call(
        attention_backward_kernel,
        out_shape=(
            shape((rows, width), full),
            shape((wide_count, rows, 2 * kv_width), low),
            shape((rows, width), low),
        ),
        in_specs=[pl.BlockSpec(memory_space=pltpu.SMEM)] + [ANY] * 7,
        out_specs=(ANY, ANY, ANY),
        scratch_shapes=[
            vm((rows, width), low), vm((rows, width), full), vm((rows, width), full),
            vm((rows, width), full), vm(kv_all.shape, low), vm(back_rows.shape, low),
            vm(out_w.shape, low), vm((rows, width), full),
            vm((wide_count, rows, 2 * kv_width), low), vm((rows, width), low),
            vm((keys, kv_width), full), vm((keys, kv_width), full),
            vm((groups, LANES, per * (rows // blocks)), full), vm((kv_width, keys), low),
            vm((rows, width), full),
            DMA((7,)), DMA((3, blocks)),
        ],
        compiler_params=pltpu.CompilerParams(vmem_limit_bytes=VMEM_LIMIT),
        cost_estimate=pl.CostEstimate(
            flops=10 * rows * width * 2048, bytes_accessed=20 << 20, transcendentals=0
        ),
        name="attention_backward",
    )(
        doc_lengths, query_low, attended, inverse, gate_pre, kv_all, back_rows, out_w
    )


def ffn_kernel(
    gated_ref, gain_ref, x_any, cot_any, left_any, wo_any, wg_any, wu_any, wd_any,
    out_any, mgrad_ref, gain_out, back_any, down_any, fgate_any, fup_any, owg_any,
    wo, wg, wu, wd, cots, rows, hid, gg, ug, terms_own, outs_own, passed, into,
    passed2, into2, dterms, dinto, hterms, hinto, middle, back, local_sem,
    ds, dr, hs, hr, cs, cr, cps, cpr, fs, fr, fps, fpr, s1, r1, ps1, pr1, s2, r2, ps2, pr2, bs, br,
):
    tok, width = x_any.shape
    hidden_width = wg_any.shape[1]
    head, wide = head_ring(), wide_ring()
    pair = 2 * tok
    separate = terms_own.shape[0] > 16
    terms = terms_own if separate else cots
    outs = outs_own if separate else rows
    part = wo_any.shape[1] // lax.axis_size("head")
    loads = [
        pltpu.make_async_copy(src, dst, local_sem.at[i])
        for i, (src, dst) in enumerate(((wo_any, wo), (wd_any, wd), (wg_any, wg), (wu_any, wu)))
    ]
    split = left_any.shape[1]
    loads.append(pltpu.make_async_copy(left_any, cots.at[:, pl.ds(0, split)], local_sem.at[10]))
    for load in loads:
        load.start()
    own_wide = pl.multiple_of(lax.axis_index("wide") * tok, tok)
    own_head = pl.multiple_of(lax.axis_index("head") * tok, tok)
    own_loads = [
        pltpu.make_async_copy(
            cot_any.at[:, pl.ds(split, width - split)],
            cots.at[pl.ds(own_wide, tok), pl.ds(split, width - split)],
            local_sem.at[12],
        ),
        pltpu.make_async_copy(x_any, back.at[pl.ds(own_head, tok)], local_sem.at[13]),
    ]
    start_all(own_loads)
    meet(neighbours(head, wide))
    own_loads[0].wait()

    def slot_of(ref):
        return lambda index, start, size: ref.at[pl.ds(index * tok + start, size)]

    def cot_slot(index, start, size):
        return cots.at[pl.ds(index * tok + start, size), pl.ds(split, width - split)]

    cot_gather = PairGather(wide, cot_slot, tok, cs, cr, cps, cpr)
    row_gather = row_gather_of(wide)(wide, slot_of(rows), tok, fs, fr, fps, fpr)
    back_gather = Gather(head, slot_of(back), tok, bs, br)
    head_scatter = Scatter(head, lambda index: (hterms, index * tok), tok, hinto, hs, hr)
    grad_scatter = scatter_of(wide)(wide, terms, tok, passed, into, s1, r1, ps1, pr1)
    down_scatter = Scatter(
        head, lambda index: (dterms, index * hidden_width), hidden_width, dinto, ds, dr
    )
    out_scatter = scatter_of(wide)(wide, outs, tok, passed2, into2, s2, r2, ps2, pr2)

    def group_of(offset):
        return pl.ds(pl.multiple_of(wide.index(offset) * pair, pair), pair)

    def col_loop(total, step, body):
        @pl.loop(0, total // step)
        def _(i):
            body(pl.ds(pl.multiple_of(i * step, step), step))

    tile = 256
    line = wide.size == 4
    cot_gather.begin()

    def out_part(offset, own):
        index = head.index(offset)
        here = pl.ds(pl.multiple_of(index * tok, tok), tok)

        def body(cols):
            value = dot_nn(gated_ref[here, :], wo[:, cols])
            if own:
                middle[:, cols] = back[pl.ds(own_head, tok), cols].astype(jnp.float32) + value
            else:
                hterms[here, cols] = value.astype(jnp.bfloat16)

        col_loop(width, tile, body)

    def hidden_part(offset):
        here = group_of(offset)

        def body(cols):
            hid[here, cols] = dot_nt(cots[here, :], wd[cols, :]).astype(jnp.bfloat16)

        col_loop(hidden_width, hidden_width, body)

    loads[0].wait()
    own_loads[1].wait()
    out_part(head.half, False)
    head_scatter.start(head.half)
    for hop in range(head.half - 1, 0, -1):
        out_part(hop, False)
        out_part(-hop, False)
    out_part(0, True)
    loads[1].wait()
    loads[4].wait()
    mgrad_ref[...] = cots[pl.ds(own_wide, tok), :].astype(jnp.float32)
    cot_gather.take(0)
    hidden_part(0)
    for hop in range(head.half - 1, 0, -1):
        head_scatter.advance(hop)
    for hop in range(1, wide.half):
        cot_gather.arrive(hop)
        cot_gather.start(hop + 1)
        cot_gather.hand(hop)
        cot_gather.take(hop)
        hidden_part(hop)
        hidden_part(-hop)
    head_scatter.arrive()

    gain = gain_ref[...]

    def forward_norm(row):
        here = pl.ds(row, 32)
        value = (
            middle[here, :]
            + hinto[0, here, :].astype(jnp.float32)
            + hinto[1, here, :].astype(jnp.float32)
        )
        middle[here, :] = value
        scale = lax.rsqrt(jnp.mean(value * value, axis=-1, keepdims=True) + EPS)
        rows[pl.ds(pl.multiple_of(own_wide + row, 32), 32), :] = (value * scale * gain).astype(
            jnp.bfloat16
        )

    row_loop(tok, 32, forward_norm)
    row_gather.begin()
    cot_gather.arrive(wide.half)
    cot_gather.hand(wide.half)
    cot_gather.take(wide.half)
    hidden_part(wide.half)
    cot_gather.finish()
    loads[2].wait()
    loads[3].wait()

    def unit(offset):
        here = group_of(offset)

        def body(cols):
            gate = dot_nn(rows[here, :], wg[:, cols])
            up = dot_nn(rows[here, :], wu[:, cols])
            grad = hid[here, cols].astype(jnp.float32)
            sig = jax.nn.sigmoid(gate)
            act = gate * sig
            hid[here, cols] = (act * up).astype(jnp.bfloat16)
            gg[here, cols] = (grad * up * (sig + act * (1.0 - sig))).astype(jnp.bfloat16)
            ug[here, cols] = (grad * act).astype(jnp.bfloat16)

        col_loop(hidden_width, tile if hidden_width % tile == 0 else LANES, body)

    def down_terms(offset):
        here = group_of(offset)

        def body(cols):
            outs[here, cols] = dot_nn(hid[here, :], wd[:, cols]).astype(jnp.bfloat16)

        col_loop(width, width, body)
        if not line:
            out_scatter.hand(offset)

    def down_grads(group, add):
        @pl.loop(0, lax.axis_size("head"))
        def _(index):
            cols = pl.ds(pl.multiple_of(index * part, part), part)
            there = pl.ds(pl.multiple_of(index * hidden_width, LANES), hidden_width)
            value = sum(
                dot_tn(hid[group_of(offset), :], cots[group_of(offset), cols]) for offset in group
            )
            if add:
                value += dterms[there, :].astype(jnp.float32)
            dterms[there, :] = value.astype(jnp.bfloat16)

    def grad_terms(offset):
        here = group_of(offset)

        def body(cols):
            value = dot_nt(gg[here, :], wg[cols, :]) + dot_nt(ug[here, :], wu[cols, :])
            terms[here, cols] = value.astype(jnp.bfloat16)

        col_loop(width, 1024, body)

    emit = 256

    def stage_of(out, slot):
        cols = pl.ds(out * hidden_width, hidden_width)
        return hterms.at[pl.ds(slot * emit, emit), cols]

    def stage_copy(step, out, any_ref, slot):
        there = pl.ds(pl.multiple_of(step * emit, emit), emit)
        return pltpu.make_async_copy(
            stage_of(out, slot), any_ref.at[there], local_sem.at[5 + 2 * slot + out]
        )

    def input_grads():
        head_scatter.finish()

        @pl.loop(0, width // emit // 2)
        def _(i):
            for slot in SIDES:
                step = 2 * i + slot
                cols = pl.ds(pl.multiple_of(step * emit, emit), emit)

                @pl.when(i > 0)
                def _():
                    for out, any_ref in enumerate((fgate_any, fup_any)):
                        stage_copy(step - 2, out, any_ref, slot).wait()

                left = rows[:, cols]
                stage_of(0, slot)[...] = dot_tn(left, gg[...]).astype(jnp.bfloat16)
                stage_of(1, slot)[...] = dot_tn(left, ug[...]).astype(jnp.bfloat16)
                for out, any_ref in enumerate((fgate_any, fup_any)):
                    stage_copy(step, out, any_ref, slot).start()

    order = offsets(wide)

    def near_part(offset):
        unit(offset)
        if separate:
            down_terms(offset)

    def down_pass(kind):
        offset = out_scatter.offset(kind)
        down_terms(offset)
        out_scatter.hand_kind(kind)

    if line:

        def arrived(kind):
            row_gather.arrive(kind)
            row_gather.take(kind)
            unit(row_gather.offset(kind))
            grad_terms(grad_scatter.offset(kind))
            grad_scatter.hand_kind(kind)

        row_gather.take(None)
        unit(0)
        down_pass(None)
        down_grads([0], False)
        arrived(NEAR)
        down_pass(NEAR)
        grad_scatter.merge_kind(NEAR)
        grad_scatter.launch(NEAR)

        @pl.when(row_gather.middle)
        def _():
            arrived(OTHER)
            down_pass(OTHER)
            grad_scatter.merge_kind(OTHER)

        arrived(FAR)
        grad_scatter.merge_kind(FAR)
        grad_scatter.launch(FAR)

        @pl.when(~row_gather.middle)
        def _():
            arrived(OTHER)
            grad_scatter.merge_kind(OTHER)

        grad_scatter.launch(OTHER)
        pl.when(~row_gather.middle)(functools.partial(down_pass, OTHER))
        down_pass(FAR)
        grad_terms(0)
        grad_scatter.hand_kind(None)
        down_grads([1, 2, 3], True)
        down_scatter.start(head.half)
        grad_scatter.relay(OTHER)
        for kind in (OTHER, FAR, NEAR, None):
            out_scatter.merge_kind(kind)
        input_grads()
        out_scatter.launch(OTHER, FAR, NEAR)
        grad_scatter.merge_kind(None)
        grad_scatter.relay(FAR)
        grad_scatter.relay(NEAR)
    else:
        row_gather.take(0)
        near_part(0)
        if separate:
            down_grads([0], False)
        for hop in range(1, wide.half):
            row_gather.arrive(hop)
            row_gather.start(hop + 1)
            row_gather.hand(hop)
            row_gather.take(hop)
            near_part(hop)
            near_part(-hop)
        row_gather.arrive(wide.half)
        row_gather.hand(wide.half)
        row_gather.take(wide.half)
        unit(wide.half)
        if not separate:
            down_grads(order, False)
            down_scatter.start(head.half)
        for offset in order:
            grad_terms(offset)
            grad_scatter.hand(offset)
        grad_scatter.merge(order[0])
        grad_scatter.start(wide.half)
        if separate:
            down_grads(order[:-1], True)
            down_scatter.start(head.half)
            down_terms(order[0])
        for hop in range(wide.half - 1, 0, -1):
            grad_scatter.merge(hop)
            grad_scatter.merge(-hop)
            grad_scatter.advance(hop)
        grad_scatter.merge(0)
        input_grads()
    row_gather.finish()
    if not line:
        if not separate:
            for offset in order:
                down_terms(offset)
        out_scatter.merge(order[0])
    for hop in range(head.half - 1, 0, -1):
        down_scatter.advance(hop)
    grad_scatter.arrive()

    def backward_norm(row, gain_sum):
        here = pl.ds(row, 32)
        value = middle[here, :]
        grad = grad_scatter.total(row, 32)
        scale = lax.rsqrt(jnp.mean(value * value, axis=-1, keepdims=True) + EPS)
        scaled = value * scale
        weighted = grad * gain
        mean = jnp.mean(scaled * weighted, axis=-1, keepdims=True)
        total = mgrad_ref[here, :] + scale * (weighted - scaled * mean)
        mgrad_ref[here, :] = total
        back[pl.ds(pl.multiple_of(own_head + row, 32), 32), :] = total.astype(jnp.bfloat16)
        return gain_sum + jnp.sum(grad * scaled, axis=0, keepdims=True)

    gain_out[...] = lax.fori_loop(
        0, tok // 32,
        lambda i, carried: backward_norm(pl.multiple_of(i * 32, 32), carried),
        jnp.zeros((1, width), jnp.float32),
    )
    back_gather.start(1)
    if line:
        for kind in (FAR, OTHER, NEAR):
            out_scatter.relay(kind)
    else:
        out_scatter.start(wide.half)
        for offset in order[1:]:
            out_scatter.merge(offset)
        for hop in range(wide.half - 1, 0, -1):
            out_scatter.advance(hop)
    for hop in range(1, head.half):
        back_gather.arrive(hop)
        back_gather.start(hop + 1)
    back_gather.arrive(head.half)
    back_gather.finish()
    keep = pltpu.make_async_copy(back, back_any, local_sem.at[4])
    keep.start()
    last = width // emit
    for slot in SIDES:
        for out, any_ref in enumerate((fgate_any, fup_any)):
            stage_copy(last - 2 + slot, out, any_ref, slot).wait()
    owners = gated_ref.shape[1]

    def out_grads(cols):
        hterms[pl.ds(0, owners), cols] = dot_tn(gated_ref[...], back[:, cols]).astype(jnp.bfloat16)

    col_loop(width, 512, out_grads)
    share = pltpu.make_async_copy(hterms.at[pl.ds(0, owners)], owg_any, local_sem.at[11])
    share.start()
    down_scatter.arrive()
    own_down = pl.multiple_of(lax.axis_index("head") * hidden_width, LANES)

    def finish_down(row):
        there = pl.ds(pl.multiple_of(own_down + row, LANES), LANES)
        dterms[there, :] = down_scatter.total(row, LANES).astype(jnp.bfloat16)

    row_loop(hidden_width, LANES, finish_down)
    down_out = pltpu.make_async_copy(
        dterms.at[pl.ds(own_down, hidden_width)], down_any, local_sem.at[14]
    )
    down_out.start()
    out_scatter.arrive()

    def finish_out(row):
        here = pl.ds(row, 32)
        back[here, :] = (middle[here, :] + out_scatter.total(row, 32)).astype(jnp.bfloat16)

    keep.wait()
    row_loop(tok, 32, finish_out)
    result = pltpu.make_async_copy(back.at[pl.ds(0, tok)], out_any, local_sem.at[9])
    result.start()

    for scatter in (grad_scatter, out_scatter, down_scatter):
        scatter.finish()
    result.wait()
    share.wait()
    down_out.wait()


def ffn_block(gated_low, inputs, cotangent, cot_left, ffn_gain, out_w, gate_w, up_w, down_w):
    tok, width = inputs.shape
    head_count, wide_count = lax.axis_size("head"), lax.axis_size("wide")
    chips = wide_count // 2
    hidden_width = gate_w.shape[1]
    low, full = jnp.bfloat16, jnp.float32
    all_rows = wide_count * tok
    back_rows = head_count * tok
    roomy = all_rows * width <= 2 << 20
    shape = jax.ShapeDtypeStruct
    vm = pltpu.VMEM
    return pl.pallas_call(
        ffn_kernel,
        out_shape=(
            shape((tok, width), low),
            shape((tok, width), full),
            shape((1, width), full),
            shape((back_rows, width), low),
            shape((hidden_width, width // head_count), low),
            shape((width, hidden_width), low),
            shape((width, hidden_width), low),
            shape((gated_low.shape[1], width), low),
        ),
        in_specs=[VMEM] * 2 + [ANY] * 7,
        out_specs=(ANY, VMEM, VMEM, ANY, ANY, ANY, ANY, ANY),
        scratch_shapes=[
            vm(out_w.shape, low), vm(gate_w.shape, low), vm(up_w.shape, low),
            vm(down_w.shape, low),
            vm((all_rows, width), low), vm((all_rows, width), low),
            vm((all_rows, hidden_width), low), vm((all_rows, hidden_width), low),
            vm((all_rows, hidden_width), low),
            vm((all_rows if roomy else 16, width), low),
            vm((all_rows if roomy else 16, width), low),
            vm((chips, tok, width), low),
            scatter_into(chips, tok, width),
            vm((chips, tok, width), low),
            scatter_into(chips, tok, width),
            vm((head_count * hidden_width, width // head_count), low),
            into_shape(head_count, hidden_width, width // head_count),
            vm((back_rows, width), low), into_shape(head_count, tok, width),
            vm((tok, width), full), vm((back_rows, width), low),
            DMA((15,)),
            *ring_sems(head_count),
            *ring_sems(head_count),
            *ring_sems(chips), *pass_sems(chips),
            *gather_sems(chips),
            *scatter_sems(chips),
            *scatter_sems(chips),
            *ring_sems(head_count),
        ],
        compiler_params=pltpu.CompilerParams(
            collective_id=1, has_side_effects=True, vmem_limit_bytes=VMEM_LIMIT
        ),
        cost_estimate=pl.CostEstimate(
            flops=10 * all_rows * width * hidden_width, bytes_accessed=200 << 20, transcendentals=0
        ),
        name="ffn_block",
    )(
        gated_low, ffn_gain[None], inputs, cotangent, cot_left, out_w, gate_w, up_w, down_w
    )


def turn(values, cosine, sine_tab):
    half = LANES // 2
    lane = lax.broadcasted_iota(jnp.int32, values.shape, 1)
    turned = pltpu.roll(values, half, 1)
    return values * cosine + jnp.where(lane < half, -turned, turned) * sine_tab


def prep(pre_proj, gain, cosine, sine_tab):
    scale = lax.rsqrt(jnp.mean(pre_proj * pre_proj, axis=-1, keepdims=True) + EPS)
    return turn(pre_proj * scale * gain, cosine, sine_tab).astype(jnp.bfloat16)


def front_kernel(
    doc_ref, x_ref, gain_ref, speed_ref, qgain_ref, kgain_ref, wq_any, wk_any, wv_any, wg_any,
    query_ref, qpre_ref, kpre_ref, gpre_ref, cos_ref, sin_ref, normed_any, kv_any,
    wq, wk, wv, wg, normed, kv, local_sem, hs, hr, ks, kr, kps, kpr,
):
    tok, width = x_ref.shape
    kv_width = wk_any.shape[1]
    q_width = wq_any.shape[1]
    wide_count, head_count = lax.axis_size("wide"), lax.axis_size("head")
    head, wide = head_ring(), wide_ring()
    loads = [
        pltpu.make_async_copy(src, dst, local_sem.at[i])
        for i, (src, dst) in enumerate(((wk_any, wk), (wv_any, wv), (wq_any, wq), (wg_any, wg)))
    ]
    for load in loads:
        load.start()
    own = pl.multiple_of(lax.axis_index("head") * tok, tok)
    own_wide = lax.axis_index("wide")

    def norm(row):
        here = pl.ds(row, 32)
        value = x_ref[here, :].astype(jnp.float32)
        scale = lax.rsqrt(jnp.mean(value * value, axis=-1, keepdims=True) + EPS)
        normed[pl.ds(pl.multiple_of(own + row, 32), 32), :] = (
            value * scale * gain_ref[...]
        ).astype(jnp.bfloat16)

    row_loop(tok, 32, norm)
    meet(neighbours(head, wide))
    gather = Gather(
        head, lambda index, start, size: normed.at[pl.ds(index * tok + start, size)], tok, hs, hr
    )
    gather.start(1)
    ends = doc_ends(doc_ref)

    @pl.loop(0, head_count)
    def _(block):
        here = pl.ds(pl.multiple_of(block * tok, tok), tok)
        first_tok = (block * wide_count + own_wide) * tok
        tokens = lax.broadcasted_iota(jnp.int32, (tok, LANES), 0) + first_tok
        angles = (tokens - first_of(ends, tokens)).astype(jnp.float32) * speed_ref[...]
        cos_ref[here, :] = jnp.cos(angles)
        sin_ref[here, :] = jnp.sin(angles)

    def kv_gather(offset):
        slot = offset % head_count
        block = head.index(offset)

        def place(index, start, size):
            return kv.at[pl.ds((block * wide_count + index) * tok + start, size)]

        return row_gather_of(wide)(
            wide, place, tok, ks.at[slot], kr.at[slot], kps.at[slot], kpr.at[slot]
        )

    def project(offset):
        block = head.index(offset)
        here = pl.ds(pl.multiple_of(block * tok, tok), tok)
        there = pl.ds(pl.multiple_of((block * wide_count + own_wide) * tok, tok), tok)
        left = normed[here, :]
        cosine, sine_tab = cos_ref[here, :], sin_ref[here, :]
        pre = dot_nn(left, wk[...])
        kpre_ref[here, :] = pre
        for j in range(kv_width // LANES):
            cols = slice(j * LANES, (j + 1) * LANES)
            kv[there, cols] = prep(pre[:, cols], kgain_ref[...], cosine, sine_tab)
        kv[there, kv_width:] = dot_nn(left, wv[...]).astype(jnp.bfloat16)

    def project_rest(offset):
        block = head.index(offset)
        here = pl.ds(pl.multiple_of(block * tok, tok), tok)
        left = normed[here, :]
        cosine, sine_tab = cos_ref[here, :], sin_ref[here, :]
        pre = dot_nn(left, wq[...])
        qpre_ref[here, :] = pre
        for j in range(q_width // LANES):
            cols = slice(j * LANES, (j + 1) * LANES)
            query_ref[here, cols] = prep(pre[:, cols], qgain_ref[...], cosine, sine_tab)
        gpre_ref[here, :] = dot_nn(left, wg[...])

    gathers = {}

    def launch(offset):
        project(offset)
        gathers[offset] = kv_gather(offset)
        gathers[offset].begin()

    line = wide.size == 4

    def step(offset, hop):
        each = gathers[offset]
        if line and hop == 1:
            each.arrive(NEAR)

            @pl.when(each.middle)
            def _():
                each.arrive(OTHER)

        elif line:
            each.arrive(FAR)

            @pl.when(~each.middle)
            def _():
                each.arrive(OTHER)

        else:
            each.arrive(hop)
            if hop < wide.half:
                each.start(hop + 1)
            each.hand(hop)

    loads[0].wait()
    loads[1].wait()
    launch(0)
    loads[2].wait()
    loads[3].wait()
    project_rest(0)
    done = [0]
    for hop in range(1, head.half + 1):
        gather.arrive(hop)
        if hop < head.half:
            gather.start(hop + 1)
            launch(hop)
            launch(-hop)
            for offset in done:
                step(offset, 1)
            project_rest(hop)
            project_rest(-hop)
            done = [hop, -hop]
        else:
            launch(hop)
            for offset in done:
                step(offset, 1)
            project_rest(hop)
            done = [hop]
    gather.finish()
    keep = pltpu.make_async_copy(normed, normed_any, local_sem.at[4])
    keep.start()
    for offset in done:
        step(offset, 1)
    for hop in range(2, wide.half + 1):
        for offset in gathers:
            step(offset, hop)
    for each in gathers.values():
        for hop in (None, NEAR, OTHER, FAR) if line else range(wide.half + 1):
            each.take(hop)
    store = pltpu.make_async_copy(kv, kv_any, local_sem.at[5])
    store.start()
    for each in gathers.values():
        each.finish()
    store.wait()
    keep.wait()


def front_block(doc_lengths, inputs, attn_gain, speed, query_gain, key_gain, weights):
    tok, width = inputs.shape
    head_count, wide_count = lax.axis_size("head"), lax.axis_size("wide")
    chips = wide_count // 2
    q_width, kv_width = weights[0].shape[1], weights[1].shape[1]
    rows = head_count * tok
    low, full = jnp.bfloat16, jnp.float32
    shape, vm = jax.ShapeDtypeStruct, pltpu.VMEM
    return pl.pallas_call(
        front_kernel,
        out_shape=(
            shape((rows, q_width), low),
            shape((rows, q_width), full),
            shape((rows, kv_width), full),
            shape((rows, q_width), full),
            shape((rows, LANES), full),
            shape((rows, LANES), full),
            shape((rows, width), low),
            shape((rows * wide_count, 2 * kv_width), low),
        ),
        in_specs=[pl.BlockSpec(memory_space=pltpu.SMEM)] + [VMEM] * 5 + [ANY] * 4,
        out_specs=tuple([VMEM] * 6 + [ANY] * 2),
        scratch_shapes=[
            *[vm(weight.shape, low) for weight in weights],
            vm((rows, width), low),
            vm((rows * wide_count, 2 * kv_width), low),
            DMA((6,)),
            *ring_sems(head_count),
            *[DMA((head_count, *sem.shape)) for sem in gather_sems(chips)],
        ],
        compiler_params=pltpu.CompilerParams(
            collective_id=3, has_side_effects=True, vmem_limit_bytes=VMEM_LIMIT
        ),
        cost_estimate=pl.CostEstimate(
            flops=2 * rows * width * (2 * q_width + 2 * kv_width), bytes_accessed=100 << 20,
            transcendentals=0,
        ),
        name="front_block",
    )(
        doc_lengths, inputs, attn_gain[None], speed[None], query_gain[None], key_gain[None],
        *weights,
    )


def turn_back(grad, cosine, sine_tab):
    half = LANES // 2
    lane = lax.broadcasted_iota(jnp.int32, grad.shape, 1)
    turned = pltpu.roll(grad * sine_tab, half, 1)
    return grad * cosine + jnp.where(lane < half, turned, -turned)


def unprep(grad, pre_proj, gain, cosine, sine_tab):
    turned = turn_back(grad, cosine, sine_tab)
    scale = lax.rsqrt(jnp.mean(pre_proj * pre_proj, axis=-1, keepdims=True) + EPS)
    scaled = pre_proj * scale
    weighted = turned * gain
    mean = jnp.mean(scaled * weighted, axis=-1, keepdims=True)
    return scale * (weighted - scaled * mean), turned * scaled


def tail_kernel(
    cos_ref, sin_ref, qgain_ref, kgain_ref, gain_ref, ffn_gain_ref,
    dq_any, qpre_any, kpre_any, ggrad_any, x_any, mgrad_any,
    kvp_any, normed_any, wq_any, wk_any, wv_any, wg_any, fgate_any, fup_any,
    igrad_ref, gains_ref, query_out, key_out, value_out, gate_out, fgate_out, fup_out,
    dq_ref, qpre_ref, kpre_ref, ggrad_ref, x_ref, mgrad_ref, kvp, normed, wq, wk, wv, wg, fgate, fup, qlow, klow, vlow, early, late, hterms,
    kv_passed, kv_into, early_passed, early_into, late_passed, late_into, hinto, fgate_into,
    fup_into, gain_slots, local_sem,
    kvs, kvr, kvps, kvpr, es, er, eps, epr, ls, lr, lps, lpr, hs, hr, gs, gr, us, ur, gain_send,
    gain_recv,
):
    tok, width = x_ref.shape
    rows = dq_ref.shape[0]
    wide_count = lax.axis_size("wide")
    head_count = lax.axis_size("head")
    head, wide = head_ring(), wide_ring()
    loads = [
        pltpu.make_async_copy(src, dst, local_sem.at[i])
        for i, (src, dst) in enumerate(
            (
                (kvp_any, kvp), (fgate_any, fgate), (fup_any, fup), (normed_any, normed),
                (wq_any, wq), (wk_any, wk), (wv_any, wv), (wg_any, wg),
            )
        )
    ]
    more = [
        pltpu.make_async_copy(src, dst, local_sem.at[11 + i])
        for i, (src, dst) in enumerate(
            (
                (dq_any, dq_ref), (qpre_any, qpre_ref), (ggrad_any, ggrad_ref),
                (kpre_any, kpre_ref), (x_any, x_ref), (mgrad_any, mgrad_ref),
            )
        )
    ]
    start_all(loads[:1] + more[:3] + loads[1:] + more[3:])
    meet(everyone(head, wide))
    kv_width = wk.shape[1]
    q_width = wq.shape[1]
    block = normed.shape[1] // wide_count
    ffn_rows = fgate.shape[0] // head_count
    kv_scatter = PairScatter(wide, kvp, rows, kv_passed, kv_into, kvs, kvr, kvps, kvpr)
    early_scatter = PairScatter(wide, early, block, early_passed, early_into, es, er, eps, epr)
    late_scatter = PairScatter(wide, late, block, late_passed, late_into, ls, lr, lps, lpr)
    head_scatter = Scatter(head, lambda index: (hterms, index * tok), tok, hinto, hs, hr)
    gate_scatter = Scatter(
        head, lambda index: (fgate, index * ffn_rows), ffn_rows, fgate_into, gs, gr
    )
    up_scatter = Scatter(head, lambda index: (fup, index * ffn_rows), ffn_rows, fup_into, us, ur)
    order = offsets(wide)

    loads[0].wait()
    for offset in order:
        kv_scatter.hand(offset)
    loads[1].wait()
    gate_scatter.start(head.half)
    loads[2].wait()
    up_scatter.start(head.half)

    for load in more[:3]:
        load.wait()
    chunk = 128

    def query_back(row, total):
        here = pl.ds(row, chunk)
        for j in range(q_width // LANES):
            cols = slice(j * LANES, (j + 1) * LANES)
            value, terms = unprep(
                dq_ref[here, cols], qpre_ref[here, cols], qgain_ref[...], cos_ref[here, :],
                sin_ref[here, :],
            )
            qlow[here, cols] = value.astype(jnp.bfloat16)
            total = total + jnp.sum(terms, axis=0, keepdims=True)
        return total

    def over_rows(count, body, start):
        return lax.fori_loop(
            0, count // chunk, lambda i, carried: body(pl.multiple_of(i * chunk, chunk), carried),
            start,
        )

    qgain_sum = over_rows(rows, query_back, jnp.zeros((1, LANES), jnp.float32))

    kv_scatter.merge(order[0])
    kv_scatter.start(wide.half)
    loads[3].wait()

    def early_part(offset):
        index = wide.index(offset)

        @pl.loop(0, 2)
        def _(core):
            target = 2 * index + core
            cols = pl.ds(pl.multiple_of(target * block, block), block)
            there = pl.ds(pl.multiple_of(target * block, block), block)
            left = normed[:, cols]
            early[there, :q_width] = dot_tn(left, qlow[...]).astype(jnp.bfloat16)
            early[there, q_width:] = dot_tn(left, ggrad_ref[...]).astype(jnp.bfloat16)

    for offset in order:
        early_part(offset)
        early_scatter.hand(offset)
    for offset in order[1:]:
        kv_scatter.merge(offset)
    early_scatter.merge(order[0])
    for hop in range(wide.half - 1, 0, -1):
        kv_scatter.advance(hop)
    early_scatter.start(wide.half)
    for offset in order[1:]:
        early_scatter.merge(offset)
    for hop in range(head.half - 1, 0, -1):
        gate_scatter.advance(hop)
        up_scatter.advance(hop)
    for load in loads[4:] + more[3:]:
        load.wait()
    kv_scatter.arrive()
    for hop in range(wide.half - 1, 0, -1):
        early_scatter.advance(hop)

    def key_back(row, total):
        here = pl.ds(row, chunk)
        both = kv_scatter.total(row, chunk)
        for j in range(kv_width // LANES):
            cols = slice(j * LANES, (j + 1) * LANES)
            value, terms = unprep(
                both[:, cols], kpre_ref[here, cols], kgain_ref[...], cos_ref[here, :],
                sin_ref[here, :],
            )
            klow[here, cols] = value.astype(jnp.bfloat16)
            total = total + jnp.sum(terms, axis=0, keepdims=True)
        vlow[here, :] = both[:, kv_width:].astype(jnp.bfloat16)
        return total

    kgain_sum = over_rows(rows, key_back, jnp.zeros((1, LANES), jnp.float32))

    def head_part(offset):
        here = pl.ds(pl.multiple_of(head.index(offset) * tok, tok), tok)

        @pl.loop(0, width // 256)
        def _(i):
            cols = pl.ds(pl.multiple_of(i * 256, 256), 256)
            value = dot_nt(qlow[here, :], wq[cols, :]) + dot_nt(ggrad_ref[here, :], wg[cols, :])
            value += dot_nt(klow[here, :], wk[cols, :]) + dot_nt(vlow[here, :], wv[cols, :])
            hterms[here, cols] = value.astype(jnp.bfloat16)

    head_part(head.half)
    head_scatter.start(head.half)

    def late_part(offset):
        index = wide.index(offset)

        @pl.loop(0, 2)
        def _(core):
            target = 2 * index + core
            cols = pl.ds(pl.multiple_of(target * block, block), block)
            left = normed[:, cols]
            late[cols, :kv_width] = dot_tn(left, klow[...]).astype(jnp.bfloat16)
            late[cols, kv_width:] = dot_tn(left, vlow[...]).astype(jnp.bfloat16)

    for offset in order:
        late_part(offset)
        late_scatter.hand(offset)
    late_scatter.merge(order[0])
    late_scatter.start(wide.half)
    for hop in range(head.half - 1, 0, -1):
        head_part(hop)
        head_part(-hop)
        head_scatter.advance(hop)
    head_part(0)
    for offset in order[1:]:
        late_scatter.merge(offset)
    for hop in range(wide.half - 1, 0, -1):
        late_scatter.advance(hop)

    gate_scatter.arrive()
    up_scatter.arrive()
    own_ffn = pl.multiple_of(lax.axis_index("head") * ffn_rows, ffn_rows)
    pending = []
    for scatter, ref, out in ((gate_scatter, fgate, fgate_out), (up_scatter, fup, fup_out)):

        def finish_ffn(row, scatter=scatter, ref=ref):
            there = pl.ds(pl.multiple_of(own_ffn + row, 64), 64)
            ref[there, :] = scatter.total(row, 64).astype(jnp.bfloat16)

        row_loop(ffn_rows, 64, finish_ffn)
        pending.append(
            pltpu.make_async_copy(
                ref.at[pl.ds(own_ffn, ffn_rows)], out, local_sem.at[9 + len(pending)]
            )
        )
        pending[-1].start()

    head_scatter.arrive()
    gain = gain_ref[...]

    def input_back(row, total):
        here = pl.ds(row, 32)
        value = x_ref[here, :].astype(jnp.float32)
        grad = head_scatter.total(row, 32)
        scale = lax.rsqrt(jnp.mean(value * value, axis=-1, keepdims=True) + EPS)
        scaled = value * scale
        weighted = grad * gain
        mean = jnp.mean(scaled * weighted, axis=-1, keepdims=True)
        igrad_ref[here, :] = mgrad_ref[here, :] + scale * (weighted - scaled * mean)
        return total + jnp.sum(grad * scaled, axis=0, keepdims=True)

    gain_sum = lax.fori_loop(
        0, tok // 32, lambda i, carried: input_back(pl.multiple_of(i * 32, 32), carried),
        jnp.zeros((1, width), jnp.float32),
    )
    chips = wide.size
    pair_slot, chip_slot = 0, 2
    head_slot = 2 + chips
    mine = gain_slots.at[pair_slot]
    mine[...] = jnp.zeros(mine.shape, jnp.float32)
    mine[0:1, :] = gain_sum
    mine[1:2, :] = ffn_gain_ref[...]
    mine[2:3, 0:LANES] = qgain_sum
    mine[3:4, 0:LANES] = kgain_sum
    swap = remote(
        mine, gain_slots.at[1], gain_send.at[0], gain_recv.at[0], wide.sibling
    )
    swap.start()
    swap.wait_recv()

    def spread(ring, own, base, sem):
        here = gain_slots.at[base + own]
        copies = [
            remote(here, here, gain_send.at[sem + d], gain_recv.at[sem + d], ring.device(d))
            for d in range(1, ring.size)
        ]
        for copy in copies:
            copy.start()
        for copy in copies:
            copy.wait_recv()
        return copies

    own_chip = wide.index(0)
    gain_slots[chip_slot + own_chip] = gain_slots[0] + gain_slots[1]
    sent = [swap] + spread(wide, own_chip, chip_slot, 0)
    total = gain_slots[chip_slot]
    for i in range(1, chips):
        total = total + gain_slots[chip_slot + i]
    own_head = lax.axis_index("head")
    gain_slots[head_slot + own_head] = total
    sent += spread(head, own_head, head_slot, chips - 1)
    total = gain_slots[head_slot]
    for i in range(1, head_count):
        total = total + gain_slots[head_slot + i]
    gains_ref[...] = total

    early_scatter.arrive()

    def early_out(row):
        here = pl.ds(row, 32)
        both = early_scatter.total(row, 32)
        query_out[here, :] = both[:, :q_width].astype(jnp.bfloat16)
        gate_out[here, :] = both[:, q_width:].astype(jnp.bfloat16)

    row_loop(block, 32, early_out)
    late_scatter.arrive()

    def late_out(row):
        here = pl.ds(row, 32)
        both = late_scatter.total(row, 32)
        key_out[here, :] = both[:, :kv_width].astype(jnp.bfloat16)
        value_out[here, :] = both[:, kv_width:].astype(jnp.bfloat16)

    row_loop(block, 32, late_out)
    for scatter in (
        kv_scatter, early_scatter, late_scatter, head_scatter, gate_scatter, up_scatter
    ):
        scatter.finish()
    for copy in sent:
        copy.wait_send()
    for copy in pending:
        copy.wait()


def tail_block(
    dq, kv_parts, query_pre, key_pre, gate_grad, cosine, sine_tab, query_gain, key_gain, inputs,
    middle_grad, attn_gain, ffn_gain_part, normed, weights, fgate, fup,
):
    tok, width = inputs.shape
    head_count, wide_count = lax.axis_size("head"), lax.axis_size("wide")
    chips = wide_count // 2
    rows, q_width = dq.shape
    kv_width = key_pre.shape[1]
    block = width // wide_count
    hidden_width = fgate.shape[1]
    ffn_rows = width // head_count
    low, full = jnp.bfloat16, jnp.float32
    shape, vm = jax.ShapeDtypeStruct, pltpu.VMEM
    early_width = 2 * q_width
    pair = [*ring_sems(chips), DMA((chips,)), DMA((chips,))]
    peers = chips + head_count
    return pl.pallas_call(
        tail_kernel,
        out_shape=(
            shape((tok, width), full),
            shape((8, width), full),
            shape((block, q_width), low),
            shape((block, kv_width), low),
            shape((block, kv_width), low),
            shape((block, q_width), low),
            shape((ffn_rows, hidden_width), low),
            shape((ffn_rows, hidden_width), low),
        ),
        in_specs=[VMEM] * 6 + [ANY] * 14,
        out_specs=tuple([VMEM] * 6 + [ANY] * 2),
        scratch_shapes=[
            vm(dq.shape, full), vm(query_pre.shape, full), vm(key_pre.shape, full),
            vm(gate_grad.shape, low), vm(inputs.shape, low), vm(middle_grad.shape, full),
            vm(kv_parts.shape, low), vm(normed.shape, low),
            *[vm(weight.shape, low) for weight in weights],
            vm(fgate.shape, low), vm(fup.shape, low),
            vm((rows, q_width), low), vm((rows, kv_width), low), vm((rows, kv_width), low),
            vm((width, early_width), low), vm((width, 2 * kv_width), low),
            vm((head_count * tok, width), low),
            vm((chips, rows, 2 * kv_width), low), into_shape(chips, rows, 2 * kv_width),
            vm((chips, block, early_width), low), into_shape(chips, block, early_width),
            vm((chips, block, 2 * kv_width), low), into_shape(chips, block, 2 * kv_width),
            into_shape(head_count, tok, width),
            into_shape(head_count, ffn_rows, hidden_width),
            into_shape(head_count, ffn_rows, hidden_width),
            vm((2 + chips + head_count, 8, width), full),
            DMA((17,)),
            *pair, *pair, *pair,
            *ring_sems(head_count), *ring_sems(head_count), *ring_sems(head_count),
            DMA((peers,)), DMA((peers,)),
        ],
        compiler_params=pltpu.CompilerParams(
            collective_id=2, has_side_effects=True, vmem_limit_bytes=VMEM_LIMIT
        ),
        cost_estimate=pl.CostEstimate(
            flops=20 * rows * width * q_width, bytes_accessed=300 << 20, transcendentals=0
        ),
        name="tail_block",
    )(
        cosine, sine_tab, query_gain[None], key_gain[None], attn_gain[None], ffn_gain_part,
        dq, query_pre, key_pre, gate_grad, inputs, middle_grad,
        kv_parts, normed, *weights, fgate, fup,
    )


def finish_kernel(count, *refs):
    sources, gains_any = refs[:count], refs[count]
    results = refs[count + 1 : 2 * count + 1]
    gain_outs = refs[2 * count + 1 : 2 * count + 5]
    landed = refs[2 * count + 5 : 3 * count + 5]
    *spare, gains, in_sem, out_sem = refs[3 * count + 5 :]
    loads = [
        pltpu.make_async_copy(sources[i], landed[i], in_sem.at[i]) for i in range(count)
    ]
    last = pltpu.make_async_copy(gains_any, gains, in_sem.at[count])
    start_all([*loads, last])
    stores = []
    for i in range(count):
        ready = landed[i]
        loads[i].wait()
        if sources[i].dtype != results[i].dtype:
            ready = spare.pop(0)
            rows = ready.shape[0]
            step = min(rows, 128)

            def convert(row, src=landed[i], dst=ready, step=step):
                here = pl.ds(row, step)
                dst[here, :] = src[here, :].astype(jnp.float32)

            row_loop(rows, step, convert)
        stores.append(pltpu.make_async_copy(ready, results[i], out_sem.at[i]))
        stores[-1].start()
    last.wait()
    for row, out in enumerate(gain_outs):
        out[...] = gains[row : row + 1, : out.shape[1]]
    for store in stores:
        store.wait()


def finish_block(arrays, dtypes, gains, head_width):
    shape, vm = jax.ShapeDtypeStruct, pltpu.VMEM
    width = gains.shape[1]
    sizes = (width, width, head_width, head_width)
    outs = pl.pallas_call(
        functools.partial(finish_kernel, len(arrays)),
        out_shape=tuple(shape(a.shape, d) for a, d in zip(arrays, dtypes))
        + tuple(shape((1, size), jnp.float32) for size in sizes),
        in_specs=[ANY] * (len(arrays) + 1),
        out_specs=tuple([ANY] * len(arrays) + [VMEM] * 4),
        scratch_shapes=[
            *[vm(a.shape, a.dtype) for a in arrays],
            *[vm(a.shape, d) for a, d in zip(arrays, dtypes) if a.dtype != d],
            vm(gains.shape, jnp.float32),
            DMA((len(arrays) + 1,)), DMA((len(arrays),)),
        ],
        compiler_params=pltpu.CompilerParams(vmem_limit_bytes=VMEM_LIMIT),
        name="finish_block",
    )(*arrays, gains)
    return outs[: len(arrays)], [gain.reshape(-1) for gain in outs[len(arrays) :]]


def shards(
    inputs,
    attn_gain,
    query_weight,
    key_projection,
    value_projection,
    attn_gate_weight,
    output_weight,
    query_gain,
    key_gain,
    ffn_gain,
    ffn_gate_weight,
    ffn_up_weight,
    ffn_down_weight,
    doc_lengths,
    cotangent,
):
    head_width = query_gain.shape[0]
    cot_left = lax.all_gather(
        cotangent[:, : cotangent.shape[1] // 4], "wide", axis=0, tiled=True
    )
    weights = (query_weight, key_projection, value_projection, attn_gate_weight)
    query_low, query_pre, key_pre, gate_pre, cosine, sine_tab, gathered, kv_all = front_block(
        doc_lengths, inputs, attn_gain, rotation_speed(head_width), query_gain, key_gain, weights
    )
    attended, inverse, gated_low = attention_forward(doc_lengths, query_low, kv_all, gate_pre)
    (
        outputs,
        middle_grad,
        ffn_gain_part,
        back_rows,
        ffn_down_grad,
        gate_wgrad,
        up_wgrad,
        out_wgrad,
    ) = ffn_block(
        gated_low,
        inputs,
        cotangent,
        cot_left,
        ffn_gain,
        output_weight,
        ffn_gate_weight,
        ffn_up_weight,
        ffn_down_weight,
    )
    output_grad = lax.psum_scatter(out_wgrad, "wide", scatter_dimension=1, tiled=True)
    query_rot_grad, kv_parts, gate_pre_grad = attention_backward(
        doc_lengths, query_low, attended, inverse, gate_pre, kv_all, back_rows, output_weight
    )
    kv_parts = kv_parts.reshape(-1, kv_parts.shape[2])
    (
        input_grad,
        gains,
        query_grad,
        key_grad,
        value_grad,
        attn_gate_grad,
        ffn_gate_grad,
        ffn_up_grad,
    ) = tail_block(
        query_rot_grad,
        kv_parts,
        query_pre,
        key_pre,
        gate_pre_grad,
        cosine,
        sine_tab,
        query_gain,
        key_gain,
        inputs,
        middle_grad,
        attn_gain,
        ffn_gain_part,
        gathered,
        weights,
        gate_wgrad,
        up_wgrad,
    )
    full = jnp.float32
    results, gain_grads = finish_block(
        [
            outputs,
            input_grad,
            query_grad,
            key_grad,
            value_grad,
            attn_gate_grad,
            output_grad,
            ffn_gate_grad,
            ffn_up_grad,
            ffn_down_grad,
        ],
        [jnp.bfloat16] + [full] * 9,
        gains,
        head_width,
    )
    outputs, input_grad, query_grad, key_grad, value_grad = results[:5]
    attn_gate_grad, output_grad, ffn_gate_grad, ffn_up_grad, ffn_down_grad = results[5:]
    attn_gain_grad, ffn_gain_grad, query_gain_grad, key_gain_grad = gain_grads
    return (
        outputs,
        input_grad,
        attn_gain_grad,
        query_grad,
        key_grad,
        value_grad,
        attn_gate_grad,
        output_grad,
        query_gain_grad,
        key_gain_grad,
        ffn_gain_grad,
        ffn_gate_grad,
        ffn_up_grad,
        ffn_down_grad,
    )


def solution(mesh):
    placed = (
        P(("head", "wide"), None),
        P(),
        P(None, "head"),
        P(None, "head"),
        P(None, "head"),
        P(None, "head"),
        P("head", None),
        P(),
        P(),
        P(),
        P(None, "wide"),
        P(None, "wide"),
        P("wide", None),
        P(),
        P(("head", "wide"), None),
    )
    return jax.shard_map(
        shards,
        mesh=mesh,
        in_specs=placed,
        out_specs=(
            P(("head", "wide"), None),
            P(("head", "wide"), None),
            P(),
            P("wide", "head"),
            P("wide", "head"),
            P("wide", "head"),
            P("wide", "head"),
            P("head", "wide"),
            P(),
            P(),
            P(),
            P("head", "wide"),
            P("head", "wide"),
            P("wide", "head"),
        ),
        check_vma=False,
    )
```

```python
import functools

import jax
import jax.numpy as jnp
from jax import lax
from jax.experimental import pallas as pl
from jax.experimental.pallas import tpu as pltpu
from jax.sharding import PartitionSpec as P

EPS = 1e-06
THETA = 1000000.0
VMEM_LIMIT = 63 << 20


def rotation_speed(head_width):
    inverse = THETA ** (-(jnp.arange(head_width // 2, dtype=jnp.float32) * 2.0 / head_width))
    return jnp.concatenate([inverse, inverse])


MESH = pl.DeviceIdType.MESH
ANY = pl.BlockSpec(memory_space=pl.ANY)
VMEM = pl.BlockSpec(memory_space=pltpu.VMEM)
DMA = pltpu.SemaphoreType.DMA
SIDES = (0, 1)


class Ring:
    def __init__(self, size, pos, index, device):
        self.size, self.pos, self.half = size, pos, size // 2
        self._index, self._device = index, device

    def at(self, offset):
        return lax.rem(self.pos + (offset + 2 * self.size), self.size)

    def index(self, offset):
        return self._index(self.at(offset))

    def device(self, offset):
        return self._device(self.at(offset))


def head_ring():
    size = lax.axis_size("head")
    spread = size // 2
    own, wide = lax.axis_index("head"), lax.axis_index("wide")
    major, minor = lax.div(own, 2), lax.rem(own, 2)
    pos = major + minor * (size - 1 - 2 * major)

    def index(place):
        upper = lax.div(place, spread)
        return 2 * (place + upper * (size - 1 - 2 * place)) + upper

    return Ring(size, pos, index, lambda place: (index(place), wide))


def wide_ring():
    size = lax.axis_size("wide") // 2
    head, wide = lax.axis_index("head"), lax.axis_index("wide")
    core = lax.rem(wide, 2)
    ring = Ring(
        size, lax.div(wide, 2), lambda place: place, lambda place: (head, 2 * place + core)
    )
    ring.core = core
    ring.sibling = (head, wide + 1 - 2 * core)
    return ring


def meet(devices):
    barrier = pltpu.get_barrier_semaphore()
    for device in devices:
        pl.semaphore_signal(barrier, inc=1, device_id=device, device_id_type=MESH)
    pl.semaphore_wait(barrier, len(devices))


def neighbours(*rings):
    found = []
    for ring in rings:
        found += [ring.device(1), ring.device(-1)]
        if hasattr(ring, "sibling"):
            found.append(ring.sibling)
    return found


def remote(src, dst, send, recv, device):
    return pltpu.make_async_remote_copy(
        src_ref=src, dst_ref=dst, send_sem=send, recv_sem=recv, device_id=device,
        device_id_type=MESH,
    )


class Ways:
    def span(self, hop, side, piece=None):
        half = self.rows // 2
        if hop == self.ring.half:
            return side * half, half
        if piece is not None:
            return piece * half, half
        return 0, self.rows

    def halved(self, hop):
        return hop == self.ring.half - 1

    def pieces(self, hop, side):
        return (side, 1 - side) if self.halved(hop) else (None,)

    def all_copies(self, hop):
        for nth in range(2 if self.halved(hop) else 1):
            for side in SIDES:
                yield self.copy(hop, side, self.pieces(hop, side)[nth])

    def start(self, hop):
        for copy in self.all_copies(hop):
            copy.start()

    def sems(self, hop, side, piece):
        which = 0 if piece is None else piece
        return self.send.at[side, hop - 1, which], self.recv.at[side, hop - 1, which]

    def finish(self):
        for hop in range(1, self.ring.half + 1):
            for copy in self.all_copies(hop):
                copy.wait_send()


class Gather(Ways):
    def __init__(self, ring, slot, rows, send, recv):
        self.ring, self.slot, self.rows = ring, slot, rows
        self.send, self.recv = send, recv

    def copy(self, hop, side, piece=None):
        way = 1 - 2 * side
        ref = self.slot(self.ring.index(-way * (hop - 1)), *self.span(hop, side, piece))
        return remote(ref, ref, *self.sems(hop, side, piece), self.ring.device(way))

    def arrive(self, hop):
        for copy in self.all_copies(hop):
            copy.wait_recv()

    def step(self, hop):
        if not self.halved(hop):
            self.arrive(hop)
            self.start(hop + 1)
            return
        for side in SIDES:
            self.copy(hop, side, side).wait_recv()
            self.copy(hop + 1, side).start()
        for side in SIDES:
            self.copy(hop, side, 1 - side).wait_recv()


class PairGather(Gather):
    def __init__(self, ring, slot, rows, send, recv, pass_send, pass_recv):
        core = ring.core
        super().__init__(
            ring, lambda index, start, size: slot(2 * index + core, start, size), rows, send, recv
        )
        self.pass_send, self.pass_recv = pass_send, pass_recv

    def handed(self, hop, side):
        way = 1 - 2 * side
        span = self.span(hop, side) if hop else (0, self.rows)
        ref = self.slot(self.ring.index(-way * hop), *span)
        return remote(
            ref, ref, self.pass_send.at[side, hop], self.pass_recv.at[side, hop],
            self.ring.sibling,
        )

    def hand(self, hop):
        for side in SIDES if hop else (0,):
            self.handed(hop, side).start()

    def take(self, hop):
        for side in SIDES if hop else (0,):
            self.handed(hop, side).wait_recv()

    def begin(self):
        self.start(1)
        self.hand(0)

    def finish(self):
        super().finish()
        for hop in range(self.ring.half + 1):
            for side in SIDES if hop else (0,):
                self.handed(hop, side).wait_send()


def row_loop(rows, chunk, body):
    @pl.loop(0, rows // chunk)
    def _(step):
        body(pl.multiple_of(step * chunk, chunk))


class Scatter(Ways):
    def __init__(self, ring, part, rows, into, send, recv):
        self.ring, self.part, self.rows, self.into = ring, part, rows, into
        self.send, self.recv = send, recv
        self.freed = False

    def inside(self, hop, row):
        return row % (self.rows // 2) if hop == self.ring.half else row

    def copy(self, hop, side, piece=None):
        way = 1 - 2 * side
        first, count = self.span(hop, side, piece)
        ref, base = self.part(self.ring.index(way * hop))
        return remote(
            ref.at[pl.ds(base + first, count)],
            self.into.at[side, pl.ds((hop - 1) * self.rows + self.inside(hop, first), count)],
            *self.sems(hop, side, piece), self.ring.device(way),
        )

    def start_free(self):
        self.freed = True
        if self.ring.half > 1:
            for side in SIDES:
                self.copy(self.ring.half - 1, side, 1 - side).start()

    def fold(self, hop, side):
        way = 1 - 2 * side
        for copy in [self.copy(hop + 1, side, piece) for piece in self.pieces(hop + 1, side)]:
            copy.wait_recv()
        first, count = self.span(hop + 1, side)
        ref, base = self.part(self.ring.index(way * hop))
        chunk = min(count, 32)

        def add(row):
            there = pl.ds(pl.multiple_of(base + first + row, chunk), chunk)
            start = hop * self.rows + self.inside(hop + 1, first)
            here = pl.ds(pl.multiple_of(start + row, chunk), chunk)
            ref[there, :] = (
                ref[there, :].astype(jnp.float32) + self.into[side, here, :].astype(jnp.float32)
            ).astype(ref.dtype)

        row_loop(count, chunk, add)

    def advance(self, hop):
        if self.halved(hop) and not self.freed:
            self.start_free()
        for side in SIDES:
            self.fold(hop, side)
            self.copy(hop, side, self.pieces(hop, side)[0]).start()

    def arrive(self):
        for copy in self.all_copies(1):
            copy.wait_recv()

    def total(self, row, count):
        ref, base = self.part(self.ring.index(0))
        there = pl.ds(pl.multiple_of(base + row, count), count)
        here = pl.ds(row, count)
        return (
            ref[there, :].astype(jnp.float32)
            + self.into[0, here, :].astype(jnp.float32)
            + self.into[1, here, :].astype(jnp.float32)
        )


class PairScatter(Scatter):
    def __init__(self, ring, terms, rows, passed, into, send, recv, pass_send, pass_recv):
        core = ring.core
        super().__init__(
            ring, lambda index: (terms, (2 * index + core) * rows), rows, into, send, recv
        )
        self.terms, self.passed = terms, passed
        self.pass_send, self.pass_recv = pass_send, pass_recv

    def handed(self, offset):
        ring = self.ring
        index = ring.index(offset)
        other = pl.multiple_of((2 * index + 1 - ring.core) * self.rows, self.rows)
        slot = offset % ring.size
        return remote(
            self.terms.at[pl.ds(other, self.rows)],
            self.passed.at[slot],
            self.pass_send.at[slot], self.pass_recv.at[slot], ring.sibling,
        )

    def hand(self, offset):
        self.handed(offset).start()

    def merge(self, offset):
        self.handed(offset).wait_recv()
        slot = offset % self.ring.size
        ref, base = self.part(self.ring.index(offset))
        chunk = 32

        def add(row):
            there = pl.ds(pl.multiple_of(base + row, chunk), chunk)
            ref[there, :] = (
                ref[there, :].astype(jnp.float32)
                + self.passed[slot, pl.ds(row, chunk), :].astype(jnp.float32)
            ).astype(ref.dtype)

        row_loop(self.rows, chunk, add)

    def finish(self):
        super().finish()
        for offset in range(self.ring.size):
            self.handed(offset).wait_send()


def offsets(ring):
    order = [ring.half]
    for hop in range(ring.half - 1, 0, -1):
        order += [hop, -hop]
    return order + [0]


def into_shape(size, rows, columns):
    return pltpu.VMEM((2, (size - 1) * rows // 2, columns), jnp.bfloat16)


def everyone(*rings):
    found = []
    for ring in rings:
        found += [ring.device(offset) for offset in range(1, ring.size)]
        if hasattr(ring, "sibling"):
            found.append(ring.sibling)
    return found


def ring_sems(size):
    return [DMA((2, size // 2, 2)), DMA((2, size // 2, 2))]


def pass_sems(size):
    return [DMA((2, size // 2 + 1)), DMA((2, size // 2 + 1))]


NEAR, OTHER, FAR = 0, 1, 2


class LineGather:
    pieces = 2

    def __init__(self, ring, slot, rows, send, recv, pass_send, pass_recv):
        self.ring, self.slot, self.rows = ring, slot, rows // self.pieces
        self.send, self.recv, self.pass_send, self.pass_recv = send, recv, pass_send, pass_recv
        pos = ring.pos
        half, odd = lax.div(pos, 2), lax.rem(pos, 2)
        self.way = 1 - 2 * odd
        self.middle = half + odd == 1

    def offset(self, kind):
        return {NEAR: self.way, OTHER: -self.way, FAR: 2}[kind]

    def ref(self, offset, piece):
        index = 2 * self.ring.index(offset) + self.ring.core
        return self.slot(index, piece * self.rows, self.rows)

    def copy(self, which, offset, kind, piece, way):
        ref = self.ref(offset, piece)
        return remote(
            ref, ref, self.send.at[which, piece], self.recv.at[kind, piece],
            self.ring.device(way),
        )

    def own(self, piece):
        return self.copy(0, 0, NEAR, piece, self.way)

    def own_other(self, piece):
        return self.copy(1, 0, OTHER, piece, -self.way)

    def onward(self, kind, piece):
        arrives = {NEAR: FAR, OTHER: FAR, FAR: OTHER}[kind]
        way = -self.way if kind == NEAR else self.way
        return self.copy(2 + kind, self.offset(kind), arrives, piece, way)

    def incoming(self, kind, piece):
        return self.copy(0, self.offset(kind), kind, piece, self.way)

    def handed(self, kind, piece):
        ref = self.ref(0 if kind is None else self.offset(kind), piece)
        slot = 3 if kind is None else kind
        return remote(
            ref, ref, self.pass_send.at[slot, piece], self.pass_recv.at[slot, piece],
            self.ring.sibling,
        )

    def begin(self):
        for piece in range(self.pieces):
            self.own(piece).start()

            @pl.when(self.middle)
            def _():
                self.own_other(piece).start()

            self.handed(None, piece).start()

    def arrive(self, kind):
        for piece in range(self.pieces):
            self.incoming(kind, piece).wait_recv()

            @pl.when(self.middle)
            def _():
                self.onward(kind, piece).start()

            self.handed(kind, piece).start()

    def take(self, kind):
        for piece in range(self.pieces):
            self.handed(kind, piece).wait_recv()

    def finish(self):
        for piece in range(self.pieces):
            self.own(piece).wait_send()

            @pl.when(self.middle)
            def _():
                self.own_other(piece).wait_send()
                for kind in (NEAR, OTHER, FAR):
                    self.onward(kind, piece).wait_send()

            for kind in (None, NEAR, OTHER, FAR):
                self.handed(kind, piece).wait_send()


class LineScatter(PairScatter):
    pieces = 2

    def __init__(self, *args):
        super().__init__(*args)
        pos = self.ring.pos
        half, odd = lax.div(pos, 2), lax.rem(pos, 2)
        self.way = 1 - 2 * odd
        self.middle = half + odd == 1
        self.waited = set()

    def offset(self, kind):
        return {NEAR: self.way, OTHER: -self.way, FAR: 2, None: 0}[kind]

    def piece_of(self, piece):
        size = self.rows // self.pieces
        return piece * size, size

    def outgoing(self, kind, slot, piece, way):
        first, size = self.piece_of(piece)
        ref, base = self.part(self.ring.index(self.offset(kind)))
        return remote(
            ref.at[pl.ds(pl.multiple_of(base + first, size), size)],
            self.into.at[slot, pl.ds(first, size)],
            self.send.at[kind, piece], self.recv.at[slot, piece], self.ring.device(way),
        )

    def from_end(self, kind, piece):
        return self.outgoing(kind, {OTHER: 0, FAR: 1, NEAR: 2}[kind], piece, self.way)

    def from_middle(self, kind, piece):
        slot = {FAR: 3, OTHER: 4, NEAR: 0}[kind]
        return self.outgoing(kind, slot, piece, self.way if kind == NEAR else -self.way)

    def landed(self, slot, piece):
        first, size = self.piece_of(piece)
        ref = self.into.at[slot, pl.ds(first, size)]
        remote(
            ref, ref, self.send.at[0, piece], self.recv.at[slot, piece], self.ring.device(self.way)
        ).wait_recv()

    def hand_kind(self, kind):
        self.swap(kind).start()

    def swap(self, kind):
        index = self.ring.index(self.offset(kind))
        other = pl.multiple_of((2 * index + 1 - self.ring.core) * self.rows, self.rows)
        slot = 3 if kind is None else kind
        return remote(
            self.terms.at[pl.ds(other, self.rows)], self.passed.at[slot],
            self.pass_send.at[slot], self.pass_recv.at[slot], self.ring.sibling,
        )

    def merge_kind(self, kind):
        self.swap(kind).wait_recv()
        slot = 3 if kind is None else kind
        ref, base = self.part(self.ring.index(self.offset(kind)))

        def add(row):
            there = pl.ds(pl.multiple_of(base + row, 32), 32)
            ref[there, :] = (
                ref[there, :].astype(jnp.float32)
                + self.passed[slot, pl.ds(row, 32), :].astype(jnp.float32)
            ).astype(ref.dtype)

        row_loop(self.rows, 32, add)

    def launch(self, *kinds):
        @pl.when(~self.middle)
        def _():
            for kind in kinds:
                for piece in range(self.pieces):
                    self.from_end(kind, piece).start()

    def sent(self, kind):
        self.waited.add(kind)

        @pl.when(~self.middle)
        def _():
            for piece in range(self.pieces):
                self.from_end(kind, piece).wait_send()

    def relay(self, kind):
        slot = {FAR: 0, OTHER: 1, NEAR: 3}[kind]

        @pl.when(self.middle)
        def _():
            ref, base = self.part(self.ring.index(self.offset(kind)))
            for piece in range(self.pieces):
                first, size = self.piece_of(piece)
                self.landed(slot, piece)

                def add(row):
                    there = pl.ds(pl.multiple_of(base + first + row, 32), 32)
                    here = pl.ds(pl.multiple_of(first + row, 32), 32)
                    ref[there, :] = (
                        ref[there, :].astype(jnp.float32)
                        + self.into[slot, here, :].astype(jnp.float32)
                    ).astype(ref.dtype)

                row_loop(size, 32, add)
                self.from_middle(kind, piece).start()

    def arrive(self):
        @pl.when(self.middle)
        def _():
            for piece in range(self.pieces):
                self.landed(2, piece)
                self.landed(4, piece)

            def add(row):
                here = pl.ds(row, 32)
                self.into[0, here, :] = (
                    self.into[2, here, :].astype(jnp.float32)
                    + self.into[4, here, :].astype(jnp.float32)
                ).astype(self.into.dtype)

            row_loop(self.rows, 32, add)

        @pl.when(~self.middle)
        def _():
            for piece in range(self.pieces):
                self.landed(0, piece)

    def total(self, row, count):
        ref, base = self.part(self.ring.index(0))
        there = pl.ds(pl.multiple_of(base + row, count), count)
        return ref[there, :].astype(jnp.float32) + self.into[0, pl.ds(row, count), :].astype(
            jnp.float32
        )

    def finish(self):
        for piece in range(self.pieces):

            @pl.when(self.middle)
            def _():
                for kind in (NEAR, OTHER, FAR):
                    self.from_middle(kind, piece).wait_send()

            @pl.when(~self.middle)
            def _():
                for kind in (NEAR, OTHER, FAR):
                    if kind not in self.waited:
                        self.from_end(kind, piece).wait_send()

        for kind in (NEAR, OTHER, FAR, None):
            self.swap(kind).wait_send()


def scatter_of(ring):
    return LineScatter if ring.size == 4 else PairScatter


def scatter_into(size, rows, columns):
    if size == 4:
        return pltpu.VMEM((5, rows, columns), jnp.bfloat16)
    return into_shape(size, rows, columns)


def scatter_sems(size):
    passed = [DMA((size,)), DMA((size,))]
    if size == 4:
        pieces = LineScatter.pieces
        return [DMA((3, pieces)), DMA((5, pieces)), *passed]
    return [*ring_sems(size), *passed]


def line_sems():
    pieces = LineGather.pieces
    return [DMA((5, pieces)), DMA((3, pieces)), DMA((4, pieces)), DMA((4, pieces))]


def gather_sems(size):
    return line_sems() if size == 4 else [*ring_sems(size), *pass_sems(size)]


def row_gather_of(ring):
    return LineGather if ring.size == 4 else PairGather


def dot_nn(left, right):
    return jnp.dot(left, right, preferred_element_type=jnp.float32)


def dot_nt(left, right):
    return lax.dot_general(
        left, right, (((1,), (1,)), ((), ())), preferred_element_type=jnp.float32
    )


def dot_tn(left, right):
    return lax.dot_general(
        left, right, (((0,), (0,)), ((), ())), preferred_element_type=jnp.float32
    )


LANES = 128
FORWARD_KEYS = 1024
BACKWARD_KEYS = 512
LOG2E = 1.4426950408889634


def doc_ends(doc_ref):
    ends, total = [], jnp.int32(0)
    for row in range(doc_ref.shape[0]):
        for doc in range(doc_ref.shape[1]):
            total = total + doc_ref[row, doc]
            ends.append(total)
    return ends


def first_of(ends, tokens):
    first = jnp.zeros_like(tokens)
    for end in ends:
        first = jnp.maximum(first, jnp.where(tokens >= end, end, 0))
    return first


def start_all(copies):
    for copy in copies:
        copy.start()


def attention_forward_kernel(
    doc_ref, query_any, kv_any, gate_any, att_any, inv_any, gated_any,
    query, kv, gate, att, inv, gated, acc, kv_sem, in_sem, out_sem,
):
    wide_count = lax.axis_size("wide")
    wide_pos = lax.axis_index("wide")
    kv_width = kv.shape[1] // 2
    groups = kv_width // LANES
    per = query.shape[1] // kv_width
    blocks = kv_sem.shape[0]
    rows = query.shape[0] // blocks
    step = min(FORWARD_KEYS, rows * wide_count)
    factor = LANES ** (-0.5) * LOG2E
    chunk = rows * wide_count

    def kv_copy(blk):
        there = pl.ds(pl.multiple_of(blk * chunk, chunk), chunk)
        return pltpu.make_async_copy(kv_any.at[there], kv.at[there], kv_sem.at[blk])

    early = [
        pltpu.make_async_copy(query_any, query, in_sem.at[0]),
        pltpu.make_async_copy(gate_any, gate, in_sem.at[1]),
    ]
    early[0].start()
    for blk in range(blocks):
        kv_copy(blk).start()
    early[1].start()
    ends = doc_ends(doc_ref)
    early[0].wait()

    def out_copies(blk):
        here = pl.ds(pl.multiple_of(blk * rows, rows), rows)
        return [
            pltpu.make_async_copy(src.at[here], dst.at[here], out_sem.at[i, blk])
            for i, (src, dst) in enumerate(((att, att_any), (inv, inv_any), (gated, gated_any)))
        ]

    @pl.loop(0, blocks)
    def _(blk):
        here = pl.ds(pl.multiple_of(blk * rows, rows), rows)
        first_tok = (blk * wide_count + wide_pos) * rows
        key_lane = lax.broadcasted_iota(jnp.int32, (rows, step), 1)
        tokens = lax.broadcasted_iota(jnp.int32, (rows, 1), 0) + first_tok
        upper = key_lane - tokens
        lower = key_lane - first_of(ends, tokens)
        queries = [
            jnp.concatenate(
                [query[here, (g * per + j) * LANES : (g * per + j + 1) * LANES] for j in range(per)],
                axis=0,
            )
            for g in range(groups)
        ]
        acc[...] = jnp.zeros_like(acc)
        kv_copy(blk).wait()

        @pl.loop(first_of(ends, first_tok) // step, (first_tok + rows + step - 1) // step)
        def _(tile):
            base = tile * step
            there = pl.ds(pl.multiple_of(base, step), step)
            allowed = (upper <= -base) & (lower >= -base)
            allowed = jnp.concatenate([allowed] * per, axis=0)
            for g in range(groups):
                cols = slice(g * LANES, (g + 1) * LANES)
                value_cols = slice(kv_width + g * LANES, kv_width + (g + 1) * LANES)
                scores = dot_nt(queries[g], kv[there, cols])
                probs = jnp.where(allowed, jnp.exp2(scores * factor), 0.0).astype(jnp.bfloat16)
                values = jnp.concatenate(
                    [kv[there, value_cols], jnp.ones((step, LANES), jnp.bfloat16)], axis=1
                )
                acc[g] += dot_nn(probs, values)

        @pl.when(blk == 0)
        def _():
            early[1].wait()

        for g in range(groups):
            for j in range(per):
                part = acc[g, j * rows : (j + 1) * rows, :]
                cols = slice((g * per + j) * LANES, (g * per + j + 1) * LANES)
                inverse = 1.0 / part[:, LANES:]
                out = part[:, :LANES] * inverse
                att[here, cols] = out
                inv[here, cols] = inverse
                gated[here, cols] = (out * jax.nn.sigmoid(gate[here, cols])).astype(jnp.bfloat16)
        start_all(out_copies(blk))

    for blk in range(blocks):
        for copy in out_copies(blk):
            copy.wait()


def attention_forward(doc_lengths, query_low, kv_all, gate_pre):
    rows, width = query_low.shape
    kv_width = kv_all.shape[1] // 2
    groups = kv_width // LANES
    per = width // kv_width
    blocks = lax.axis_size("head")
    low, full = jnp.bfloat16, jnp.float32
    shape, vm = jax.ShapeDtypeStruct, pltpu.VMEM
    return pl.pallas_call(
        attention_forward_kernel,
        out_shape=(
            shape((rows, width), full),
            shape((rows, width), full),
            shape((rows, width), low),
        ),
        in_specs=[pl.BlockSpec(memory_space=pltpu.SMEM)] + [ANY] * 3,
        out_specs=(ANY, ANY, ANY),
        scratch_shapes=[
            vm((rows, width), low), vm(kv_all.shape, low), vm((rows, width), full),
            vm((rows, width), full), vm((rows, width), full), vm((rows, width), low),
            vm((groups, per * (rows // blocks), 2 * LANES), full),
            DMA((blocks,)), DMA((2,)), DMA((3, blocks)),
        ],
        compiler_params=pltpu.CompilerParams(vmem_limit_bytes=VMEM_LIMIT),
        cost_estimate=pl.CostEstimate(
            flops=4 * rows * width * 2048, bytes_accessed=12 << 20, transcendentals=0
        ),
        name="attention_forward",
    )(doc_lengths, query_low, kv_all, gate_pre)


def attention_backward_kernel(
    doc_ref, query_any, att_any, inv_any, gate_any, kv_any, back_any, wo_any,
    dq_any, parts_any, ggrad_any,
    query, att, inv, gate, kv, back, wo, dq, parts, ggrad, dk_acc, dv_acc, dqt, keyt, dout,
    in_sem, out_sem,
):
    wide_count = lax.axis_size("wide")
    wide_pos = lax.axis_index("wide")
    kv_width = kv.shape[1] // 2
    groups = kv_width // LANES
    per = query.shape[1] // kv_width
    blocks = out_sem.shape[1]
    rows = query.shape[0] // blocks
    step = min(BACKWARD_KEYS, rows * wide_count)
    scale = LANES ** (-0.5)
    loads = [
        pltpu.make_async_copy(src, dst, in_sem.at[i])
        for i, (src, dst) in enumerate(
            (
                (back_any, back), (wo_any, wo), (gate_any, gate), (att_any, att),
                (inv_any, inv), (query_any, query), (kv_any, kv),
            )
        )
    ]
    start_all(loads)
    ends = doc_ends(doc_ref)
    dk_acc[...] = jnp.zeros_like(dk_acc)
    dv_acc[...] = jnp.zeros_like(dv_acc)
    for load in loads[:4]:
        load.wait()

    @pl.loop(0, blocks)
    def _(blk):
        here = pl.ds(pl.multiple_of(blk * rows, rows), rows)
        gated_grad = dot_nt(back[here, :], wo[...])
        sig = jax.nn.sigmoid(gate[here, :])
        grad = gated_grad * sig
        dout[here, :] = grad
        ggrad[here, :] = (grad * att[here, :] * (1.0 - sig)).astype(jnp.bfloat16)

    for load in loads[4:]:
        load.wait()

    @pl.loop(0, kv.shape[0] // step)
    def _(tile):
        there = pl.ds(pl.multiple_of(tile * step, step), step)
        for g in range(groups):
            cols = slice(g * LANES, (g + 1) * LANES)
            keyt[cols, there] = jnp.transpose(kv[there, cols])

    def out_copies(blk):
        here = pl.ds(pl.multiple_of(blk * rows, rows), rows)
        return [
            pltpu.make_async_copy(dq.at[here], dq_any.at[here], out_sem.at[0, blk]),
            pltpu.make_async_copy(parts.at[:, here], parts_any.at[:, here], out_sem.at[1, blk]),
            pltpu.make_async_copy(ggrad.at[here], ggrad_any.at[here], out_sem.at[2, blk]),
        ]

    @pl.loop(0, blocks)
    def _(turn_of):
        blk = blocks - 1 - turn_of
        here = pl.ds(pl.multiple_of(blk * rows, rows), rows)
        first_tok = (blk * wide_count + wide_pos) * rows
        key_row = lax.broadcasted_iota(jnp.int32, (step, rows), 0)
        tokens = lax.broadcasted_iota(jnp.int32, (1, rows), 1) + first_tok
        upper = key_row - tokens
        lower = key_row - first_of(ends, tokens)
        queries, grads, deltas = [], [], []
        for g in range(groups):
            qs, gs, ds = [], [], []
            for j in range(per):
                cols = slice((g * per + j) * LANES, (g * per + j + 1) * LANES)
                both = dout[here, cols] * inv[here, cols]
                delta = jnp.sum(both * att[here, cols], axis=1, keepdims=True)
                ds.append(jnp.transpose(jnp.broadcast_to(delta, (rows, LANES)))[0:1, :])
                qs.append(query[here, cols])
                gs.append(both.astype(jnp.bfloat16))
            queries.append(jnp.concatenate(qs, axis=0))
            grads.append(jnp.concatenate(gs, axis=0))
            deltas.append(jnp.concatenate(ds, axis=1))
        dqt[...] = jnp.zeros_like(dqt)

        @pl.loop(first_of(ends, first_tok) // step, (first_tok + rows + step - 1) // step)
        def _(tile):
            base = tile * step
            there = pl.ds(pl.multiple_of(base, step), step)
            allowed = (upper <= -base) & (lower >= -base)
            allowed = jnp.concatenate([allowed] * per, axis=1)
            for g in range(groups):
                cols = slice(g * LANES, (g + 1) * LANES)
                value_cols = slice(kv_width + g * LANES, kv_width + (g + 1) * LANES)
                scores = dot_nt(kv[there, cols], queries[g])
                probs = jnp.where(allowed, jnp.exp2(scores * (scale * LOG2E)), 0.0)
                dprobs = dot_nt(kv[there, value_cols], grads[g])
                dscores = (probs * (dprobs - deltas[g])).astype(jnp.bfloat16)
                dv_acc[there, cols] += dot_nn(probs.astype(jnp.bfloat16), grads[g])
                dk_acc[there, cols] += dot_nn(dscores, queries[g])
                dqt[g] += dot_nn(keyt[cols, there], dscores)

        for g in range(groups):
            for j in range(per):
                cols = slice((g * per + j) * LANES, (g * per + j + 1) * LANES)
                dq[here, cols] = jnp.transpose(dqt[g, :, j * rows : (j + 1) * rows]) * scale

        @pl.loop(0, wide_count)
        def _(target):
            source = pl.ds(pl.multiple_of((blk * wide_count + target) * rows, rows), rows)
            parts[target, here, :kv_width] = (dk_acc[source, :] * scale).astype(jnp.bfloat16)
            parts[target, here, kv_width:] = dv_acc[source, :].astype(jnp.bfloat16)

        start_all(out_copies(blk))

    for blk in range(blocks):
        for copy in out_copies(blk):
            copy.wait()


def attention_backward(
    doc_lengths, query_low, attended, inverse, gate_pre, kv_all, back_rows, out_w
):
    rows, width = query_low.shape
    keys, kv_width = kv_all.shape[0], kv_all.shape[1] // 2
    groups = kv_width // LANES
    per = width // kv_width
    blocks, wide_count = lax.axis_size("head"), lax.axis_size("wide")
    low, full = jnp.bfloat16, jnp.float32
    shape, vm = jax.ShapeDtypeStruct, pltpu.VMEM
    return pl.pallas_call(
        attention_backward_kernel,
        out_shape=(
            shape((rows, width), full),
            shape((wide_count, rows, 2 * kv_width), low),
            shape((rows, width), low),
        ),
        in_specs=[pl.BlockSpec(memory_space=pltpu.SMEM)] + [ANY] * 7,
        out_specs=(ANY, ANY, ANY),
        scratch_shapes=[
            vm((rows, width), low), vm((rows, width), full), vm((rows, width), full),
            vm((rows, width), full), vm(kv_all.shape, low), vm(back_rows.shape, low),
            vm(out_w.shape, low), vm((rows, width), full),
            vm((wide_count, rows, 2 * kv_width), low), vm((rows, width), low),
            vm((keys, kv_width), full), vm((keys, kv_width), full),
            vm((groups, LANES, per * (rows // blocks)), full), vm((kv_width, keys), low),
            vm((rows, width), full),
            DMA((7,)), DMA((3, blocks)),
        ],
        compiler_params=pltpu.CompilerParams(vmem_limit_bytes=VMEM_LIMIT),
        cost_estimate=pl.CostEstimate(
            flops=10 * rows * width * 2048, bytes_accessed=20 << 20, transcendentals=0
        ),
        name="attention_backward",
    )(
        doc_lengths, query_low, attended, inverse, gate_pre, kv_all, back_rows, out_w
    )


def ffn_kernel(
    gated_ref, gain_ref, x_any, cot_any, left_any, wo_any, wg_any, wu_any, wd_any,
    out_any, mgrad_ref, gain_out, back_any, down_any, fgate_any, fup_any, owg_any,
    wo, wg, wu, wd, cots, rows, hid, gg, ug, terms_own, outs_own, passed, into,
    passed2, into2, dterms, dinto, hterms, hinto, middle, back, local_sem,
    ds, dr, hs, hr, cs, cr, cps, cpr, fs, fr, fps, fpr, s1, r1, ps1, pr1, s2, r2, ps2, pr2, bs, br,
):
    tok, width = x_any.shape
    hidden_width = wg_any.shape[1]
    head, wide = head_ring(), wide_ring()
    pair = 2 * tok
    separate = terms_own.shape[0] > 16
    terms = terms_own if separate else cots
    outs = outs_own if separate else rows
    part = wo_any.shape[1] // lax.axis_size("head")
    loads = [
        pltpu.make_async_copy(src, dst, local_sem.at[i])
        for i, (src, dst) in enumerate(((wo_any, wo), (wd_any, wd), (wg_any, wg), (wu_any, wu)))
    ]
    split = left_any.shape[1]
    loads.append(pltpu.make_async_copy(left_any, cots.at[:, pl.ds(0, split)], local_sem.at[10]))
    for load in loads:
        load.start()
    own_wide = pl.multiple_of(lax.axis_index("wide") * tok, tok)
    own_head = pl.multiple_of(lax.axis_index("head") * tok, tok)
    own_loads = [
        pltpu.make_async_copy(
            cot_any.at[:, pl.ds(split, width - split)],
            cots.at[pl.ds(own_wide, tok), pl.ds(split, width - split)],
            local_sem.at[12],
        ),
        pltpu.make_async_copy(x_any, back.at[pl.ds(own_head, tok)], local_sem.at[13]),
    ]
    start_all(own_loads)
    meet(neighbours(head, wide))
    own_loads[0].wait()

    def slot_of(ref):
        return lambda index, start, size: ref.at[pl.ds(index * tok + start, size)]

    def cot_slot(index, start, size):
        return cots.at[pl.ds(index * tok + start, size), pl.ds(split, width - split)]

    cot_gather = PairGather(wide, cot_slot, tok, cs, cr, cps, cpr)
    row_gather = row_gather_of(wide)(wide, slot_of(rows), tok, fs, fr, fps, fpr)
    back_gather = Gather(head, slot_of(back), tok, bs, br)
    head_scatter = Scatter(head, lambda index: (hterms, index * tok), tok, hinto, hs, hr)
    grad_scatter = scatter_of(wide)(wide, terms, tok, passed, into, s1, r1, ps1, pr1)
    down_scatter = Scatter(
        head, lambda index: (dterms, index * hidden_width), hidden_width, dinto, ds, dr
    )
    out_scatter = scatter_of(wide)(wide, outs, tok, passed2, into2, s2, r2, ps2, pr2)

    def group_of(offset):
        return pl.ds(pl.multiple_of(wide.index(offset) * pair, pair), pair)

    def col_loop(total, step, body):
        @pl.loop(0, total // step)
        def _(i):
            body(pl.ds(pl.multiple_of(i * step, step), step))

    tile = 256
    line = wide.size == 4
    cot_gather.begin()

    def out_part(offset, own):
        index = head.index(offset)
        here = pl.ds(pl.multiple_of(index * tok, tok), tok)

        def body(cols):
            value = dot_nn(gated_ref[here, :], wo[:, cols])
            if own:
                middle[:, cols] = back[pl.ds(own_head, tok), cols].astype(jnp.float32) + value
            else:
                hterms[here, cols] = value.astype(jnp.bfloat16)

        col_loop(width, tile, body)

    def hidden_part(offset):
        here = group_of(offset)

        def body(cols):
            hid[here, cols] = dot_nt(cots[here, :], wd[cols, :]).astype(jnp.bfloat16)

        col_loop(hidden_width, hidden_width, body)

    loads[0].wait()
    own_loads[1].wait()
    out_part(head.half, False)
    head_scatter.start(head.half)
    for hop in range(head.half - 1, 0, -1):
        out_part(hop, False)
        out_part(-hop, False)
        if hop == head.half - 1:
            head_scatter.start_free()
    out_part(0, True)
    loads[1].wait()
    loads[4].wait()
    mgrad_ref[...] = cots[pl.ds(own_wide, tok), :].astype(jnp.float32)
    cot_gather.take(0)
    hidden_part(0)
    for hop in range(head.half - 1, 0, -1):
        head_scatter.advance(hop)
    for hop in range(1, wide.half):
        cot_gather.arrive(hop)
        cot_gather.start(hop + 1)
        cot_gather.hand(hop)
        cot_gather.take(hop)
        hidden_part(hop)
        hidden_part(-hop)
    head_scatter.arrive()

    gain = gain_ref[...]

    def forward_norm(row):
        here = pl.ds(row, 32)
        value = (
            middle[here, :]
            + hinto[0, here, :].astype(jnp.float32)
            + hinto[1, here, :].astype(jnp.float32)
        )
        middle[here, :] = value
        scale = lax.rsqrt(jnp.mean(value * value, axis=-1, keepdims=True) + EPS)
        rows[pl.ds(pl.multiple_of(own_wide + row, 32), 32), :] = (value * scale * gain).astype(
            jnp.bfloat16
        )

    row_loop(tok, 32, forward_norm)
    row_gather.begin()
    cot_gather.arrive(wide.half)
    cot_gather.hand(wide.half)
    cot_gather.take(wide.half)
    hidden_part(wide.half)
    cot_gather.finish()
    loads[2].wait()
    loads[3].wait()

    def unit(offset):
        here = group_of(offset)

        def body(cols):
            gate = dot_nn(rows[here, :], wg[:, cols])
            up = dot_nn(rows[here, :], wu[:, cols])
            grad = hid[here, cols].astype(jnp.float32)
            sig = jax.nn.sigmoid(gate)
            act = gate * sig
            hid[here, cols] = (act * up).astype(jnp.bfloat16)
            gg[here, cols] = (grad * up * (sig + act * (1.0 - sig))).astype(jnp.bfloat16)
            ug[here, cols] = (grad * act).astype(jnp.bfloat16)

        col_loop(hidden_width, tile if hidden_width % tile == 0 else LANES, body)

    def down_terms(offset):
        here = group_of(offset)

        def body(cols):
            outs[here, cols] = dot_nn(hid[here, :], wd[:, cols]).astype(jnp.bfloat16)

        col_loop(width, width, body)
        if not line:
            out_scatter.hand(offset)

    def down_grads(group, add):
        @pl.loop(0, lax.axis_size("head"))
        def _(index):
            cols = pl.ds(pl.multiple_of(index * part, part), part)
            there = pl.ds(pl.multiple_of(index * hidden_width, LANES), hidden_width)
            value = sum(
                dot_tn(hid[group_of(offset), :], cots[group_of(offset), cols]) for offset in group
            )
            if add:
                value += dterms[there, :].astype(jnp.float32)
            dterms[there, :] = value.astype(jnp.bfloat16)

    def grad_terms(offset):
        here = group_of(offset)

        def body(cols):
            value = dot_nt(gg[here, :], wg[cols, :]) + dot_nt(ug[here, :], wu[cols, :])
            terms[here, cols] = value.astype(jnp.bfloat16)

        col_loop(width, 1024, body)

    emit = 256

    def stage_of(out, slot):
        cols = pl.ds(out * hidden_width, hidden_width)
        return hterms.at[pl.ds(slot * emit, emit), cols]

    def stage_copy(step, out, any_ref, slot):
        there = pl.ds(pl.multiple_of(step * emit, emit), emit)
        return pltpu.make_async_copy(
            stage_of(out, slot), any_ref.at[there], local_sem.at[5 + 2 * slot + out]
        )

    def input_grads():
        head_scatter.finish()

        @pl.loop(0, width // emit // 2)
        def _(i):
            for slot in SIDES:
                step = 2 * i + slot
                cols = pl.ds(pl.multiple_of(step * emit, emit), emit)

                @pl.when(i > 0)
                def _():
                    for out, any_ref in enumerate((fgate_any, fup_any)):
                        stage_copy(step - 2, out, any_ref, slot).wait()

                left = rows[:, cols]
                stage_of(0, slot)[...] = dot_tn(left, gg[...]).astype(jnp.bfloat16)
                stage_of(1, slot)[...] = dot_tn(left, ug[...]).astype(jnp.bfloat16)
                for out, any_ref in enumerate((fgate_any, fup_any)):
                    stage_copy(step, out, any_ref, slot).start()

    order = offsets(wide)

    def near_part(offset):
        unit(offset)
        if separate:
            down_terms(offset)

    def down_pass(kind):
        offset = out_scatter.offset(kind)
        down_terms(offset)
        out_scatter.hand_kind(kind)

    if line:

        def arrived(kind):
            row_gather.arrive(kind)
            row_gather.take(kind)
            unit(row_gather.offset(kind))
            grad_terms(grad_scatter.offset(kind))
            grad_scatter.hand_kind(kind)

        row_gather.take(None)
        unit(0)
        down_pass(None)
        down_grads([0], False)
        arrived(NEAR)
        down_pass(NEAR)
        grad_scatter.merge_kind(NEAR)
        grad_scatter.launch(NEAR)

        @pl.when(row_gather.middle)
        def _():
            arrived(OTHER)
            down_pass(OTHER)
            grad_scatter.merge_kind(OTHER)

        arrived(FAR)
        grad_scatter.merge_kind(FAR)
        grad_scatter.launch(FAR)

        @pl.when(~row_gather.middle)
        def _():
            arrived(OTHER)
            grad_scatter.merge_kind(OTHER)

        grad_scatter.launch(OTHER)
        pl.when(~row_gather.middle)(functools.partial(down_pass, OTHER))
        down_pass(FAR)
        grad_terms(0)
        grad_scatter.hand_kind(None)
        down_grads([1, 2, 3], True)
        down_scatter.start(head.half)
        down_scatter.start_free()
        grad_scatter.relay(OTHER)
        for kind in (OTHER, FAR, NEAR, None):
            out_scatter.merge_kind(kind)
        input_grads()
        out_scatter.launch(OTHER, FAR, NEAR)
        grad_scatter.merge_kind(None)
        grad_scatter.relay(FAR)
        grad_scatter.relay(NEAR)
    else:
        row_gather.take(0)
        near_part(0)
        if separate:
            down_grads([0], False)
        for hop in range(1, wide.half):
            row_gather.arrive(hop)
            row_gather.start(hop + 1)
            row_gather.hand(hop)
            row_gather.take(hop)
            near_part(hop)
            near_part(-hop)
        row_gather.arrive(wide.half)
        row_gather.hand(wide.half)
        row_gather.take(wide.half)
        unit(wide.half)
        if not separate:
            down_grads(order, False)
            down_scatter.start(head.half)
        for offset in order:
            grad_terms(offset)
            grad_scatter.hand(offset)
        grad_scatter.merge(order[0])
        grad_scatter.start(wide.half)
        if separate:
            down_grads(order[:-1], True)
            down_scatter.start(head.half)
            down_terms(order[0])
        for hop in range(wide.half - 1, 0, -1):
            grad_scatter.merge(hop)
            grad_scatter.merge(-hop)
            grad_scatter.advance(hop)
        grad_scatter.merge(0)
        input_grads()
    row_gather.finish()
    if not line:
        if not separate:
            for offset in order:
                down_terms(offset)
        out_scatter.merge(order[0])
    for hop in range(head.half - 1, 0, -1):
        down_scatter.advance(hop)
    grad_scatter.arrive()

    def backward_norm(row, gain_sum):
        here = pl.ds(row, 32)
        value = middle[here, :]
        grad = grad_scatter.total(row, 32)
        scale = lax.rsqrt(jnp.mean(value * value, axis=-1, keepdims=True) + EPS)
        scaled = value * scale
        weighted = grad * gain
        mean = jnp.mean(scaled * weighted, axis=-1, keepdims=True)
        total = mgrad_ref[here, :] + scale * (weighted - scaled * mean)
        mgrad_ref[here, :] = total
        back[pl.ds(pl.multiple_of(own_head + row, 32), 32), :] = total.astype(jnp.bfloat16)
        return gain_sum + jnp.sum(grad * scaled, axis=0, keepdims=True)

    gain_out[...] = lax.fori_loop(
        0, tok // 32,
        lambda i, carried: backward_norm(pl.multiple_of(i * 32, 32), carried),
        jnp.zeros((1, width), jnp.float32),
    )
    back_gather.start(1)
    if line:
        for kind in (FAR, OTHER, NEAR):
            out_scatter.relay(kind)
    else:
        out_scatter.start(wide.half)
        for offset in order[1:]:
            out_scatter.merge(offset)
        for hop in range(wide.half - 1, 0, -1):
            out_scatter.advance(hop)
    for hop in range(1, head.half):
        back_gather.step(hop)
    back_gather.arrive(head.half)
    back_gather.finish()
    keep = pltpu.make_async_copy(back, back_any, local_sem.at[4])
    keep.start()
    last = width // emit
    for slot in SIDES:
        for out, any_ref in enumerate((fgate_any, fup_any)):
            stage_copy(last - 2 + slot, out, any_ref, slot).wait()
    owners = gated_ref.shape[1]

    def out_grads(cols):
        hterms[pl.ds(0, owners), cols] = dot_tn(gated_ref[...], back[:, cols]).astype(jnp.bfloat16)

    col_loop(width, 512, out_grads)
    share = pltpu.make_async_copy(hterms.at[pl.ds(0, owners)], owg_any, local_sem.at[11])
    share.start()
    down_scatter.arrive()
    own_down = pl.multiple_of(lax.axis_index("head") * hidden_width, LANES)

    def finish_down(row):
        there = pl.ds(pl.multiple_of(own_down + row, LANES), LANES)
        dterms[there, :] = down_scatter.total(row, LANES).astype(jnp.bfloat16)

    row_loop(hidden_width, LANES, finish_down)
    down_out = pltpu.make_async_copy(
        dterms.at[pl.ds(own_down, hidden_width)], down_any, local_sem.at[14]
    )
    down_out.start()
    out_scatter.arrive()

    def finish_out(row):
        here = pl.ds(row, 32)
        back[here, :] = (middle[here, :] + out_scatter.total(row, 32)).astype(jnp.bfloat16)

    keep.wait()
    row_loop(tok, 32, finish_out)
    result = pltpu.make_async_copy(back.at[pl.ds(0, tok)], out_any, local_sem.at[9])
    result.start()

    for scatter in (grad_scatter, out_scatter, down_scatter):
        scatter.finish()
    result.wait()
    share.wait()
    down_out.wait()


def ffn_block(gated_low, inputs, cotangent, cot_left, ffn_gain, out_w, gate_w, up_w, down_w):
    tok, width = inputs.shape
    head_count, wide_count = lax.axis_size("head"), lax.axis_size("wide")
    chips = wide_count // 2
    hidden_width = gate_w.shape[1]
    low, full = jnp.bfloat16, jnp.float32
    all_rows = wide_count * tok
    back_rows = head_count * tok
    roomy = all_rows * width <= 2 << 20
    shape = jax.ShapeDtypeStruct
    vm = pltpu.VMEM
    return pl.pallas_call(
        ffn_kernel,
        out_shape=(
            shape((tok, width), low),
            shape((tok, width), full),
            shape((1, width), full),
            shape((back_rows, width), low),
            shape((hidden_width, width // head_count), low),
            shape((width, hidden_width), low),
            shape((width, hidden_width), low),
            shape((gated_low.shape[1], width), low),
        ),
        in_specs=[VMEM] * 2 + [ANY] * 7,
        out_specs=(ANY, VMEM, VMEM, ANY, ANY, ANY, ANY, ANY),
        scratch_shapes=[
            vm(out_w.shape, low), vm(gate_w.shape, low), vm(up_w.shape, low),
            vm(down_w.shape, low),
            vm((all_rows, width), low), vm((all_rows, width), low),
            vm((all_rows, hidden_width), low), vm((all_rows, hidden_width), low),
            vm((all_rows, hidden_width), low),
            vm((all_rows if roomy else 16, width), low),
            vm((all_rows if roomy else 16, width), low),
            vm((chips, tok, width), low),
            scatter_into(chips, tok, width),
            vm((chips, tok, width), low),
            scatter_into(chips, tok, width),
            vm((head_count * hidden_width, width // head_count), low),
            into_shape(head_count, hidden_width, width // head_count),
            vm((back_rows, width), low), into_shape(head_count, tok, width),
            vm((tok, width), full), vm((back_rows, width), low),
            DMA((15,)),
            *ring_sems(head_count),
            *ring_sems(head_count),
            *ring_sems(chips), *pass_sems(chips),
            *gather_sems(chips),
            *scatter_sems(chips),
            *scatter_sems(chips),
            *ring_sems(head_count),
        ],
        compiler_params=pltpu.CompilerParams(
            collective_id=1, has_side_effects=True, vmem_limit_bytes=VMEM_LIMIT
        ),
        cost_estimate=pl.CostEstimate(
            flops=10 * all_rows * width * hidden_width, bytes_accessed=200 << 20, transcendentals=0
        ),
        name="ffn_block",
    )(
        gated_low, ffn_gain[None], inputs, cotangent, cot_left, out_w, gate_w, up_w, down_w
    )


def turn(values, cosine, sine_tab):
    half = LANES // 2
    lane = lax.broadcasted_iota(jnp.int32, values.shape, 1)
    turned = pltpu.roll(values, half, 1)
    return values * cosine + jnp.where(lane < half, -turned, turned) * sine_tab


def prep(pre_proj, gain, cosine, sine_tab):
    scale = lax.rsqrt(jnp.mean(pre_proj * pre_proj, axis=-1, keepdims=True) + EPS)
    return turn(pre_proj * scale * gain, cosine, sine_tab).astype(jnp.bfloat16)


def front_kernel(
    doc_ref, x_ref, gain_ref, speed_ref, qgain_ref, kgain_ref, wq_any, wk_any, wv_any, wg_any,
    query_ref, qpre_ref, kpre_ref, gpre_ref, cos_ref, sin_ref, normed_any, kv_any,
    wq, wk, wv, wg, normed, kv, local_sem, hs, hr, ks, kr, kps, kpr,
):
    tok, width = x_ref.shape
    kv_width = wk_any.shape[1]
    q_width = wq_any.shape[1]
    wide_count, head_count = lax.axis_size("wide"), lax.axis_size("head")
    head, wide = head_ring(), wide_ring()
    loads = [
        pltpu.make_async_copy(src, dst, local_sem.at[i])
        for i, (src, dst) in enumerate(((wk_any, wk), (wv_any, wv), (wq_any, wq), (wg_any, wg)))
    ]
    for load in loads:
        load.start()
    own = pl.multiple_of(lax.axis_index("head") * tok, tok)
    own_wide = lax.axis_index("wide")

    def norm(row):
        here = pl.ds(row, 32)
        value = x_ref[here, :].astype(jnp.float32)
        scale = lax.rsqrt(jnp.mean(value * value, axis=-1, keepdims=True) + EPS)
        normed[pl.ds(pl.multiple_of(own + row, 32), 32), :] = (
            value * scale * gain_ref[...]
        ).astype(jnp.bfloat16)

    row_loop(tok, 32, norm)
    meet(neighbours(head, wide))
    gather = Gather(
        head, lambda index, start, size: normed.at[pl.ds(index * tok + start, size)], tok, hs, hr
    )
    gather.start(1)
    ends = doc_ends(doc_ref)

    @pl.loop(0, head_count)
    def _(block):
        here = pl.ds(pl.multiple_of(block * tok, tok), tok)
        first_tok = (block * wide_count + own_wide) * tok
        tokens = lax.broadcasted_iota(jnp.int32, (tok, LANES), 0) + first_tok
        angles = (tokens - first_of(ends, tokens)).astype(jnp.float32) * speed_ref[...]
        cos_ref[here, :] = jnp.cos(angles)
        sin_ref[here, :] = jnp.sin(angles)

    def kv_gather(offset):
        slot = offset % head_count
        block = head.index(offset)

        def place(index, start, size):
            return kv.at[pl.ds((block * wide_count + index) * tok + start, size)]

        return row_gather_of(wide)(
            wide, place, tok, ks.at[slot], kr.at[slot], kps.at[slot], kpr.at[slot]
        )

    def project(offset):
        block = head.index(offset)
        here = pl.ds(pl.multiple_of(block * tok, tok), tok)
        there = pl.ds(pl.multiple_of((block * wide_count + own_wide) * tok, tok), tok)
        left = normed[here, :]
        cosine, sine_tab = cos_ref[here, :], sin_ref[here, :]
        pre = dot_nn(left, wk[...])
        kpre_ref[here, :] = pre
        for j in range(kv_width // LANES):
            cols = slice(j * LANES, (j + 1) * LANES)
            kv[there, cols] = prep(pre[:, cols], kgain_ref[...], cosine, sine_tab)
        kv[there, kv_width:] = dot_nn(left, wv[...]).astype(jnp.bfloat16)

    def project_rest(offset):
        block = head.index(offset)
        here = pl.ds(pl.multiple_of(block * tok, tok), tok)
        left = normed[here, :]
        cosine, sine_tab = cos_ref[here, :], sin_ref[here, :]
        pre = dot_nn(left, wq[...])
        qpre_ref[here, :] = pre
        for j in range(q_width // LANES):
            cols = slice(j * LANES, (j + 1) * LANES)
            query_ref[here, cols] = prep(pre[:, cols], qgain_ref[...], cosine, sine_tab)
        gpre_ref[here, :] = dot_nn(left, wg[...])

    gathers = {}

    def launch(offset):
        project(offset)
        gathers[offset] = kv_gather(offset)
        gathers[offset].begin()

    line = wide.size == 4

    def step(offset, hop):
        each = gathers[offset]
        if line and hop == 1:
            each.arrive(NEAR)

            @pl.when(each.middle)
            def _():
                each.arrive(OTHER)

        elif line:
            each.arrive(FAR)

            @pl.when(~each.middle)
            def _():
                each.arrive(OTHER)

        else:
            each.arrive(hop)
            if hop < wide.half:
                each.start(hop + 1)
            each.hand(hop)

    loads[0].wait()
    loads[1].wait()
    launch(0)
    loads[2].wait()
    loads[3].wait()
    project_rest(0)
    done = [0]
    for hop in range(1, head.half + 1):
        if hop < head.half:
            gather.step(hop)
            launch(hop)
            launch(-hop)
            for offset in done:
                step(offset, 1)
            project_rest(hop)
            project_rest(-hop)
            done = [hop, -hop]
        else:
            gather.arrive(hop)
            launch(hop)
            for offset in done:
                step(offset, 1)
            project_rest(hop)
            done = [hop]
    gather.finish()
    keep = pltpu.make_async_copy(normed, normed_any, local_sem.at[4])
    keep.start()
    for offset in done:
        step(offset, 1)
    for hop in range(2, wide.half + 1):
        for offset in gathers:
            step(offset, hop)
    for each in gathers.values():
        for hop in (None, NEAR, OTHER, FAR) if line else range(wide.half + 1):
            each.take(hop)
    store = pltpu.make_async_copy(kv, kv_any, local_sem.at[5])
    store.start()
    for each in gathers.values():
        each.finish()
    store.wait()
    keep.wait()


def front_block(doc_lengths, inputs, attn_gain, speed, query_gain, key_gain, weights):
    tok, width = inputs.shape
    head_count, wide_count = lax.axis_size("head"), lax.axis_size("wide")
    chips = wide_count // 2
    q_width, kv_width = weights[0].shape[1], weights[1].shape[1]
    rows = head_count * tok
    low, full = jnp.bfloat16, jnp.float32
    shape, vm = jax.ShapeDtypeStruct, pltpu.VMEM
    return pl.pallas_call(
        front_kernel,
        out_shape=(
            shape((rows, q_width), low),
            shape((rows, q_width), full),
            shape((rows, kv_width), full),
            shape((rows, q_width), full),
            shape((rows, LANES), full),
            shape((rows, LANES), full),
            shape((rows, width), low),
            shape((rows * wide_count, 2 * kv_width), low),
        ),
        in_specs=[pl.BlockSpec(memory_space=pltpu.SMEM)] + [VMEM] * 5 + [ANY] * 4,
        out_specs=tuple([VMEM] * 6 + [ANY] * 2),
        scratch_shapes=[
            *[vm(weight.shape, low) for weight in weights],
            vm((rows, width), low),
            vm((rows * wide_count, 2 * kv_width), low),
            DMA((6,)),
            *ring_sems(head_count),
            *[DMA((head_count, *sem.shape)) for sem in gather_sems(chips)],
        ],
        compiler_params=pltpu.CompilerParams(
            collective_id=3, has_side_effects=True, vmem_limit_bytes=VMEM_LIMIT
        ),
        cost_estimate=pl.CostEstimate(
            flops=2 * rows * width * (2 * q_width + 2 * kv_width), bytes_accessed=100 << 20,
            transcendentals=0,
        ),
        name="front_block",
    )(
        doc_lengths, inputs, attn_gain[None], speed[None], query_gain[None], key_gain[None],
        *weights,
    )


def turn_back(grad, cosine, sine_tab):
    half = LANES // 2
    lane = lax.broadcasted_iota(jnp.int32, grad.shape, 1)
    turned = pltpu.roll(grad * sine_tab, half, 1)
    return grad * cosine + jnp.where(lane < half, turned, -turned)


def unprep(grad, pre_proj, gain, cosine, sine_tab):
    turned = turn_back(grad, cosine, sine_tab)
    scale = lax.rsqrt(jnp.mean(pre_proj * pre_proj, axis=-1, keepdims=True) + EPS)
    scaled = pre_proj * scale
    weighted = turned * gain
    mean = jnp.mean(scaled * weighted, axis=-1, keepdims=True)
    return scale * (weighted - scaled * mean), turned * scaled


def tail_kernel(
    cos_ref, sin_ref, qgain_ref, kgain_ref, gain_ref, ffn_gain_ref,
    dq_any, qpre_any, kpre_any, ggrad_any, x_any, mgrad_any,
    kvp_any, normed_any, wq_any, wk_any, wv_any, wg_any, fgate_any, fup_any,
    igrad_ref, gains_ref, query_out, key_out, value_out, gate_out, fgate_out, fup_out,
    dq_ref, qpre_ref, kpre_ref, ggrad_ref, x_ref, mgrad_ref, kvp, normed, wq, wk, wv, wg, fgate, fup, qlow, klow, vlow, early, late, hterms,
    kv_passed, kv_into, early_passed, early_into, late_passed, late_into, hinto, fgate_into,
    fup_into, gain_slots, local_sem,
    kvs, kvr, kvps, kvpr, es, er, eps, epr, ls, lr, lps, lpr, hs, hr, gs, gr, us, ur, gain_send,
    gain_recv,
):
    tok, width = x_ref.shape
    rows = dq_ref.shape[0]
    wide_count = lax.axis_size("wide")
    head_count = lax.axis_size("head")
    head, wide = head_ring(), wide_ring()
    loads = [
        pltpu.make_async_copy(src, dst, local_sem.at[i])
        for i, (src, dst) in enumerate(
            (
                (kvp_any, kvp), (fgate_any, fgate), (fup_any, fup), (normed_any, normed),
                (wq_any, wq), (wk_any, wk), (wv_any, wv), (wg_any, wg),
            )
        )
    ]
    more = [
        pltpu.make_async_copy(src, dst, local_sem.at[11 + i])
        for i, (src, dst) in enumerate(
            (
                (dq_any, dq_ref), (qpre_any, qpre_ref), (ggrad_any, ggrad_ref),
                (kpre_any, kpre_ref), (x_any, x_ref), (mgrad_any, mgrad_ref),
            )
        )
    ]
    start_all(loads[:1] + more[:3] + loads[1:] + more[3:])
    meet(everyone(head, wide))
    kv_width = wk.shape[1]
    q_width = wq.shape[1]
    block = normed.shape[1] // wide_count
    ffn_rows = fgate.shape[0] // head_count
    kv_scatter = PairScatter(wide, kvp, rows, kv_passed, kv_into, kvs, kvr, kvps, kvpr)
    early_scatter = PairScatter(wide, early, block, early_passed, early_into, es, er, eps, epr)
    late_scatter = PairScatter(wide, late, block, late_passed, late_into, ls, lr, lps, lpr)
    head_scatter = Scatter(head, lambda index: (hterms, index * tok), tok, hinto, hs, hr)
    gate_scatter = Scatter(
        head, lambda index: (fgate, index * ffn_rows), ffn_rows, fgate_into, gs, gr
    )
    up_scatter = Scatter(head, lambda index: (fup, index * ffn_rows), ffn_rows, fup_into, us, ur)
    order = offsets(wide)

    loads[0].wait()
    for offset in order:
        kv_scatter.hand(offset)
    loads[1].wait()
    gate_scatter.start(head.half)
    gate_scatter.start_free()
    loads[2].wait()
    up_scatter.start(head.half)
    up_scatter.start_free()

    for load in more[:3]:
        load.wait()
    chunk = 128

    def query_back(row, total):
        here = pl.ds(row, chunk)
        for j in range(q_width // LANES):
            cols = slice(j * LANES, (j + 1) * LANES)
            value, terms = unprep(
                dq_ref[here, cols], qpre_ref[here, cols], qgain_ref[...], cos_ref[here, :],
                sin_ref[here, :],
            )
            qlow[here, cols] = value.astype(jnp.bfloat16)
            total = total + jnp.sum(terms, axis=0, keepdims=True)
        return total

    def over_rows(count, body, start):
        return lax.fori_loop(
            0, count // chunk, lambda i, carried: body(pl.multiple_of(i * chunk, chunk), carried),
            start,
        )

    qgain_sum = over_rows(rows, query_back, jnp.zeros((1, LANES), jnp.float32))

    kv_scatter.merge(order[0])
    kv_scatter.start(wide.half)
    for offset in order[1:]:
        kv_scatter.merge(offset)
    kv_scatter.start_free()
    loads[3].wait()

    def early_part(offset):
        index = wide.index(offset)

        @pl.loop(0, 2)
        def _(core):
            target = 2 * index + core
            cols = pl.ds(pl.multiple_of(target * block, block), block)
            there = pl.ds(pl.multiple_of(target * block, block), block)
            left = normed[:, cols]
            early[there, :q_width] = dot_tn(left, qlow[...]).astype(jnp.bfloat16)
            early[there, q_width:] = dot_tn(left, ggrad_ref[...]).astype(jnp.bfloat16)

    for offset in order:
        early_part(offset)
        early_scatter.hand(offset)
    early_scatter.merge(order[0])
    for hop in range(wide.half - 1, 0, -1):
        kv_scatter.advance(hop)
    early_scatter.start(wide.half)
    for offset in order[1:]:
        early_scatter.merge(offset)
    early_scatter.start_free()
    for hop in range(head.half - 1, 0, -1):
        gate_scatter.advance(hop)
        up_scatter.advance(hop)
    for load in loads[4:] + more[3:]:
        load.wait()
    kv_scatter.arrive()
    for hop in range(wide.half - 1, 0, -1):
        early_scatter.advance(hop)

    def key_back(row, total):
        here = pl.ds(row, chunk)
        both = kv_scatter.total(row, chunk)
        for j in range(kv_width // LANES):
            cols = slice(j * LANES, (j + 1) * LANES)
            value, terms = unprep(
                both[:, cols], kpre_ref[here, cols], kgain_ref[...], cos_ref[here, :],
                sin_ref[here, :],
            )
            klow[here, cols] = value.astype(jnp.bfloat16)
            total = total + jnp.sum(terms, axis=0, keepdims=True)
        vlow[here, :] = both[:, kv_width:].astype(jnp.bfloat16)
        return total

    kgain_sum = over_rows(rows, key_back, jnp.zeros((1, LANES), jnp.float32))

    def head_part(offset):
        here = pl.ds(pl.multiple_of(head.index(offset) * tok, tok), tok)

        @pl.loop(0, width // 256)
        def _(i):
            cols = pl.ds(pl.multiple_of(i * 256, 256), 256)
            value = dot_nt(qlow[here, :], wq[cols, :]) + dot_nt(ggrad_ref[here, :], wg[cols, :])
            value += dot_nt(klow[here, :], wk[cols, :]) + dot_nt(vlow[here, :], wv[cols, :])
            hterms[here, cols] = value.astype(jnp.bfloat16)

    head_part(head.half)
    head_scatter.start(head.half)

    def late_part(offset):
        index = wide.index(offset)

        @pl.loop(0, 2)
        def _(core):
            target = 2 * index + core
            cols = pl.ds(pl.multiple_of(target * block, block), block)
            left = normed[:, cols]
            late[cols, :kv_width] = dot_tn(left, klow[...]).astype(jnp.bfloat16)
            late[cols, kv_width:] = dot_tn(left, vlow[...]).astype(jnp.bfloat16)

    for offset in order:
        late_part(offset)
        late_scatter.hand(offset)
    late_scatter.merge(order[0])
    late_scatter.start(wide.half)
    for offset in order[1:]:
        late_scatter.merge(offset)
    late_scatter.start_free()
    for hop in range(head.half - 1, 0, -1):
        head_part(hop)
        head_part(-hop)
        head_scatter.advance(hop)
    head_part(0)
    for hop in range(wide.half - 1, 0, -1):
        late_scatter.advance(hop)

    gate_scatter.arrive()
    up_scatter.arrive()
    own_ffn = pl.multiple_of(lax.axis_index("head") * ffn_rows, ffn_rows)
    pending = []
    for scatter, ref, out in ((gate_scatter, fgate, fgate_out), (up_scatter, fup, fup_out)):

        def finish_ffn(row, scatter=scatter, ref=ref):
            there = pl.ds(pl.multiple_of(own_ffn + row, 64), 64)
            ref[there, :] = scatter.total(row, 64).astype(jnp.bfloat16)

        row_loop(ffn_rows, 64, finish_ffn)
        pending.append(
            pltpu.make_async_copy(
                ref.at[pl.ds(own_ffn, ffn_rows)], out, local_sem.at[9 + len(pending)]
            )
        )
        pending[-1].start()

    head_scatter.arrive()
    gain = gain_ref[...]

    def input_back(row, total):
        here = pl.ds(row, 32)
        value = x_ref[here, :].astype(jnp.float32)
        grad = head_scatter.total(row, 32)
        scale = lax.rsqrt(jnp.mean(value * value, axis=-1, keepdims=True) + EPS)
        scaled = value * scale
        weighted = grad * gain
        mean = jnp.mean(scaled * weighted, axis=-1, keepdims=True)
        igrad_ref[here, :] = mgrad_ref[here, :] + scale * (weighted - scaled * mean)
        return total + jnp.sum(grad * scaled, axis=0, keepdims=True)

    gain_sum = lax.fori_loop(
        0, tok // 32, lambda i, carried: input_back(pl.multiple_of(i * 32, 32), carried),
        jnp.zeros((1, width), jnp.float32),
    )
    chips = wide.size
    pair_slot, chip_slot = 0, 2
    head_slot = 2 + chips
    mine = gain_slots.at[pair_slot]
    mine[...] = jnp.zeros(mine.shape, jnp.float32)
    mine[0:1, :] = gain_sum
    mine[1:2, :] = ffn_gain_ref[...]
    mine[2:3, 0:LANES] = qgain_sum
    mine[3:4, 0:LANES] = kgain_sum
    swap = remote(
        mine, gain_slots.at[1], gain_send.at[0], gain_recv.at[0], wide.sibling
    )
    swap.start()
    swap.wait_recv()

    def spread(ring, own, base, sem):
        here = gain_slots.at[base + own]
        copies = [
            remote(here, here, gain_send.at[sem + d], gain_recv.at[sem + d], ring.device(d))
            for d in range(1, ring.size)
        ]
        for copy in copies:
            copy.start()
        for copy in copies:
            copy.wait_recv()
        return copies

    own_chip = wide.index(0)
    gain_slots[chip_slot + own_chip] = gain_slots[0] + gain_slots[1]
    sent = [swap] + spread(wide, own_chip, chip_slot, 0)
    total = gain_slots[chip_slot]
    for i in range(1, chips):
        total = total + gain_slots[chip_slot + i]
    own_head = lax.axis_index("head")
    gain_slots[head_slot + own_head] = total
    sent += spread(head, own_head, head_slot, chips - 1)
    total = gain_slots[head_slot]
    for i in range(1, head_count):
        total = total + gain_slots[head_slot + i]
    gains_ref[...] = total

    early_scatter.arrive()

    def early_out(row):
        here = pl.ds(row, 32)
        both = early_scatter.total(row, 32)
        query_out[here, :] = both[:, :q_width].astype(jnp.bfloat16)
        gate_out[here, :] = both[:, q_width:].astype(jnp.bfloat16)

    row_loop(block, 32, early_out)
    late_scatter.arrive()

    def late_out(row):
        here = pl.ds(row, 32)
        both = late_scatter.total(row, 32)
        key_out[here, :] = both[:, :kv_width].astype(jnp.bfloat16)
        value_out[here, :] = both[:, kv_width:].astype(jnp.bfloat16)

    row_loop(block, 32, late_out)
    for scatter in (
        kv_scatter, early_scatter, late_scatter, head_scatter, gate_scatter, up_scatter
    ):
        scatter.finish()
    for copy in sent:
        copy.wait_send()
    for copy in pending:
        copy.wait()


def tail_block(
    dq, kv_parts, query_pre, key_pre, gate_grad, cosine, sine_tab, query_gain, key_gain, inputs,
    middle_grad, attn_gain, ffn_gain_part, normed, weights, fgate, fup,
):
    tok, width = inputs.shape
    head_count, wide_count = lax.axis_size("head"), lax.axis_size("wide")
    chips = wide_count // 2
    rows, q_width = dq.shape
    kv_width = key_pre.shape[1]
    block = width // wide_count
    hidden_width = fgate.shape[1]
    ffn_rows = width // head_count
    low, full = jnp.bfloat16, jnp.float32
    shape, vm = jax.ShapeDtypeStruct, pltpu.VMEM
    early_width = 2 * q_width
    pair = [*ring_sems(chips), DMA((chips,)), DMA((chips,))]
    peers = chips + head_count
    return pl.pallas_call(
        tail_kernel,
        out_shape=(
            shape((tok, width), full),
            shape((8, width), full),
            shape((block, q_width), low),
            shape((block, kv_width), low),
            shape((block, kv_width), low),
            shape((block, q_width), low),
            shape((ffn_rows, hidden_width), low),
            shape((ffn_rows, hidden_width), low),
        ),
        in_specs=[VMEM] * 6 + [ANY] * 14,
        out_specs=tuple([VMEM] * 6 + [ANY] * 2),
        scratch_shapes=[
            vm(dq.shape, full), vm(query_pre.shape, full), vm(key_pre.shape, full),
            vm(gate_grad.shape, low), vm(inputs.shape, low), vm(middle_grad.shape, full),
            vm(kv_parts.shape, low), vm(normed.shape, low),
            *[vm(weight.shape, low) for weight in weights],
            vm(fgate.shape, low), vm(fup.shape, low),
            vm((rows, q_width), low), vm((rows, kv_width), low), vm((rows, kv_width), low),
            vm((width, early_width), low), vm((width, 2 * kv_width), low),
            vm((head_count * tok, width), low),
            vm((chips, rows, 2 * kv_width), low), into_shape(chips, rows, 2 * kv_width),
            vm((chips, block, early_width), low), into_shape(chips, block, early_width),
            vm((chips, block, 2 * kv_width), low), into_shape(chips, block, 2 * kv_width),
            into_shape(head_count, tok, width),
            into_shape(head_count, ffn_rows, hidden_width),
            into_shape(head_count, ffn_rows, hidden_width),
            vm((2 + chips + head_count, 8, width), full),
            DMA((17,)),
            *pair, *pair, *pair,
            *ring_sems(head_count), *ring_sems(head_count), *ring_sems(head_count),
            DMA((peers,)), DMA((peers,)),
        ],
        compiler_params=pltpu.CompilerParams(
            collective_id=2, has_side_effects=True, vmem_limit_bytes=VMEM_LIMIT
        ),
        cost_estimate=pl.CostEstimate(
            flops=20 * rows * width * q_width, bytes_accessed=300 << 20, transcendentals=0
        ),
        name="tail_block",
    )(
        cosine, sine_tab, query_gain[None], key_gain[None], attn_gain[None], ffn_gain_part,
        dq, query_pre, key_pre, gate_grad, inputs, middle_grad,
        kv_parts, normed, *weights, fgate, fup,
    )


def finish_kernel(count, *refs):
    sources, gains_any = refs[:count], refs[count]
    results = refs[count + 1 : 2 * count + 1]
    gain_outs = refs[2 * count + 1 : 2 * count + 5]
    landed = refs[2 * count + 5 : 3 * count + 5]
    *spare, gains, in_sem, out_sem = refs[3 * count + 5 :]
    loads = [
        pltpu.make_async_copy(sources[i], landed[i], in_sem.at[i]) for i in range(count)
    ]
    last = pltpu.make_async_copy(gains_any, gains, in_sem.at[count])
    start_all([*loads, last])
    stores = []
    for i in range(count):
        ready = landed[i]
        loads[i].wait()
        if sources[i].dtype != results[i].dtype:
            ready = spare.pop(0)
            rows = ready.shape[0]
            step = min(rows, 128)

            def convert(row, src=landed[i], dst=ready, step=step):
                here = pl.ds(row, step)
                dst[here, :] = src[here, :].astype(jnp.float32)

            row_loop(rows, step, convert)
        stores.append(pltpu.make_async_copy(ready, results[i], out_sem.at[i]))
        stores[-1].start()
    last.wait()
    for row, out in enumerate(gain_outs):
        out[...] = gains[row : row + 1, : out.shape[1]]
    for store in stores:
        store.wait()


def finish_block(arrays, dtypes, gains, head_width):
    shape, vm = jax.ShapeDtypeStruct, pltpu.VMEM
    width = gains.shape[1]
    sizes = (width, width, head_width, head_width)
    outs = pl.pallas_call(
        functools.partial(finish_kernel, len(arrays)),
        out_shape=tuple(shape(a.shape, d) for a, d in zip(arrays, dtypes))
        + tuple(shape((1, size), jnp.float32) for size in sizes),
        in_specs=[ANY] * (len(arrays) + 1),
        out_specs=tuple([ANY] * len(arrays) + [VMEM] * 4),
        scratch_shapes=[
            *[vm(a.shape, a.dtype) for a in arrays],
            *[vm(a.shape, d) for a, d in zip(arrays, dtypes) if a.dtype != d],
            vm(gains.shape, jnp.float32),
            DMA((len(arrays) + 1,)), DMA((len(arrays),)),
        ],
        compiler_params=pltpu.CompilerParams(vmem_limit_bytes=VMEM_LIMIT),
        name="finish_block",
    )(*arrays, gains)
    return outs[: len(arrays)], [gain.reshape(-1) for gain in outs[len(arrays) :]]


def shards(
    inputs,
    attn_gain,
    query_weight,
    key_projection,
    value_projection,
    attn_gate_weight,
    output_weight,
    query_gain,
    key_gain,
    ffn_gain,
    ffn_gate_weight,
    ffn_up_weight,
    ffn_down_weight,
    doc_lengths,
    cotangent,
):
    head_width = query_gain.shape[0]
    cot_left = lax.all_gather(
        cotangent[:, : cotangent.shape[1] // 4], "wide", axis=0, tiled=True
    )
    weights = (query_weight, key_projection, value_projection, attn_gate_weight)
    query_low, query_pre, key_pre, gate_pre, cosine, sine_tab, gathered, kv_all = front_block(
        doc_lengths, inputs, attn_gain, rotation_speed(head_width), query_gain, key_gain, weights
    )
    attended, inverse, gated_low = attention_forward(doc_lengths, query_low, kv_all, gate_pre)
    (
        outputs,
        middle_grad,
        ffn_gain_part,
        back_rows,
        ffn_down_grad,
        gate_wgrad,
        up_wgrad,
        out_wgrad,
    ) = ffn_block(
        gated_low,
        inputs,
        cotangent,
        cot_left,
        ffn_gain,
        output_weight,
        ffn_gate_weight,
        ffn_up_weight,
        ffn_down_weight,
    )
    output_grad = lax.psum_scatter(out_wgrad, "wide", scatter_dimension=1, tiled=True)
    query_rot_grad, kv_parts, gate_pre_grad = attention_backward(
        doc_lengths, query_low, attended, inverse, gate_pre, kv_all, back_rows, output_weight
    )
    kv_parts = kv_parts.reshape(-1, kv_parts.shape[2])
    (
        input_grad,
        gains,
        query_grad,
        key_grad,
        value_grad,
        attn_gate_grad,
        ffn_gate_grad,
        ffn_up_grad,
    ) = tail_block(
        query_rot_grad,
        kv_parts,
        query_pre,
        key_pre,
        gate_pre_grad,
        cosine,
        sine_tab,
        query_gain,
        key_gain,
        inputs,
        middle_grad,
        attn_gain,
        ffn_gain_part,
        gathered,
        weights,
        gate_wgrad,
        up_wgrad,
    )
    full = jnp.float32
    results, gain_grads = finish_block(
        [
            outputs,
            input_grad,
            query_grad,
            key_grad,
            value_grad,
            attn_gate_grad,
            output_grad,
            ffn_gate_grad,
            ffn_up_grad,
            ffn_down_grad,
        ],
        [jnp.bfloat16] + [full] * 9,
        gains,
        head_width,
    )
    outputs, input_grad, query_grad, key_grad, value_grad = results[:5]
    attn_gate_grad, output_grad, ffn_gate_grad, ffn_up_grad, ffn_down_grad = results[5:]
    attn_gain_grad, ffn_gain_grad, query_gain_grad, key_gain_grad = gain_grads
    return (
        outputs,
        input_grad,
        attn_gain_grad,
        query_grad,
        key_grad,
        value_grad,
        attn_gate_grad,
        output_grad,
        query_gain_grad,
        key_gain_grad,
        ffn_gain_grad,
        ffn_gate_grad,
        ffn_up_grad,
        ffn_down_grad,
    )


def solution(mesh):
    placed = (
        P(("head", "wide"), None),
        P(),
        P(None, "head"),
        P(None, "head"),
        P(None, "head"),
        P(None, "head"),
        P("head", None),
        P(),
        P(),
        P(),
        P(None, "wide"),
        P(None, "wide"),
        P("wide", None),
        P(),
        P(("head", "wide"), None),
    )
    return jax.shard_map(
        shards,
        mesh=mesh,
        in_specs=placed,
        out_specs=(
            P(("head", "wide"), None),
            P(("head", "wide"), None),
            P(),
            P("wide", "head"),
            P("wide", "head"),
            P("wide", "head"),
            P("wide", "head"),
            P("head", "wide"),
            P(),
            P(),
            P(),
            P("head", "wide"),
            P("head", "wide"),
            P("wide", "head"),
        ),
        check_vma=False,
    )
```

```python
import functools

import jax
import jax.numpy as jnp
from jax import lax
from jax.experimental import pallas as pl
from jax.experimental.pallas import tpu as pltpu
from jax.sharding import PartitionSpec as P

EPS = 1e-06
THETA = 1000000.0
VMEM_LIMIT = 63 << 20


def rotation_speed(head_width):
    inverse = THETA ** (-(jnp.arange(head_width // 2, dtype=jnp.float32) * 2.0 / head_width))
    return jnp.concatenate([inverse, inverse])


MESH = pl.DeviceIdType.MESH
ANY = pl.BlockSpec(memory_space=pl.ANY)
VMEM = pl.BlockSpec(memory_space=pltpu.VMEM)
DMA = pltpu.SemaphoreType.DMA
SIDES = (0, 1)


class Ring:
    def __init__(self, size, pos, index, device):
        self.size, self.pos, self.half = size, pos, size // 2
        self._index, self._device = index, device

    def at(self, offset):
        return lax.rem(self.pos + (offset + 2 * self.size), self.size)

    def index(self, offset):
        return self._index(self.at(offset))

    def device(self, offset):
        return self._device(self.at(offset))


def head_ring():
    size = lax.axis_size("head")
    spread = size // 2
    own, wide = lax.axis_index("head"), lax.axis_index("wide")
    major, minor = lax.div(own, 2), lax.rem(own, 2)
    pos = major + minor * (size - 1 - 2 * major)

    def index(place):
        upper = lax.div(place, spread)
        return 2 * (place + upper * (size - 1 - 2 * place)) + upper

    return Ring(size, pos, index, lambda place: (index(place), wide))


def wide_ring():
    size = lax.axis_size("wide") // 2
    head, wide = lax.axis_index("head"), lax.axis_index("wide")
    core = lax.rem(wide, 2)
    ring = Ring(
        size, lax.div(wide, 2), lambda place: place, lambda place: (head, 2 * place + core)
    )
    ring.core = core
    ring.sibling = (head, wide + 1 - 2 * core)
    return ring


def meet(devices):
    barrier = pltpu.get_barrier_semaphore()
    for device in devices:
        pl.semaphore_signal(barrier, inc=1, device_id=device, device_id_type=MESH)
    pl.semaphore_wait(barrier, len(devices))


def neighbours(*rings):
    found = []
    for ring in rings:
        found += [ring.device(1), ring.device(-1)]
        if hasattr(ring, "sibling"):
            found.append(ring.sibling)
    return found


def remote(src, dst, send, recv, device):
    return pltpu.make_async_remote_copy(
        src_ref=src, dst_ref=dst, send_sem=send, recv_sem=recv, device_id=device,
        device_id_type=MESH,
    )


class Ways:
    def span(self, hop, side, piece=None):
        half = self.rows // 2
        if hop == self.ring.half:
            return side * half, half
        if piece is not None:
            return piece * half, half
        return 0, self.rows

    def halved(self, hop):
        return hop == self.ring.half - 1

    def pieces(self, hop, side):
        return (side, 1 - side) if self.halved(hop) else (None,)

    def all_copies(self, hop):
        for nth in range(2 if self.halved(hop) else 1):
            for side in SIDES:
                yield self.copy(hop, side, self.pieces(hop, side)[nth])

    def start(self, hop):
        for copy in self.all_copies(hop):
            copy.start()

    def sems(self, hop, side, piece):
        which = 0 if piece is None else piece
        return self.send.at[side, hop - 1, which], self.recv.at[side, hop - 1, which]

    def finish(self):
        for hop in range(1, self.ring.half + 1):
            for copy in self.all_copies(hop):
                copy.wait_send()


class Gather(Ways):
    def __init__(self, ring, slot, rows, send, recv):
        self.ring, self.slot, self.rows = ring, slot, rows
        self.send, self.recv = send, recv

    def copy(self, hop, side, piece=None):
        way = 1 - 2 * side
        ref = self.slot(self.ring.index(-way * (hop - 1)), *self.span(hop, side, piece))
        return remote(ref, ref, *self.sems(hop, side, piece), self.ring.device(way))

    def arrive(self, hop):
        for copy in self.all_copies(hop):
            copy.wait_recv()

    def step(self, hop):
        if not self.halved(hop):
            self.arrive(hop)
            self.start(hop + 1)
            return
        for side in SIDES:
            self.copy(hop, side, side).wait_recv()
            self.copy(hop + 1, side).start()
        for side in SIDES:
            self.copy(hop, side, 1 - side).wait_recv()


class PairGather(Gather):
    def __init__(self, ring, slot, rows, send, recv, pass_send, pass_recv):
        core = ring.core
        super().__init__(
            ring, lambda index, start, size: slot(2 * index + core, start, size), rows, send, recv
        )
        self.pass_send, self.pass_recv = pass_send, pass_recv

    def handed(self, hop, side):
        way = 1 - 2 * side
        span = self.span(hop, side) if hop else (0, self.rows)
        ref = self.slot(self.ring.index(-way * hop), *span)
        return remote(
            ref, ref, self.pass_send.at[side, hop], self.pass_recv.at[side, hop],
            self.ring.sibling,
        )

    def hand(self, hop):
        for side in SIDES if hop else (0,):
            self.handed(hop, side).start()

    def take(self, hop):
        for side in SIDES if hop else (0,):
            self.handed(hop, side).wait_recv()

    def begin(self):
        self.start(1)
        self.hand(0)

    def finish(self):
        super().finish()
        for hop in range(self.ring.half + 1):
            for side in SIDES if hop else (0,):
                self.handed(hop, side).wait_send()


def row_loop(rows, chunk, body):
    @pl.loop(0, rows // chunk)
    def _(step):
        body(pl.multiple_of(step * chunk, chunk))


class Scatter(Ways):
    def __init__(self, ring, part, rows, into, send, recv):
        self.ring, self.part, self.rows, self.into = ring, part, rows, into
        self.send, self.recv = send, recv
        self.freed = False

    def inside(self, hop, row):
        return row % (self.rows // 2) if hop == self.ring.half else row

    def copy(self, hop, side, piece=None):
        way = 1 - 2 * side
        first, count = self.span(hop, side, piece)
        ref, base = self.part(self.ring.index(way * hop))
        return remote(
            ref.at[pl.ds(base + first, count)],
            self.into.at[side, pl.ds((hop - 1) * self.rows + self.inside(hop, first), count)],
            *self.sems(hop, side, piece), self.ring.device(way),
        )

    def start_free(self):
        self.freed = True
        if self.ring.half > 1:
            for side in SIDES:
                self.copy(self.ring.half - 1, side, 1 - side).start()

    def fold(self, hop, side):
        way = 1 - 2 * side
        for copy in [self.copy(hop + 1, side, piece) for piece in self.pieces(hop + 1, side)]:
            copy.wait_recv()
        first, count = self.span(hop + 1, side)
        ref, base = self.part(self.ring.index(way * hop))
        chunk = min(count, 32)

        def add(row):
            there = pl.ds(pl.multiple_of(base + first + row, chunk), chunk)
            start = hop * self.rows + self.inside(hop + 1, first)
            here = pl.ds(pl.multiple_of(start + row, chunk), chunk)
            ref[there, :] = (
                ref[there, :].astype(jnp.float32) + self.into[side, here, :].astype(jnp.float32)
            ).astype(ref.dtype)

        row_loop(count, chunk, add)

    def advance(self, hop):
        if self.halved(hop) and not self.freed:
            self.start_free()
        for side in SIDES:
            self.fold(hop, side)
            self.copy(hop, side, self.pieces(hop, side)[0]).start()

    def arrive(self):
        for copy in self.all_copies(1):
            copy.wait_recv()

    def total(self, row, count):
        ref, base = self.part(self.ring.index(0))
        there = pl.ds(pl.multiple_of(base + row, count), count)
        here = pl.ds(row, count)
        return (
            ref[there, :].astype(jnp.float32)
            + self.into[0, here, :].astype(jnp.float32)
            + self.into[1, here, :].astype(jnp.float32)
        )


class PairScatter(Scatter):
    def __init__(self, ring, terms, rows, passed, into, send, recv, pass_send, pass_recv):
        core = ring.core
        super().__init__(
            ring, lambda index: (terms, (2 * index + core) * rows), rows, into, send, recv
        )
        self.terms, self.passed = terms, passed
        self.pass_send, self.pass_recv = pass_send, pass_recv

    def handed(self, offset):
        ring = self.ring
        index = ring.index(offset)
        other = pl.multiple_of((2 * index + 1 - ring.core) * self.rows, self.rows)
        slot = offset % ring.size
        return remote(
            self.terms.at[pl.ds(other, self.rows)],
            self.passed.at[slot],
            self.pass_send.at[slot], self.pass_recv.at[slot], ring.sibling,
        )

    def hand(self, offset):
        self.handed(offset).start()

    def merge(self, offset):
        self.handed(offset).wait_recv()
        slot = offset % self.ring.size
        ref, base = self.part(self.ring.index(offset))
        chunk = 32

        def add(row):
            there = pl.ds(pl.multiple_of(base + row, chunk), chunk)
            ref[there, :] = (
                ref[there, :].astype(jnp.float32)
                + self.passed[slot, pl.ds(row, chunk), :].astype(jnp.float32)
            ).astype(ref.dtype)

        row_loop(self.rows, chunk, add)

    def finish(self):
        super().finish()
        for offset in range(self.ring.size):
            self.handed(offset).wait_send()


def offsets(ring):
    order = [ring.half]
    for hop in range(ring.half - 1, 0, -1):
        order += [hop, -hop]
    return order + [0]


def into_shape(size, rows, columns):
    return pltpu.VMEM((2, (size - 1) * rows // 2, columns), jnp.bfloat16)


def everyone(*rings):
    found = []
    for ring in rings:
        found += [ring.device(offset) for offset in range(1, ring.size)]
        if hasattr(ring, "sibling"):
            found.append(ring.sibling)
    return found


def ring_sems(size):
    return [DMA((2, size // 2, 2)), DMA((2, size // 2, 2))]


def pass_sems(size):
    return [DMA((2, size // 2 + 1)), DMA((2, size // 2 + 1))]


NEAR, OTHER, FAR = 0, 1, 2


class LineGather:
    pieces = 2

    def __init__(self, ring, slot, rows, send, recv, pass_send, pass_recv):
        self.ring, self.slot, self.rows = ring, slot, rows // self.pieces
        self.send, self.recv, self.pass_send, self.pass_recv = send, recv, pass_send, pass_recv
        pos = ring.pos
        half, odd = lax.div(pos, 2), lax.rem(pos, 2)
        self.way = 1 - 2 * odd
        self.middle = half + odd == 1

    def offset(self, kind):
        return {NEAR: self.way, OTHER: -self.way, FAR: 2}[kind]

    def ref(self, offset, piece):
        index = 2 * self.ring.index(offset) + self.ring.core
        return self.slot(index, piece * self.rows, self.rows)

    def copy(self, which, offset, kind, piece, way):
        ref = self.ref(offset, piece)
        return remote(
            ref, ref, self.send.at[which, piece], self.recv.at[kind, piece],
            self.ring.device(way),
        )

    def own(self, piece):
        return self.copy(0, 0, NEAR, piece, self.way)

    def own_other(self, piece):
        return self.copy(1, 0, OTHER, piece, -self.way)

    def onward(self, kind, piece):
        arrives = {NEAR: FAR, OTHER: FAR, FAR: OTHER}[kind]
        way = -self.way if kind == NEAR else self.way
        return self.copy(2 + kind, self.offset(kind), arrives, piece, way)

    def incoming(self, kind, piece):
        return self.copy(0, self.offset(kind), kind, piece, self.way)

    def handed(self, kind, piece):
        ref = self.ref(0 if kind is None else self.offset(kind), piece)
        slot = 3 if kind is None else kind
        return remote(
            ref, ref, self.pass_send.at[slot, piece], self.pass_recv.at[slot, piece],
            self.ring.sibling,
        )

    def begin(self):
        for piece in range(self.pieces):
            self.own(piece).start()

            @pl.when(self.middle)
            def _():
                self.own_other(piece).start()

            self.handed(None, piece).start()

    def arrive(self, kind):
        for piece in range(self.pieces):
            self.incoming(kind, piece).wait_recv()

            @pl.when(self.middle)
            def _():
                self.onward(kind, piece).start()

            self.handed(kind, piece).start()

    def take(self, kind):
        for piece in range(self.pieces):
            self.handed(kind, piece).wait_recv()

    def finish(self):
        for piece in range(self.pieces):
            self.own(piece).wait_send()

            @pl.when(self.middle)
            def _():
                self.own_other(piece).wait_send()
                for kind in (NEAR, OTHER, FAR):
                    self.onward(kind, piece).wait_send()

            for kind in (None, NEAR, OTHER, FAR):
                self.handed(kind, piece).wait_send()


class LineScatter(PairScatter):
    pieces = 2

    def __init__(self, *args):
        super().__init__(*args)
        pos = self.ring.pos
        half, odd = lax.div(pos, 2), lax.rem(pos, 2)
        self.way = 1 - 2 * odd
        self.middle = half + odd == 1
        self.waited = set()

    def offset(self, kind):
        return {NEAR: self.way, OTHER: -self.way, FAR: 2, None: 0}[kind]

    def piece_of(self, piece):
        size = self.rows // self.pieces
        return piece * size, size

    def outgoing(self, kind, slot, piece, way):
        first, size = self.piece_of(piece)
        ref, base = self.part(self.ring.index(self.offset(kind)))
        return remote(
            ref.at[pl.ds(pl.multiple_of(base + first, size), size)],
            self.into.at[slot, pl.ds(first, size)],
            self.send.at[kind, piece], self.recv.at[slot, piece], self.ring.device(way),
        )

    def from_end(self, kind, piece):
        return self.outgoing(kind, {OTHER: 0, FAR: 1, NEAR: 2}[kind], piece, self.way)

    def from_middle(self, kind, piece):
        slot = {FAR: 3, OTHER: 4, NEAR: 0}[kind]
        return self.outgoing(kind, slot, piece, self.way if kind == NEAR else -self.way)

    def landed(self, slot, piece):
        first, size = self.piece_of(piece)
        ref = self.into.at[slot, pl.ds(first, size)]
        remote(
            ref, ref, self.send.at[0, piece], self.recv.at[slot, piece], self.ring.device(self.way)
        ).wait_recv()

    def hand_kind(self, kind):
        self.swap(kind).start()

    def swap(self, kind):
        index = self.ring.index(self.offset(kind))
        other = pl.multiple_of((2 * index + 1 - self.ring.core) * self.rows, self.rows)
        slot = 3 if kind is None else kind
        return remote(
            self.terms.at[pl.ds(other, self.rows)], self.passed.at[slot],
            self.pass_send.at[slot], self.pass_recv.at[slot], self.ring.sibling,
        )

    def merge_kind(self, kind):
        self.swap(kind).wait_recv()
        slot = 3 if kind is None else kind
        ref, base = self.part(self.ring.index(self.offset(kind)))

        def add(row):
            there = pl.ds(pl.multiple_of(base + row, 32), 32)
            ref[there, :] = (
                ref[there, :].astype(jnp.float32)
                + self.passed[slot, pl.ds(row, 32), :].astype(jnp.float32)
            ).astype(ref.dtype)

        row_loop(self.rows, 32, add)

    def launch(self, *kinds):
        @pl.when(~self.middle)
        def _():
            for kind in kinds:
                for piece in range(self.pieces):
                    self.from_end(kind, piece).start()

    def sent(self, kind):
        self.waited.add(kind)

        @pl.when(~self.middle)
        def _():
            for piece in range(self.pieces):
                self.from_end(kind, piece).wait_send()

    def relay(self, kind):
        slot = {FAR: 0, OTHER: 1, NEAR: 3}[kind]

        @pl.when(self.middle)
        def _():
            ref, base = self.part(self.ring.index(self.offset(kind)))
            for piece in range(self.pieces):
                first, size = self.piece_of(piece)
                self.landed(slot, piece)

                def add(row):
                    there = pl.ds(pl.multiple_of(base + first + row, 32), 32)
                    here = pl.ds(pl.multiple_of(first + row, 32), 32)
                    ref[there, :] = (
                        ref[there, :].astype(jnp.float32)
                        + self.into[slot, here, :].astype(jnp.float32)
                    ).astype(ref.dtype)

                row_loop(size, 32, add)
                self.from_middle(kind, piece).start()

    def arrive(self):
        @pl.when(self.middle)
        def _():
            for piece in range(self.pieces):
                self.landed(2, piece)
                self.landed(4, piece)

            def add(row):
                here = pl.ds(row, 32)
                self.into[0, here, :] = (
                    self.into[2, here, :].astype(jnp.float32)
                    + self.into[4, here, :].astype(jnp.float32)
                ).astype(self.into.dtype)

            row_loop(self.rows, 32, add)

        @pl.when(~self.middle)
        def _():
            for piece in range(self.pieces):
                self.landed(0, piece)

    def total(self, row, count):
        ref, base = self.part(self.ring.index(0))
        there = pl.ds(pl.multiple_of(base + row, count), count)
        return ref[there, :].astype(jnp.float32) + self.into[0, pl.ds(row, count), :].astype(
            jnp.float32
        )

    def finish(self):
        for piece in range(self.pieces):

            @pl.when(self.middle)
            def _():
                for kind in (NEAR, OTHER, FAR):
                    self.from_middle(kind, piece).wait_send()

            @pl.when(~self.middle)
            def _():
                for kind in (NEAR, OTHER, FAR):
                    if kind not in self.waited:
                        self.from_end(kind, piece).wait_send()

        for kind in (NEAR, OTHER, FAR, None):
            self.swap(kind).wait_send()


def scatter_of(ring):
    return LineScatter if ring.size == 4 else PairScatter


def scatter_into(size, rows, columns):
    if size == 4:
        return pltpu.VMEM((5, rows, columns), jnp.bfloat16)
    return into_shape(size, rows, columns)


def scatter_sems(size):
    passed = [DMA((size,)), DMA((size,))]
    if size == 4:
        pieces = LineScatter.pieces
        return [DMA((3, pieces)), DMA((5, pieces)), *passed]
    return [*ring_sems(size), *passed]


def line_sems():
    pieces = LineGather.pieces
    return [DMA((5, pieces)), DMA((3, pieces)), DMA((4, pieces)), DMA((4, pieces))]


def gather_sems(size):
    return line_sems() if size == 4 else [*ring_sems(size), *pass_sems(size)]


def row_gather_of(ring):
    return LineGather if ring.size == 4 else PairGather


def dot_nn(left, right):
    return jnp.dot(left, right, preferred_element_type=jnp.float32)


def dot_nt(left, right):
    return lax.dot_general(
        left, right, (((1,), (1,)), ((), ())), preferred_element_type=jnp.float32
    )


def dot_tn(left, right):
    return lax.dot_general(
        left, right, (((0,), (0,)), ((), ())), preferred_element_type=jnp.float32
    )


LANES = 128
FORWARD_KEYS = 1024
BACKWARD_KEYS = 1024
LOG2E = 1.4426950408889634


def doc_ends(doc_ref):
    ends, total = [], jnp.int32(0)
    for row in range(doc_ref.shape[0]):
        for doc in range(doc_ref.shape[1]):
            total = total + doc_ref[row, doc]
            ends.append(total)
    return ends


def first_of(ends, tokens):
    first = jnp.zeros_like(tokens)
    for end in ends:
        first = jnp.maximum(first, jnp.where(tokens >= end, end, 0))
    return first


def start_all(copies):
    for copy in copies:
        copy.start()


def attention_forward_kernel(
    doc_ref, query_any, kv_any, gate_any, att_any, inv_any, gated_any,
    query, kv, gate, att, inv, gated, acc, kv_sem, in_sem, out_sem,
):
    wide_count = lax.axis_size("wide")
    wide_pos = lax.axis_index("wide")
    kv_width = kv.shape[1] // 2
    groups = kv_width // LANES
    per = query.shape[1] // kv_width
    blocks = kv_sem.shape[0]
    rows = query.shape[0] // blocks
    step = min(FORWARD_KEYS, rows * wide_count)
    factor = LANES ** (-0.5) * LOG2E
    chunk = rows * wide_count

    def kv_copy(blk):
        there = pl.ds(pl.multiple_of(blk * chunk, chunk), chunk)
        return pltpu.make_async_copy(kv_any.at[there], kv.at[there], kv_sem.at[blk])

    early = [
        pltpu.make_async_copy(query_any, query, in_sem.at[0]),
        pltpu.make_async_copy(gate_any, gate, in_sem.at[1]),
    ]
    early[0].start()
    for blk in range(blocks):
        kv_copy(blk).start()
    early[1].start()
    ends = doc_ends(doc_ref)
    early[0].wait()

    def out_copies(blk):
        here = pl.ds(pl.multiple_of(blk * rows, rows), rows)
        return [
            pltpu.make_async_copy(src.at[here], dst.at[here], out_sem.at[i, blk])
            for i, (src, dst) in enumerate(((att, att_any), (inv, inv_any), (gated, gated_any)))
        ]

    @pl.loop(0, blocks)
    def _(blk):
        here = pl.ds(pl.multiple_of(blk * rows, rows), rows)
        first_tok = (blk * wide_count + wide_pos) * rows
        key_lane = lax.broadcasted_iota(jnp.int32, (rows, step), 1)
        tokens = lax.broadcasted_iota(jnp.int32, (rows, 1), 0) + first_tok
        upper = key_lane - tokens
        lower = key_lane - first_of(ends, tokens)
        queries = [
            jnp.concatenate(
                [query[here, (g * per + j) * LANES : (g * per + j + 1) * LANES] for j in range(per)],
                axis=0,
            )
            for g in range(groups)
        ]
        acc[...] = jnp.zeros_like(acc)
        kv_copy(blk).wait()

        @pl.loop(first_of(ends, first_tok) // step, (first_tok + rows + step - 1) // step)
        def _(tile):
            base = tile * step
            there = pl.ds(pl.multiple_of(base, step), step)
            allowed = (upper <= -base) & (lower >= -base)
            allowed = jnp.concatenate([allowed] * per, axis=0)
            for g in range(groups):
                cols = slice(g * LANES, (g + 1) * LANES)
                value_cols = slice(kv_width + g * LANES, kv_width + (g + 1) * LANES)
                scores = dot_nt(queries[g], kv[there, cols])
                probs = jnp.where(allowed, jnp.exp2(scores * factor), 0.0).astype(jnp.bfloat16)
                values = jnp.concatenate(
                    [kv[there, value_cols], jnp.ones((step, LANES), jnp.bfloat16)], axis=1
                )
                acc[g] += dot_nn(probs, values)

        @pl.when(blk == 0)
        def _():
            early[1].wait()

        for g in range(groups):
            for j in range(per):
                part = acc[g, j * rows : (j + 1) * rows, :]
                cols = slice((g * per + j) * LANES, (g * per + j + 1) * LANES)
                inverse = 1.0 / part[:, LANES:]
                out = part[:, :LANES] * inverse
                att[here, cols] = out
                inv[here, cols] = inverse
                gated[here, cols] = (out * jax.nn.sigmoid(gate[here, cols])).astype(jnp.bfloat16)
        start_all(out_copies(blk))

    for blk in range(blocks):
        for copy in out_copies(blk):
            copy.wait()


def attention_forward(doc_lengths, query_low, kv_all, gate_pre):
    rows, width = query_low.shape
    kv_width = kv_all.shape[1] // 2
    groups = kv_width // LANES
    per = width // kv_width
    blocks = lax.axis_size("head")
    low, full = jnp.bfloat16, jnp.float32
    shape, vm = jax.ShapeDtypeStruct, pltpu.VMEM
    return pl.pallas_call(
        attention_forward_kernel,
        out_shape=(
            shape((rows, width), full),
            shape((rows, width), full),
            shape((rows, width), low),
        ),
        in_specs=[pl.BlockSpec(memory_space=pltpu.SMEM)] + [ANY] * 3,
        out_specs=(ANY, ANY, ANY),
        scratch_shapes=[
            vm((rows, width), low), vm(kv_all.shape, low), vm((rows, width), full),
            vm((rows, width), full), vm((rows, width), full), vm((rows, width), low),
            vm((groups, per * (rows // blocks), 2 * LANES), full),
            DMA((blocks,)), DMA((2,)), DMA((3, blocks)),
        ],
        compiler_params=pltpu.CompilerParams(vmem_limit_bytes=VMEM_LIMIT),
        cost_estimate=pl.CostEstimate(
            flops=4 * rows * width * 2048, bytes_accessed=12 << 20, transcendentals=0
        ),
        name="attention_forward",
    )(doc_lengths, query_low, kv_all, gate_pre)


def attention_backward_kernel(
    doc_ref, query_any, att_any, inv_any, gate_any, kv_any, back_any, wo_any,
    dq_any, parts_any, ggrad_any,
    query, att, inv, gate, kv, back, wo, dq, parts, ggrad, dk_acc, dv_acc, dqt, keyt, dout,
    in_sem, out_sem,
):
    wide_count = lax.axis_size("wide")
    wide_pos = lax.axis_index("wide")
    kv_width = kv.shape[1] // 2
    groups = kv_width // LANES
    per = query.shape[1] // kv_width
    blocks = out_sem.shape[1]
    rows = query.shape[0] // blocks
    step = min(BACKWARD_KEYS, rows * wide_count)
    scale = LANES ** (-0.5)
    loads = [
        pltpu.make_async_copy(src, dst, in_sem.at[i])
        for i, (src, dst) in enumerate(
            (
                (back_any, back), (wo_any, wo), (gate_any, gate), (att_any, att),
                (inv_any, inv), (query_any, query), (kv_any, kv),
            )
        )
    ]
    start_all(loads)
    ends = doc_ends(doc_ref)
    dk_acc[...] = jnp.zeros_like(dk_acc)
    dv_acc[...] = jnp.zeros_like(dv_acc)
    for load in loads[:4]:
        load.wait()

    @pl.loop(0, blocks)
    def _(blk):
        here = pl.ds(pl.multiple_of(blk * rows, rows), rows)
        gated_grad = dot_nt(back[here, :], wo[...])
        sig = jax.nn.sigmoid(gate[here, :])
        grad = gated_grad * sig
        dout[here, :] = grad
        ggrad[here, :] = (grad * att[here, :] * (1.0 - sig)).astype(jnp.bfloat16)

    for load in loads[4:]:
        load.wait()

    @pl.loop(0, kv.shape[0] // step)
    def _(tile):
        there = pl.ds(pl.multiple_of(tile * step, step), step)
        for g in range(groups):
            cols = slice(g * LANES, (g + 1) * LANES)
            keyt[cols, there] = jnp.transpose(kv[there, cols])

    def out_copies(blk):
        here = pl.ds(pl.multiple_of(blk * rows, rows), rows)
        return [
            pltpu.make_async_copy(dq.at[here], dq_any.at[here], out_sem.at[0, blk]),
            pltpu.make_async_copy(parts.at[:, here], parts_any.at[:, here], out_sem.at[1, blk]),
            pltpu.make_async_copy(ggrad.at[here], ggrad_any.at[here], out_sem.at[2, blk]),
        ]

    @pl.loop(0, blocks)
    def _(turn_of):
        blk = blocks - 1 - turn_of
        here = pl.ds(pl.multiple_of(blk * rows, rows), rows)
        first_tok = (blk * wide_count + wide_pos) * rows
        key_row = lax.broadcasted_iota(jnp.int32, (step, rows), 0)
        tokens = lax.broadcasted_iota(jnp.int32, (1, rows), 1) + first_tok
        upper = key_row - tokens
        lower = key_row - first_of(ends, tokens)
        queries, grads, deltas = [], [], []
        for g in range(groups):
            qs, gs, ds = [], [], []
            for j in range(per):
                cols = slice((g * per + j) * LANES, (g * per + j + 1) * LANES)
                both = dout[here, cols] * inv[here, cols]
                delta = jnp.sum(both * att[here, cols], axis=1, keepdims=True)
                ds.append(jnp.transpose(jnp.broadcast_to(delta, (rows, LANES)))[0:1, :])
                qs.append(query[here, cols])
                gs.append(both.astype(jnp.bfloat16))
            queries.append(jnp.concatenate(qs, axis=0))
            grads.append(jnp.concatenate(gs, axis=0))
            deltas.append(jnp.concatenate(ds, axis=1))
        dqt[...] = jnp.zeros_like(dqt)

        @pl.loop(first_of(ends, first_tok) // step, (first_tok + rows + step - 1) // step)
        def _(tile):
            base = tile * step
            there = pl.ds(pl.multiple_of(base, step), step)
            allowed = (upper <= -base) & (lower >= -base)
            allowed = jnp.concatenate([allowed] * per, axis=1)
            for g in range(groups):
                cols = slice(g * LANES, (g + 1) * LANES)
                value_cols = slice(kv_width + g * LANES, kv_width + (g + 1) * LANES)
                scores = dot_nt(kv[there, cols], queries[g])
                probs = jnp.where(allowed, jnp.exp2(scores * (scale * LOG2E)), 0.0)
                dprobs = dot_nt(kv[there, value_cols], grads[g])
                dscores = (probs * (dprobs - deltas[g])).astype(jnp.bfloat16)
                dv_acc[there, cols] += dot_nn(probs.astype(jnp.bfloat16), grads[g])
                dk_acc[there, cols] += dot_nn(dscores, queries[g])
                dqt[g] += dot_nn(keyt[cols, there], dscores)

        for g in range(groups):
            for j in range(per):
                cols = slice((g * per + j) * LANES, (g * per + j + 1) * LANES)
                dq[here, cols] = jnp.transpose(dqt[g, :, j * rows : (j + 1) * rows]) * scale

        @pl.loop(0, wide_count)
        def _(target):
            source = pl.ds(pl.multiple_of((blk * wide_count + target) * rows, rows), rows)
            parts[target, here, :kv_width] = (dk_acc[source, :] * scale).astype(jnp.bfloat16)
            parts[target, here, kv_width:] = dv_acc[source, :].astype(jnp.bfloat16)

        start_all(out_copies(blk))

    for blk in range(blocks):
        for copy in out_copies(blk):
            copy.wait()


def attention_backward(
    doc_lengths, query_low, attended, inverse, gate_pre, kv_all, back_rows, out_w
):
    rows, width = query_low.shape
    keys, kv_width = kv_all.shape[0], kv_all.shape[1] // 2
    groups = kv_width // LANES
    per = width // kv_width
    blocks, wide_count = lax.axis_size("head"), lax.axis_size("wide")
    low, full = jnp.bfloat16, jnp.float32
    shape, vm = jax.ShapeDtypeStruct, pltpu.VMEM
    return pl.pallas_call(
        attention_backward_kernel,
        out_shape=(
            shape((rows, width), full),
            shape((wide_count, rows, 2 * kv_width), low),
            shape((rows, width), low),
        ),
        in_specs=[pl.BlockSpec(memory_space=pltpu.SMEM)] + [ANY] * 7,
        out_specs=(ANY, ANY, ANY),
        scratch_shapes=[
            vm((rows, width), low), vm((rows, width), full), vm((rows, width), full),
            vm((rows, width), full), vm(kv_all.shape, low), vm(back_rows.shape, low),
            vm(out_w.shape, low), vm((rows, width), full),
            vm((wide_count, rows, 2 * kv_width), low), vm((rows, width), low),
            vm((keys, kv_width), full), vm((keys, kv_width), full),
            vm((groups, LANES, per * (rows // blocks)), full), vm((kv_width, keys), low),
            vm((rows, width), full),
            DMA((7,)), DMA((3, blocks)),
        ],
        compiler_params=pltpu.CompilerParams(vmem_limit_bytes=VMEM_LIMIT),
        cost_estimate=pl.CostEstimate(
            flops=10 * rows * width * 2048, bytes_accessed=20 << 20, transcendentals=0
        ),
        name="attention_backward",
    )(
        doc_lengths, query_low, attended, inverse, gate_pre, kv_all, back_rows, out_w
    )


def ffn_kernel(
    gated_ref, gain_ref, x_any, cot_any, left_any, wo_any, wg_any, wu_any, wd_any,
    out_any, mgrad_ref, gain_out, back_any, down_any, fgate_any, fup_any, owg_any,
    wo, wg, wu, wd, cots, rows, hid, gg, ug, terms_own, outs_own, passed, into,
    passed2, into2, dterms, dinto, hterms, hinto, middle, back, local_sem, left_sem,
    ds, dr, hs, hr, cs, cr, cps, cpr, fs, fr, fps, fpr, s1, r1, ps1, pr1, s2, r2, ps2, pr2, bs, br,
):
    tok, width = x_any.shape
    hidden_width = wg_any.shape[1]
    head, wide = head_ring(), wide_ring()
    pair = 2 * tok
    separate = terms_own.shape[0] > 16
    terms = terms_own if separate else cots
    outs = outs_own if separate else rows
    part = wo_any.shape[1] // lax.axis_size("head")
    loads = [
        pltpu.make_async_copy(src, dst, local_sem.at[i])
        for i, (src, dst) in enumerate(((wo_any, wo), (wd_any, wd), (wg_any, wg), (wu_any, wu)))
    ]
    split = left_any.shape[0] // lax.axis_size("wide")
    left = [
        pltpu.make_async_copy(
            left_any.at[pl.ds(i * split, split)], cots.at[pl.ds(i * tok, split)], left_sem.at[i]
        )
        for i in range(lax.axis_size("wide"))
    ]
    loads.extend(left)
    for load in loads:
        load.start()
    own_wide = pl.multiple_of(lax.axis_index("wide") * tok, tok)
    own_head = pl.multiple_of(lax.axis_index("head") * tok, tok)
    own_loads = [
        pltpu.make_async_copy(
            cot_any.at[pl.ds(split, tok - split)],
            cots.at[pl.ds(own_wide + split, tok - split)],
            local_sem.at[12],
        ),
        pltpu.make_async_copy(x_any, back.at[pl.ds(own_head, tok)], local_sem.at[13]),
    ]
    start_all(own_loads)
    meet(neighbours(head, wide))
    own_loads[0].wait()

    def slot_of(ref):
        return lambda index, start, size: ref.at[pl.ds(index * tok + start, size)]

    def cot_slot(index, start, size):
        return cots.at[pl.ds(index * tok + split + start, size)]

    cot_gather = PairGather(wide, cot_slot, tok - split, cs, cr, cps, cpr)
    row_gather = row_gather_of(wide)(wide, slot_of(rows), tok, fs, fr, fps, fpr)
    back_gather = Gather(head, slot_of(back), tok, bs, br)
    head_scatter = Scatter(head, lambda index: (hterms, index * tok), tok, hinto, hs, hr)
    grad_scatter = scatter_of(wide)(wide, terms, tok, passed, into, s1, r1, ps1, pr1)
    down_scatter = Scatter(
        head, lambda index: (dterms, index * hidden_width), hidden_width, dinto, ds, dr
    )
    out_scatter = scatter_of(wide)(wide, outs, tok, passed2, into2, s2, r2, ps2, pr2)

    def group_of(offset):
        return pl.ds(pl.multiple_of(wide.index(offset) * pair, pair), pair)

    def col_loop(total, step, body):
        @pl.loop(0, total // step)
        def _(i):
            body(pl.ds(pl.multiple_of(i * step, step), step))

    tile = 256
    line = wide.size == 4
    cot_gather.begin()

    def out_part(offset, own):
        index = head.index(offset)
        here = pl.ds(pl.multiple_of(index * tok, tok), tok)

        def body(cols):
            value = dot_nn(gated_ref[here, :], wo[:, cols])
            if own:
                middle[:, cols] = back[pl.ds(own_head, tok), cols].astype(jnp.float32) + value
            else:
                hterms[here, cols] = value.astype(jnp.bfloat16)

        col_loop(width, tile, body)

    def hidden_part(offset):
        here = group_of(offset)

        def body(cols):
            hid[here, cols] = dot_nt(cots[here, :], wd[cols, :]).astype(jnp.bfloat16)

        col_loop(hidden_width, hidden_width, body)

    loads[0].wait()
    own_loads[1].wait()
    out_part(head.half, False)
    head_scatter.start(head.half)
    for hop in range(head.half - 1, 0, -1):
        out_part(hop, False)
        out_part(-hop, False)
        if hop == head.half - 1:
            head_scatter.start_free()
    out_part(0, True)
    loads[1].wait()
    for load in left:
        load.wait()
    mgrad_ref[...] = cots[pl.ds(own_wide, tok), :].astype(jnp.float32)
    cot_gather.take(0)
    hidden_part(0)
    for hop in range(head.half - 1, 0, -1):
        head_scatter.advance(hop)
    for hop in range(1, wide.half):
        cot_gather.step(hop)
        cot_gather.hand(hop)
        cot_gather.take(hop)
        hidden_part(hop)
        hidden_part(-hop)
    head_scatter.arrive()

    gain = gain_ref[...]

    def forward_norm(row):
        here = pl.ds(row, 32)
        value = (
            middle[here, :]
            + hinto[0, here, :].astype(jnp.float32)
            + hinto[1, here, :].astype(jnp.float32)
        )
        middle[here, :] = value
        scale = lax.rsqrt(jnp.mean(value * value, axis=-1, keepdims=True) + EPS)
        rows[pl.ds(pl.multiple_of(own_wide + row, 32), 32), :] = (value * scale * gain).astype(
            jnp.bfloat16
        )

    row_loop(tok, 32, forward_norm)
    row_gather.begin()
    cot_gather.arrive(wide.half)
    cot_gather.hand(wide.half)
    cot_gather.take(wide.half)
    hidden_part(wide.half)
    cot_gather.finish()
    loads[2].wait()
    loads[3].wait()

    def unit(offset):
        here = group_of(offset)

        def body(cols):
            gate = dot_nn(rows[here, :], wg[:, cols])
            up = dot_nn(rows[here, :], wu[:, cols])
            grad = hid[here, cols].astype(jnp.float32)
            sig = jax.nn.sigmoid(gate)
            act = gate * sig
            hid[here, cols] = (act * up).astype(jnp.bfloat16)
            gg[here, cols] = (grad * up * (sig + act * (1.0 - sig))).astype(jnp.bfloat16)
            ug[here, cols] = (grad * act).astype(jnp.bfloat16)

        col_loop(hidden_width, tile if hidden_width % tile == 0 else LANES, body)

    def down_terms(offset):
        here = group_of(offset)

        def body(cols):
            outs[here, cols] = dot_nn(hid[here, :], wd[:, cols]).astype(jnp.bfloat16)

        col_loop(width, width, body)
        if not line:
            out_scatter.hand(offset)

    def down_grads(group, add):
        @pl.loop(0, lax.axis_size("head"))
        def _(index):
            cols = pl.ds(pl.multiple_of(index * part, part), part)
            there = pl.ds(pl.multiple_of(index * hidden_width, LANES), hidden_width)
            value = sum(
                dot_tn(hid[group_of(offset), :], cots[group_of(offset), cols]) for offset in group
            )
            if add:
                value += dterms[there, :].astype(jnp.float32)
            dterms[there, :] = value.astype(jnp.bfloat16)

    def grad_terms(offset):
        here = group_of(offset)

        def body(cols):
            value = dot_nt(gg[here, :], wg[cols, :]) + dot_nt(ug[here, :], wu[cols, :])
            terms[here, cols] = value.astype(jnp.bfloat16)

        col_loop(width, 1024, body)

    emit = 256

    def stage_of(out, slot):
        cols = pl.ds(out * hidden_width, hidden_width)
        return hterms.at[pl.ds(slot * emit, emit), cols]

    def stage_copy(step, out, any_ref, slot):
        there = pl.ds(pl.multiple_of(step * emit, emit), emit)
        return pltpu.make_async_copy(
            stage_of(out, slot), any_ref.at[there], local_sem.at[5 + 2 * slot + out]
        )

    def input_grads():
        head_scatter.finish()

        @pl.loop(0, width // emit // 2)
        def _(i):
            for slot in SIDES:
                step = 2 * i + slot
                cols = pl.ds(pl.multiple_of(step * emit, emit), emit)

                @pl.when(i > 0)
                def _():
                    for out, any_ref in enumerate((fgate_any, fup_any)):
                        stage_copy(step - 2, out, any_ref, slot).wait()

                left = rows[:, cols]
                stage_of(0, slot)[...] = dot_tn(left, gg[...]).astype(jnp.bfloat16)
                stage_of(1, slot)[...] = dot_tn(left, ug[...]).astype(jnp.bfloat16)
                for out, any_ref in enumerate((fgate_any, fup_any)):
                    stage_copy(step, out, any_ref, slot).start()

    order = offsets(wide)

    def near_part(offset):
        unit(offset)
        if separate:
            down_terms(offset)

    def down_pass(kind):
        offset = out_scatter.offset(kind)
        down_terms(offset)
        out_scatter.hand_kind(kind)

    if line:

        def arrived(kind):
            row_gather.arrive(kind)
            row_gather.take(kind)
            unit(row_gather.offset(kind))
            grad_terms(grad_scatter.offset(kind))
            grad_scatter.hand_kind(kind)

        row_gather.take(None)
        unit(0)
        down_pass(None)
        down_grads([0], False)
        arrived(NEAR)
        down_pass(NEAR)
        grad_scatter.merge_kind(NEAR)
        grad_scatter.launch(NEAR)

        @pl.when(row_gather.middle)
        def _():
            arrived(OTHER)
            down_pass(OTHER)
            grad_scatter.merge_kind(OTHER)

        arrived(FAR)
        grad_scatter.merge_kind(FAR)
        grad_scatter.launch(FAR)

        @pl.when(~row_gather.middle)
        def _():
            arrived(OTHER)
            grad_scatter.merge_kind(OTHER)

        grad_scatter.launch(OTHER)
        pl.when(~row_gather.middle)(functools.partial(down_pass, OTHER))
        down_pass(FAR)
        grad_terms(0)
        grad_scatter.hand_kind(None)
        down_grads([1, 2, 3], True)
        down_scatter.start(head.half)
        down_scatter.start_free()
        grad_scatter.relay(OTHER)
        for kind in (OTHER, FAR, NEAR, None):
            out_scatter.merge_kind(kind)
        input_grads()
        out_scatter.launch(OTHER, FAR, NEAR)
        grad_scatter.merge_kind(None)
        grad_scatter.relay(FAR)
        grad_scatter.relay(NEAR)
    else:
        row_gather.take(0)
        near_part(0)
        if separate:
            down_grads([0], False)
        for hop in range(1, wide.half):
            row_gather.arrive(hop)
            row_gather.start(hop + 1)
            row_gather.hand(hop)
            row_gather.take(hop)
            near_part(hop)
            near_part(-hop)
        row_gather.arrive(wide.half)
        row_gather.hand(wide.half)
        row_gather.take(wide.half)
        unit(wide.half)
        if not separate:
            down_grads(order, False)
            down_scatter.start(head.half)
        for offset in order:
            grad_terms(offset)
            grad_scatter.hand(offset)
        grad_scatter.merge(order[0])
        grad_scatter.start(wide.half)
        if separate:
            down_grads(order[:-1], True)
            down_scatter.start(head.half)
            down_terms(order[0])
        for hop in range(wide.half - 1, 0, -1):
            grad_scatter.merge(hop)
            grad_scatter.merge(-hop)
            grad_scatter.advance(hop)
        grad_scatter.merge(0)
        input_grads()
    row_gather.finish()
    if not line:
        if not separate:
            for offset in order:
                down_terms(offset)
        out_scatter.merge(order[0])
    for hop in range(head.half - 1, 0, -1):
        down_scatter.advance(hop)
    grad_scatter.arrive()

    def backward_norm(row, gain_sum):
        here = pl.ds(row, 32)
        value = middle[here, :]
        grad = grad_scatter.total(row, 32)
        scale = lax.rsqrt(jnp.mean(value * value, axis=-1, keepdims=True) + EPS)
        scaled = value * scale
        weighted = grad * gain
        mean = jnp.mean(scaled * weighted, axis=-1, keepdims=True)
        total = mgrad_ref[here, :] + scale * (weighted - scaled * mean)
        mgrad_ref[here, :] = total
        back[pl.ds(pl.multiple_of(own_head + row, 32), 32), :] = total.astype(jnp.bfloat16)
        return gain_sum + jnp.sum(grad * scaled, axis=0, keepdims=True)

    gain_out[...] = lax.fori_loop(
        0, tok // 32,
        lambda i, carried: backward_norm(pl.multiple_of(i * 32, 32), carried),
        jnp.zeros((1, width), jnp.float32),
    )
    back_gather.start(1)
    if line:
        for kind in (FAR, OTHER, NEAR):
            out_scatter.relay(kind)
    else:
        out_scatter.start(wide.half)
        for offset in order[1:]:
            out_scatter.merge(offset)
        for hop in range(wide.half - 1, 0, -1):
            out_scatter.advance(hop)
    for hop in range(1, head.half):
        back_gather.step(hop)
    back_gather.arrive(head.half)
    back_gather.finish()
    keep = pltpu.make_async_copy(back, back_any, local_sem.at[4])
    keep.start()
    last = width // emit
    for slot in SIDES:
        for out, any_ref in enumerate((fgate_any, fup_any)):
            stage_copy(last - 2 + slot, out, any_ref, slot).wait()
    owners = gated_ref.shape[1]

    def out_grads(cols):
        hterms[pl.ds(0, owners), cols] = dot_tn(gated_ref[...], back[:, cols]).astype(jnp.bfloat16)

    col_loop(width, 512, out_grads)
    share = pltpu.make_async_copy(hterms.at[pl.ds(0, owners)], owg_any, local_sem.at[11])
    share.start()
    down_scatter.arrive()
    own_down = pl.multiple_of(lax.axis_index("head") * hidden_width, LANES)

    def finish_down(row):
        there = pl.ds(pl.multiple_of(own_down + row, LANES), LANES)
        dterms[there, :] = down_scatter.total(row, LANES).astype(jnp.bfloat16)

    row_loop(hidden_width, LANES, finish_down)
    down_out = pltpu.make_async_copy(
        dterms.at[pl.ds(own_down, hidden_width)], down_any, local_sem.at[14]
    )
    down_out.start()
    out_scatter.arrive()

    def finish_out(row):
        here = pl.ds(row, 32)
        back[here, :] = (middle[here, :] + out_scatter.total(row, 32)).astype(jnp.bfloat16)

    keep.wait()
    row_loop(tok, 32, finish_out)
    result = pltpu.make_async_copy(back.at[pl.ds(0, tok)], out_any, local_sem.at[9])
    result.start()

    for scatter in (grad_scatter, out_scatter, down_scatter):
        scatter.finish()
    result.wait()
    share.wait()
    down_out.wait()


def ffn_block(gated_low, inputs, cotangent, cot_left, ffn_gain, out_w, gate_w, up_w, down_w):
    tok, width = inputs.shape
    head_count, wide_count = lax.axis_size("head"), lax.axis_size("wide")
    chips = wide_count // 2
    hidden_width = gate_w.shape[1]
    low, full = jnp.bfloat16, jnp.float32
    all_rows = wide_count * tok
    back_rows = head_count * tok
    roomy = all_rows * width <= 2 << 20
    shape = jax.ShapeDtypeStruct
    vm = pltpu.VMEM
    return pl.pallas_call(
        ffn_kernel,
        out_shape=(
            shape((tok, width), low),
            shape((tok, width), full),
            shape((1, width), full),
            shape((back_rows, width), low),
            shape((hidden_width, width // head_count), low),
            shape((width, hidden_width), low),
            shape((width, hidden_width), low),
            shape((gated_low.shape[1], width), low),
        ),
        in_specs=[VMEM] * 2 + [ANY] * 7,
        out_specs=(ANY, VMEM, VMEM, ANY, ANY, ANY, ANY, ANY),
        scratch_shapes=[
            vm(out_w.shape, low), vm(gate_w.shape, low), vm(up_w.shape, low),
            vm(down_w.shape, low),
            vm((all_rows, width), low), vm((all_rows, width), low),
            vm((all_rows, hidden_width), low), vm((all_rows, hidden_width), low),
            vm((all_rows, hidden_width), low),
            vm((all_rows if roomy else 16, width), low),
            vm((all_rows if roomy else 16, width), low),
            vm((chips, tok, width), low),
            scatter_into(chips, tok, width),
            vm((chips, tok, width), low),
            scatter_into(chips, tok, width),
            vm((head_count * hidden_width, width // head_count), low),
            into_shape(head_count, hidden_width, width // head_count),
            vm((back_rows, width), low), into_shape(head_count, tok, width),
            vm((tok, width), full), vm((back_rows, width), low),
            DMA((15,)), DMA((wide_count,)),
            *ring_sems(head_count),
            *ring_sems(head_count),
            *ring_sems(chips), *pass_sems(chips),
            *gather_sems(chips),
            *scatter_sems(chips),
            *scatter_sems(chips),
            *ring_sems(head_count),
        ],
        compiler_params=pltpu.CompilerParams(
            collective_id=1, has_side_effects=True, vmem_limit_bytes=VMEM_LIMIT
        ),
        cost_estimate=pl.CostEstimate(
            flops=10 * all_rows * width * hidden_width, bytes_accessed=200 << 20, transcendentals=0
        ),
        name="ffn_block",
    )(
        gated_low, ffn_gain[None], inputs, cotangent, cot_left, out_w, gate_w, up_w, down_w
    )


def turn(values, cosine, sine_tab):
    half = LANES // 2
    lane = lax.broadcasted_iota(jnp.int32, values.shape, 1)
    turned = pltpu.roll(values, half, 1)
    return values * cosine + jnp.where(lane < half, -turned, turned) * sine_tab


def prep(pre_proj, gain, cosine, sine_tab):
    scale = lax.rsqrt(jnp.mean(pre_proj * pre_proj, axis=-1, keepdims=True) + EPS)
    return turn(pre_proj * scale * gain, cosine, sine_tab).astype(jnp.bfloat16)


def front_kernel(
    doc_ref, x_ref, gain_ref, speed_ref, qgain_ref, kgain_ref, wq_any, wk_any, wv_any, wg_any,
    query_ref, qpre_ref, kpre_ref, gpre_ref, cos_ref, sin_ref, normed_any, kv_any,
    wq, wk, wv, wg, normed, kv, local_sem, hs, hr, ks, kr, kps, kpr,
):
    tok, width = x_ref.shape
    kv_width = wk_any.shape[1]
    q_width = wq_any.shape[1]
    wide_count, head_count = lax.axis_size("wide"), lax.axis_size("head")
    head, wide = head_ring(), wide_ring()
    loads = [
        pltpu.make_async_copy(src, dst, local_sem.at[i])
        for i, (src, dst) in enumerate(((wk_any, wk), (wv_any, wv), (wq_any, wq), (wg_any, wg)))
    ]
    for load in loads:
        load.start()
    own = pl.multiple_of(lax.axis_index("head") * tok, tok)
    own_wide = lax.axis_index("wide")

    def norm(row):
        here = pl.ds(row, 32)
        value = x_ref[here, :].astype(jnp.float32)
        scale = lax.rsqrt(jnp.mean(value * value, axis=-1, keepdims=True) + EPS)
        normed[pl.ds(pl.multiple_of(own + row, 32), 32), :] = (
            value * scale * gain_ref[...]
        ).astype(jnp.bfloat16)

    row_loop(tok, 32, norm)
    meet(neighbours(head, wide))
    gather = Gather(
        head, lambda index, start, size: normed.at[pl.ds(index * tok + start, size)], tok, hs, hr
    )
    gather.start(1)
    ends = doc_ends(doc_ref)

    def tables(block):
        here = pl.ds(pl.multiple_of(block * tok, tok), tok)
        first_tok = (block * wide_count + own_wide) * tok
        tokens = lax.broadcasted_iota(jnp.int32, (tok, LANES), 0) + first_tok
        angles = (tokens - first_of(ends, tokens)).astype(jnp.float32) * speed_ref[...]
        cos_ref[here, :] = jnp.cos(angles)
        sin_ref[here, :] = jnp.sin(angles)

    tables(lax.axis_index("head"))

    def kv_gather(offset):
        slot = offset % head_count
        block = head.index(offset)

        def place(index, start, size):
            return kv.at[pl.ds((block * wide_count + index) * tok + start, size)]

        return PairGather(
            wide, place, tok, ks.at[slot], kr.at[slot], kps.at[slot], kpr.at[slot]
        )

    def project(offset):
        block = head.index(offset)
        here = pl.ds(pl.multiple_of(block * tok, tok), tok)
        there = pl.ds(pl.multiple_of((block * wide_count + own_wide) * tok, tok), tok)
        left = normed[here, :]
        cosine, sine_tab = cos_ref[here, :], sin_ref[here, :]
        pre = dot_nn(left, wk[...])
        kpre_ref[here, :] = pre
        for j in range(kv_width // LANES):
            cols = slice(j * LANES, (j + 1) * LANES)
            kv[there, cols] = prep(pre[:, cols], kgain_ref[...], cosine, sine_tab)
        kv[there, kv_width:] = dot_nn(left, wv[...]).astype(jnp.bfloat16)

    def project_rest(offset):
        block = head.index(offset)
        here = pl.ds(pl.multiple_of(block * tok, tok), tok)
        left = normed[here, :]
        cosine, sine_tab = cos_ref[here, :], sin_ref[here, :]
        pre = dot_nn(left, wq[...])
        qpre_ref[here, :] = pre
        for j in range(q_width // LANES):
            cols = slice(j * LANES, (j + 1) * LANES)
            query_ref[here, cols] = prep(pre[:, cols], qgain_ref[...], cosine, sine_tab)
        gpre_ref[here, :] = dot_nn(left, wg[...])

    gathers = {}

    def launch(offset):
        project(offset)
        gathers[offset] = kv_gather(offset)
        gathers[offset].begin()

    def step(offset, hop):
        if hop < wide.half:
            gathers[offset].step(hop)
        else:
            gathers[offset].arrive(hop)
        gathers[offset].hand(hop)

    loads[0].wait()
    loads[1].wait()
    launch(0)
    for offset in range(1, head_count):
        tables(head.index(offset))
    loads[2].wait()
    loads[3].wait()
    project_rest(0)
    done = [0]
    for hop in range(1, head.half + 1):
        if hop < head.half:
            gather.step(hop)
            launch(hop)
            launch(-hop)
            for offset in done:
                step(offset, 1)
            project_rest(hop)
            project_rest(-hop)
            done = [hop, -hop]
        else:
            gather.arrive(hop)
            launch(hop)
            for offset in done:
                step(offset, 1)
            project_rest(hop)
            done = [hop]
    gather.finish()
    keep = pltpu.make_async_copy(normed, normed_any, local_sem.at[4])
    keep.start()
    for offset in done:
        step(offset, 1)
    for hop in range(2, wide.half + 1):
        for offset in gathers:
            step(offset, hop)
    for each in gathers.values():
        for hop in range(wide.half + 1):
            each.take(hop)
    store = pltpu.make_async_copy(kv, kv_any, local_sem.at[5])
    store.start()
    for each in gathers.values():
        each.finish()
    store.wait()
    keep.wait()


def front_block(doc_lengths, inputs, attn_gain, speed, query_gain, key_gain, weights):
    tok, width = inputs.shape
    head_count, wide_count = lax.axis_size("head"), lax.axis_size("wide")
    chips = wide_count // 2
    q_width, kv_width = weights[0].shape[1], weights[1].shape[1]
    rows = head_count * tok
    low, full = jnp.bfloat16, jnp.float32
    shape, vm = jax.ShapeDtypeStruct, pltpu.VMEM
    return pl.pallas_call(
        front_kernel,
        out_shape=(
            shape((rows, q_width), low),
            shape((rows, q_width), full),
            shape((rows, kv_width), full),
            shape((rows, q_width), full),
            shape((rows, LANES), full),
            shape((rows, LANES), full),
            shape((rows, width), low),
            shape((rows * wide_count, 2 * kv_width), low),
        ),
        in_specs=[pl.BlockSpec(memory_space=pltpu.SMEM)] + [VMEM] * 5 + [ANY] * 4,
        out_specs=tuple([VMEM] * 6 + [ANY] * 2),
        scratch_shapes=[
            *[vm(weight.shape, low) for weight in weights],
            vm((rows, width), low),
            vm((rows * wide_count, 2 * kv_width), low),
            DMA((6,)),
            *ring_sems(head_count),
            *[DMA((head_count, *sem.shape)) for sem in [*ring_sems(chips), *pass_sems(chips)]],
        ],
        compiler_params=pltpu.CompilerParams(
            collective_id=3, has_side_effects=True, vmem_limit_bytes=VMEM_LIMIT
        ),
        cost_estimate=pl.CostEstimate(
            flops=2 * rows * width * (2 * q_width + 2 * kv_width), bytes_accessed=100 << 20,
            transcendentals=0,
        ),
        name="front_block",
    )(
        doc_lengths, inputs, attn_gain[None], speed[None], query_gain[None], key_gain[None],
        *weights,
    )


def turn_back(grad, cosine, sine_tab):
    half = LANES // 2
    lane = lax.broadcasted_iota(jnp.int32, grad.shape, 1)
    turned = pltpu.roll(grad * sine_tab, half, 1)
    return grad * cosine + jnp.where(lane < half, turned, -turned)


def unprep(grad, pre_proj, gain, cosine, sine_tab):
    turned = turn_back(grad, cosine, sine_tab)
    scale = lax.rsqrt(jnp.mean(pre_proj * pre_proj, axis=-1, keepdims=True) + EPS)
    scaled = pre_proj * scale
    weighted = turned * gain
    mean = jnp.mean(scaled * weighted, axis=-1, keepdims=True)
    return scale * (weighted - scaled * mean), turned * scaled


def tail_kernel(
    cos_ref, sin_ref, qgain_ref, kgain_ref, gain_ref, ffn_gain_ref,
    dq_any, qpre_any, kpre_any, ggrad_any, x_any, mgrad_any,
    kvp_any, normed_any, wq_any, wk_any, wv_any, wg_any, fgate_any, fup_any,
    igrad_ref, gains_ref, query_out, key_out, value_out, gate_out, fgate_out, fup_out,
    dq_ref, qpre_ref, kpre_ref, ggrad_ref, x_ref, mgrad_ref, kvp, normed, wq, wk, wv, wg, fgate, fup, qlow, klow, vlow, early, late, hterms,
    kv_passed, kv_into, early_passed, early_into, late_passed, late_into, hinto, fgate_into,
    fup_into, gain_slots, local_sem,
    kvs, kvr, kvps, kvpr, es, er, eps, epr, ls, lr, lps, lpr, hs, hr, gs, gr, us, ur, gain_send,
    gain_recv,
):
    tok, width = x_ref.shape
    rows = dq_ref.shape[0]
    wide_count = lax.axis_size("wide")
    head_count = lax.axis_size("head")
    head, wide = head_ring(), wide_ring()
    loads = [
        pltpu.make_async_copy(src, dst, local_sem.at[i])
        for i, (src, dst) in enumerate(
            (
                (kvp_any, kvp), (fgate_any, fgate), (fup_any, fup), (normed_any, normed),
                (wq_any, wq), (wk_any, wk), (wv_any, wv), (wg_any, wg),
            )
        )
    ]
    more = [
        pltpu.make_async_copy(src, dst, local_sem.at[11 + i])
        for i, (src, dst) in enumerate(
            (
                (dq_any, dq_ref), (qpre_any, qpre_ref), (ggrad_any, ggrad_ref),
                (kpre_any, kpre_ref), (x_any, x_ref), (mgrad_any, mgrad_ref),
            )
        )
    ]
    start_all(loads[:1] + more[:3] + loads[1:] + more[3:])
    meet(everyone(head, wide))
    kv_width = wk.shape[1]
    q_width = wq.shape[1]
    block = normed.shape[1] // wide_count
    ffn_rows = fgate.shape[0] // head_count
    kv_scatter = PairScatter(wide, kvp, rows, kv_passed, kv_into, kvs, kvr, kvps, kvpr)
    early_scatter = PairScatter(wide, early, block, early_passed, early_into, es, er, eps, epr)
    late_scatter = PairScatter(wide, late, block, late_passed, late_into, ls, lr, lps, lpr)
    head_scatter = Scatter(head, lambda index: (hterms, index * tok), tok, hinto, hs, hr)
    gate_scatter = Scatter(
        head, lambda index: (fgate, index * ffn_rows), ffn_rows, fgate_into, gs, gr
    )
    up_scatter = Scatter(head, lambda index: (fup, index * ffn_rows), ffn_rows, fup_into, us, ur)
    order = offsets(wide)

    loads[0].wait()
    for offset in order:
        kv_scatter.hand(offset)
    loads[1].wait()
    gate_scatter.start(head.half)
    gate_scatter.start_free()
    loads[2].wait()
    up_scatter.start(head.half)
    up_scatter.start_free()

    for load in more[:3]:
        load.wait()
    chunk = 128

    def query_back(row, total):
        here = pl.ds(row, chunk)
        for j in range(q_width // LANES):
            cols = slice(j * LANES, (j + 1) * LANES)
            value, terms = unprep(
                dq_ref[here, cols], qpre_ref[here, cols], qgain_ref[...], cos_ref[here, :],
                sin_ref[here, :],
            )
            qlow[here, cols] = value.astype(jnp.bfloat16)
            total = total + jnp.sum(terms, axis=0, keepdims=True)
        return total

    def over_rows(count, body, start):
        return lax.fori_loop(
            0, count // chunk, lambda i, carried: body(pl.multiple_of(i * chunk, chunk), carried),
            start,
        )

    qgain_sum = over_rows(rows, query_back, jnp.zeros((1, LANES), jnp.float32))

    kv_scatter.merge(order[0])
    kv_scatter.start(wide.half)
    for offset in order[1:]:
        kv_scatter.merge(offset)
    kv_scatter.start_free()
    loads[3].wait()

    def early_part(offset):
        index = wide.index(offset)

        @pl.loop(0, 2)
        def _(core):
            target = 2 * index + core
            cols = pl.ds(pl.multiple_of(target * block, block), block)
            there = pl.ds(pl.multiple_of(target * block, block), block)
            left = normed[:, cols]
            early[there, :q_width] = dot_tn(left, qlow[...]).astype(jnp.bfloat16)
            early[there, q_width:] = dot_tn(left, ggrad_ref[...]).astype(jnp.bfloat16)

    for offset in order:
        early_part(offset)
        early_scatter.hand(offset)
    early_scatter.merge(order[0])
    for hop in range(wide.half - 1, 0, -1):
        kv_scatter.advance(hop)
    early_scatter.start(wide.half)
    for offset in order[1:]:
        early_scatter.merge(offset)
    early_scatter.start_free()
    for hop in range(head.half - 1, 0, -1):
        gate_scatter.advance(hop)
        up_scatter.advance(hop)
    for load in loads[4:] + more[3:]:
        load.wait()
    kv_scatter.arrive()
    for hop in range(wide.half - 1, 0, -1):
        early_scatter.advance(hop)

    def key_back(row, total):
        here = pl.ds(row, chunk)
        both = kv_scatter.total(row, chunk)
        for j in range(kv_width // LANES):
            cols = slice(j * LANES, (j + 1) * LANES)
            value, terms = unprep(
                both[:, cols], kpre_ref[here, cols], kgain_ref[...], cos_ref[here, :],
                sin_ref[here, :],
            )
            klow[here, cols] = value.astype(jnp.bfloat16)
            total = total + jnp.sum(terms, axis=0, keepdims=True)
        vlow[here, :] = both[:, kv_width:].astype(jnp.bfloat16)
        return total

    kgain_sum = over_rows(rows, key_back, jnp.zeros((1, LANES), jnp.float32))

    def head_part(offset):
        here = pl.ds(pl.multiple_of(head.index(offset) * tok, tok), tok)

        @pl.loop(0, width // 256)
        def _(i):
            cols = pl.ds(pl.multiple_of(i * 256, 256), 256)
            value = dot_nt(qlow[here, :], wq[cols, :]) + dot_nt(ggrad_ref[here, :], wg[cols, :])
            value += dot_nt(klow[here, :], wk[cols, :]) + dot_nt(vlow[here, :], wv[cols, :])
            hterms[here, cols] = value.astype(jnp.bfloat16)

    head_part(head.half)
    head_scatter.start(head.half)

    def late_part(offset):
        index = wide.index(offset)

        @pl.loop(0, 2)
        def _(core):
            target = 2 * index + core
            cols = pl.ds(pl.multiple_of(target * block, block), block)
            left = normed[:, cols]
            late[cols, :kv_width] = dot_tn(left, klow[...]).astype(jnp.bfloat16)
            late[cols, kv_width:] = dot_tn(left, vlow[...]).astype(jnp.bfloat16)

    for offset in order:
        late_part(offset)
        late_scatter.hand(offset)
    late_scatter.merge(order[0])
    late_scatter.start(wide.half)
    for offset in order[1:]:
        late_scatter.merge(offset)
    late_scatter.start_free()
    for hop in range(head.half - 1, 0, -1):
        head_part(hop)
        head_part(-hop)
        head_scatter.advance(hop)
    head_part(0)
    for hop in range(wide.half - 1, 0, -1):
        late_scatter.advance(hop)

    gate_scatter.arrive()
    up_scatter.arrive()
    own_ffn = pl.multiple_of(lax.axis_index("head") * ffn_rows, ffn_rows)
    pending = []
    for scatter, ref, out in ((gate_scatter, fgate, fgate_out), (up_scatter, fup, fup_out)):

        def finish_ffn(row, scatter=scatter, ref=ref):
            there = pl.ds(pl.multiple_of(own_ffn + row, 64), 64)
            ref[there, :] = scatter.total(row, 64).astype(jnp.bfloat16)

        row_loop(ffn_rows, 64, finish_ffn)
        pending.append(
            pltpu.make_async_copy(
                ref.at[pl.ds(own_ffn, ffn_rows)], out, local_sem.at[9 + len(pending)]
            )
        )
        pending[-1].start()

    head_scatter.arrive()
    gain = gain_ref[...]

    def input_back(row, total):
        here = pl.ds(row, 32)
        value = x_ref[here, :].astype(jnp.float32)
        grad = head_scatter.total(row, 32)
        scale = lax.rsqrt(jnp.mean(value * value, axis=-1, keepdims=True) + EPS)
        scaled = value * scale
        weighted = grad * gain
        mean = jnp.mean(scaled * weighted, axis=-1, keepdims=True)
        igrad_ref[here, :] = mgrad_ref[here, :] + scale * (weighted - scaled * mean)
        return total + jnp.sum(grad * scaled, axis=0, keepdims=True)

    gain_sum = lax.fori_loop(
        0, tok // 32, lambda i, carried: input_back(pl.multiple_of(i * 32, 32), carried),
        jnp.zeros((1, width), jnp.float32),
    )
    chips = wide.size
    pair_slot, chip_slot = 0, 2
    head_slot = 2 + chips
    mine = gain_slots.at[pair_slot]
    mine[...] = jnp.zeros(mine.shape, jnp.float32)
    mine[0:1, :] = gain_sum
    mine[1:2, :] = ffn_gain_ref[...]
    mine[2:3, 0:LANES] = qgain_sum
    mine[3:4, 0:LANES] = kgain_sum
    swap = remote(
        mine, gain_slots.at[1], gain_send.at[0], gain_recv.at[0], wide.sibling
    )
    swap.start()
    swap.wait_recv()

    def spread(ring, own, base, sem):
        here = gain_slots.at[base + own]
        copies = [
            remote(here, here, gain_send.at[sem + d], gain_recv.at[sem + d], ring.device(d))
            for d in range(1, ring.size)
        ]
        for copy in copies:
            copy.start()
        for copy in copies:
            copy.wait_recv()
        return copies

    own_chip = wide.index(0)
    gain_slots[chip_slot + own_chip] = gain_slots[0] + gain_slots[1]
    sent = [swap] + spread(wide, own_chip, chip_slot, 0)
    total = gain_slots[chip_slot]
    for i in range(1, chips):
        total = total + gain_slots[chip_slot + i]
    own_head = lax.axis_index("head")
    gain_slots[head_slot + own_head] = total
    sent += spread(head, own_head, head_slot, chips - 1)
    total = gain_slots[head_slot]
    for i in range(1, head_count):
        total = total + gain_slots[head_slot + i]
    gains_ref[...] = total

    early_scatter.arrive()

    def early_out(row):
        here = pl.ds(row, 32)
        both = early_scatter.total(row, 32)
        query_out[here, :] = both[:, :q_width].astype(jnp.bfloat16)
        gate_out[here, :] = both[:, q_width:].astype(jnp.bfloat16)

    row_loop(block, 32, early_out)
    late_scatter.arrive()

    def late_out(row):
        here = pl.ds(row, 32)
        both = late_scatter.total(row, 32)
        key_out[here, :] = both[:, :kv_width].astype(jnp.bfloat16)
        value_out[here, :] = both[:, kv_width:].astype(jnp.bfloat16)

    row_loop(block, 32, late_out)
    for scatter in (
        kv_scatter, early_scatter, late_scatter, head_scatter, gate_scatter, up_scatter
    ):
        scatter.finish()
    for copy in sent:
        copy.wait_send()
    for copy in pending:
        copy.wait()


def tail_block(
    dq, kv_parts, query_pre, key_pre, gate_grad, cosine, sine_tab, query_gain, key_gain, inputs,
    middle_grad, attn_gain, ffn_gain_part, normed, weights, fgate, fup,
):
    tok, width = inputs.shape
    head_count, wide_count = lax.axis_size("head"), lax.axis_size("wide")
    chips = wide_count // 2
    rows, q_width = dq.shape
    kv_width = key_pre.shape[1]
    block = width // wide_count
    hidden_width = fgate.shape[1]
    ffn_rows = width // head_count
    low, full = jnp.bfloat16, jnp.float32
    shape, vm = jax.ShapeDtypeStruct, pltpu.VMEM
    early_width = 2 * q_width
    pair = [*ring_sems(chips), DMA((chips,)), DMA((chips,))]
    peers = chips + head_count
    return pl.pallas_call(
        tail_kernel,
        out_shape=(
            shape((tok, width), full),
            shape((8, width), full),
            shape((block, q_width), low),
            shape((block, kv_width), low),
            shape((block, kv_width), low),
            shape((block, q_width), low),
            shape((ffn_rows, hidden_width), low),
            shape((ffn_rows, hidden_width), low),
        ),
        in_specs=[VMEM] * 6 + [ANY] * 14,
        out_specs=tuple([VMEM] * 6 + [ANY] * 2),
        scratch_shapes=[
            vm(dq.shape, full), vm(query_pre.shape, full), vm(key_pre.shape, full),
            vm(gate_grad.shape, low), vm(inputs.shape, low), vm(middle_grad.shape, full),
            vm(kv_parts.shape, low), vm(normed.shape, low),
            *[vm(weight.shape, low) for weight in weights],
            vm(fgate.shape, low), vm(fup.shape, low),
            vm((rows, q_width), low), vm((rows, kv_width), low), vm((rows, kv_width), low),
            vm((width, early_width), low), vm((width, 2 * kv_width), low),
            vm((head_count * tok, width), low),
            vm((chips, rows, 2 * kv_width), low), into_shape(chips, rows, 2 * kv_width),
            vm((chips, block, early_width), low), into_shape(chips, block, early_width),
            vm((chips, block, 2 * kv_width), low), into_shape(chips, block, 2 * kv_width),
            into_shape(head_count, tok, width),
            into_shape(head_count, ffn_rows, hidden_width),
            into_shape(head_count, ffn_rows, hidden_width),
            vm((2 + chips + head_count, 8, width), full),
            DMA((17,)),
            *pair, *pair, *pair,
            *ring_sems(head_count), *ring_sems(head_count), *ring_sems(head_count),
            DMA((peers,)), DMA((peers,)),
        ],
        compiler_params=pltpu.CompilerParams(
            collective_id=2, has_side_effects=True, vmem_limit_bytes=VMEM_LIMIT
        ),
        cost_estimate=pl.CostEstimate(
            flops=20 * rows * width * q_width, bytes_accessed=300 << 20, transcendentals=0
        ),
        name="tail_block",
    )(
        cosine, sine_tab, query_gain[None], key_gain[None], attn_gain[None], ffn_gain_part,
        dq, query_pre, key_pre, gate_grad, inputs, middle_grad,
        kv_parts, normed, *weights, fgate, fup,
    )


def finish_kernel(count, *refs):
    sources, gains_any = refs[:count], refs[count]
    results = refs[count + 1 : 2 * count + 1]
    gain_outs = refs[2 * count + 1 : 2 * count + 5]
    landed = refs[2 * count + 5 : 3 * count + 5]
    *spare, gains, in_sem, out_sem = refs[3 * count + 5 :]
    loads = [
        pltpu.make_async_copy(sources[i], landed[i], in_sem.at[i]) for i in range(count)
    ]
    last = pltpu.make_async_copy(gains_any, gains, in_sem.at[count])
    start_all([*loads, last])
    stores = []
    for i in range(count):
        ready = landed[i]
        loads[i].wait()
        if sources[i].dtype != results[i].dtype:
            ready = spare.pop(0)
            rows = ready.shape[0]
            step = min(rows, 128)

            def convert(row, src=landed[i], dst=ready, step=step):
                here = pl.ds(row, step)
                dst[here, :] = src[here, :].astype(jnp.float32)

            row_loop(rows, step, convert)
        stores.append(pltpu.make_async_copy(ready, results[i], out_sem.at[i]))
        stores[-1].start()
    last.wait()
    for row, out in enumerate(gain_outs):
        out[...] = gains[row : row + 1, : out.shape[1]]
    for store in stores:
        store.wait()


def finish_block(arrays, dtypes, gains, head_width):
    shape, vm = jax.ShapeDtypeStruct, pltpu.VMEM
    width = gains.shape[1]
    sizes = (width, width, head_width, head_width)
    outs = pl.pallas_call(
        functools.partial(finish_kernel, len(arrays)),
        out_shape=tuple(shape(a.shape, d) for a, d in zip(arrays, dtypes))
        + tuple(shape((1, size), jnp.float32) for size in sizes),
        in_specs=[ANY] * (len(arrays) + 1),
        out_specs=tuple([ANY] * len(arrays) + [VMEM] * 4),
        scratch_shapes=[
            *[vm(a.shape, a.dtype) for a in arrays],
            *[vm(a.shape, d) for a, d in zip(arrays, dtypes) if a.dtype != d],
            vm(gains.shape, jnp.float32),
            DMA((len(arrays) + 1,)), DMA((len(arrays),)),
        ],
        compiler_params=pltpu.CompilerParams(vmem_limit_bytes=VMEM_LIMIT),
        name="finish_block",
    )(*arrays, gains)
    return outs[: len(arrays)], [gain.reshape(-1) for gain in outs[len(arrays) :]]


def shards(
    inputs,
    attn_gain,
    query_weight,
    key_projection,
    value_projection,
    attn_gate_weight,
    output_weight,
    query_gain,
    key_gain,
    ffn_gain,
    ffn_gate_weight,
    ffn_up_weight,
    ffn_down_weight,
    doc_lengths,
    cotangent,
):
    head_width = query_gain.shape[0]
    cot_left = lax.all_gather(
        cotangent[: cotangent.shape[0] // 4], "wide", axis=0, tiled=True
    )
    weights = (query_weight, key_projection, value_projection, attn_gate_weight)
    query_low, query_pre, key_pre, gate_pre, cosine, sine_tab, gathered, kv_all = front_block(
        doc_lengths, inputs, attn_gain, rotation_speed(head_width), query_gain, key_gain, weights
    )
    attended, inverse, gated_low = attention_forward(doc_lengths, query_low, kv_all, gate_pre)
    (
        outputs,
        middle_grad,
        ffn_gain_part,
        back_rows,
        ffn_down_grad,
        gate_wgrad,
        up_wgrad,
        out_wgrad,
    ) = ffn_block(
        gated_low,
        inputs,
        cotangent,
        cot_left,
        ffn_gain,
        output_weight,
        ffn_gate_weight,
        ffn_up_weight,
        ffn_down_weight,
    )
    output_grad = lax.psum_scatter(out_wgrad, "wide", scatter_dimension=1, tiled=True)
    query_rot_grad, kv_parts, gate_pre_grad = attention_backward(
        doc_lengths, query_low, attended, inverse, gate_pre, kv_all, back_rows, output_weight
    )
    kv_parts = kv_parts.reshape(-1, kv_parts.shape[2])
    (
        input_grad,
        gains,
        query_grad,
        key_grad,
        value_grad,
        attn_gate_grad,
        ffn_gate_grad,
        ffn_up_grad,
    ) = tail_block(
        query_rot_grad,
        kv_parts,
        query_pre,
        key_pre,
        gate_pre_grad,
        cosine,
        sine_tab,
        query_gain,
        key_gain,
        inputs,
        middle_grad,
        attn_gain,
        ffn_gain_part,
        gathered,
        weights,
        gate_wgrad,
        up_wgrad,
    )
    full = jnp.float32
    results, gain_grads = finish_block(
        [
            outputs,
            input_grad,
            query_grad,
            key_grad,
            value_grad,
            attn_gate_grad,
            output_grad,
            ffn_gate_grad,
            ffn_up_grad,
            ffn_down_grad,
        ],
        [jnp.bfloat16] + [full] * 9,
        gains,
        head_width,
    )
    outputs, input_grad, query_grad, key_grad, value_grad = results[:5]
    attn_gate_grad, output_grad, ffn_gate_grad, ffn_up_grad, ffn_down_grad = results[5:]
    attn_gain_grad, ffn_gain_grad, query_gain_grad, key_gain_grad = gain_grads
    return (
        outputs,
        input_grad,
        attn_gain_grad,
        query_grad,
        key_grad,
        value_grad,
        attn_gate_grad,
        output_grad,
        query_gain_grad,
        key_gain_grad,
        ffn_gain_grad,
        ffn_gate_grad,
        ffn_up_grad,
        ffn_down_grad,
    )


def solution(mesh):
    placed = (
        P(("head", "wide"), None),
        P(),
        P(None, "head"),
        P(None, "head"),
        P(None, "head"),
        P(None, "head"),
        P("head", None),
        P(),
        P(),
        P(),
        P(None, "wide"),
        P(None, "wide"),
        P("wide", None),
        P(),
        P(("head", "wide"), None),
    )
    return jax.shard_map(
        shards,
        mesh=mesh,
        in_specs=placed,
        out_specs=(
            P(("head", "wide"), None),
            P(("head", "wide"), None),
            P(),
            P("wide", "head"),
            P("wide", "head"),
            P("wide", "head"),
            P("wide", "head"),
            P("head", "wide"),
            P(),
            P(),
            P(),
            P("head", "wide"),
            P("head", "wide"),
            P("wide", "head"),
        ),
        check_vma=False,
    )
```
